32 devices in a mesh: dp: 8 (over z, core), seq: 4 (over y, x).
Axes of the slice: x: 2, y: 2, z: 4, core: 2. Of those that a mesh axis runs over, the one named last changes fastest.
Arguments:
- tokens: bfloat16 [8, 4096, 1024], P('dp', 'seq'), may hold values from -6 to 6
- cotangent: bfloat16 [8, 4096, 1024], P('dp', 'seq'), may hold values from -6 to 6
- lengths: int32 [8], P('dp'), may hold values from 512 to 4096, as said below
- norm_one: float32 [1024], replicated, may hold values from 0.5 to 1.5
- w_query: bfloat16 [1024, 512], replicated, may hold values from -0.1875 to 0.1875
- w_key: bfloat16 [1024, 128], replicated, may hold values from -0.1875 to 0.1875
- w_value: bfloat16 [1024, 128], replicated, may hold values from -0.1875 to 0.1875
- w_gatez: bfloat16 [1024, 1536], replicated, may hold values from -0.1875 to 0.1875
- w_conv_in: bfloat16 [1024, 1792], replicated, may hold values from -0.1875 to 0.1875
- w_step: bfloat16 [1024, 24], replicated, may hold values from -0.1875 to 0.1875
- conv_weight: float32 [4, 1792], replicated, may hold values from -3 to 3
- conv_bias: float32 [1792], replicated, may hold values from -3 to 3
- step_bias: float32 [24], replicated, may hold values from -2 to 0
- decay_log: float32 [24], replicated, may hold values from -12 to 0
- skip_gain: float32 [24], replicated, may hold values from 0.5 to 1.5
- gated_gain: float32 [1536], replicated, may hold values from 0.5 to 1.5
- w_attn_out: bfloat16 [512, 1024], replicated, may hold values from -1 to 1
- w_mix_out: bfloat16 [1536, 1024], replicated, may hold values from -0.15625 to 0.15625
- norm_two: float32 [1024], replicated, may hold values from 0.5 to 1.5
- w_gate: bfloat16 [1024, 2048], replicated, may hold values from -0.1875 to 0.1875
- w_up: bfloat16 [1024, 2048], replicated, may hold values from -0.1875 to 0.1875
- w_down: bfloat16 [2048, 1024], replicated, may hold values from -0.125 to 0.125
Outputs:
- output: bfloat16 [8, 4096, 1024], P('dp', 'seq')
- grad_tokens: float32 [8, 4096, 1024], P('dp', 'seq')
- grad_norm_one: float32 [1024], P('seq')
- grad_w_query: float32 [1024, 512], P('seq')
- grad_w_key: float32 [1024, 128], P('seq')
- grad_w_value: float32 [1024, 128], P('seq')
- grad_w_gatez: float32 [1024, 1536], P('seq')
- grad_w_conv_in: float32 [1024, 1792], P('seq')
- grad_w_step: float32 [1024, 24], P('seq')
- grad_conv_weight: float32 [4, 1792], replicated
- grad_conv_bias: float32 [1792], replicated
- grad_step_bias: float32 [24], replicated
- grad_decay_log: float32 [24], replicated
- grad_skip_gain: float32 [24], replicated
- grad_gated_gain: float32 [1536], P('seq')
- grad_w_attn_out: float32 [512, 1024], P('seq')
- grad_w_mix_out: float32 [1536, 1024], P('seq')
- grad_norm_two: float32 [1024], P('seq')
- grad_w_gate: float32 [1024, 2048], P('seq')
- grad_w_up: float32 [1024, 2048], P('seq')
- grad_w_down: float32 [2048, 1024], P('seq')
The draws below stay inside these ranges and needn't reach their ends.
Inputs may be any that keep to these rules, and one draw needn't show every extreme that they name: `lengths`: in every group of 1 sequence of one index of dp, one sequence, drawn from the seed, has length 4096; the others are drawn evenly.
All inputs are finite; a program needn't handle non-finite values.
Results may differ from the reference program's by a relative error of at most 0.02.
Values may be sent and summed in bfloat16 or wider, within the bound.
No kernel may reach another device: no remote copies, remote signals or barrier semaphores. Data moves between devices by JAX's collectives and lax.ppermute only.
A program may use at most 576 MiB of HBM per device.

```python
import math
import jax
import jax.numpy as jnp
from jax import lax

D = 1024
HEADS = 8
KV_HEADS = 2
HEAD = 64
SSM_HEADS = 24
SSM_HEAD = 64
STATE = 128
CONV = 4
FF = 2048
SPAN = 1024
SEQS = 1
LEN = 4096
BATCH = 8


def draw_lengths(key, part):
    key = jax.random.fold_in(key, 11)
    key_one, key_two = jax.random.split(key)
    uniform_len = jax.random.randint(key_one, (BATCH,), LEN // 8, LEN + 1)
    chosen = jax.random.randint(key_two, (BATCH // SEQS,), 0, SEQS)
    position = jnp.arange(BATCH)
    full_row = position % SEQS == jnp.repeat(chosen, SEQS)
    return jnp.where(full_row, LEN, uniform_len).astype(jnp.int32)


def draw_decay_log(key, part):
    key = jax.random.fold_in(key, 23)
    key_one, key_two, key_three = jax.random.split(key, 3)
    slow_rate = jnp.log(jax.random.uniform(key_one, (SSM_HEADS,), jnp.float32, 1.0, 4.0) / LEN)
    fast_rate = jnp.log(jax.random.uniform(key_two, (SSM_HEADS,), jnp.float32, 0.05, 0.12))
    slow_share = 0.5
    is_slow = jax.random.bernoulli(key_three, slow_share, (SSM_HEADS,))
    return jnp.where(is_slow, slow_rate, fast_rate).astype(jnp.float32)


def shard_levels(stream_key, dims, cuts, least, top_value):
    def one(axis_at, parts):
        steps = jax.random.uniform(jax.random.fold_in(jax.random.fold_in(stream_key, 6), axis_at), (parts,), jnp.float32, least / len(cuts), top_value / len(cuts))
        return jnp.repeat(jnp.exp(steps), dims[axis_at] // parts).reshape((-1,) + (1,) * (len(dims) - axis_at - 1))

    level = one(*cuts[0])
    for cut in cuts[1:]:
        level = level * one(*cut)
    return level


def centred(key, dims, deviation, reach, pieces=(), held_as=jnp.bfloat16):
    drawn = deviation * jax.random.normal(key, dims, jnp.float32)
    if pieces:
        drawn = drawn * shard_levels(key, dims, pieces, -0.22, 0.18)
    return jnp.clip(drawn, -reach, reach).astype(held_as)


def setup_inputs(seed: int = 0) -> dict:
    arg_keys = jax.random.split(jax.random.key(seed), 23)
    tokens = centred(arg_keys[0], (BATCH, LEN, D), 1.0, 6.0, ((0, 8), (1, 4)))
    cotangent = centred(arg_keys[1], (BATCH, LEN, D), 1.0, 6.0, ((0, 8), (1, 4)))
    lengths = draw_lengths(jax.random.fold_in(arg_keys[22], 71), 0)
    norm_one = jnp.clip(1.0 + 0.1 * jax.random.normal(arg_keys[3], (D,), jnp.float32), 0.5, 1.5)
    w_query = centred(arg_keys[4], (D, HEADS * HEAD), D ** -0.5, 0.1875)
    w_key = centred(arg_keys[5], (D, KV_HEADS * HEAD), D ** -0.5, 0.1875)
    w_value = centred(arg_keys[6], (D, KV_HEADS * HEAD), D ** -0.5, 0.1875)
    w_gatez = centred(arg_keys[7], (D, SSM_HEADS * SSM_HEAD), D ** -0.5, 0.1875)
    w_conv_in = centred(arg_keys[8], (D, SSM_HEADS * SSM_HEAD + 2 * STATE), D ** -0.5, 0.1875)
    w_step = centred(arg_keys[9], (D, SSM_HEADS), D ** -0.5, 0.1875)
    conv_weight = centred(arg_keys[10], (CONV, SSM_HEADS * SSM_HEAD + 2 * STATE), 0.5, 3.0, (), jnp.float32)
    conv_bias = centred(arg_keys[11], (SSM_HEADS * SSM_HEAD + 2 * STATE,), 0.3, 3.0, (), jnp.float32)
    step_bias = jnp.clip(jax.random.uniform(arg_keys[12], (SSM_HEADS,), jnp.float32, -2.0, 0.0), -2.0, 0.0)
    decay_log = draw_decay_log(jax.random.fold_in(arg_keys[22], 71), 0)
    skip_gain = jnp.clip(jax.random.uniform(arg_keys[14], (SSM_HEADS,), jnp.float32, 0.5, 1.5), 0.5, 1.5)
    gated_gain = jnp.clip(1.0 + 0.1 * jax.random.normal(arg_keys[15], (SSM_HEADS * SSM_HEAD,), jnp.float32), 0.5, 1.5)
    w_attn_out = centred(arg_keys[16], (HEADS * HEAD, D), (HEADS * HEAD // 16) ** -0.5, 1.0)
    w_mix_out = centred(arg_keys[17], (SSM_HEADS * SSM_HEAD, D), (SSM_HEADS * SSM_HEAD) ** -0.5, 0.15625)
    norm_two = jnp.clip(1.0 + 0.1 * jax.random.normal(arg_keys[18], (D,), jnp.float32), 0.5, 1.5)
    w_gate = centred(arg_keys[19], (D, FF), D ** -0.5, 0.1875)
    w_up = centred(arg_keys[20], (D, FF), D ** -0.5, 0.1875)
    w_down = centred(arg_keys[21], (FF, D), FF ** -0.5, 0.125)
    return dict(tokens=tokens, cotangent=cotangent, lengths=lengths, norm_one=norm_one, w_query=w_query, w_key=w_key, w_value=w_value, w_gatez=w_gatez, w_conv_in=w_conv_in, w_step=w_step, conv_weight=conv_weight, conv_bias=conv_bias, step_bias=step_bias, decay_log=decay_log, skip_gain=skip_gain, gated_gain=gated_gain, w_attn_out=w_attn_out, w_mix_out=w_mix_out, norm_two=norm_two, w_gate=w_gate, w_up=w_up, w_down=w_down)


@jax.custom_vjp
def low(v):
    return lax.optimization_barrier(v.astype(jnp.bfloat16)).astype(jnp.float32)

@jax.custom_vjp
def low_back(v):
    return v

def low_keep(v):
    return (low(v), None)

def low_pass(kept, grad):
    return (grad,)

def back_keep(v):
    return (v, None)

def back_low(kept, grad):
    return (low(grad),)
low.defvjp(low_keep, low_pass)
low_back.defvjp(back_keep, back_low)
highest = lax.Precision.HIGHEST
epsilon = 1e-05
rope_base = 100000000000.0
lowest_score = -1e+30

def matmul(left, right):
    return jnp.dot(left, right, precision=highest, preferred_element_type=jnp.float32)

def normed(value, gain):
    return value * lax.rsqrt(lax.optimization_barrier(jnp.mean(value * value, -1, keepdims=True)) + epsilon) * gain

def gated_norm(mixed, gatez, gain):
    return normed(mixed * jax.nn.silu(gatez), gain)

def rope_tables(positions, head_size):
    inverse = 1.0 / rope_base ** (jnp.arange(0, head_size, 2).astype(jnp.float32) / head_size)
    angles = positions.astype(jnp.float32)[:, None] * inverse[None, :]
    return (jnp.cos(angles)[:, None, :], jnp.sin(angles)[:, None, :])

def rotate(value, cosine, sine):
    half_size = value.shape[-1] // 2
    former, latter = (value[..., :half_size], value[..., half_size:])
    return jnp.concatenate([former * cosine - latter * sine, latter * cosine + former * sine], -1)

def convolve(extended, conv_weight, conv_bias):
    taps = conv_weight.shape[0]
    rows_here = extended.shape[1] - taps + 1
    summed = conv_bias
    for offset in range(taps):
        summed = summed + conv_weight[offset] * extended[:, offset:offset + rows_here]
    return jax.nn.silu(summed)

def lower_ones(rows_here):
    return (jnp.arange(rows_here)[None, :] <= jnp.arange(rows_here)[:, None]).astype(jnp.float32)

def span_terms(ssm_in, in_keys, steps, decay_log):
    lower_tri = lower_ones(steps.shape[1])
    log_decay = steps * -jnp.exp(decay_log)
    cumulative = jnp.einsum('tu,suh->sth', lower_tri, log_decay, precision=highest)
    final_log = cumulative[:, -1]
    weights = jnp.exp(final_log[:, None] - cumulative) * steps
    state_part = jnp.einsum('suh,suhp,sun->shpn', weights, ssm_in, in_keys, precision=highest)
    return (state_part, jnp.exp(final_log))

def span_out(ssm_in, in_keys, in_queries, steps, decay_log, skip_gain, state_in):
    lower_tri = lower_ones(steps.shape[1])
    log_decay = steps * -jnp.exp(decay_log)
    cumulative = jnp.einsum('tu,suh->sth', lower_tri, log_decay, precision=highest)
    differ = cumulative[:, :, None, :] - cumulative[:, None, :, :]
    mixing = jnp.exp(jnp.where(lower_tri[None, :, :, None] > 0, differ, lowest_score)) * steps[:, None, :, :]
    intersection = jnp.einsum('stn,sun->stu', in_queries, in_keys, precision=highest)
    combined = intersection[..., None] * mixing
    inner = jnp.einsum('stuh,suhp->sthp', combined, ssm_in, precision=highest)
    carried = jnp.einsum('stn,shpn->sthp', in_queries, state_in, precision=highest) * jnp.exp(cumulative)[..., None]
    return inner + carried + skip_gain[:, None] * ssm_in

def recurrence(ssm_in, in_keys, in_queries, steps, decay_log, skip_gain):
    groups, rows_all = (steps.shape[0], steps.shape[1])
    span_count = rows_all // SPAN

    def split_rows(value):
        return jnp.moveaxis(value.reshape((groups, span_count, SPAN) + value.shape[2:]), 1, 0)

    def advance(state, packed):
        piece_in, piece_keys, piece_queries, piece_steps = packed
        mixed = span_out(piece_in, piece_keys, piece_queries, piece_steps, decay_log, skip_gain, state)
        state_part, totals = span_terms(piece_in, piece_keys, piece_steps, decay_log)
        return (totals[:, :, None, None] * state + state_part, mixed)
    start_state = jnp.zeros((groups, SSM_HEADS, SSM_HEAD, STATE), ssm_in.dtype)
    packed = (split_rows(ssm_in), split_rows(in_keys), split_rows(in_queries), split_rows(steps))
    unused, mixed = lax.scan(jax.checkpoint(advance), start_state, packed)
    return jnp.moveaxis(mixed, 0, 1).reshape(ssm_in.shape)

def attention(queries, keys_rot, values_low, lengths):
    groups, rows_all = (keys_rot.shape[0], keys_rot.shape[1])
    block_rows = min(512, rows_all)
    block_count = rows_all // block_rows
    grouped = HEADS // KV_HEADS
    blocks = jnp.moveaxis(queries.reshape(groups, block_count, block_rows, KV_HEADS, grouped, HEAD), 1, 0)
    key_pos = jnp.arange(rows_all)
    live_keys = key_pos[None, :] < lengths[:, None]

    def one_block(packed):
        query_part, first_pos = packed
        scores = low_back(jnp.einsum('scjqd,srjd->scjqr', query_part, keys_rot, precision=highest) * 0.125)
        query_pos = first_pos + jnp.arange(block_rows)
        allowed = (key_pos[None, :] <= query_pos[:, None])[None] & live_keys[:, None, :]
        scores = jnp.where(allowed[:, :, None, None, :], scores, lowest_score)
        probs = jax.nn.softmax(scores, axis=-1)
        return jnp.einsum('scjqr,srjd->scjqd', probs, values_low, precision=highest)
    results = lax.map(jax.checkpoint(one_block), (blocks, jnp.arange(block_count) * block_rows))
    return jnp.moveaxis(results, 0, 1).reshape(groups, rows_all, HEADS * HEAD)

def layer(tokens, params, lengths):
    norm_one, w_query, w_key, w_value, w_gatez, w_conv_in, w_step, conv_weight, conv_bias, step_bias, decay_log, skip_gain, gated_gain, w_attn_out, w_mix_out, norm_two, w_gate, w_up, w_down = params
    groups, rows_all = (tokens.shape[0], tokens.shape[1])
    live = (jnp.arange(rows_all)[None, :] < lengths[:, None]).astype(tokens.dtype)[..., None]
    cosine, sine = rope_tables(jnp.arange(rows_all), HEAD)
    hidden = low(normed(tokens, norm_one))
    query_lin = low_back(matmul(hidden, w_query))
    key_lin = low_back(matmul(hidden, w_key))
    values_low = low(low_back(matmul(hidden, w_value))).reshape(groups, rows_all, KV_HEADS, HEAD)
    queries = low(rotate(query_lin.reshape(groups, rows_all, HEADS, HEAD), cosine, sine))
    queries = queries.reshape(groups, rows_all, KV_HEADS, HEADS // KV_HEADS, HEAD)
    keys_rot = low(rotate(key_lin.reshape(groups, rows_all, KV_HEADS, HEAD), cosine, sine))
    attn_low = low_back(low(attention(queries, keys_rot, values_low, lengths)))
    conv_lin = low_back(matmul(hidden, w_conv_in))
    gatez = low_back(matmul(hidden, w_gatez))
    step_lin = low_back(matmul(hidden, w_step))
    taps = conv_weight.shape[0]
    extended = jnp.pad(conv_lin, ((0, 0), (taps - 1, 0), (0, 0)))
    activated = convolve(extended, conv_weight, conv_bias)
    ssm_width = SSM_HEADS * SSM_HEAD
    ssm_in = low(activated[..., :ssm_width]).reshape(groups, rows_all, SSM_HEADS, SSM_HEAD)
    in_keys = low(activated[..., ssm_width:ssm_width + STATE])
    in_queries = low(activated[..., ssm_width + STATE:])
    steps = jax.nn.softplus(step_lin + step_bias) * live
    mixed = recurrence(ssm_in, in_keys, in_queries, steps, decay_log, skip_gain)
    mix_low = low_back(low(gated_norm(mixed.reshape(groups, rows_all, ssm_width), gatez, gated_gain)))
    branch = low_back(matmul(attn_low, w_attn_out) + matmul(mix_low, w_mix_out))
    after_mix = tokens + live * branch
    hidden_two = low(normed(after_mix, norm_two))
    gate_lin = low_back(matmul(hidden_two, w_gate))
    up_lin = low_back(matmul(hidden_two, w_up))
    act_low = low(jax.nn.silu(gate_lin) * up_lin)
    ffn_out = low_back(matmul(act_low, w_down))
    return after_mix + live * ffn_out

def reference(tokens, cotangent, lengths, norm_one, w_query, w_key, w_value, w_gatez, w_conv_in, w_step, conv_weight, conv_bias, step_bias, decay_log, skip_gain, gated_gain, w_attn_out, w_mix_out, norm_two, w_gate, w_up, w_down):
    params = (norm_one, w_query, w_key, w_value, w_gatez, w_conv_in, w_step, conv_weight, conv_bias, step_bias, decay_log, skip_gain, gated_gain, w_attn_out, w_mix_out, norm_two, w_gate, w_up, w_down)
    params = tuple((entry.astype(jnp.float32) for entry in params))
    group_size = math.gcd(BATCH, max(1, 4096 // LEN))
    group_count = BATCH // group_size

    def regroup(value):
        return value.reshape((group_count, group_size) + value.shape[1:])

    def one_group(totals, packed):
        inputs, grad_out, group_len = packed

        def forward(first_arg, *others):
            return layer(first_arg, others, group_len)
        result, pull = jax.vjp(forward, inputs.astype(jnp.float32), *params)
        grads = pull(grad_out.astype(jnp.float32))
        totals = tuple((total + grad for total, grad in zip(totals, grads[1:])))
        return (totals, (result.astype(jnp.bfloat16), grads[0]))
    zeros = tuple((jnp.zeros_like(entry) for entry in params))
    totals, (outputs, grad_inputs) = lax.scan(one_group, zeros, (regroup(tokens), regroup(cotangent), regroup(lengths)))
    g_norm_one, g_query, g_key, g_value, g_gatez, g_conv_in, g_step, g_conv_weight, g_conv_bias, g_step_bias, g_decay, g_skip, g_gated, g_attn_out, g_mix_out, g_norm_two, g_gate, g_up, g_down = totals
    return (outputs.reshape(tokens.shape), grad_inputs.reshape(tokens.shape), g_norm_one, g_query, g_key, g_value, g_gatez, g_conv_in, g_step, g_conv_weight, g_conv_bias, g_step_bias, g_decay, g_skip, g_gated, g_attn_out, g_mix_out, g_norm_two, g_gate, g_up, g_down)
```

```python
import functools

import jax
import jax.numpy as jnp
import numpy as np
from jax import lax
from jax.experimental import pallas as pl
from jax.experimental.pallas import tpu as pltpu
from jax.sharding import PartitionSpec as P

HEADS = 8
KV_HEADS = 2
HEAD = 64
SSM_HEADS = 24
SSM_HEAD = 64
STATE = 128
WIDE = SSM_HEADS * SSM_HEAD
CHUNK = 128
EPS = 1e-05
ROPE_BASE = 100000000000.0
LOG2E = 1.4426950408889634
SCORE2 = 0.125 * LOG2E
LOWEST = -1e30
F32 = jnp.float32
BF16 = jnp.bfloat16
NN = (((1,), (0,)), ((), ()))
NT = (((1,), (1,)), ((), ()))
TN = (((0,), (0,)), ((), ()))
VMEM_LIMIT = 60 << 20


def dot(a, b, dims=NN):
    return lax.dot_general(a, b, dims, preferred_element_type=F32)


def dot_exact(a, b, dims=NN):
    return lax.dot_general(a, b, dims, precision=lax.Precision.HIGHEST, preferred_element_type=F32)


def low(v):
    return v.astype(BF16)


def sigmoid(v):
    return 1.0 / (1.0 + jnp.exp(-v))


def softplus(v):
    e = jnp.exp(-jnp.abs(v))
    tail = jnp.where(e < 1e-2, e * (1.0 - e * (0.5 - e * (1.0 / 3.0))), jnp.log(1.0 + e))
    return jnp.maximum(v, 0.0) + tail


def split_low(v):
    high = low(v)
    return high, low(v - high.astype(F32))


def widen(v, expand):
    return dot(jnp.concatenate(split_low(v), 1), expand)


def head_sums(v, expand):
    high, rest = split_low(v)
    ones = expand[:128]
    return dot(high, ones, NT) + dot(rest, ones, NT)


def full_spec(shape):
    return pl.BlockSpec(shape, lambda *_: (0,) * len(shape), pipeline_mode=pl.Buffered(1))


def params(limit=VMEM_LIMIT):
    return pltpu.CompilerParams(
        vmem_limit_bytes=limit, dimension_semantics=("arbitrary", "arbitrary")
    )


def low_rows(rows):
    t = lax.broadcasted_iota(jnp.int32, (rows, rows), 0)
    u = lax.broadcasted_iota(jnp.int32, (rows, rows), 1)
    return t >= u


def swap_halves(v):
    lane = lax.broadcasted_iota(jnp.int32, v.shape, 1)
    return jnp.where((lane & 63) < 32, pltpu.roll(v, 96, 1), pltpu.roll(v, 32, 1))


def pair_rows(v):
    lane = lax.broadcasted_iota(jnp.int32, v.shape, 1)
    none = jnp.zeros_like(v)
    return jnp.concatenate([jnp.where(lane < 64, v, none), jnp.where(lane >= 64, v, none)], 0)


def enter_body(
    pos_ref, len_ref, tok_ref, halo_ref, gain_ref, wq_ref, wk_ref, wv_ref, wz_ref, wc_ref, ws_ref,
    cw_ref, cb_ref, sb_ref, a_ref, cos_ref, sin_ref, exp_ref,
    hid_ref, q_ref, kv_ref, z_ref, cl_ref, pre_ref, x_ref, bk_ref, cq_ref,
    dt_ref, sg_ref, cum_ref, cumt_ref, st_ref, tot_ref,
    prev, state, total, *, rows, blocks,
):
    s = pl.program_id(0)
    b = pl.program_id(1)

    def normed(v):
        v = v.astype(F32)
        return low(v * lax.rsqrt(jnp.mean(v * v, -1, keepdims=True) + EPS) * gain_ref[...])

    @pl.when(b == 0)
    def _():
        prev[...] = dot(normed(halo_ref[0]), wc_ref[...])[8:]
        state[...] = jnp.zeros_like(state)
        total[...] = jnp.zeros_like(total)

    hid = normed(tok_ref[0])
    hid_ref[0] = hid
    cosine, sine = cos_ref[...], sin_ref[...]
    q = dot(hid, wq_ref[...])
    for g in range(4):
        t = q[:, g * 128 : g * 128 + 128]
        q_ref[0, :, g * 128 : g * 128 + 128] = low(t * cosine + swap_halves(t) * sine)
    t = dot(hid, wk_ref[...])
    kv_ref[0, :, :128] = low(t * cosine + swap_halves(t) * sine)
    kv_ref[0, :, 128:] = low(dot(hid, wv_ref[...]))
    z_ref[0] = low(dot(hid, wz_ref[...]))
    conv = dot(hid, wc_ref[...])
    cl_ref[0] = low(conv)
    ext = jnp.concatenate([prev[...], conv], 0)
    prev[...] = conv[rows - 8 :]
    pre = cb_ref[...] + cw_ref[3:4] * conv
    for back in range(1, 4):
        pre = pre + cw_ref[3 - back : 4 - back] * pltpu.roll(ext, back, 0)[8:]
    pre_ref[0] = low(pre)
    act = low(pre * sigmoid(pre))
    x = act[:, :WIDE]
    bk = act[:, WIDE : WIDE + STATE]
    x_ref[0] = x
    bk_ref[0] = bk
    cq_ref[0] = act[:, WIDE + STATE :]
    raw = dot(hid, ws_ref[...]) + sb_ref[...]
    at = pos_ref[0] + b * rows + lax.broadcasted_iota(jnp.int32, raw.shape, 0)
    live = jnp.where(at < len_ref[s], 1.0, 0.0)
    dt = softplus(raw) * live
    dt_ref[0] = dt
    sg_ref[0] = sigmoid(raw) * live
    log_decay = dt * a_ref[...]
    tri = jnp.where(low_rows(CHUNK), 1.0, 0.0)
    for c in range(rows // CHUNK):
        here = slice(c * CHUNK, (c + 1) * CHUNK)
        cum = dot_exact(tri, log_decay[here])
        cum_ref[0, here] = cum
        cumt_ref[0, :, here] = cum.T[:32]
        last = cum[CHUNK - 1 :]
        weight = dt[here] * jnp.exp2(last - cum)
        wide = widen(jnp.concatenate([weight, jnp.broadcast_to(jnp.exp2(last), (16, 128))], 0), exp_ref[...])
        xw = low(x[here].astype(F32) * wide[:CHUNK])
        state[...] = state[...] * wide[CHUNK : CHUNK + 1] + dot(bk[here], xw, TN)
        total[...] = total[...] + last

    @pl.when(b == blocks - 1)
    def _():
        st_ref[0] = low(state[...])
        tot_ref[0] = jnp.broadcast_to(total[...], (8, 128))


def enter(pos, lens, tokens, halo, gain, wq, wk, wv, wz, wc, ws, cw, cb, sb, a, cosine, sine, expand):
    seqs, span, width = tokens.shape
    rows = min(256, span)
    blocks = span // rows
    conv_width = wc.shape[1]

    def row(n):
        return pl.BlockSpec((1, rows, n), lambda s, b, *_: (s, b, 0))

    def shape(n, kind):
        return jax.ShapeDtypeStruct((seqs, span, n), kind)

    table = pl.BlockSpec((rows, 128), lambda s, b, *_: (b, 0))
    return pl.pallas_call(
        functools.partial(enter_body, rows=rows, blocks=blocks),
        grid_spec=pltpu.PrefetchScalarGridSpec(
            num_scalar_prefetch=2,
            grid=(seqs, blocks),
            in_specs=[
                row(width),
                pl.BlockSpec((1, 16, width), lambda s, b, *_: (s, 0, 0)),
                full_spec(gain.shape), full_spec(wq.shape), full_spec(wk.shape), full_spec(wv.shape),
                full_spec(wz.shape), full_spec(wc.shape), full_spec(ws.shape), full_spec(cw.shape),
                full_spec(cb.shape), full_spec(sb.shape), full_spec(a.shape), table, table,
                full_spec(expand.shape),
            ],
            out_specs=[
                row(width), row(512), row(256), row(WIDE), row(conv_width), row(conv_width),
                row(WIDE), row(STATE), row(STATE), row(128), row(128), row(128),
                pl.BlockSpec((1, 32, rows), lambda s, b, *_: (s, 0, b)),
                pl.BlockSpec((1, STATE, WIDE), lambda s, b, *_: (s, 0, 0)),
                pl.BlockSpec((1, 8, 128), lambda s, b, *_: (s, 0, 0)),
            ],
            scratch_shapes=[
                pltpu.VMEM((8, conv_width), F32), pltpu.VMEM((STATE, WIDE), F32), pltpu.VMEM((1, 128), F32),
            ],
        ),
        out_shape=[
            shape(width, BF16), shape(512, BF16), shape(256, BF16), shape(WIDE, BF16),
            shape(conv_width, BF16), shape(conv_width, BF16), shape(WIDE, BF16), shape(STATE, BF16),
            shape(STATE, BF16), shape(128, F32), shape(128, F32), shape(128, F32),
            jax.ShapeDtypeStruct((seqs, 32, span), F32),
            jax.ShapeDtypeStruct((seqs, STATE, WIDE), BF16),
            jax.ShapeDtypeStruct((seqs, 8, 128), F32),
        ],
        compiler_params=params(),
        name="enter",
    )(pos, lens, tokens, halo, gain, wq, wk, wv, wz, wc, ws, cw, cb, sb, a, cosine, sine, expand)


def scan_body(
    x_ref, bk_ref, cq_ref, dt_ref, cum_ref, cumt_ref, sin_ref, skip_ref, z_ref, gain_ref, exp_ref,
    mix_ref, low_ref, st_ref, state, y,
):
    c = pl.program_id(1)

    @pl.when(c == 0)
    def _():
        state[...] = sin_ref[0]

    x = x_ref[0].astype(F32)
    bk, cq = bk_ref[0], cq_ref[0]
    cum = cum_ref[0]
    last = cum[CHUNK - 1 :]
    expand = exp_ref[...]
    xdt = x * widen(dt_ref[0], expand)
    ends = widen(
        jnp.concatenate([jnp.exp2(cum), jnp.exp2(last - cum), jnp.broadcast_to(jnp.exp2(last), (16, 128))], 0),
        expand,
    )
    inter = jnp.where(low_rows(CHUNK), dot(cq, bk, NT), 0.0)
    held = low(state[...])
    st_ref[0, 0] = held
    y[...] = dot(cq, held) * ends[:CHUNK] + skip_ref[...] * x
    state[...] = state[...] * ends[2 * CHUNK : 2 * CHUNK + 1] + dot(bk, low(xdt * ends[CHUNK : 2 * CHUNK]), TN)
    xdt = low(xdt)
    for p in range(SSM_HEADS // 2):
        parts = []
        for h in (2 * p, 2 * p + 1):
            differ = jnp.minimum(cum[:, h : h + 1] - cumt_ref[0, h : h + 1, :], 0.0)
            parts.append(low(inter * jnp.exp2(differ)))
        cols = slice(p * 128, p * 128 + 128)
        y[:, cols] += dot(jnp.concatenate(parts, 1), pair_rows(xdt[:, cols]))
    mixed = y[...]
    mix_ref[0] = mixed
    z = z_ref[0].astype(F32)
    v = mixed * (z * sigmoid(z))
    low_ref[0] = low(v * lax.rsqrt(jnp.mean(v * v, -1, keepdims=True) + EPS) * gain_ref[...])


def scan_forward(x, bk, cq, dt, cum, cumt, state_in, skip, z, gain, expand):
    seqs, span, _ = x.shape
    chunks = span // CHUNK

    def row(n):
        return pl.BlockSpec((1, CHUNK, n), lambda s, c: (s, c, 0))

    return pl.pallas_call(
        scan_body,
        grid=(seqs, chunks),
        in_specs=[
            row(WIDE), row(STATE), row(STATE), row(128), row(128),
            pl.BlockSpec((1, 32, CHUNK), lambda s, c: (s, 0, c)),
            pl.BlockSpec((1, STATE, WIDE), lambda s, c: (s, 0, 0)),
            full_spec(skip.shape), row(WIDE), full_spec(gain.shape), full_spec(expand.shape),
        ],
        out_specs=[row(WIDE), row(WIDE), pl.BlockSpec((1, 1, STATE, WIDE), lambda s, c: (s, c, 0, 0))],
        out_shape=[
            jax.ShapeDtypeStruct((seqs, span, WIDE), F32),
            jax.ShapeDtypeStruct((seqs, span, WIDE), BF16),
            jax.ShapeDtypeStruct((seqs, chunks, STATE, WIDE), BF16),
        ],
        scratch_shapes=[pltpu.VMEM((STATE, WIDE), F32), pltpu.VMEM((CHUNK, WIDE), F32)],
        compiler_params=params(),
        name="scan_forward",
    )(x, bk, cq, dt, cum, cumt, state_in, skip, z, gain, expand)


def middle_body(
    pos_ref, len_ref, attn_ref, mix_ref, tok_ref, cot_ref, mixed_ref, z_ref, cq_ref, cum_ref,
    wao_ref, wmo_ref, wg_ref, wu_ref, wd_ref, gain2_ref, gated_ref, exp_ref,
    out_ref, h2_ref, act_ref, gffn_ref, gg_ref, gu_ref, gmid_ref, gb_ref, gattn_ref, gmixed_ref, gz_ref,
    delta_ref, gn2_ref, ggain_ref, adj_ref,
    gn2_s, ggain_s, adj, offset, *, rows, blocks, seqs,
):
    s = pl.program_id(0)
    b = pl.program_id(1)

    @pl.when((s == 0) & (b == 0))
    def _():
        gn2_s[...] = jnp.zeros_like(gn2_s)
        ggain_s[...] = jnp.zeros_like(ggain_s)

    @pl.when(b == 0)
    def _():
        adj[...] = jnp.zeros_like(adj)
        offset[...] = jnp.zeros_like(offset)

    at = pos_ref[0] + b * rows + lax.broadcasted_iota(jnp.int32, (rows, 1), 0)
    live = jnp.where(at < len_ref[s], 1.0, 0.0)
    attn = attn_ref[0]
    branch = dot(attn, wao_ref[...]) + dot(mix_ref[0], wmo_ref[...])
    after = tok_ref[0].astype(F32) + live * branch
    scale = lax.rsqrt(jnp.mean(after * after, -1, keepdims=True) + EPS)
    unit = after * scale
    gain = gain2_ref[...]
    h2 = low(unit * gain)
    h2_ref[0] = h2
    gate = dot(h2, wg_ref[...])
    up = dot(h2, wu_ref[...])
    sg = sigmoid(gate)
    silu = gate * sg
    act = low(silu * up)
    act_ref[0] = act
    out_ref[0] = low(after + live * dot(act, wd_ref[...]))
    cot = cot_ref[0].astype(F32)
    gffn = low(live * cot)
    gffn_ref[0] = gffn
    gact = dot(gffn, wd_ref[...], NT)
    gg = low(gact * up * (sg * (1.0 + gate * (1.0 - sg))))
    gu = low(gact * silu)
    gg_ref[0] = gg
    gu_ref[0] = gu
    gh2 = dot(gg, wg_ref[...], NT) + dot(gu, wu_ref[...], NT)
    gn2_s[...] += jnp.sum(gh2 * unit, 0, keepdims=True)
    g = gh2 * gain
    gmid = cot + scale * (g - unit * jnp.mean(g * unit, -1, keepdims=True))
    gmid_ref[0] = gmid
    gb = low(live * gmid)
    gb_ref[0] = gb
    gattn = low(dot(gb, wao_ref[...], NT))
    gattn_ref[0] = gattn
    prod = gattn.astype(F32) * attn.astype(F32)
    col = lax.broadcasted_iota(jnp.int32, (8, 512), 1) // HEAD
    ones = low(jnp.where(col == lax.broadcasted_iota(jnp.int32, (8, 512), 0), 1.0, 0.0))
    high, rest = split_low(prod)
    delta_ref[0] = dot(ones, high, NT) + dot(ones, rest, NT)
    gn = low(dot(gb, wmo_ref[...], NT)).astype(F32)
    mixed = mixed_ref[0]
    z = z_ref[0].astype(F32)
    sg = sigmoid(z)
    silu = z * sg
    v = mixed * silu
    scale = lax.rsqrt(jnp.mean(v * v, -1, keepdims=True) + EPS)
    unit = v * scale
    ggain_s[...] += jnp.sum(gn * unit, 0, keepdims=True)
    g = gn * gated_ref[...]
    g = scale * (g - unit * jnp.mean(g * unit, -1, keepdims=True))
    gmixed = g * silu
    gmixed_ref[0] = low(gmixed)
    gz_ref[0] = low(g * mixed * (sg * (1.0 + z * (1.0 - sg))))
    cum = cum_ref[0]
    logs = []
    for c in range(rows // CHUNK):
        here = cum[c * CHUNK : (c + 1) * CHUNK]
        logs.append(here + offset[...])
        offset[...] += here[CHUNK - 1 :]
    wide = widen(jnp.exp2(jnp.concatenate(logs, 0)), exp_ref[...])
    adj[...] += dot(cq_ref[0], low(gmixed * wide), TN)

    @pl.when(b == blocks - 1)
    def _():
        adj_ref[0] = low(adj[...])

    @pl.when((s == seqs - 1) & (b == blocks - 1))
    def _():
        gn2_ref[...] = gn2_s[...]
        ggain_ref[...] = ggain_s[...]


def middle(pos, lens, attn, mix, tokens, cot, mixed, z, cq, cum, wao, wmo, wg, wu, wd, gain2, gated, expand):
    seqs, span, width = tokens.shape
    rows = min(256, span)
    blocks = span // rows
    ff = wg.shape[1]

    def row(n):
        return pl.BlockSpec((1, rows, n), lambda s, b, *_: (s, b, 0))

    def shape(n, kind):
        return jax.ShapeDtypeStruct((seqs, span, n), kind)

    def once(n):
        return pl.BlockSpec((1, n), lambda s, b, *_: (0, 0))

    return pl.pallas_call(
        functools.partial(middle_body, rows=rows, blocks=blocks, seqs=seqs),
        grid_spec=pltpu.PrefetchScalarGridSpec(
            num_scalar_prefetch=2,
            grid=(seqs, blocks),
            in_specs=[
                row(512), row(WIDE), row(width), row(width), row(WIDE), row(WIDE), row(STATE), row(128),
                full_spec(wao.shape), full_spec(wmo.shape), full_spec(wg.shape), full_spec(wu.shape),
                full_spec(wd.shape), full_spec(gain2.shape), full_spec(gated.shape), full_spec(expand.shape),
            ],
            out_specs=[
                row(width), row(width), row(ff), row(width), row(ff), row(ff), row(width), row(width),
                row(512), row(WIDE), row(WIDE),
                pl.BlockSpec((1, 8, rows), lambda s, b, *_: (s, 0, b)),
                once(width), once(WIDE),
                pl.BlockSpec((1, STATE, WIDE), lambda s, b, *_: (s, 0, 0)),
            ],
            scratch_shapes=[
                pltpu.VMEM((1, width), F32), pltpu.VMEM((1, WIDE), F32), pltpu.VMEM((STATE, WIDE), F32),
                pltpu.VMEM((1, 128), F32),
            ],
        ),
        out_shape=[
            shape(width, BF16), shape(width, BF16), shape(ff, BF16), shape(width, BF16), shape(ff, BF16),
            shape(ff, BF16), shape(width, F32), shape(width, BF16), shape(512, BF16), shape(WIDE, BF16),
            shape(WIDE, BF16),
            jax.ShapeDtypeStruct((seqs, 8, span), F32),
            jax.ShapeDtypeStruct((1, width), F32), jax.ShapeDtypeStruct((1, WIDE), F32),
            jax.ShapeDtypeStruct((seqs, STATE, WIDE), BF16),
        ],
        compiler_params=params(),
        name="middle",
    )(pos, lens, attn, mix, tokens, cot, mixed, z, cq, cum, wao, wmo, wg, wu, wd, gain2, gated, expand)


def scan_back_body(
    x_ref, bk_ref, cq_ref, dt_ref, sg_ref, cum_ref, cumt_ref, dy_ref, mix_ref, st_ref, adj_ref, pre_ref, cl_ref,
    skip_ref, a_ref, cw_ref, exp_ref,
    gc_ref, gs_ref, tail_ref, head_ref, gw_ref, gskip_ref, small_ref,
    adj, after, gact, *, chunks,
):
    s = pl.program_id(0)
    c = pl.program_id(1)

    @pl.when((s == 0) & (c == 0))
    def _():
        gw_ref[...] = jnp.zeros_like(gw_ref)
        gskip_ref[...] = jnp.zeros_like(gskip_ref)
        small_ref[...] = jnp.zeros_like(small_ref)

    @pl.when(c == 0)
    def _():
        adj[...] = adj_ref[0]
        after[...] = jnp.zeros_like(after)

    x = x_ref[0].astype(F32)
    bk, cq = bk_ref[0], cq_ref[0]
    dt = dt_ref[0]
    cum = cum_ref[0]
    last = cum[CHUNK - 1 :]
    expand = exp_ref[...]
    dt_wide = widen(dt, expand)
    ends = widen(
        jnp.concatenate([jnp.exp2(cum), jnp.exp2(last - cum), jnp.broadcast_to(jnp.exp2(last), (16, 128))], 0),
        expand,
    )
    to_end = ends[CHUNK : 2 * CHUNK]
    all_wide = ends[2 * CHUNK : 2 * CHUNK + 1]
    xdt = x * dt_wide
    dy_low = dy_ref[0]
    dy = dy_low.astype(F32)
    dy_in = low(dy * ends[:CHUNK])
    state = st_ref[0, 0]
    gstate = adj[...]
    gstate_low = low(gstate)
    from_end = dot(bk, gstate_low) * to_end
    gb = dot(low(xdt * to_end), gstate_low, NT)
    gc = dot(dy_in, state, NT)
    gfinal = all_wide * jnp.sum(gstate * state.astype(F32), 0, keepdims=True) + jnp.sum(
        xdt * from_end, 0, keepdims=True
    )
    adj[...] = gstate * all_wide + dot(cq, dy_in, TN)
    xdt_low = low(xdt)
    u = lax.broadcasted_iota(jnp.int32, (CHUNK, CHUNK), 0)
    t = lax.broadcasted_iota(jnp.int32, (CHUNK, CHUNK), 1)
    inter = jnp.where(t >= u, dot(bk, cq, NT), 0.0)
    ginter = jnp.zeros((CHUNK, CHUNK), F32)
    for p in range(SSM_HEADS // 2):
        cols = slice(p * 128, p * 128 + 128)
        dy_rows = pair_rows(dy_low[:, cols])
        gmix = dot(xdt_low[:, cols], dy_rows, NT)
        parts = []
        for n, h in enumerate((2 * p, 2 * p + 1)):
            decay = jnp.exp2(jnp.minimum(cumt_ref[0, h : h + 1, :] - cum[:, h : h + 1], 0.0))
            parts.append(low(inter * decay))
            ginter = ginter + gmix[:, n * CHUNK : (n + 1) * CHUNK] * decay
        gact[:, cols] = dot(jnp.concatenate(parts, 1), dy_rows)
    ginter = low(jnp.where(t >= u, ginter, 0.0))
    gact[:, WIDE : WIDE + STATE] = gb + dot(ginter, cq)
    gact[:, WIDE + STATE :] = gc + dot(ginter, bk, TN)
    gxdt = gact[:, :WIDE] + from_end
    skip = skip_ref[...]
    gact[:, :WIDE] = dt_wide * gxdt + skip * dy
    gskip_ref[...] += jnp.sum(dy * x, 0, keepdims=True)
    sums = head_sums(
        jnp.concatenate([x * gxdt, dy * (mix_ref[0] - skip * x), jnp.broadcast_to(gfinal, (16, WIDE))], 0), expand
    )
    direct = sums[:CHUNK]
    gcum = sums[CHUNK : 2 * CHUNK] - dt * direct
    gld = dot_exact(jnp.where(t >= u, 1.0, 0.0), gcum) + sums[2 * CHUNK : 2 * CHUNK + 1]
    a = a_ref[...]
    gstep = (direct + a * gld) * sg_ref[0]
    gs_ref[0] = low(gstep)
    small_ref[0:1] += jnp.sum(dt * gld, 0, keepdims=True) * a
    small_ref[1:2] += jnp.sum(gstep, 0, keepdims=True)
    pre = pre_ref[0].astype(F32)
    sg = sigmoid(pre)
    gpre = gact[...] * (sg * (1.0 + pre * (1.0 - sg)))
    ext = jnp.concatenate([gpre, after[...]], 0)
    after[...] = gpre[:8]
    conv = cl_ref[0].astype(F32)
    gconv = cw_ref[3:4] * gpre
    gw_ref[3:4] += jnp.sum(conv * gpre, 0, keepdims=True)
    gw_ref[4:5] += jnp.sum(gpre, 0, keepdims=True)
    for ahead in range(1, 4):
        moved = pltpu.roll(ext, CHUNK + 8 - ahead, 0)[:CHUNK]
        gconv = gconv + cw_ref[3 - ahead : 4 - ahead] * moved
        gw_ref[3 - ahead : 4 - ahead] += jnp.sum(conv * moved, 0, keepdims=True)
    gc_ref[0] = low(gconv)

    @pl.when(c == 0)
    def _():
        tail_ref[0] = gconv[CHUNK - 8 :]

    @pl.when(c == chunks - 1)
    def _():
        head_ref[0] = gpre[:8]


def scan_backward(x, bk, cq, dt, sg, cum, cumt, dy, mixed, states, adj_in, pre, conv, skip, a, cw, expand):
    seqs, span, _ = x.shape
    chunks = span // CHUNK
    conv_width = pre.shape[2]

    def row(n):
        return pl.BlockSpec((1, CHUNK, n), lambda s, c: (s, chunks - 1 - c, 0))

    def once(m, n):
        return pl.BlockSpec((m, n), lambda s, c: (0, 0))

    edge = pl.BlockSpec((1, 8, conv_width), lambda s, c: (s, 0, 0))
    return pl.pallas_call(
        functools.partial(scan_back_body, chunks=chunks),
        grid=(seqs, chunks),
        in_specs=[
            row(WIDE), row(STATE), row(STATE), row(128), row(128), row(128),
            pl.BlockSpec((1, 32, CHUNK), lambda s, c: (s, 0, chunks - 1 - c)),
            row(WIDE), row(WIDE),
            pl.BlockSpec((1, 1, STATE, WIDE), lambda s, c: (s, chunks - 1 - c, 0, 0)),
            pl.BlockSpec((1, STATE, WIDE), lambda s, c: (s, 0, 0)),
            row(conv_width), row(conv_width),
            full_spec(skip.shape), full_spec(a.shape), full_spec(cw.shape), full_spec(expand.shape),
        ],
        out_specs=[row(conv_width), row(128), edge, edge, once(8, conv_width), once(1, WIDE), once(8, 128)],
        out_shape=[
            jax.ShapeDtypeStruct((seqs, span, conv_width), BF16),
            jax.ShapeDtypeStruct((seqs, span, 128), BF16),
            jax.ShapeDtypeStruct((seqs, 8, conv_width), F32),
            jax.ShapeDtypeStruct((seqs, 8, conv_width), F32),
            jax.ShapeDtypeStruct((8, conv_width), F32),
            jax.ShapeDtypeStruct((1, WIDE), F32),
            jax.ShapeDtypeStruct((8, 128), F32),
        ],
        scratch_shapes=[
            pltpu.VMEM((STATE, WIDE), F32), pltpu.VMEM((8, conv_width), F32), pltpu.VMEM((CHUNK, conv_width), F32),
        ],
        compiler_params=params(),
        name="scan_backward",
    )(x, bk, cq, dt, sg, cum, cumt, dy, mixed, states, adj_in, pre, conv, skip, a, cw, expand)


def leave_body(
    tok_ref, gmid_ref, gq_ref, gk_ref, gv_ref, gz_ref, gc_ref, gs_ref, gain_ref,
    wq_ref, wk_ref, wv_ref, wz_ref, wc_ref, ws_ref,
    gt_ref, gn_ref,
):
    @pl.when((pl.program_id(0) == 0) & (pl.program_id(1) == 0))
    def _():
        gn_ref[...] = jnp.zeros_like(gn_ref)

    gh = dot(gq_ref[0], wq_ref[...], NT) + dot(gk_ref[0], wk_ref[...], NT) + dot(gv_ref[0], wv_ref[...], NT)
    gh = gh + dot(gz_ref[0], wz_ref[...], NT) + dot(gc_ref[0], wc_ref[...], NT) + dot(gs_ref[0], ws_ref[...], NT)
    v = tok_ref[0].astype(F32)
    scale = lax.rsqrt(jnp.mean(v * v, -1, keepdims=True) + EPS)
    unit = v * scale
    gn_ref[...] += jnp.sum(gh * unit, 0, keepdims=True)
    g = gh * gain_ref[...]
    gt_ref[0] = gmid_ref[0] + scale * (g - unit * jnp.mean(g * unit, -1, keepdims=True))


def leave(tokens, gmid, gq, gk, gv, gz, gc, gs, gain, wq, wk, wv, wz, wc, ws):
    seqs, span, width = tokens.shape
    rows = min(256, span)

    def row(a):
        return pl.BlockSpec((1, rows, a.shape[2]), lambda s, b: (s, b, 0))

    return pl.pallas_call(
        leave_body,
        grid=(seqs, span // rows),
        in_specs=[row(v) for v in (tokens, gmid, gq, gk, gv, gz, gc, gs)]
        + [full_spec(v.shape) for v in (gain, wq, wk, wv, wz, wc, ws)],
        out_specs=[row(tokens), pl.BlockSpec((1, width), lambda s, b: (0, 0))],
        out_shape=[jax.ShapeDtypeStruct((seqs, span, width), F32), jax.ShapeDtypeStruct((1, width), F32)],
        compiler_params=params(),
        name="leave",
    )(tokens, gmid, gq, gk, gv, gz, gc, gs, gain, wq, wk, wv, wz, wc, ws)


def dup_halves(v):
    lane = lax.broadcasted_iota(jnp.int32, v.shape, 1)
    other = pltpu.roll(v, 64, 1)
    return low(jnp.where(lane < 64, v, other)), low(jnp.where(lane < 64, other, v))


def head_rows(ref, rows):
    lane = lax.broadcasted_iota(jnp.int32, (rows, 128), 1)
    heads = []
    for h in range(HEADS):
        t = ref[0, :, (h // 2) * 128 : (h // 2) * 128 + 128]
        heads.append(jnp.where((lane < 64) if h % 2 == 0 else (lane >= 64), t, jnp.zeros_like(t)))
    return heads


def key_range(first, length, rows, keys):
    whole = jnp.minimum((first + 1) // keys, length // keys)
    some = jnp.minimum((first + rows + keys - 1) // keys, (length + keys - 1) // keys)
    return whole, some


def seen(i, first, length, rows, keys):
    key_at = i * keys + lax.broadcasted_iota(jnp.int32, (keys, rows), 0)
    query_at = first + lax.broadcasted_iota(jnp.int32, (keys, rows), 1)
    return (key_at <= query_at) & (key_at < length)


def attend_body(
    pos_ref, len_ref, q_ref, kv_ref, o_ref, lse_ref, kd, vt, top, acc, score_a, score_b, top_a, top_b,
    *, rows, keys, total, prep,
):
    s = pl.program_id(0)
    b = pl.program_id(1)

    @pl.when(b == 0)
    def _():
        def one(i, _):
            at = pl.ds(pl.multiple_of(i * prep, prep), prep)
            kd[0, at, :], kd[1, at, :] = dup_halves(kv_ref[0, at, :128].astype(F32))
            t = kv_ref[0, at, 128:].astype(F32).T
            ones = jnp.ones((16, prep), F32)
            vt[0, :, at] = low(jnp.concatenate([t[:64], ones], 0))
            vt[1, :, at] = low(jnp.concatenate([t[64:], ones], 0))
            return 0

        lax.fori_loop(0, total // prep, one, 0)

    first = pos_ref[b]
    length = len_ref[s]
    heads = head_rows(q_ref, rows)
    top[...] = jnp.full_like(top, LOWEST)
    acc[...] = jnp.zeros_like(acc)
    whole, some = key_range(first, length, rows, keys)

    def scores(i, buffer, tops, h, mask=None):
        at = pl.ds(pl.multiple_of(i * keys, keys), keys)
        t = dot(kd[h // 4, at, :], heads[h], NT)
        if mask is not None:
            t = jnp.where(mask, t, LOWEST)
        buffer[h] = t
        tops[h] = jnp.max(t, 0, keepdims=True)

    def add(i, buffer, tops, h):
        at = pl.ds(pl.multiple_of(i * keys, keys), keys)
        before = top[h]
        now = jnp.maximum(before, tops[h])
        p = low(jnp.exp2((buffer[h] - now) * SCORE2))
        acc[h] = acc[h] * jnp.exp2((before - now) * SCORE2) + dot(vt[h // 4, :, at], p)
        top[h] = now

    def edge(i, _):
        mask = seen(i, first, length, rows, keys)
        for h in range(HEADS):
            scores(i, score_a, top_a, h, mask)
        for h in range(HEADS):
            add(i, score_a, top_a, h)
        return 0

    lax.fori_loop(whole, some, edge, 0)
    last = jnp.maximum(whole - 1, 0)
    for h in range(HEADS):
        scores(0, score_a, top_a, h)

    def two(i, _):
        for h in range(HEADS):
            scores(2 * i + 1, score_b, top_b, h)
            add(2 * i, score_a, top_a, h)
        following = jnp.minimum(2 * i + 2, last)
        for h in range(HEADS):
            scores(following, score_a, top_a, h)
            add(2 * i + 1, score_b, top_b, h)
        return 0

    lax.fori_loop(0, whole // 2, two, 0)

    @pl.when(whole % 2 == 1)
    def _():
        for h in range(HEADS):
            add(last, score_a, top_a, h)

    outs = []
    for h in range(HEADS):
        t = acc[h]
        weight = t[64:65]
        outs.append(t[:64] / weight)
        lse_ref[0, h : h + 1, :] = top[h] * SCORE2 + jnp.log2(weight)
    for g in range(HEADS // 2):
        o_ref[0, :, g * 128 : g * 128 + 128] = low(jnp.concatenate(outs[2 * g : 2 * g + 2], 0).T)


def attend(pos, lens, q, kv):
    seqs, span, _ = q.shape
    total = kv.shape[1]
    rows = min(256, span)
    keys = 256
    blocks = span // rows
    return pl.pallas_call(
        functools.partial(attend_body, rows=rows, keys=keys, total=total, prep=512),
        grid_spec=pltpu.PrefetchScalarGridSpec(
            num_scalar_prefetch=2,
            grid=(seqs, blocks),
            in_specs=[
                pl.BlockSpec((1, rows, 512), lambda s, b, *_: (s, b, 0)),
                pl.BlockSpec((1, total, 256), lambda s, b, *_: (s, 0, 0)),
            ],
            out_specs=[
                pl.BlockSpec((1, rows, 512), lambda s, b, *_: (s, b, 0)),
                pl.BlockSpec((1, 8, rows), lambda s, b, *_: (s, 0, b)),
            ],
            scratch_shapes=[
                pltpu.VMEM((2, total, 128), BF16), pltpu.VMEM((2, 80, total), BF16),
                pltpu.VMEM((8, 1, rows), F32), pltpu.VMEM((8, 80, rows), F32),
                pltpu.VMEM((8, keys, rows), F32), pltpu.VMEM((8, keys, rows), F32),
                pltpu.VMEM((8, 1, rows), F32), pltpu.VMEM((8, 1, rows), F32),
            ],
        ),
        out_shape=[
            jax.ShapeDtypeStruct((seqs, span, 512), BF16),
            jax.ShapeDtypeStruct((seqs, 8, span), F32),
        ],
        compiler_params=params(),
        name="attend",
    )(pos, lens, q, kv)


def attend_back_body(
    pos_ref, len_ref, q_ref, do_ref, lse_ref, delta_ref, cos_ref, sin_ref, kv_ref, dq_ref, dkv_ref,
    kd, vd, kt, dk, dv, dq, *, rows, keys, total, blocks, prep,
):
    s = pl.program_id(0)
    b = pl.program_id(1)

    @pl.when(b == 0)
    def _():
        def one(i, _):
            at = pl.ds(pl.multiple_of(i * prep, prep), prep)
            k = kv_ref[0, at, :128].astype(F32)
            kd[0, at, :], kd[1, at, :] = dup_halves(k)
            vd[0, at, :], vd[1, at, :] = dup_halves(kv_ref[0, at, 128:].astype(F32))
            kt[:, at] = low(k.T)
            return 0

        lax.fori_loop(0, total // prep, one, 0)
        dk[...] = jnp.zeros_like(dk)
        dv[...] = jnp.zeros_like(dv)

    first = pos_ref[b]
    length = len_ref[s]
    heads = head_rows(q_ref, rows)
    grads = head_rows(do_ref, rows)
    dq[...] = jnp.zeros_like(dq)
    whole, some = key_range(first, length, rows, keys)

    def step(i, masked):
        at = pl.ds(pl.multiple_of(i * keys, keys), keys)
        mask = seen(i, first, length, rows, keys) if masked else None
        for j in range(KV_HEADS):
            dv_sum = dk_sum = None
            for h in range(4 * j, 4 * j + 4):
                x = dot(kd[j, at, :], heads[h], NT) * SCORE2 - lse_ref[0, h : h + 1, :]
                dp = dot(vd[j, at, :], grads[h], NT)
                if masked:
                    x = jnp.where(mask, x, LOWEST)
                p = jnp.exp2(x)
                ds = low(p * (dp - delta_ref[0, h : h + 1, :]))
                dv_part = dot(low(p), grads[h])
                dk_part = dot(ds, heads[h])
                dv_sum = dv_part if dv_sum is None else dv_sum + dv_part
                dk_sum = dk_part if dk_sum is None else dk_sum + dk_part
                dq[h] += dot(kt[64 * j : 64 * j + 64, at], ds)
            dv[j, at, :] += dv_sum
            dk[j, at, :] += dk_sum

    lax.fori_loop(0, whole, lambda i, _: (step(i, False), 0)[1], 0)
    lax.fori_loop(whole, some, lambda i, _: (step(i, True), 0)[1], 0)
    cosine, sine = cos_ref[...], sin_ref[...]
    for g in range(HEADS // 2):
        parts = []
        for h in (2 * g, 2 * g + 1):
            t = dq[h] * 0.125
            former, latter = t[:32], t[32:]
            parts += [former * cosine + latter * sine, latter * cosine - former * sine]
        dq_ref[0, :, g * 128 : g * 128 + 128] = low(jnp.concatenate(parts, 0).T)

    @pl.when(b == blocks - 1)
    def _():
        def one(i, _):
            at = pl.ds(pl.multiple_of(i * prep, prep), prep)
            lane = lax.broadcasted_iota(jnp.int32, (prep, 128), 1)
            for source, columns, scale in ((dk, slice(0, 128), 0.125), (dv, slice(128, 256), 1.0)):
                pair = [source[j, at, :] for j in range(2)]
                pair = [t + pltpu.roll(t, 64, 1) for t in pair]
                dkv_ref[0, at, columns] = low(jnp.where(lane < 64, pair[0], pair[1]) * scale)
            return 0

        lax.fori_loop(0, total // prep, one, 0)


def attend_backward(pos, lens, q, do, lse, delta, cosine, sine, kv):
    seqs, span, _ = q.shape
    total = kv.shape[1]
    rows = min(256, span)
    keys = 512
    blocks = span // rows
    row = pl.BlockSpec((1, rows, 512), lambda s, b, *_: (s, b, 0))
    stat = pl.BlockSpec((1, 8, rows), lambda s, b, *_: (s, 0, b))
    table = pl.BlockSpec((32, rows), lambda s, b, *_: (0, b))
    every = pl.BlockSpec((1, total, 256), lambda s, b, *_: (s, 0, 0))
    return pl.pallas_call(
        functools.partial(attend_back_body, rows=rows, keys=keys, total=total, blocks=blocks, prep=512),
        grid_spec=pltpu.PrefetchScalarGridSpec(
            num_scalar_prefetch=2,
            grid=(seqs, blocks),
            in_specs=[row, row, stat, stat, table, table, every],
            out_specs=[row, every],
            scratch_shapes=[
                pltpu.VMEM((2, total, 128), BF16), pltpu.VMEM((2, total, 128), BF16), pltpu.VMEM((128, total), BF16),
                pltpu.VMEM((2, total, 128), F32), pltpu.VMEM((2, total, 128), F32), pltpu.VMEM((8, 64, rows), F32),
            ],
        ),
        out_shape=[
            jax.ShapeDtypeStruct((seqs, span, 512), BF16),
            jax.ShapeDtypeStruct((seqs, total, 256), BF16),
        ],
        compiler_params=params(),
        name="attend_backward",
    )(pos, lens, q, do, lse, delta, cosine, sine, kv)


def from_behind(value, axis, steps):
    count = lax.axis_size(axis)
    initial, last = (max(0, -steps), min(count, count - steps))
    return lax.ppermute(value, axis, [(source, source + steps) for source in range(initial, last)])


def weight_grad(left, grad):
    return low(jnp.einsum("sck,scm->km", left, grad, preferred_element_type=F32))


def joined(states, totals, between, taken):
    logs = jnp.einsum("ij,jsh->ish", between.astype(F32), totals, precision=lax.Precision.HIGHEST)
    weights = jnp.where(taken[:, None, None], jnp.exp2(logs), 0.0)[..., :SSM_HEADS]
    weights = jnp.repeat(weights, SSM_HEAD, -1)[:, :, None, :]
    return jnp.sum(states.astype(F32) * weights, 0)


def on_device(
    tokens, cotangent, lengths, norm_one, w_query, w_key, w_value, w_gatez, w_conv_in, w_step, conv_weight,
    conv_bias, step_bias, decay_log, skip_gain, gated_gain, w_attn_out, w_mix_out, norm_two, w_gate, w_up, w_down,
):
    seqs, span, width = tokens.shape
    taps = conv_weight.shape[0]
    count = lax.axis_size("seq")
    place = lax.axis_index("seq")
    first = place * span
    positions = first + jnp.arange(span)
    inverse = 1.0 / ROPE_BASE ** (jnp.arange(0, HEAD, 2).astype(F32) / HEAD)
    angles = positions.astype(F32)[:, None] * inverse[None, :]
    cosine, sine = jnp.cos(angles), jnp.sin(angles)
    cos_row = jnp.concatenate([cosine] * 4, 1)
    sin_row = jnp.concatenate([-sine, sine] * 2, 1)
    rate = -jnp.exp(decay_log)
    pad = (0, 128 - SSM_HEADS)
    rate_row = jnp.pad(rate, pad)[None]
    step_row = jnp.pad(step_bias, pad)[None]
    w_step_wide = jnp.pad(w_step, ((0, 0), pad))
    skip_row = jnp.repeat(skip_gain, SSM_HEAD)[None]
    ones = (np.arange(WIDE)[None, :] // SSM_HEAD == np.arange(128)[:, None]).astype(np.float32)
    expand = jnp.asarray(np.concatenate([ones, ones], 0), BF16)
    pos = first[None].astype(jnp.int32)
    blocks = first + jnp.arange(0, span, min(256, span), dtype=jnp.int32)

    halo = from_behind(tokens[:, span - 16 :], "seq", 1)
    (hidden, q, kv, z, conv, pre, x, bk, cq, dt, sg, cum, cumt, state, total) = enter(
        pos, lengths, tokens, halo, norm_one[None], w_query, w_key, w_value, w_gatez, w_conv_in, w_step_wide,
        conv_weight, conv_bias[None], step_row, rate_row * LOG2E, cos_row, sin_row, expand,
    )
    kv_all = lax.all_gather(kv, "seq", axis=1, tiled=True)
    states = lax.all_gather(state, "seq")
    totals = lax.all_gather(total[:, 0], "seq")
    i = jnp.arange(count)
    state_in = joined(states, totals, (i[None, :] > i[:, None]) & (i[None, :] < place), i < place)
    mixed, mix_low, held = scan_forward(
        x, bk, cq, dt, cum, cumt, state_in, skip_row, z, gated_gain[None], expand
    )
    attn, lse = attend(blocks, lengths, q, kv_all)
    (
        output, hidden_two, act, grad_ffn, grad_gate, grad_up, grad_mid, grad_branch, grad_attn, grad_mixed,
        grad_z, delta, g_norm_two, g_gated, adjoint,
    ) = middle(
        pos, lengths, attn, mix_low, tokens, cotangent, mixed, z, cq, cum, w_attn_out, w_mix_out, w_gate, w_up,
        w_down, norm_two[None], gated_gain[None], expand,
    )
    adjoints = lax.all_gather(adjoint, "seq")
    g_down = weight_grad(act, grad_ffn)
    g_gate = weight_grad(hidden_two, grad_gate)
    g_up = weight_grad(hidden_two, grad_up)
    g_attn_out = weight_grad(attn, grad_branch)
    g_mix_out = weight_grad(mix_low, grad_branch)
    grad_q, grad_kv = attend_backward(blocks, lengths, q, grad_attn, lse, delta, cosine.T, sine.T, kv_all)
    grad_kv = lax.psum_scatter(grad_kv, "seq", scatter_dimension=1, tiled=True)
    adjoint_in = joined(adjoints, totals, (i[None, :] < i[:, None]) & (i[None, :] > place), i > place)
    grad_conv, grad_step, tail, head, g_conv_small, g_skip, g_small = scan_backward(
        x, bk, cq, dt, sg, cum, cumt, grad_mixed, mixed, held, adjoint_in, pre, conv, skip_row, rate_row,
        conv_weight, expand,
    )
    returned = from_behind(low(head), "seq", -1).astype(F32)[:, : taps - 1]
    g_conv_weight = g_conv_small[:taps]
    for ahead in range(1, taps):
        tap = taps - 1 - ahead
        rows = jnp.pad(returned[:, :ahead], ((0, 0), (8 - ahead, 0), (0, 0)))
        tail = tail + conv_weight[tap] * rows
        g_conv_weight = g_conv_weight.at[tap].add(jnp.sum(rows * conv[:, span - 8 :].astype(F32), (0, 1)))
    grad_conv = lax.dynamic_update_slice(grad_conv, low(tail), (0, span - 8, 0))
    grad_key = grad_kv[:, :, :128].astype(F32).reshape(seqs, span, KV_HEADS, 2, HEAD // 2)
    c4, s4 = cosine[None, :, None, :], sine[None, :, None, :]
    former, latter = grad_key[:, :, :, 0], grad_key[:, :, :, 1]
    grad_key = jnp.concatenate([former * c4 + latter * s4, latter * c4 - former * s4], -1)
    grad_key = low(grad_key.reshape(seqs, span, 128))
    grad_value = grad_kv[:, :, 128:]
    grad_tokens, g_norm_one = leave(
        tokens, grad_mid, grad_q, grad_key, grad_value, grad_z, grad_conv, grad_step, norm_one[None],
        w_query, w_key, w_value, w_gatez, w_conv_in, w_step_wide,
    )
    g_query = weight_grad(hidden, grad_q)
    g_key = weight_grad(hidden, grad_key)
    g_value = weight_grad(hidden, grad_value)
    g_gatez = weight_grad(hidden, grad_z)
    g_conv_in = weight_grad(hidden, grad_conv)
    g_step = weight_grad(hidden, grad_step)

    def reduced(g):
        part = lax.psum_scatter(g, "seq", scatter_dimension=0, tiled=True)
        return lax.psum(part, "dp").astype(F32)

    small = [
        g_norm_one[0], g_norm_two[0], g_gated[0], g_conv_weight.reshape(-1), g_conv_small[taps], g_skip[0],
        g_small[0], g_small[1],
    ]
    sizes = [v.shape[0] for v in small]
    flat = lax.psum(jnp.concatenate(small), ("dp", "seq"))
    starts = np.cumsum([0] + sizes)
    small = [flat[a:b] for a, b in zip(starts[:-1], starts[1:])]

    def mine(v):
        n = v.shape[0] // count
        return lax.dynamic_slice(v, (place * n,), (n,))

    s_norm_one, s_norm_two, s_gated = [mine(v) for v in small[:3]]
    s_skip = jnp.sum(small[5].reshape(SSM_HEADS, SSM_HEAD), 1)
    return (
        output,
        grad_tokens,
        s_norm_one,
        reduced(g_query),
        reduced(g_key),
        reduced(g_value),
        reduced(g_gatez),
        reduced(g_conv_in),
        reduced(g_step)[:, :SSM_HEADS],
        small[3].reshape(taps, -1),
        small[4],
        small[7][:SSM_HEADS],
        small[6][:SSM_HEADS],
        s_skip,
        s_gated,
        reduced(g_attn_out),
        reduced(g_mix_out),
        s_norm_two,
        reduced(g_gate),
        reduced(g_up),
        reduced(g_down),
    )


def solution(mesh):
    copied = (P(),) * 19
    return jax.shard_map(
        on_device,
        mesh=mesh,
        in_specs=(P("dp", "seq", None), P("dp", "seq", None), P("dp")) + copied,
        out_specs=(
            P("dp", "seq", None), P("dp", "seq", None), P("seq"),
            P("seq", None), P("seq", None), P("seq", None), P("seq", None), P("seq", None), P("seq", None),
            P(), P(), P(), P(), P(),
            P("seq"), P("seq", None), P("seq", None), P("seq"), P("seq", None), P("seq", None), P("seq", None),
        ),
        check_vma=False,
    )
```

```python
import functools

import jax
import jax.numpy as jnp
import numpy as np
from jax import lax
from jax.experimental import pallas as pl
from jax.experimental.pallas import tpu as pltpu
from jax.sharding import PartitionSpec as P

HEADS = 8
KV_HEADS = 2
HEAD = 64
SSM_HEADS = 24
SSM_HEAD = 64
STATE = 128
WIDE = SSM_HEADS * SSM_HEAD
CHUNK = 128
EPS = 1e-05
ROPE_BASE = 100000000000.0
LOG2E = 1.4426950408889634
SCORE2 = 0.125 * LOG2E
LOWEST = -1e30
F32 = jnp.float32
BF16 = jnp.bfloat16
NN = (((1,), (0,)), ((), ()))
NT = (((1,), (1,)), ((), ()))
TN = (((0,), (0,)), ((), ()))
VMEM_LIMIT = 60 << 20


def dot(a, b, dims=NN):
    return lax.dot_general(a, b, dims, preferred_element_type=F32)


def dot_exact(a, b, dims=NN):
    return lax.dot_general(a, b, dims, precision=lax.Precision.HIGHEST, preferred_element_type=F32)


def low(v):
    return v.astype(BF16)


def sigmoid(v):
    return 1.0 / (1.0 + jnp.exp(-v))


def softplus(v):
    e = jnp.exp(-jnp.abs(v))
    tail = jnp.where(e < 1e-2, e * (1.0 - e * (0.5 - e * (1.0 / 3.0))), jnp.log(1.0 + e))
    return jnp.maximum(v, 0.0) + tail


def split_low(v):
    high = low(v)
    return high, low(v - high.astype(F32))


def widen(v, expand):
    return dot(jnp.concatenate(split_low(v), 1), expand)


def head_sums(v, expand):
    high, rest = split_low(v)
    ones = expand[:128]
    return dot(high, ones, NT) + dot(rest, ones, NT)


def cost(micros):
    return pl.CostEstimate(flops=int(micros * 3e9), bytes_accessed=int(micros * 1e5), transcendentals=0)


def full_spec(shape):
    return pl.BlockSpec(shape, lambda *_: (0,) * len(shape), pipeline_mode=pl.Buffered(1))


def params(limit=VMEM_LIMIT):
    return pltpu.CompilerParams(
        vmem_limit_bytes=limit, dimension_semantics=("arbitrary", "arbitrary")
    )


def low_rows(rows):
    t = lax.broadcasted_iota(jnp.int32, (rows, rows), 0)
    u = lax.broadcasted_iota(jnp.int32, (rows, rows), 1)
    return t >= u


def swap_halves(v):
    lane = lax.broadcasted_iota(jnp.int32, v.shape, 1)
    return jnp.where((lane & 63) < 32, pltpu.roll(v, 96, 1), pltpu.roll(v, 32, 1))


def pair_rows(v):
    lane = lax.broadcasted_iota(jnp.int32, v.shape, 1)
    none = jnp.zeros_like(v)
    return jnp.concatenate([jnp.where(lane < 64, v, none), jnp.where(lane >= 64, v, none)], 0)


def first_norm(v, gain):
    v = v.astype(F32)
    return low(v * lax.rsqrt(jnp.mean(v * v, -1, keepdims=True) + EPS) * gain)


def enter_body(tok_ref, gain_ref, wq_ref, wk_ref, wv_ref, cos_ref, sin_ref, hid_ref, q_ref, kv_ref):
    hid = first_norm(tok_ref[0], gain_ref[...])
    hid_ref[0] = hid
    cosine, sine = cos_ref[...], sin_ref[...]
    t = dot(hid, wk_ref[...])
    kv_ref[0, :, :128] = low(t * cosine + swap_halves(t) * sine)
    kv_ref[0, :, 128:] = low(dot(hid, wv_ref[...]))
    q = dot(hid, wq_ref[...])
    for g in range(4):
        t = q[:, g * 128 : g * 128 + 128]
        q_ref[0, :, g * 128 : g * 128 + 128] = low(t * cosine + swap_halves(t) * sine)


def enter(tokens, gain, wq, wk, wv, cosine, sine):
    seqs, span, width = tokens.shape
    rows = min(256, span)

    def row(n):
        return pl.BlockSpec((1, rows, n), lambda s, b: (s, b, 0))

    table = pl.BlockSpec((rows, 128), lambda s, b: (b, 0))
    return pl.pallas_call(
        enter_body,
        grid=(seqs, span // rows),
        in_specs=[row(width)] + [full_spec(v.shape) for v in (gain, wq, wk, wv)] + [table, table],
        out_specs=[row(width), row(512), row(256)],
        out_shape=[jax.ShapeDtypeStruct((seqs, span, n), BF16) for n in (width, 512, 256)],
        compiler_params=params(),
        cost_estimate=cost(8),
        name="enter",
    )(tokens, gain, wq, wk, wv, cosine, sine)


def mixer_body(
    pos_ref, len_ref, hid_ref, halo_ref, gain_ref, wz_ref, wc_ref, ws_ref, cw_ref, cb_ref, sb_ref, a_ref, exp_ref,
    z_ref, cl_ref, pre_ref, x_ref, bk_ref, cq_ref, dt_ref, sg_ref, cum_ref, cumt_ref, st_ref,
    prev, state, total, *, rows, blocks,
):
    s = pl.program_id(0)
    b = pl.program_id(1)

    @pl.when(b == 0)
    def _():
        prev[...] = dot(first_norm(halo_ref[0], gain_ref[...]), wc_ref[...])[8:]
        state[...] = jnp.zeros_like(state)
        total[...] = jnp.zeros_like(total)

    hid = hid_ref[0]
    conv = dot(hid, wc_ref[...])
    raw = dot(hid, ws_ref[...]) + sb_ref[...]
    z_ref[0] = low(dot(hid, wz_ref[...]))
    cl_ref[0] = low(conv)
    ext = jnp.concatenate([prev[...], conv], 0)
    prev[...] = conv[rows - 8 :]
    pre = cb_ref[...] + cw_ref[3:4] * conv
    for back in range(1, 4):
        pre = pre + cw_ref[3 - back : 4 - back] * pltpu.roll(ext, back, 0)[8:]
    pre_ref[0] = low(pre)
    act = low(pre * sigmoid(pre))
    x = act[:, :WIDE]
    bk = act[:, WIDE : WIDE + STATE]
    x_ref[0] = x
    bk_ref[0] = bk
    cq_ref[0] = act[:, WIDE + STATE :]
    at = pos_ref[0] + b * rows + lax.broadcasted_iota(jnp.int32, raw.shape, 0)
    live = jnp.where(at < len_ref[s], 1.0, 0.0)
    dt = softplus(raw) * live
    dt_ref[0] = dt
    sg_ref[0] = sigmoid(raw) * live
    log_decay = dt * a_ref[...]
    tri = jnp.where(low_rows(CHUNK), 1.0, 0.0)
    for c in range(rows // CHUNK):
        here = slice(c * CHUNK, (c + 1) * CHUNK)
        cum = dot_exact(tri, log_decay[here])
        cum_ref[0, here] = cum
        cumt_ref[0, :, here] = cum.T[:32]
        last = cum[CHUNK - 1 :]
        weight = dt[here] * jnp.exp2(last - cum)
        wide = widen(
            jnp.concatenate([weight, jnp.broadcast_to(jnp.exp2(last), (16, 128))], 0), exp_ref[...]
        )
        xw = low(x[here].astype(F32) * wide[:CHUNK])
        state[...] = state[...] * wide[CHUNK : CHUNK + 1] + dot(bk[here], xw, TN)
        total[...] = total[...] + last

    @pl.when(b == blocks - 1)
    def _():
        st_ref[0, :STATE] = low(state[...])
        st_ref[0, STATE:] = total_rows(total[...], exp_ref[...])


def total_rows(total, expand):
    wide = widen(jnp.broadcast_to(total, (8, 128)), expand)
    high = wide.astype(BF16).astype(F32)
    return low(jnp.concatenate([high, wide - high], 0))


def mixer(pos, lens, hid, halo, gain, wz, wc, ws, cw, cb, sb, a, expand):
    seqs, span, width = hid.shape
    rows = min(256, span)
    blocks = span // rows
    conv_width = wc.shape[1]

    def row(n):
        return pl.BlockSpec((1, rows, n), lambda s, b, *_: (s, b, 0))

    def shape(n, kind):
        return jax.ShapeDtypeStruct((seqs, span, n), kind)

    return pl.pallas_call(
        functools.partial(mixer_body, rows=rows, blocks=blocks),
        grid_spec=pltpu.PrefetchScalarGridSpec(
            num_scalar_prefetch=2,
            grid=(seqs, blocks),
            in_specs=[row(width), pl.BlockSpec((1, 16, width), lambda s, b, *_: (s, 0, 0))]
            + [full_spec(v.shape) for v in (gain, wz, wc, ws, cw, cb, sb, a, expand)],
            out_specs=[
                row(WIDE), row(conv_width), row(conv_width), row(WIDE), row(STATE), row(STATE),
                row(128), row(128), row(128),
                pl.BlockSpec((1, 32, rows), lambda s, b, *_: (s, 0, b)),
                pl.BlockSpec((1, STATE + 16, WIDE), lambda s, b, *_: (s, 0, 0)),
            ],
            scratch_shapes=[
                pltpu.VMEM((8, conv_width), F32), pltpu.VMEM((STATE, WIDE), F32), pltpu.VMEM((1, 128), F32),
            ],
        ),
        out_shape=[
            shape(WIDE, BF16), shape(conv_width, BF16), shape(conv_width, BF16), shape(WIDE, BF16),
            shape(STATE, BF16), shape(STATE, BF16), shape(128, F32), shape(128, F32), shape(128, F32),
            jax.ShapeDtypeStruct((seqs, 32, span), F32),
            jax.ShapeDtypeStruct((seqs, STATE + 16, WIDE), BF16),
        ],
        compiler_params=params(),
        cost_estimate=cost(20),
        name="mixer",
    )(pos, lens, hid, halo, gain, wz, wc, ws, cw, cb, sb, a, expand)


def joined(place, ref):
    state = jnp.zeros((STATE, WIDE), F32)
    for i in range(ref.shape[0]):
        logs = ref[i, 0, STATE : STATE + 1].astype(F32) + ref[i, 0, STATE + 8 : STATE + 9].astype(F32)
        state = jnp.where(i < place, state * jnp.exp2(logs) + ref[i, 0, :STATE].astype(F32), state)
    return state


def joined_later(refs):
    state = jnp.zeros((STATE, WIDE), F32)
    for ref in reversed(refs):
        logs = ref[0, STATE : STATE + 1].astype(F32) + ref[0, STATE + 8 : STATE + 9].astype(F32)
        state = state * jnp.exp2(logs) + ref[0, :STATE].astype(F32)
    return state


def gathered_spec(states):
    return pl.BlockSpec((states.shape[0], 1) + states.shape[2:], lambda s, c: (0, s, 0, 0), pipeline_mode=pl.Buffered(1))


SCALARS = pl.BlockSpec(memory_space=pltpu.SMEM)


def scan_body(
    place_ref, x_ref, bk_ref, cq_ref, dt_ref, cum_ref, cumt_ref, skip_ref, z_ref, gain_ref, exp_ref, all_ref,
    mix_ref, low_ref, st_ref, state, y,
):
    c = pl.program_id(1)

    @pl.when(c == 0)
    def _():
        state[...] = joined(place_ref[0], all_ref)

    x = x_ref[0].astype(F32)
    bk, cq = bk_ref[0], cq_ref[0]
    cum = cum_ref[0]
    last = cum[CHUNK - 1 :]
    expand = exp_ref[...]
    xdt = x * widen(dt_ref[0], expand)
    ends = widen(
        jnp.concatenate([jnp.exp2(cum), jnp.exp2(last - cum), jnp.broadcast_to(jnp.exp2(last), (16, 128))], 0),
        expand,
    )
    inter = jnp.where(low_rows(CHUNK), dot(cq, bk, NT), 0.0)
    held = low(state[...])
    st_ref[0, 0] = held
    y[...] = dot(cq, held) * ends[:CHUNK] + skip_ref[...] * x
    state[...] = state[...] * ends[2 * CHUNK : 2 * CHUNK + 1] + dot(bk, low(xdt * ends[CHUNK : 2 * CHUNK]), TN)
    xdt = low(xdt)
    for p in range(SSM_HEADS // 2):
        parts = []
        for h in (2 * p, 2 * p + 1):
            differ = jnp.minimum(cum[:, h : h + 1] - cumt_ref[0, h : h + 1, :], 0.0)
            parts.append(low(inter * jnp.exp2(differ)))
        cols = slice(p * 128, p * 128 + 128)
        y[:, cols] += dot(jnp.concatenate(parts, 1), pair_rows(xdt[:, cols]))
    mixed = y[...]
    mix_ref[0] = mixed
    z = z_ref[0].astype(F32)
    v = mixed * (z * sigmoid(z))
    low_ref[0] = low(v * lax.rsqrt(jnp.mean(v * v, -1, keepdims=True) + EPS) * gain_ref[...])


def scan_forward(place, x, bk, cq, dt, cum, cumt, skip, z, gain, expand, states):
    seqs, span, _ = x.shape
    chunks = span // CHUNK

    def row(n):
        return pl.BlockSpec((1, CHUNK, n), lambda s, c: (s, c, 0))

    return pl.pallas_call(
        scan_body,
        grid=(seqs, chunks),
        in_specs=[
            SCALARS, row(WIDE), row(STATE), row(STATE), row(128), row(128),
            pl.BlockSpec((1, 32, CHUNK), lambda s, c: (s, 0, c)),
            full_spec(skip.shape), row(WIDE), full_spec(gain.shape), full_spec(expand.shape), gathered_spec(states),
        ],
        out_specs=[row(WIDE), row(WIDE), pl.BlockSpec((1, 1, STATE, WIDE), lambda s, c: (s, c, 0, 0))],
        out_shape=[
            jax.ShapeDtypeStruct((seqs, span, WIDE), F32),
            jax.ShapeDtypeStruct((seqs, span, WIDE), BF16),
            jax.ShapeDtypeStruct((seqs, chunks, STATE, WIDE), BF16),
        ],
        scratch_shapes=[pltpu.VMEM((STATE, WIDE), F32), pltpu.VMEM((CHUNK, WIDE), F32)],
        compiler_params=params(),
        cost_estimate=cost(16),
        name="scan_forward",
    )(place, x, bk, cq, dt, cum, cumt, skip, z, gain, expand, states)


def middle_body(
    pos_ref, len_ref, near_ref, far_ref, mix_ref, tok_ref, cot_ref, mixed_ref, z_ref, cq_ref, cum_ref,
    wao_ref, wmo_ref, wg_ref, wu_ref, wd_ref, gain2_ref, gated_ref, exp_ref,
    out_ref, h2_ref, act_ref, gffn_ref, gg_ref, gu_ref, gmid_ref, gb_ref, gnear_ref, gfar_ref, gmixed_ref,
    gz_ref, attn_ref, gn2_ref, ggain_ref, adj_ref,
    gn2_s, ggain_s, adj, offset, *, rows, blocks, seqs,
):
    s = pl.program_id(0)
    b = pl.program_id(1)

    @pl.when((s == 0) & (b == 0))
    def _():
        gn2_s[...] = jnp.zeros_like(gn2_s)
        ggain_s[...] = jnp.zeros_like(ggain_s)

    @pl.when(b == 0)
    def _():
        adj[...] = jnp.zeros_like(adj)
        offset[...] = jnp.zeros_like(offset)

    at = pos_ref[0] + b * rows + lax.broadcasted_iota(jnp.int32, (rows, 1), 0)
    live = jnp.where(at < len_ref[s], 1.0, 0.0)
    attn = jnp.where(b < blocks // 2, near_ref[0], far_ref[0])
    attn_ref[0] = attn
    branch = dot(attn, wao_ref[...]) + dot(mix_ref[0], wmo_ref[...])
    after = tok_ref[0].astype(F32) + live * branch
    scale = lax.rsqrt(jnp.mean(after * after, -1, keepdims=True) + EPS)
    unit = after * scale
    gain = gain2_ref[...]
    h2 = low(unit * gain)
    h2_ref[0] = h2
    gate = dot(h2, wg_ref[...])
    up = dot(h2, wu_ref[...])
    sg = sigmoid(gate)
    silu = gate * sg
    act = low(silu * up)
    act_ref[0] = act
    out_ref[0] = low(after + live * dot(act, wd_ref[...]))
    cot = cot_ref[0].astype(F32)
    gffn = low(live * cot)
    gffn_ref[0] = gffn
    gact = dot(gffn, wd_ref[...], NT)
    gg = low(gact * up * (sg * (1.0 + gate * (1.0 - sg))))
    gu = low(gact * silu)
    gg_ref[0] = gg
    gu_ref[0] = gu
    gh2 = dot(gg, wg_ref[...], NT) + dot(gu, wu_ref[...], NT)
    gn2_s[...] += jnp.sum(gh2 * unit, 0, keepdims=True)
    g = gh2 * gain
    gmid = cot + scale * (g - unit * jnp.mean(g * unit, -1, keepdims=True))
    gmid_ref[0] = gmid
    gb = low(live * gmid)
    gb_ref[0] = gb
    gattn = low(dot(gb, wao_ref[...], NT))

    @pl.when(b < blocks // 2)
    def _():
        gnear_ref[0] = gattn

    @pl.when(b >= blocks // 2)
    def _():
        gfar_ref[0] = gattn

    gn = low(dot(gb, wmo_ref[...], NT)).astype(F32)
    mixed = mixed_ref[0]
    z = z_ref[0].astype(F32)
    sg = sigmoid(z)
    silu = z * sg
    v = mixed * silu
    scale = lax.rsqrt(jnp.mean(v * v, -1, keepdims=True) + EPS)
    unit = v * scale
    ggain_s[...] += jnp.sum(gn * unit, 0, keepdims=True)
    g = gn * gated_ref[...]
    g = scale * (g - unit * jnp.mean(g * unit, -1, keepdims=True))
    gmixed = g * silu
    gmixed_ref[0] = low(gmixed)
    gz_ref[0] = low(g * mixed * (sg * (1.0 + z * (1.0 - sg))))
    cum = cum_ref[0]
    logs = []
    for c in range(rows // CHUNK):
        here = cum[c * CHUNK : (c + 1) * CHUNK]
        logs.append(here + offset[...])
        offset[...] += here[CHUNK - 1 :]
    wide = widen(jnp.exp2(jnp.concatenate(logs, 0)), exp_ref[...])
    adj[...] += dot(cq_ref[0], low(gmixed * wide), TN)

    @pl.when(b == blocks - 1)
    def _():
        adj_ref[0, :STATE] = low(adj[...])
        adj_ref[0, STATE:] = total_rows(offset[...], exp_ref[...])

    @pl.when((s == seqs - 1) & (b == blocks - 1))
    def _():
        gn2_ref[...] = gn2_s[...]
        ggain_ref[...] = ggain_s[...]


def middle(pos, lens, near, far, mix, tokens, cot, mixed, z, cq, cum, wao, wmo, wg, wu, wd, gain2, gated, expand):
    seqs, span, width = tokens.shape
    rows = min(256, span // 2)
    blocks = span // rows
    ff = wg.shape[1]
    lower = pl.BlockSpec((1, rows, 512), lambda s, b, *_: (s, jnp.minimum(b, blocks // 2 - 1), 0))
    upper = pl.BlockSpec((1, rows, 512), lambda s, b, *_: (s, jnp.maximum(b - blocks // 2, 0), 0))

    def row(n):
        return pl.BlockSpec((1, rows, n), lambda s, b, *_: (s, b, 0))

    def shape(n, kind):
        return jax.ShapeDtypeStruct((seqs, span, n), kind)

    def once(n):
        return pl.BlockSpec((1, n), lambda s, b, *_: (0, 0))

    return pl.pallas_call(
        functools.partial(middle_body, rows=rows, blocks=blocks, seqs=seqs),
        grid_spec=pltpu.PrefetchScalarGridSpec(
            num_scalar_prefetch=2,
            grid=(seqs, blocks),
            in_specs=[
                lower, upper, row(WIDE), row(width), row(width), row(WIDE), row(WIDE), row(STATE), row(128),
                full_spec(wao.shape), full_spec(wmo.shape), full_spec(wg.shape), full_spec(wu.shape),
                full_spec(wd.shape), full_spec(gain2.shape), full_spec(gated.shape), full_spec(expand.shape),
            ],
            out_specs=[
                row(width), row(width), row(ff), row(width), row(ff), row(ff), row(width), row(width),
                lower, upper, row(WIDE), row(WIDE), row(512),
                once(width), once(WIDE),
                pl.BlockSpec((1, STATE + 16, WIDE), lambda s, b, *_: (s, 0, 0)),
            ],
            scratch_shapes=[
                pltpu.VMEM((1, width), F32), pltpu.VMEM((1, WIDE), F32), pltpu.VMEM((STATE, WIDE), F32),
                pltpu.VMEM((1, 128), F32),
            ],
        ),
        out_shape=[
            shape(width, BF16), shape(width, BF16), shape(ff, BF16), shape(width, BF16), shape(ff, BF16),
            shape(ff, BF16), shape(width, F32), shape(width, BF16),
            jax.ShapeDtypeStruct((seqs, span // 2, 512), BF16), jax.ShapeDtypeStruct((seqs, span // 2, 512), BF16),
            shape(WIDE, BF16), shape(WIDE, BF16), shape(512, BF16),
            jax.ShapeDtypeStruct((1, width), F32), jax.ShapeDtypeStruct((1, WIDE), F32),
            jax.ShapeDtypeStruct((seqs, STATE + 16, WIDE), BF16),
        ],
        compiler_params=params(),
        cost_estimate=cost(60),
        name="middle",
    )(pos, lens, near, far, mix, tokens, cot, mixed, z, cq, cum, wao, wmo, wg, wu, wd, gain2, gated, expand)


def scan_back_body(
    x_ref, bk_ref, cq_ref, dt_ref, sg_ref, cum_ref, cumt_ref, dy_ref, mix_ref, st_ref, pre_ref, cl_ref,
    skip_ref, a_ref, cw_ref, exp_ref, *rest, chunks, conv_width,
):
    *later, gc_ref, tail_ref, head_ref, gw_ref, gskip_ref, small_ref, adj, after, gact = rest
    s = pl.program_id(0)
    c = pl.program_id(1)

    @pl.when((s == 0) & (c == 0))
    def _():
        gw_ref[...] = jnp.zeros_like(gw_ref)
        gskip_ref[...] = jnp.zeros_like(gskip_ref)
        small_ref[...] = jnp.zeros_like(small_ref)

    @pl.when(c == 0)
    def _():
        adj[...] = joined_later(later)
        after[...] = jnp.zeros_like(after)

    x = x_ref[0].astype(F32)
    bk, cq = bk_ref[0], cq_ref[0]
    dt = dt_ref[0]
    cum = cum_ref[0]
    last = cum[CHUNK - 1 :]
    expand = exp_ref[...]
    dt_wide = widen(dt, expand)
    ends = widen(
        jnp.concatenate([jnp.exp2(cum), jnp.exp2(last - cum), jnp.broadcast_to(jnp.exp2(last), (16, 128))], 0),
        expand,
    )
    to_end = ends[CHUNK : 2 * CHUNK]
    all_wide = ends[2 * CHUNK : 2 * CHUNK + 1]
    xdt = x * dt_wide
    dy_low = dy_ref[0]
    dy = dy_low.astype(F32)
    dy_in = low(dy * ends[:CHUNK])
    state = st_ref[0, 0]
    gstate = adj[...]
    gstate_low = low(gstate)
    from_end = dot(bk, gstate_low) * to_end
    gb = dot(low(xdt * to_end), gstate_low, NT)
    gc = dot(dy_in, state, NT)
    gfinal = all_wide * jnp.sum(gstate * state.astype(F32), 0, keepdims=True) + jnp.sum(
        xdt * from_end, 0, keepdims=True
    )
    adj[...] = gstate * all_wide + dot(cq, dy_in, TN)
    xdt_low = low(xdt)
    u = lax.broadcasted_iota(jnp.int32, (CHUNK, CHUNK), 0)
    t = lax.broadcasted_iota(jnp.int32, (CHUNK, CHUNK), 1)
    inter = jnp.where(t >= u, dot(bk, cq, NT), 0.0)
    ginter = jnp.zeros((CHUNK, CHUNK), F32)
    for p in range(SSM_HEADS // 2):
        cols = slice(p * 128, p * 128 + 128)
        dy_rows = pair_rows(dy_low[:, cols])
        gmix = dot(xdt_low[:, cols], dy_rows, NT)
        parts = []
        for n, h in enumerate((2 * p, 2 * p + 1)):
            decay = jnp.exp2(jnp.minimum(cumt_ref[0, h : h + 1, :] - cum[:, h : h + 1], 0.0))
            parts.append(low(inter * decay))
            ginter = ginter + gmix[:, n * CHUNK : (n + 1) * CHUNK] * decay
        gact[:, cols] = dot(jnp.concatenate(parts, 1), dy_rows)
    ginter = low(jnp.where(t >= u, ginter, 0.0))
    gact[:, WIDE : WIDE + STATE] = gb + dot(ginter, cq)
    gact[:, WIDE + STATE :] = gc + dot(ginter, bk, TN)
    gxdt = gact[:, :WIDE] + from_end
    skip = skip_ref[...]
    gact[:, :WIDE] = dt_wide * gxdt + skip * dy
    gskip_ref[...] += jnp.sum(dy * x, 0, keepdims=True)
    sums = head_sums(
        jnp.concatenate([x * gxdt, dy * (mix_ref[0] - skip * x), jnp.broadcast_to(gfinal, (16, WIDE))], 0), expand
    )
    direct = sums[:CHUNK]
    gcum = sums[CHUNK : 2 * CHUNK] - dt * direct
    gld = dot_exact(jnp.where(t >= u, 1.0, 0.0), gcum) + sums[2 * CHUNK : 2 * CHUNK + 1]
    a = a_ref[...]
    gstep = (direct + a * gld) * sg_ref[0]
    gc_ref[0, :, conv_width : conv_width + 128] = low(gstep)
    gc_ref[0, :, conv_width + 128 :] = jnp.zeros((CHUNK, 128), BF16)
    small_ref[0:1] += jnp.sum(dt * gld, 0, keepdims=True) * a
    small_ref[1:2] += jnp.sum(gstep, 0, keepdims=True)
    pre = pre_ref[0].astype(F32)
    sg = sigmoid(pre)
    gpre = gact[...] * (sg * (1.0 + pre * (1.0 - sg)))
    ext = jnp.concatenate([gpre, after[...]], 0)
    after[...] = gpre[:8]
    conv = cl_ref[0].astype(F32)
    gconv = cw_ref[3:4] * gpre
    gw_ref[3:4] += jnp.sum(conv * gpre, 0, keepdims=True)
    gw_ref[4:5] += jnp.sum(gpre, 0, keepdims=True)
    for ahead in range(1, 4):
        moved = pltpu.roll(ext, CHUNK + 8 - ahead, 0)[:CHUNK]
        gconv = gconv + cw_ref[3 - ahead : 4 - ahead] * moved
        gw_ref[3 - ahead : 4 - ahead] += jnp.sum(conv * moved, 0, keepdims=True)
    gc_ref[0, :, :conv_width] = low(gconv)

    @pl.when(c == 0)
    def _():
        tail_ref[0] = gconv[CHUNK - 8 :]

    @pl.when(c == chunks - 1)
    def _():
        head_ref[0] = gpre[:8]


def scan_backward(x, bk, cq, dt, sg, cum, cumt, dy, mixed, states, pre, conv, skip, a, cw, expand, adjoints):
    seqs, span, _ = x.shape
    chunks = span // CHUNK
    conv_width = pre.shape[2]

    def row(n):
        return pl.BlockSpec((1, CHUNK, n), lambda s, c: (s, chunks - 1 - c, 0))

    def once(m, n):
        return pl.BlockSpec((m, n), lambda s, c: (0, 0))

    edge = pl.BlockSpec((1, 8, conv_width), lambda s, c: (s, 0, 0))
    return pl.pallas_call(
        functools.partial(scan_back_body, chunks=chunks, conv_width=conv_width),
        grid=(seqs, chunks),
        in_specs=[
            row(WIDE), row(STATE), row(STATE), row(128), row(128), row(128),
            pl.BlockSpec((1, 32, CHUNK), lambda s, c: (s, 0, chunks - 1 - c)),
            row(WIDE), row(WIDE),
            pl.BlockSpec((1, 1, STATE, WIDE), lambda s, c: (s, chunks - 1 - c, 0, 0)),
            row(conv_width), row(conv_width),
            full_spec(skip.shape), full_spec(a.shape), full_spec(cw.shape), full_spec(expand.shape),
        ]
        + [
            pl.BlockSpec((1, STATE + 16, WIDE), lambda s, c: (s, 0, 0), pipeline_mode=pl.Buffered(1))
            for _ in adjoints
        ],
        out_specs=[row(conv_width + 256), edge, edge, once(8, conv_width), once(1, WIDE), once(8, 128)],
        out_shape=[
            jax.ShapeDtypeStruct((seqs, span, conv_width + 256), BF16),
            jax.ShapeDtypeStruct((seqs, 8, conv_width), F32),
            jax.ShapeDtypeStruct((seqs, 8, conv_width), F32),
            jax.ShapeDtypeStruct((8, conv_width), F32),
            jax.ShapeDtypeStruct((1, WIDE), F32),
            jax.ShapeDtypeStruct((8, 128), F32),
        ],
        scratch_shapes=[
            pltpu.VMEM((STATE, WIDE), F32), pltpu.VMEM((8, conv_width), F32), pltpu.VMEM((CHUNK, conv_width), F32),
        ],
        compiler_params=params(),
        cost_estimate=cost(35),
        name="scan_backward",
    )(x, bk, cq, dt, sg, cum, cumt, dy, mixed, states, pre, conv, skip, a, cw, expand, *adjoints)


def leave_mixer_body(gz_ref, gc_ref, wz_ref, wc_ref, ws_ref, gh_ref, *, conv_width):
    gh = dot(gz_ref[0], wz_ref[...], NT) + dot(gc_ref[0, :, :conv_width], wc_ref[...], NT)
    gh_ref[0] = gh + dot(gc_ref[0, :, conv_width : conv_width + 128], ws_ref[...], NT)


def leave_mixer(gz, gc, wz, wc, ws):
    seqs, span, _ = gz.shape
    rows = min(256, span)

    def row(n):
        return pl.BlockSpec((1, rows, n), lambda s, b: (s, b, 0))

    width = wz.shape[0]
    return pl.pallas_call(
        functools.partial(leave_mixer_body, conv_width=wc.shape[1]),
        grid=(seqs, span // rows),
        in_specs=[row(gz.shape[2]), row(gc.shape[2])] + [full_spec(v.shape) for v in (wz, wc, ws)],
        out_specs=row(width),
        out_shape=jax.ShapeDtypeStruct((seqs, span, width), F32),
        compiler_params=params(),
        cost_estimate=cost(0),
        name="leave_mixer",
    )(gz, gc, wz, wc, ws)


def leave_body(tok_ref, gmid_ref, gh_ref, gain_ref, wq_ref, wk_ref, wv_ref, cos_ref, sin_ref, *rest, blocks, count):
    near, far = rest[:2], rest[2:4]
    pieces = rest[4 : 4 + 2 * count]
    gt_ref, gn_ref, gq_ref, gkv_ref = rest[4 + 2 * count :]
    b = pl.program_id(1)

    @pl.when((pl.program_id(0) == 0) & (b == 0))
    def _():
        gn_ref[...] = jnp.zeros_like(gn_ref)

    for j in range(2):
        gq_ref[0, :, 256 * j : 256 * j + 256] = jnp.where(b < blocks // 2, near[j][0], far[j][0])
    sums = []
    for j in range(2):
        t = pieces[j * count][0].astype(F32)
        for r in range(1, count):
            t = t + pieces[j * count + r][0].astype(F32)
        sums.append(t)
    lane = lax.broadcasted_iota(jnp.int32, sums[0].shape, 1)
    gk = jnp.where(lane < 64, sums[0], pltpu.roll(sums[1], 64, 1))
    gv = low(jnp.where(lane < 64, pltpu.roll(sums[0], 64, 1), sums[1]))
    gk = low(gk * cos_ref[...] - swap_halves(gk) * sin_ref[...])
    gkv_ref[0, :, :128] = gk
    gkv_ref[0, :, 128:] = gv
    gh = gh_ref[0] + dot(gq_ref[0], wq_ref[...], NT) + dot(gk, wk_ref[...], NT) + dot(gv, wv_ref[...], NT)
    v = tok_ref[0].astype(F32)
    scale = lax.rsqrt(jnp.mean(v * v, -1, keepdims=True) + EPS)
    unit = v * scale
    gn_ref[...] += jnp.sum(gh * unit, 0, keepdims=True)
    g = gh * gain_ref[...]
    gt_ref[0] = gmid_ref[0] + scale * (g - unit * jnp.mean(g * unit, -1, keepdims=True))


def leave(tokens, gmid, gh, gain, wq, wk, wv, cosine, sine, near, far, pieces):
    seqs, span, width = tokens.shape
    rows = min(256, span // 2)
    blocks = span // rows
    count = len(pieces) // 2

    def row(n):
        return pl.BlockSpec((1, rows, n), lambda s, b: (s, b, 0))

    table = pl.BlockSpec((rows, 128), lambda s, b: (b, 0))
    lower = pl.BlockSpec((1, rows, 256), lambda s, b: (s, jnp.minimum(b, blocks // 2 - 1), 0))
    upper = pl.BlockSpec((1, rows, 256), lambda s, b: (s, jnp.maximum(b - blocks // 2, 0), 0))
    return pl.pallas_call(
        functools.partial(leave_body, blocks=blocks, count=count),
        grid=(seqs, blocks),
        in_specs=[row(width)] * 3
        + [full_spec(v.shape) for v in (gain, wq, wk, wv)]
        + [table, table, lower, lower, upper, upper]
        + [row(128)] * (2 * count),
        out_specs=[row(width), pl.BlockSpec((1, width), lambda s, b: (0, 0)), row(512), row(256)],
        out_shape=[
            jax.ShapeDtypeStruct((seqs, span, width), F32), jax.ShapeDtypeStruct((1, width), F32),
            jax.ShapeDtypeStruct((seqs, span, 512), BF16), jax.ShapeDtypeStruct((seqs, span, 256), BF16),
        ],
        compiler_params=params(),
        cost_estimate=cost(10),
        name="leave",
    )(tokens, gmid, gh, gain, wq, wk, wv, cosine, sine, *near, *far, *pieces)


def dup_halves(v):
    lane = lax.broadcasted_iota(jnp.int32, v.shape, 1)
    other = pltpu.roll(v, 64, 1)
    return low(jnp.where(lane < 64, v, other)), low(jnp.where(lane < 64, other, v))


def head_rows(v):
    lane = lax.broadcasted_iota(jnp.int32, (v.shape[0], 128), 1)
    heads = []
    for h in range(v.shape[1] // HEAD):
        t = v[:, (h // 2) * 128 : (h // 2) * 128 + 128]
        heads.append(jnp.where((lane < 64) if h % 2 == 0 else (lane >= 64), t, jnp.zeros_like(t)))
    return heads


def key_range(first, length, rows, keys):
    whole = jnp.minimum((first + 1) // keys, length // keys)
    some = jnp.minimum((first + rows + keys - 1) // keys, (length + keys - 1) // keys)
    return whole, some


def seen(i, first, length, rows, keys):
    key_at = i * keys + lax.broadcasted_iota(jnp.int32, (keys, rows), 0)
    query_at = first + lax.broadcasted_iota(jnp.int32, (keys, rows), 1)
    return (key_at <= query_at) & (key_at < length)


def attend_body(
    pos_ref, len_ref, from_ref, q_ref, other_ref, *rest, rows, keys, blocks, count, span,
):
    kv_refs = rest[:count]
    near_ref, far_ref, lse_ref, kd, vt, top, acc, score_a, score_b, top_a, top_b = rest[count:]
    s = pl.program_id(0)
    b = pl.program_id(1)
    prep = min(512, span)

    @pl.when(b == 0)
    def _():
        ones = jnp.ones((16, prep), F32)
        for r, kv_ref in enumerate(kv_refs):
            for i in range(span // prep):
                here = slice(i * prep, (i + 1) * prep)
                at = pl.ds(pl.multiple_of(from_ref[r] * span + i * prep, prep), prep)
                kd[0, at, :], kd[1, at, :] = dup_halves(kv_ref[0, here, :128].astype(F32))
                t = kv_ref[0, here, 128:].astype(F32).T
                vt[0, :, at] = low(jnp.concatenate([t[:64], ones], 0))
                vt[1, :, at] = low(jnp.concatenate([t[64:], ones], 0))

    first = pos_ref[b]
    length = len_ref[s]
    heads = head_rows(jnp.where(b < blocks // 2, q_ref[0], other_ref[0]))
    top[...] = jnp.full_like(top, LOWEST)
    acc[...] = jnp.zeros_like(acc)
    whole, some = key_range(first, length, rows, keys)

    def scores(i, buffer, tops, h, mask=None):
        at = pl.ds(pl.multiple_of(i * keys, keys), keys)
        t = dot(kd[h // 4, at, :], heads[h], NT)
        if mask is not None:
            t = jnp.where(mask, t, LOWEST)
        buffer[h] = t
        tops[h] = jnp.max(t, 0, keepdims=True)

    def add(i, buffer, tops, h):
        at = pl.ds(pl.multiple_of(i * keys, keys), keys)
        before = top[h]
        now = jnp.maximum(before, tops[h])
        p = low(jnp.exp2((buffer[h] - now) * SCORE2))
        acc[h] = acc[h] * jnp.exp2((before - now) * SCORE2) + dot(vt[h // 4, :, at], p)
        top[h] = now

    def edge(i, _):
        mask = seen(i, first, length, rows, keys)
        for h in range(HEADS):
            scores(i, score_a, top_a, h, mask)
        for h in range(HEADS):
            add(i, score_a, top_a, h)
        return 0

    lax.fori_loop(whole, some, edge, 0)
    last = jnp.maximum(whole - 1, 0)
    for h in range(HEADS):
        scores(0, score_a, top_a, h)

    def two(i, _):
        for h in range(HEADS):
            scores(2 * i + 1, score_b, top_b, h)
            add(2 * i, score_a, top_a, h)
        following = jnp.minimum(2 * i + 2, last)
        for h in range(HEADS):
            scores(following, score_a, top_a, h)
            add(2 * i + 1, score_b, top_b, h)
        return 0

    lax.fori_loop(0, whole // 2, two, 0)

    @pl.when(whole % 2 == 1)
    def _():
        for h in range(HEADS):
            add(last, score_a, top_a, h)

    outs = []
    for h in range(HEADS):
        t = acc[h]
        weight = t[64:65]
        outs.append(t[:64] / weight)
        lse_ref[0, h : h + 1, :] = top[h] * SCORE2 + jnp.log2(weight)
    result = low(jnp.concatenate(outs, 0).T)

    @pl.when(b < blocks // 2)
    def _():
        near_ref[0] = result

    @pl.when(b >= blocks // 2)
    def _():
        far_ref[0] = result


def halves_specs(rows, blocks, columns):
    lower = pl.BlockSpec((1, rows, columns), lambda s, b, *_: (s, jnp.minimum(b, blocks // 2 - 1), 0))
    upper = pl.BlockSpec((1, rows, columns), lambda s, b, *_: (s, jnp.maximum(b - blocks // 2, 0), 0))
    return lower, upper


def attend(pos, lens, sources, q, other, kvs):
    seqs, span, _ = q.shape
    count = len(kvs)
    total = count * span
    rows = min(256, span // 2)
    keys = 256
    blocks = span // rows
    lower, upper = halves_specs(rows, blocks, 512)
    half = jax.ShapeDtypeStruct((seqs, span // 2, 512), BF16)
    return pl.pallas_call(
        functools.partial(attend_body, rows=rows, keys=keys, blocks=blocks, count=count, span=span),
        grid_spec=pltpu.PrefetchScalarGridSpec(
            num_scalar_prefetch=3,
            grid=(seqs, blocks),
            in_specs=[lower, upper]
            + [pl.BlockSpec((1, span, 256), lambda s, b, *_: (s, 0, 0), pipeline_mode=pl.Buffered(1))] * count,
            out_specs=[lower, upper, pl.BlockSpec((1, 8, rows), lambda s, b, *_: (s, 0, b))],
            scratch_shapes=[
                pltpu.VMEM((2, total, 128), BF16), pltpu.VMEM((2, 80, total), BF16),
                pltpu.VMEM((8, 1, rows), F32), pltpu.VMEM((8, 80, rows), F32),
                pltpu.VMEM((8, keys, rows), F32), pltpu.VMEM((8, keys, rows), F32),
                pltpu.VMEM((8, 1, rows), F32), pltpu.VMEM((8, 1, rows), F32),
            ],
        ),
        out_shape=[half, half, jax.ShapeDtypeStruct((seqs, 8, span), F32)],
        compiler_params=params(),
        cost_estimate=cost(26),
        name="attend",
    )(pos, lens, sources, q, other, *kvs)


def attend_back_body(
    pos_ref, len_ref, from_ref, q_ref, other_ref, do_near_ref, do_far_ref, o_near_ref, o_far_ref, lse_ref,
    cos_ref, sin_ref, *rest, rows, keys, blocks, count, span, group,
):
    kv_refs = rest[:count]
    dq_near_ref, dq_far_ref = rest[count : count + 2]
    dkv_refs = rest[count + 2 : 2 * count + 2]
    kd, vd, kt, dk, dv, dq = rest[2 * count + 2 :]
    s = pl.program_id(0)
    b = pl.program_id(1)
    prep = min(512, span)

    @pl.when(b == 0)
    def _():
        for r, kv_ref in enumerate(kv_refs):
            for i in range(span // prep):
                here = slice(i * prep, (i + 1) * prep)
                at = pl.ds(pl.multiple_of(from_ref[r] * span + i * prep, prep), prep)
                k = kv_ref[0, here, :128].astype(F32)
                kd[at, :] = dup_halves(k)[group]
                vd[at, :] = dup_halves(kv_ref[0, here, 128:].astype(F32))[group]
                kt[:, at] = low(k.T[64 * group : 64 * group + 64])
        dk[...] = jnp.zeros_like(dk)
        dv[...] = jnp.zeros_like(dv)

    first = pos_ref[b]
    length = len_ref[s]
    is_near = b < blocks // 2
    heads = head_rows(jnp.where(is_near, q_ref[0], other_ref[0]))
    do = jnp.where(is_near, do_near_ref[0], do_far_ref[0])
    grads = head_rows(do)
    prod = do.astype(F32) * jnp.where(is_near, o_near_ref[0], o_far_ref[0]).astype(F32)
    col = lax.broadcasted_iota(jnp.int32, (8, 256), 1) // HEAD
    ones = low(jnp.where(col == lax.broadcasted_iota(jnp.int32, (8, 256), 0), 1.0, 0.0))
    high, remain = split_low(prod)
    delta = dot(ones, high, NT) + dot(ones, remain, NT)
    dq[...] = jnp.zeros_like(dq)
    whole, some = key_range(first, length, rows, keys)

    def step(i, masked):
        at = pl.ds(pl.multiple_of(i * keys, keys), keys)
        mask = seen(i, first, length, rows, keys) if masked else None
        dv_sum = dk_sum = None
        for h in range(4):
            x = dot(kd[at, :], heads[h], NT) * SCORE2 - lse_ref[0, 4 * group + h : 4 * group + h + 1, :]
            dp = dot(vd[at, :], grads[h], NT)
            if masked:
                x = jnp.where(mask, x, LOWEST)
            p = jnp.exp2(x)
            ds = low(p * (dp - delta[h : h + 1]))
            dv_part = dot(low(p), grads[h])
            dk_part = dot(ds, heads[h])
            dv_sum = dv_part if dv_sum is None else dv_sum + dv_part
            dk_sum = dk_part if dk_sum is None else dk_sum + dk_part
            dq[h] += dot(kt[:, at], ds)
        dv[at, :] += dv_sum
        dk[at, :] += dk_sum

    lax.fori_loop(0, whole, lambda i, _: (step(i, False), 0)[1], 0)
    lax.fori_loop(whole, some, lambda i, _: (step(i, True), 0)[1], 0)
    cosine, sine = cos_ref[...], sin_ref[...]
    parts = []
    for h in range(4):
        t = dq[h] * 0.125
        former, latter = t[:32], t[32:]
        parts += [former * cosine + latter * sine, latter * cosine - former * sine]
    result = low(jnp.concatenate(parts, 0).T)

    @pl.when(is_near)
    def _():
        dq_near_ref[0] = result

    @pl.when(jnp.logical_not(is_near))
    def _():
        dq_far_ref[0] = result

    @pl.when(b == blocks - 1)
    def _():
        lane = lax.broadcasted_iota(jnp.int32, (prep, 128), 1)
        for r, dkv_ref in enumerate(dkv_refs):
            for i in range(span // prep):
                at = pl.ds(pl.multiple_of(from_ref[r] * span + i * prep, prep), prep)
                k, v = dk[at, :], dv[at, :]
                k = (k + pltpu.roll(k, 64, 1)) * 0.125
                v = v + pltpu.roll(v, 64, 1)
                dkv_ref[0, i * prep : (i + 1) * prep] = low(jnp.where(lane < 64, k, v))


def attend_backward(group, pos, lens, sources, q, other, do_near, do_far, o_near, o_far, lse, cosine, sine, kvs):
    seqs, span, _ = q.shape
    count = len(kvs)
    total = count * span
    rows = min(256, span // 2)
    keys = 512
    blocks = span // rows
    lower = pl.BlockSpec((1, rows, 256), lambda s, b, *_: (s, jnp.minimum(b, blocks // 2 - 1), group))
    upper = pl.BlockSpec((1, rows, 256), lambda s, b, *_: (s, jnp.maximum(b - blocks // 2, 0), group))
    out_lower, out_upper = halves_specs(rows, blocks, 256)
    stat = pl.BlockSpec((1, 8, rows), lambda s, b, *_: (s, 0, b))
    table = pl.BlockSpec((32, rows), lambda s, b, *_: (0, b))
    half = jax.ShapeDtypeStruct((seqs, span // 2, 256), BF16)
    outs = pl.pallas_call(
        functools.partial(
            attend_back_body, rows=rows, keys=keys, blocks=blocks, count=count, span=span, group=group
        ),
        grid_spec=pltpu.PrefetchScalarGridSpec(
            num_scalar_prefetch=3,
            grid=(seqs, blocks),
            in_specs=[lower, upper, lower, upper, lower, upper, stat, table, table]
            + [pl.BlockSpec((1, span, 256), lambda s, b, *_: (s, 0, 0), pipeline_mode=pl.Buffered(1))] * count,
            out_specs=[out_lower, out_upper]
            + [pl.BlockSpec((1, span, 128), lambda s, b, *_: (s, 0, 0))] * count,
            scratch_shapes=[
                pltpu.VMEM((total, 128), BF16), pltpu.VMEM((total, 128), BF16), pltpu.VMEM((64, total), BF16),
                pltpu.VMEM((total, 128), F32), pltpu.VMEM((total, 128), F32), pltpu.VMEM((4, 64, rows), F32),
            ],
        ),
        out_shape=[half, half] + [jax.ShapeDtypeStruct((seqs, span, 128), BF16)] * count,
        compiler_params=params(),
        cost_estimate=cost(4 if group else 4),
        name="attend_backward",
    )(pos, lens, sources, q, other, do_near, do_far, o_near, o_far, lse, cosine, sine, *kvs)
    return outs[0], outs[1], outs[2:]


def tall_body(sel_ref, left_ref, *rest, n, widths, with_got, square):
    rights = rest[: len(widths)]
    rest = rest[len(widths) :]
    got_ref = rest[0] if with_got else None
    outs = rest[1:] if with_got else rest
    rows = left_ref.shape[1] // n
    i = pl.program_id(0)
    start = 0
    for part, (right, steps) in enumerate(zip(rights, widths)):

        @pl.when((i >= start) & (i < start + steps))
        def _(part=part, right=right):
            if square:
                if square == "hops":
                    own, to_x, keep_x, to_y, keep_y = outs
                    first, keep = ((to_x, keep_x), (to_y, keep_y))[part]
                for k in range(4):
                    block = jnp.bitwise_xor(sel_ref[1], k)
                    columns = pl.ds(pl.multiple_of(block * rows, rows), rows)
                    value = dot(left_ref[:, columns], right[...], TN)
                    if with_got:
                        value = value + got_ref[block].astype(F32)
                    value = low(value)
                    if square == "direct":
                        outs[k][...] = value
                    elif k == 0:
                        own[...] = value
                    elif k == 3:
                        first[1] = value
                    elif k == part + 1:
                        first[0] = value
                    else:
                        keep[...] = value
            else:
                value = dot(left_ref[...], right[...], TN)
                for j in range(n):
                    here = value[j * rows : (j + 1) * rows]
                    outs[0][j] = low(here + got_ref[j].astype(F32) if with_got else here)

        start += steps


def tall_grad(sel, left, rights, chunk, n, got=None, square="", micros=0.0, name="grad"):
    tokens, width = left.shape
    widths = [v.shape[1] // 2 // chunk for v in rights]
    steps = sum(widths)
    rows = width // n
    starts = [0, widths[0]]

    def within(k, i):
        return jnp.clip(i - starts[k], 0, widths[k] - 1)

    def right_spec(k):
        return pl.BlockSpec((tokens, chunk), lambda i, sel: (0, sel[0] * widths[k] + within(k, i)))

    whole = pl.BlockSpec((n, rows, chunk), lambda i, sel: (0, i, 0))
    extra = () if got is None else (got,)
    if square == "direct":
        out_specs = [pl.BlockSpec((rows, chunk), lambda i, sel: (i, 0))] * 4
        out_shape = [jax.ShapeDtypeStruct((steps * rows, chunk), BF16)] * 4
    elif square:
        out_specs = [pl.BlockSpec((rows, chunk), lambda i, sel: (i, 0))]
        out_shape = [jax.ShapeDtypeStruct((steps * rows, chunk), BF16)]
        for k in range(2):
            out_specs.append(pl.BlockSpec((2, rows, chunk), lambda i, sel, k=k: (0, within(k, i), 0)))
            out_specs.append(pl.BlockSpec((rows, chunk), lambda i, sel, k=k: (within(k, i), 0)))
            out_shape.append(jax.ShapeDtypeStruct((2, widths[k] * rows, chunk), BF16))
            out_shape.append(jax.ShapeDtypeStruct((widths[k] * rows, chunk), BF16))
    else:
        out_specs = whole
        out_shape = jax.ShapeDtypeStruct((n, steps * rows, chunk), BF16)
    return pl.pallas_call(
        functools.partial(tall_body, n=n, widths=widths, with_got=bool(extra), square=square),
        grid_spec=pltpu.PrefetchScalarGridSpec(
            num_scalar_prefetch=1,
            grid=(steps,),
            in_specs=[full_spec(left.shape)] + [right_spec(k) for k in range(2)] + [whole] * len(extra),
            out_specs=out_specs,
        ),
        out_shape=out_shape,
        compiler_params=pltpu.CompilerParams(vmem_limit_bytes=VMEM_LIMIT),
        cost_estimate=cost(micros),
        name=name,
    )(sel, left, *rights, *extra)


def wide_body(sel_ref, *rest, parts, group, with_got, square):
    lefts, rights = rest[:parts], rest[parts : 2 * parts]
    rest = rest[2 * parts :]
    got_ref = rest[0] if with_got else None
    outs = rest[1:] if with_got else rest
    values = [dot(left[...], right[...], TN) for left, right in zip(lefts, rights)]
    if square:
        own, to_x, keep_x, to_y, keep_y = outs
        value = jnp.concatenate(values, 0)
        if with_got:
            value = value + got_ref[0].astype(F32)
        value = low(value)
        split = values[0].shape[0]
        for k in range(4):

            @pl.when(pl.program_id(0) == k)
            def _(k=k):
                if k == 0:
                    own[...] = value
                    return
                for part, (first, keep) in enumerate(((to_x, keep_x), (to_y, keep_y))):
                    here = value[split:] if part else value[:split]
                    if k == 3:
                        first[1] = here
                    elif k == part + 1:
                        first[0] = here
                    else:
                        keep[...] = here
    else:
        for j in range(group):
            start = 0
            for v in values:
                rows = v.shape[0] // group
                here = v[j * rows : (j + 1) * rows]
                at = slice(start, start + rows)
                outs[0][j, at] = low(here + got_ref[j, at].astype(F32) if with_got else here)
                start += rows


def wide_grad(sel, lefts, rights, n, got=None, square="", micros=0.0, name="grad"):
    tokens = lefts[0].shape[0]
    chunk = rights[0].shape[1] // 2
    steps = min(n, 4)
    rows = [v.shape[1] // n for v in lefts]
    total = sum(rows)

    def turn(i, sel):
        return jnp.bitwise_xor(sel[1], i) if square else i

    def once(*dims):
        return pl.BlockSpec(dims, lambda i, sel: (0,) * len(dims))

    whole = pl.BlockSpec((n // steps, total, chunk), lambda i, sel: (turn(i, sel), 0, 0))
    extra = () if got is None else (got,)
    if square:
        a, b = rows[0], total - rows[0]
        dims = [(total, chunk), (2, a, chunk), (a, chunk), (2, b, chunk), (b, chunk)]
        out_specs = [once(*d) for d in dims]
        out_shape = [jax.ShapeDtypeStruct(d, BF16) for d in dims]
    else:
        out_specs = whole
        out_shape = jax.ShapeDtypeStruct((n, total, chunk), BF16)
    return pl.pallas_call(
        functools.partial(wide_body, parts=len(lefts), group=n // steps, with_got=bool(extra), square=square),
        grid_spec=pltpu.PrefetchScalarGridSpec(
            num_scalar_prefetch=1,
            grid=(steps,),
            in_specs=[pl.BlockSpec((tokens, v.shape[1] // steps), lambda i, sel: (0, turn(i, sel))) for v in lefts]
            + [pl.BlockSpec((tokens, chunk), lambda i, sel: (0, sel[0])) for _ in rights]
            + [whole] * len(extra),
            out_specs=out_specs,
        ),
        out_shape=out_shape,
        compiler_params=pltpu.CompilerParams(vmem_limit_bytes=VMEM_LIMIT),
        cost_estimate=cost(micros),
        name=name,
    )(sel, *lefts, *rights, *extra)


def ring(value, steps):
    n = lax.axis_size("seq")
    return lax.ppermute(value, "seq", [(i, (i + steps) % n) for i in range(n)])


def along(value, steps):
    n = lax.axis_size("seq")
    return lax.ppermute(value, "seq", [(i, i + steps) for i in range(n) if 0 <= i + steps < n])


def mirror(value):
    n = lax.axis_size("seq")
    return lax.ppermute(value, "seq", [(i, n - 1 - i) for i in range(n)])


def flip_dp(value, bit):
    n = lax.axis_size("dp")
    return lax.ppermute(value, "dp", [(i, i ^ bit) for i in range(n)])


def other_core(value):
    return flip_dp(value, 1)


def after(value, *done):
    return lax.optimization_barrier((value, done))[0]


def add_low(*values):
    total = values[0].astype(F32)
    for v in values[1:]:
        total = total + v.astype(F32)
    return low(total)


def scatter_seq(value):
    return lax.psum_scatter(value, "seq", scatter_dimension=0, tiled=True)[0]


def flip_seq(value, bit):
    n = lax.axis_size("seq")
    return lax.ppermute(value, "seq", [(i, i ^ bit) for i in range(n)])


def direct_sum(pieces):
    return add_low(pieces[0], *[flip_seq(v, k) for k, v in enumerate(pieces) if k])


def first_hop(pieces):
    own, to_x, keep_x, to_y, keep_y = pieces
    from_x, from_y = flip_seq(to_x, 1), flip_seq(to_y, 2)
    split = keep_x.shape[0]
    return (
        add_low(keep_x, from_x[1]), add_low(keep_y, from_y[1]),
        own[:split], own[split:], from_x[0], from_y[0],
    )


def second_hop(held):
    to_y, to_x, own_a, own_b, from_x, from_y = held
    return jnp.concatenate(
        [add_low(own_a, from_x, flip_seq(to_y, 2)), add_low(own_b, from_y, flip_seq(to_x, 1))], 0
    )


def offloaded_sum_z(value):
    n = lax.axis_size("dp")
    return lax.psum(value, "dp", axis_index_groups=[list(range(c, n, 2)) for c in range(2)])


def sum_z(value, first=2, last=None):
    bit = first
    while bit < (last or lax.axis_size("dp")):
        value = add_low(value, flip_dp(value, bit))
        bit *= 2
    return value


def both_cores(value):
    other = other_core(value)
    first = lax.axis_index("dp") % 2 == 0
    return jnp.where(first, value, other).astype(F32), jnp.where(first, other, value).astype(F32)


def on_device(
    tokens, cotangent, lengths, norm_one, w_query, w_key, w_value, w_gatez, w_conv_in, w_step, conv_weight,
    conv_bias, step_bias, decay_log, skip_gain, gated_gain, w_attn_out, w_mix_out, norm_two, w_gate, w_up, w_down,
):
    seqs, span, width = tokens.shape
    half = span // 2
    taps, conv_width = conv_weight.shape
    count = lax.axis_size("seq")
    place = lax.axis_index("seq").astype(jnp.int32)
    core = (lax.axis_index("dp") % 2).astype(jnp.int32)
    first = place * span
    mirrored = (count - 1 - place) * span + half
    inverse = 1.0 / ROPE_BASE ** (jnp.arange(0, HEAD, 2).astype(F32) / HEAD)

    def tables(positions):
        angles = positions.astype(F32)[:, None] * inverse[None, :]
        return jnp.cos(angles), jnp.sin(angles)

    cosine, sine = tables(first + jnp.arange(span))
    cos_row = jnp.concatenate([cosine] * 4, 1)
    sin_row = jnp.concatenate([-sine, sine] * 2, 1)
    cos_back, sin_back = tables(jnp.concatenate([first + jnp.arange(half), mirrored + jnp.arange(half)]))
    rate = -jnp.exp(decay_log)
    pad = (0, 128 - SSM_HEADS)
    rate_row = jnp.pad(rate, pad)[None]
    step_row = jnp.pad(step_bias, pad)[None]
    w_step_wide = jnp.pad(w_step, ((0, 0), pad))
    skip_row = jnp.repeat(skip_gain, SSM_HEAD)[None]
    ones = (np.arange(WIDE)[None, :] // SSM_HEAD == np.arange(128)[:, None]).astype(np.float32)
    expand = jnp.asarray(np.concatenate([ones, ones], 0), BF16)
    pos = first[None]
    rows = min(256, half)
    blocks = jnp.concatenate([base + jnp.arange(0, half, rows, dtype=jnp.int32) for base in (first, mirrored)])
    sources = lax.rem(place - jnp.arange(count, dtype=jnp.int32) + count, count)
    here = place[None]

    halo = along(tokens[:, span - 16 :], 1)
    hidden, q, kv = enter(after(tokens, halo), norm_one[None], w_query, w_key, w_value, cos_row, sin_row)
    kvs = [kv] + [ring(kv, r) for r in range(1, count)]
    q_other = mirror(q[:, half:])
    z, conv, pre, x, bk, cq, dt, sg, cum, cumt, state = mixer(
        pos, lengths, hidden, halo, norm_one[None], w_gatez, w_conv_in, w_step_wide, conv_weight, conv_bias[None],
        step_row, rate_row * LOG2E, expand,
    )
    states = lax.all_gather(state, "seq")
    o_near, o_far, lse = attend(blocks, lengths, sources, after(q, state), q_other, kvs)
    o_back = mirror(o_far)
    mixed, mix_low, held = scan_forward(
        here, after(x, o_near), bk, cq, dt, cum, cumt, skip_row, z, gated_gain[None], expand, states
    )
    (
        output, hidden_two, act, grad_ffn, grad_gate, grad_up, grad_mid, grad_branch, do_near, do_far, grad_mixed,
        grad_z, attn, g_norm_two, g_gated, adjoint,
    ) = middle(
        pos, lengths, o_near, o_back, mix_low, tokens, cotangent, mixed, z, cq, cum, w_attn_out, w_mix_out, w_gate,
        w_up, w_down, norm_two[None], gated_gain[None], expand,
    )
    adjoints = [along(adjoint, -r) for r in range(1, count)]
    do_other = mirror(do_far)

    def flat(v):
        return v.reshape(seqs * span, v.shape[2])

    mine = jnp.stack([core, place])
    yours = jnp.stack([1 - core, place])
    hid = flat(hidden)
    ffn = (flat(hidden_two), (flat(grad_gate), flat(grad_up)), 512, count)
    outs = ((flat(act), flat(attn), flat(mix_low)), (flat(grad_ffn), flat(grad_branch), flat(grad_branch)), count)

    square = "hops" if count == 4 else ""
    sent_out = wide_grad(yours, *outs, name="grad_outs")
    got_out = other_core(sent_out)
    sent_ffn = tall_grad(after(yours, sent_out), *ffn, name="grad_ffn_in")
    got_ffn = other_core(sent_ffn)
    part_out = wide_grad(after(mine, sent_ffn), *outs, got_out, square, name="grad_outs")
    part_ffn = tall_grad(after(mine, part_out), *ffn, got_ffn, name="grad_ffn_in")
    ffn_sum = scatter_seq(part_ffn)
    grad_conv, tail, head, g_conv_small, g_skip, g_small = scan_backward(
        after(x, part_ffn), bk, cq, dt, sg, cum, cumt, grad_mixed, mixed, held, pre, conv, skip_row, rate_row,
        conv_weight, expand, adjoints,
    )
    out_held = first_hop(part_out) if square else scatter_seq(part_out)
    head = after(head, out_held)
    returned = along(low(head), -1).astype(F32)[:, : taps - 1]
    g_conv_weight = g_conv_small[:taps]
    for ahead in range(1, taps):
        tap = taps - 1 - ahead
        fill = jnp.pad(returned[:, :ahead], ((0, 0), (8 - ahead, 0), (0, 0)))
        tail = tail + conv_weight[tap] * fill
        g_conv_weight = g_conv_weight.at[tap].add(jnp.sum(fill * conv[:, span - 8 :].astype(F32), (0, 1)))
    grad_conv = lax.dynamic_update_slice(grad_conv, low(tail), (0, span - 8, 0))
    inside = (hid, (flat(grad_z), flat(grad_conv)), 256, count)
    sent_in = tall_grad(yours, *inside, name="grad_mixer_in")
    got_in = other_core(sent_in)
    gh = leave_mixer(after(grad_z, sent_in), grad_conv, w_gatez, w_conv_in, w_step_wide)
    out_sum = second_hop(out_held) if square else out_held
    part_in = tall_grad(
        after(mine, gh, out_sum, ffn_sum), *inside, got_in, "direct" if square else "", name="grad_mixer_in"
    )
    ffn_sum, out_sum = offloaded_sum_z((ffn_sum, out_sum))

    def back(group, order):
        near, far, parts = attend_backward(
            group, blocks, lengths, sources, after(q, *order), q_other, do_near, do_other, o_near, o_far, lse,
            cos_back.T, sin_back.T, kvs,
        )
        return near, mirror(far), [parts[0]] + [ring(parts[r], -r) for r in range(1, count)]

    dq_near, dq_far, pieces = back(0, (part_in[0],))
    in_sum = direct_sum(part_in) if square else scatter_seq(part_in)
    results = back(1, (dq_near, in_sum))
    in_sum = sum_z(in_sum, 2, 4)
    grad_tokens, g_norm_one, grad_q, grad_kv = leave(
        tokens, grad_mid, after(gh, in_sum, ffn_sum), norm_one[None], w_query, w_key, w_value, cos_row, sin_row,
        (dq_near, results[0]), (dq_far, results[1]), pieces + results[2],
    )
    in_sum = sum_z(in_sum, 4)
    heads = (hid, (flat(grad_q), flat(grad_kv)), 128, count)
    sent_qkv = tall_grad(yours, *heads, name="grad_qkv")
    part_qkv = tall_grad(mine, *heads, other_core(sent_qkv), square, name="grad_qkv")
    qkv_sum = sum_z(second_hop(first_hop(part_qkv)) if square else scatter_seq(part_qkv))

    def spread(value, chunk_rows, chunks):
        return [
            [v[(a * chunk_rows) : (b * chunk_rows)].reshape(b - a, chunk_rows, -1) for a, b in chunks]
            for v in both_cores(value)
        ]

    def columns(pair):
        return jnp.concatenate([v[i] for v in pair for i in range(v.shape[0])], 1)

    block = width // count
    s_gate, s_up = [columns(p) for p in zip(*spread(ffn_sum, block, ((0, 2), (2, 4))))]
    z_steps, c_steps = WIDE // 512, (conv_width + 256) // 512
    s_gatez, s_conv = [columns(p) for p in zip(*spread(in_sum, block, ((0, z_steps), (z_steps, z_steps + c_steps))))]
    s_query, s_kv = [columns(p) for p in zip(*spread(qkv_sum, block, ((0, 2), (2, 3))))]
    out_all = jnp.concatenate(both_cores(out_sum), 1)
    a, b = w_down.shape[0] // count, w_attn_out.shape[0] // count
    s_down, s_attn_out, s_mix_out = out_all[:a], out_all[a : a + b], out_all[a + b :]

    small = [
        g_norm_one[0], g_norm_two[0], g_gated[0], g_conv_weight.reshape(-1), g_conv_small[taps], g_skip[0],
        g_small[0], g_small[1],
    ]
    sizes = [v.shape[0] for v in small]
    total = jnp.concatenate(small)
    bit = 1
    while bit < lax.axis_size("dp"):
        total = total + flip_dp(total, bit)
        bit *= 2
    bit = 1
    while bit < count:
        total = total + lax.ppermute(total, "seq", [(i, i ^ bit) for i in range(count)])
        bit *= 2
    starts = np.cumsum([0] + sizes)
    small = [total[a:b] for a, b in zip(starts[:-1], starts[1:])]

    def own(v):
        n = v.shape[0] // count
        return lax.dynamic_slice(v, (place * n,), (n,))

    s_norm_one, s_norm_two, s_gated = [own(v) for v in small[:3]]
    s_skip = jnp.sum(small[5].reshape(SSM_HEADS, SSM_HEAD), 1)
    return (
        output,
        grad_tokens,
        s_norm_one,
        s_query,
        s_kv[:, :128],
        s_kv[:, 128:],
        s_gatez,
        s_conv[:, :conv_width],
        s_conv[:, conv_width : conv_width + SSM_HEADS],
        small[3].reshape(taps, -1),
        small[4],
        small[7][:SSM_HEADS],
        small[6][:SSM_HEADS],
        s_skip,
        s_gated,
        s_attn_out,
        s_mix_out,
        s_norm_two,
        s_gate,
        s_up,
        s_down,
    )


def solution(mesh):
    copied = (P(),) * 19
    return jax.shard_map(
        on_device,
        mesh=mesh,
        in_specs=(P("dp", "seq", None), P("dp", "seq", None), P("dp")) + copied,
        out_specs=(
            P("dp", "seq", None), P("dp", "seq", None), P("seq"),
            P("seq", None), P("seq", None), P("seq", None), P("seq", None), P("seq", None), P("seq", None),
            P(), P(), P(), P(), P(),
            P("seq"), P("seq", None), P("seq", None), P("seq"), P("seq", None), P("seq", None), P("seq", None),
        ),
        check_vma=False,
    )
```

```python
import functools

import jax
import jax.numpy as jnp
import numpy as np
from jax import lax
from jax.experimental import pallas as pl
from jax.experimental.pallas import tpu as pltpu
from jax.sharding import PartitionSpec as P

HEADS = 8
KV_HEADS = 2
HEAD = 64
SSM_HEADS = 24
SSM_HEAD = 64
STATE = 128
WIDE = SSM_HEADS * SSM_HEAD
CHUNK = 128
EPS = 1e-05
ROPE_BASE = 100000000000.0
LOG2E = 1.4426950408889634
SCORE2 = 0.125 * LOG2E
LOWEST = -1e30
F32 = jnp.float32
BF16 = jnp.bfloat16
NN = (((1,), (0,)), ((), ()))
NT = (((1,), (1,)), ((), ()))
TN = (((0,), (0,)), ((), ()))
VMEM_LIMIT = 127 << 19


def dot(a, b, dims=NN):
    return lax.dot_general(a, b, dims, preferred_element_type=F32)


def dot_exact(a, b, dims=NN):
    return lax.dot_general(a, b, dims, precision=lax.Precision.HIGHEST, preferred_element_type=F32)


def low(v):
    return v.astype(BF16)


def sigmoid(v):
    return 1.0 / (1.0 + jnp.exp(-v))


def softplus(v):
    e = jnp.exp(-jnp.abs(v))
    tail = jnp.where(e < 1e-2, e * (1.0 - e * (0.5 - e * (1.0 / 3.0))), jnp.log(1.0 + e))
    return jnp.maximum(v, 0.0) + tail


def split_low(v):
    high = low(v)
    return high, low(v - high.astype(F32))


def widen(v, expand):
    return dot(jnp.concatenate(split_low(v), 1), expand)


def head_sums(v, expand):
    high, rest = split_low(v)
    ones = expand[:128]
    return dot(high, ones, NT) + dot(rest, ones, NT)


def cost(micros):
    return pl.CostEstimate(flops=int(micros * 3e9), bytes_accessed=int(micros * 1e5), transcendentals=0)


def full_spec(shape):
    return pl.BlockSpec(shape, lambda *_: (0,) * len(shape), pipeline_mode=pl.Buffered(1))


def params(limit=VMEM_LIMIT):
    return pltpu.CompilerParams(
        vmem_limit_bytes=limit, dimension_semantics=("arbitrary", "arbitrary")
    )


SCALARS = pl.BlockSpec(memory_space=pltpu.SMEM)


def halves_out(core, values, mine_ref, yours_ref):
    first = core == 0
    start = 0
    for value in values:
        size = value.shape[1] // 2
        lower, upper = value[:, :size], value[:, size:]
        mine_ref[0, :, start : start + size] = jnp.where(first, lower, upper)
        yours_ref[0, :, start : start + size] = jnp.where(first, upper, lower)
        start += size


def halves_in(core, mine, yours):
    first = core == 0
    return jnp.concatenate([jnp.where(first, mine, yours), jnp.where(first, yours, mine)], 1)


def low_rows(rows):
    t = lax.broadcasted_iota(jnp.int32, (rows, rows), 0)
    u = lax.broadcasted_iota(jnp.int32, (rows, rows), 1)
    return t >= u


def swap_halves(v):
    lane = lax.broadcasted_iota(jnp.int32, v.shape, 1)
    return jnp.where((lane & 63) < 32, pltpu.roll(v, 96, 1), pltpu.roll(v, 32, 1))


def pair_rows(v):
    lane = lax.broadcasted_iota(jnp.int32, v.shape, 1)
    none = jnp.zeros_like(v)
    return jnp.concatenate([jnp.where(lane < 64, v, none), jnp.where(lane >= 64, v, none)], 0)


def first_norm(v, gain):
    v = v.astype(F32)
    return low(v * lax.rsqrt(jnp.mean(v * v, -1, keepdims=True) + EPS) * gain)


def enter_body(tok_ref, gain_ref, wq_ref, wk_ref, wv_ref, cos_ref, sin_ref, hid_ref, q_ref, kv_ref):
    hid = first_norm(tok_ref[0], gain_ref[...])
    hid_ref[0] = hid
    cosine, sine = cos_ref[...], sin_ref[...]
    t = dot(hid, wk_ref[...])
    kv_ref[0, :, :128] = low(t * cosine + swap_halves(t) * sine)
    kv_ref[0, :, 128:] = low(dot(hid, wv_ref[...]))
    q = dot(hid, wq_ref[...])
    for g in range(4):
        t = q[:, g * 128 : g * 128 + 128]
        q_ref[0, :, g * 128 : g * 128 + 128] = low(t * cosine + swap_halves(t) * sine)


def enter(tokens, gain, wq, wk, wv, cosine, sine):
    seqs, span, width = tokens.shape
    rows = min(256, span)

    def row(n):
        return pl.BlockSpec((1, rows, n), lambda s, b: (s, b, 0))

    table = pl.BlockSpec((rows, 128), lambda s, b: (b, 0))
    return pl.pallas_call(
        enter_body,
        grid=(seqs, span // rows),
        in_specs=[row(width)] + [full_spec(v.shape) for v in (gain, wq, wk, wv)] + [table, table],
        out_specs=[row(width), row(512), row(256)],
        out_shape=[jax.ShapeDtypeStruct((seqs, span, n), BF16) for n in (width, 512, 256)],
        compiler_params=params(),
        cost_estimate=cost(8),
        name="enter",
    )(tokens, gain, wq, wk, wv, cosine, sine)


def mixer_body(
    pos_ref, len_ref, hid_ref, halo_ref, gain_ref, wz_ref, wc_ref, ws_ref, cw_ref, cb_ref, sb_ref, a_ref, exp_ref,
    z_ref, cl_ref, pre_ref, x_ref, bk_ref, cq_ref, dt_ref, sg_ref, cum_ref, cumt_ref, st_ref,
    prev, state, total, *, rows, blocks,
):
    s = pl.program_id(0)
    b = pl.program_id(1)

    @pl.when(b == 0)
    def _():
        prev[...] = dot(first_norm(halo_ref[0], gain_ref[...]), wc_ref[...])[8:]
        state[...] = jnp.zeros_like(state)
        total[...] = jnp.zeros_like(total)

    hid = hid_ref[0]
    conv = dot(hid, wc_ref[...])
    raw = dot(hid, ws_ref[...]) + sb_ref[...]
    z_ref[0] = low(dot(hid, wz_ref[...]))
    cl_ref[0] = low(conv)
    ext = jnp.concatenate([prev[...], conv], 0)
    prev[...] = conv[rows - 8 :]
    pre = cb_ref[...] + cw_ref[3:4] * conv
    for back in range(1, 4):
        pre = pre + cw_ref[3 - back : 4 - back] * pltpu.roll(ext, back, 0)[8:]
    pre_ref[0] = low(pre)
    act = low(pre * sigmoid(pre))
    x = act[:, :WIDE]
    bk = act[:, WIDE : WIDE + STATE]
    x_ref[0] = x
    bk_ref[0] = bk
    cq_ref[0] = act[:, WIDE + STATE :]
    at = pos_ref[0] + b * rows + lax.broadcasted_iota(jnp.int32, raw.shape, 0)
    live = jnp.where(at < len_ref[s], 1.0, 0.0)
    dt = softplus(raw) * live
    dt_ref[0] = dt
    sg_ref[0] = sigmoid(raw) * live
    log_decay = dt * a_ref[...]
    tri = jnp.where(low_rows(CHUNK), 1.0, 0.0)
    for c in range(rows // CHUNK):
        here = slice(c * CHUNK, (c + 1) * CHUNK)
        cum = dot_exact(tri, log_decay[here])
        cum_ref[0, here] = cum
        cumt_ref[0, :, here] = cum.T[:32]
        last = cum[CHUNK - 1 :]
        weight = dt[here] * jnp.exp2(last - cum)
        wide = widen(
            jnp.concatenate([weight, jnp.broadcast_to(jnp.exp2(last), (16, 128))], 0), exp_ref[...]
        )
        xw = low(x[here].astype(F32) * wide[:CHUNK])
        state[...] = state[...] * wide[CHUNK : CHUNK + 1] + dot(bk[here], xw, TN)
        total[...] = total[...] + last

    @pl.when(b == blocks - 1)
    def _():
        st_ref[0, :STATE] = low(state[...])
        st_ref[0, STATE:] = total_rows(total[...], exp_ref[...])


def total_rows(total, expand):
    wide = widen(jnp.broadcast_to(total, (8, 128)), expand)
    high = wide.astype(BF16).astype(F32)
    return low(jnp.concatenate([high, wide - high], 0))


def mixer(pos, lens, hid, halo, gain, wz, wc, ws, cw, cb, sb, a, expand):
    seqs, span, width = hid.shape
    rows = min(256, span)
    blocks = span // rows
    conv_width = wc.shape[1]

    def row(n):
        return pl.BlockSpec((1, rows, n), lambda s, b, *_: (s, b, 0))

    def shape(n, kind):
        return jax.ShapeDtypeStruct((seqs, span, n), kind)

    return pl.pallas_call(
        functools.partial(mixer_body, rows=rows, blocks=blocks),
        grid_spec=pltpu.PrefetchScalarGridSpec(
            num_scalar_prefetch=2,
            grid=(seqs, blocks),
            in_specs=[row(width), pl.BlockSpec((1, 16, width), lambda s, b, *_: (s, 0, 0))]
            + [full_spec(v.shape) for v in (gain, wz, wc, ws, cw, cb, sb, a, expand)],
            out_specs=[
                row(WIDE), row(conv_width), row(conv_width), row(WIDE), row(STATE), row(STATE),
                row(128), row(128), row(128),
                pl.BlockSpec((1, 32, rows), lambda s, b, *_: (s, 0, b)),
                pl.BlockSpec((1, STATE + 16, WIDE), lambda s, b, *_: (s, 0, 0)),
            ],
            scratch_shapes=[
                pltpu.VMEM((8, conv_width), F32), pltpu.VMEM((STATE, WIDE), F32), pltpu.VMEM((1, 128), F32),
            ],
        ),
        out_shape=[
            shape(WIDE, BF16), shape(conv_width, BF16), shape(conv_width, BF16), shape(WIDE, BF16),
            shape(STATE, BF16), shape(STATE, BF16), shape(128, F32), shape(128, F32), shape(128, F32),
            jax.ShapeDtypeStruct((seqs, 32, span), F32),
            jax.ShapeDtypeStruct((seqs, STATE + 16, WIDE), BF16),
        ],
        compiler_params=params(),
        cost_estimate=cost(20),
        name="mixer",
    )(pos, lens, hid, halo, gain, wz, wc, ws, cw, cb, sb, a, expand)


def joined(place, ref):
    state = jnp.zeros((STATE, WIDE), F32)
    for i in range(ref.shape[0]):
        logs = ref[i, 0, STATE : STATE + 1].astype(F32) + ref[i, 0, STATE + 8 : STATE + 9].astype(F32)
        state = jnp.where(i < place, state * jnp.exp2(logs) + ref[i, 0, :STATE].astype(F32), state)
    return state


def joined_later(refs):
    state = jnp.zeros((STATE, WIDE), F32)
    for ref in reversed(refs):
        logs = ref[0, STATE : STATE + 1].astype(F32) + ref[0, STATE + 8 : STATE + 9].astype(F32)
        state = state * jnp.exp2(logs) + ref[0, :STATE].astype(F32)
    return state


def gathered_spec(states):
    return pl.BlockSpec((states.shape[0], 1) + states.shape[2:], lambda s, c: (0, s, 0, 0), pipeline_mode=pl.Buffered(1))


def scan_body(
    place_ref, x_ref, bk_ref, cq_ref, dt_ref, cum_ref, cumt_ref, skip_ref, z_ref, gain_ref, exp_ref, all_ref,
    mix_ref, low_ref, st_ref, state, y,
):
    c = pl.program_id(1)

    @pl.when(c == 0)
    def _():
        state[...] = joined(place_ref[0], all_ref)

    x = x_ref[0].astype(F32)
    bk, cq = bk_ref[0], cq_ref[0]
    cum = cum_ref[0]
    last = cum[CHUNK - 1 :]
    expand = exp_ref[...]
    xdt = x * widen(dt_ref[0], expand)
    ends = widen(
        jnp.concatenate([jnp.exp2(cum), jnp.exp2(last - cum), jnp.broadcast_to(jnp.exp2(last), (16, 128))], 0),
        expand,
    )
    inter = jnp.where(low_rows(CHUNK), dot(cq, bk, NT), 0.0)
    held = low(state[...])
    st_ref[0, 0] = held
    y[...] = dot(cq, held) * ends[:CHUNK] + skip_ref[...] * x
    state[...] = state[...] * ends[2 * CHUNK : 2 * CHUNK + 1] + dot(bk, low(xdt * ends[CHUNK : 2 * CHUNK]), TN)
    xdt = low(xdt)
    for p in range(SSM_HEADS // 2):
        parts = []
        for h in (2 * p, 2 * p + 1):
            differ = jnp.minimum(cum[:, h : h + 1] - cumt_ref[0, h : h + 1, :], 0.0)
            parts.append(low(inter * jnp.exp2(differ)))
        cols = slice(p * 128, p * 128 + 128)
        y[:, cols] += dot(jnp.concatenate(parts, 1), pair_rows(xdt[:, cols]))
    mixed = y[...]
    mix_ref[0] = mixed
    z = z_ref[0].astype(F32)
    v = mixed * (z * sigmoid(z))
    low_ref[0] = low(v * lax.rsqrt(jnp.mean(v * v, -1, keepdims=True) + EPS) * gain_ref[...])


def scan_forward(place, x, bk, cq, dt, cum, cumt, skip, z, gain, expand, states):
    seqs, span, _ = x.shape
    chunks = span // CHUNK

    def row(n):
        return pl.BlockSpec((1, CHUNK, n), lambda s, c: (s, c, 0))

    return pl.pallas_call(
        scan_body,
        grid=(seqs, chunks),
        in_specs=[
            SCALARS, row(WIDE), row(STATE), row(STATE), row(128), row(128),
            pl.BlockSpec((1, 32, CHUNK), lambda s, c: (s, 0, c)),
            full_spec(skip.shape), row(WIDE), full_spec(gain.shape), full_spec(expand.shape), gathered_spec(states),
        ],
        out_specs=[row(WIDE), row(WIDE), pl.BlockSpec((1, 1, STATE, WIDE), lambda s, c: (s, c, 0, 0))],
        out_shape=[
            jax.ShapeDtypeStruct((seqs, span, WIDE), F32),
            jax.ShapeDtypeStruct((seqs, span, WIDE), BF16),
            jax.ShapeDtypeStruct((seqs, chunks, STATE, WIDE), BF16),
        ],
        scratch_shapes=[pltpu.VMEM((STATE, WIDE), F32), pltpu.VMEM((CHUNK, WIDE), F32)],
        compiler_params=params(),
        cost_estimate=cost(16),
        name="scan_forward",
    )(place, x, bk, cq, dt, cum, cumt, skip, z, gain, expand, states)


def middle_body(
    pos_ref, len_ref, near_ref, far_ref, mix_ref, tok_ref, cot_ref,
    wao_ref, wmo_ref, wg_ref, wu_ref, wd_ref, gain2_ref,
    out_ref, left_ref, mine_ref, yours_ref, gmid_ref, gn2_ref, *, rows, blocks,
):
    s = pl.program_id(0)
    b = pl.program_id(1)

    @pl.when((s == 0) & (b == 0))
    def _():
        gn2_ref[...] = jnp.zeros_like(gn2_ref)

    at = pos_ref[0] + b * rows + lax.broadcasted_iota(jnp.int32, (rows, 1), 0)
    live = jnp.where(at < len_ref[s], 1.0, 0.0)
    attn = jnp.where(b < blocks // 2, near_ref[0], far_ref[0])
    width, ff = wd_ref.shape[1], wd_ref.shape[0]
    left_ref[0, :, width + ff :] = attn
    branch = dot(attn, wao_ref[...]) + dot(mix_ref[0], wmo_ref[...])
    after = tok_ref[0].astype(F32) + live * branch
    scale = lax.rsqrt(jnp.mean(after * after, -1, keepdims=True) + EPS)
    unit = after * scale
    gain = gain2_ref[...]
    h2 = low(unit * gain)
    left_ref[0, :, :width] = h2
    gate = dot(h2, wg_ref[...])
    up = dot(h2, wu_ref[...])
    sg = sigmoid(gate)
    silu = gate * sg
    act = low(silu * up)
    left_ref[0, :, width : width + ff] = act
    out_ref[0] = low(after + live * dot(act, wd_ref[...]))
    cot = cot_ref[0].astype(F32)
    gffn = low(live * cot)
    gact = dot(gffn, wd_ref[...], NT)
    gg = low(gact * up * (sg * (1.0 + gate * (1.0 - sg))))
    gu = low(gact * silu)
    gh2 = dot(gg, wg_ref[...], NT) + dot(gu, wu_ref[...], NT)
    gn2_ref[...] += jnp.sum(gh2 * unit, 0, keepdims=True)
    g = gh2 * gain
    gmid = cot + scale * (g - unit * jnp.mean(g * unit, -1, keepdims=True))
    gmid_ref[0] = gmid
    halves_out(pos_ref[1], (gg, gu, gffn, low(live * gmid)), mine_ref, yours_ref)


def middle(pos, lens, near, far, mix, tokens, cot, wao, wmo, wg, wu, wd, gain2):
    seqs, span, width = tokens.shape
    rows = min(256, span // 2)
    blocks = span // rows
    ff = wg.shape[1]
    lower = pl.BlockSpec((1, rows, 512), lambda s, b, *_: (s, jnp.minimum(b, blocks // 2 - 1), 0))
    upper = pl.BlockSpec((1, rows, 512), lambda s, b, *_: (s, jnp.maximum(b - blocks // 2, 0), 0))

    def row(n):
        return pl.BlockSpec((1, rows, n), lambda s, b, *_: (s, b, 0))

    def shape(n, kind):
        return jax.ShapeDtypeStruct((seqs, span, n), kind)

    return pl.pallas_call(
        functools.partial(middle_body, rows=rows, blocks=blocks),
        grid_spec=pltpu.PrefetchScalarGridSpec(
            num_scalar_prefetch=2,
            grid=(seqs, blocks),
            in_specs=[lower, upper, row(WIDE), row(width), row(width)]
            + [full_spec(v.shape) for v in (wao, wmo, wg, wu, wd, gain2)],
            out_specs=[
                row(width), row(width + ff + 512), row(width + ff), row(width + ff), row(width),
                pl.BlockSpec((1, width), lambda s, b, *_: (0, 0)),
            ],
        ),
        out_shape=[
            shape(width, BF16), shape(width + ff + 512, BF16), shape(width + ff, BF16), shape(width + ff, BF16),
            shape(width, F32),
            jax.ShapeDtypeStruct((1, width), F32),
        ],
        compiler_params=params(),
        cost_estimate=cost(45),
        name="middle",
    )(pos, lens, near, far, mix, tokens, cot, wao, wmo, wg, wu, wd, gain2)


def branch_body(
    core_ref, gb_m, gb_y, mixed_ref, z_ref, cq_ref, cum_ref, wao_ref, wmo_ref, gated_ref, exp_ref,
    gnear_ref, gfar_ref, gmixed_ref, gz_m, gz_y, ggain_ref, adj_ref, adj, offset, *, rows, blocks,
):
    s = pl.program_id(0)
    b = pl.program_id(1)

    @pl.when((s == 0) & (b == 0))
    def _():
        ggain_ref[...] = jnp.zeros_like(ggain_ref)

    @pl.when(b == 0)
    def _():
        adj[...] = jnp.zeros_like(adj)
        offset[...] = jnp.zeros_like(offset)

    core = core_ref[0]
    gb = halves_in(core, gb_m[0], gb_y[0])
    gattn = low(dot(gb, wao_ref[...], NT))

    @pl.when(b < blocks // 2)
    def _():
        gnear_ref[0] = gattn

    @pl.when(b >= blocks // 2)
    def _():
        gfar_ref[0] = gattn

    gn = low(dot(gb, wmo_ref[...], NT)).astype(F32)
    mixed = mixed_ref[0]
    z = z_ref[0].astype(F32)
    sg = sigmoid(z)
    silu = z * sg
    v = mixed * silu
    scale = lax.rsqrt(jnp.mean(v * v, -1, keepdims=True) + EPS)
    unit = v * scale
    ggain_ref[...] += jnp.sum(gn * unit, 0, keepdims=True)
    g = gn * gated_ref[...]
    g = scale * (g - unit * jnp.mean(g * unit, -1, keepdims=True))
    gmixed = g * silu
    gmixed_ref[0] = low(gmixed)
    halves_out(core, (low(g * mixed * (sg * (1.0 + z * (1.0 - sg)))),), gz_m, gz_y)
    cum = cum_ref[0]
    logs = []
    for c in range(rows // CHUNK):
        here = cum[c * CHUNK : (c + 1) * CHUNK]
        logs.append(here + offset[...])
        offset[...] += here[CHUNK - 1 :]
    wide = widen(jnp.exp2(jnp.concatenate(logs, 0)), exp_ref[...])
    adj[...] += dot(cq_ref[0], low(gmixed * wide), TN)

    @pl.when(b == blocks - 1)
    def _():
        adj_ref[0, :STATE] = low(adj[...])
        adj_ref[0, STATE:] = total_rows(offset[...], exp_ref[...])


def branch_back(core, mine, yours, mixed, z, cq, cum, wao, wmo, gated, expand):
    seqs, span, packed = mine.shape
    half_width = wao.shape[1] // 2
    gb = pl.BlockSpec((1, min(256, span // 2), half_width), lambda s, b: (s, b, packed // half_width - 1))
    rows = min(256, span // 2)
    blocks = span // rows
    lower = pl.BlockSpec((1, rows, 512), lambda s, b: (s, jnp.minimum(b, blocks // 2 - 1), 0))
    upper = pl.BlockSpec((1, rows, 512), lambda s, b: (s, jnp.maximum(b - blocks // 2, 0), 0))

    def row(n):
        return pl.BlockSpec((1, rows, n), lambda s, b: (s, b, 0))

    def shape(n, kind):
        return jax.ShapeDtypeStruct((seqs, span, n), kind)

    half = jax.ShapeDtypeStruct((seqs, span // 2, 512), BF16)
    return pl.pallas_call(
        functools.partial(branch_body, rows=rows, blocks=blocks),
        grid=(seqs, blocks),
        in_specs=[SCALARS, gb, gb, row(WIDE), row(WIDE), row(STATE), row(128)]
        + [full_spec(v.shape) for v in (wao, wmo, gated, expand)],
        out_specs=[
            lower, upper, row(WIDE), row(WIDE // 2), row(WIDE // 2), pl.BlockSpec((1, WIDE), lambda s, b: (0, 0)),
            pl.BlockSpec((1, STATE + 16, WIDE), lambda s, b: (s, 0, 0)),
        ],
        out_shape=[
            half, half, shape(WIDE, BF16), shape(WIDE // 2, BF16), shape(WIDE // 2, BF16),
            jax.ShapeDtypeStruct((1, WIDE), F32),
            jax.ShapeDtypeStruct((seqs, STATE + 16, WIDE), BF16),
        ],
        scratch_shapes=[pltpu.VMEM((STATE, WIDE), F32), pltpu.VMEM((1, 128), F32)],
        compiler_params=params(),
        cost_estimate=cost(6),
        name="branch_back",
    )(core, mine, yours, mixed, z, cq, cum, wao, wmo, gated, expand)


def scan_back_body(
    x_ref, bk_ref, cq_ref, dt_ref, sg_ref, cum_ref, cumt_ref, dy_ref, mix_ref, st_ref, pre_ref, cl_ref,
    skip_ref, a_ref, cw_ref, exp_ref, core_ref, *rest, chunks, conv_width,
):
    *later, gc_m, gc_y, tail_ref, head_ref, gw_ref, gskip_ref, small_ref, adj, after, gact = rest
    s = pl.program_id(0)
    c = pl.program_id(1)

    @pl.when((s == 0) & (c == 0))
    def _():
        gw_ref[...] = jnp.zeros_like(gw_ref)
        gskip_ref[...] = jnp.zeros_like(gskip_ref)
        small_ref[...] = jnp.zeros_like(small_ref)

    @pl.when(c == 0)
    def _():
        adj[...] = joined_later(later)
        after[...] = jnp.zeros_like(after)

    x = x_ref[0].astype(F32)
    bk, cq = bk_ref[0], cq_ref[0]
    dt = dt_ref[0]
    cum = cum_ref[0]
    last = cum[CHUNK - 1 :]
    expand = exp_ref[...]
    dt_wide = widen(dt, expand)
    ends = widen(
        jnp.concatenate([jnp.exp2(cum), jnp.exp2(last - cum), jnp.broadcast_to(jnp.exp2(last), (16, 128))], 0),
        expand,
    )
    to_end = ends[CHUNK : 2 * CHUNK]
    all_wide = ends[2 * CHUNK : 2 * CHUNK + 1]
    xdt = x * dt_wide
    dy_low = dy_ref[0]
    dy = dy_low.astype(F32)
    dy_in = low(dy * ends[:CHUNK])
    state = st_ref[0, 0]
    gstate = adj[...]
    gstate_low = low(gstate)
    from_end = dot(bk, gstate_low) * to_end
    gb = dot(low(xdt * to_end), gstate_low, NT)
    gc = dot(dy_in, state, NT)
    gfinal = all_wide * jnp.sum(gstate * state.astype(F32), 0, keepdims=True) + jnp.sum(
        xdt * from_end, 0, keepdims=True
    )
    adj[...] = gstate * all_wide + dot(cq, dy_in, TN)
    xdt_low = low(xdt)
    u = lax.broadcasted_iota(jnp.int32, (CHUNK, CHUNK), 0)
    t = lax.broadcasted_iota(jnp.int32, (CHUNK, CHUNK), 1)
    inter = jnp.where(t >= u, dot(bk, cq, NT), 0.0)
    ginter = jnp.zeros((CHUNK, CHUNK), F32)
    for p in range(SSM_HEADS // 2):
        cols = slice(p * 128, p * 128 + 128)
        dy_rows = pair_rows(dy_low[:, cols])
        gmix = dot(xdt_low[:, cols], dy_rows, NT)
        parts = []
        for n, h in enumerate((2 * p, 2 * p + 1)):
            decay = jnp.exp2(jnp.minimum(cumt_ref[0, h : h + 1, :] - cum[:, h : h + 1], 0.0))
            parts.append(low(inter * decay))
            ginter = ginter + gmix[:, n * CHUNK : (n + 1) * CHUNK] * decay
        gact[:, cols] = dot(jnp.concatenate(parts, 1), dy_rows)
    ginter = low(jnp.where(t >= u, ginter, 0.0))
    gact[:, WIDE : WIDE + STATE] = gb + dot(ginter, cq)
    gact[:, WIDE + STATE :] = gc + dot(ginter, bk, TN)
    gxdt = gact[:, :WIDE] + from_end
    skip = skip_ref[...]
    gact[:, :WIDE] = dt_wide * gxdt + skip * dy
    gskip_ref[...] += jnp.sum(dy * x, 0, keepdims=True)
    sums = head_sums(
        jnp.concatenate([x * gxdt, dy * (mix_ref[0] - skip * x), jnp.broadcast_to(gfinal, (16, WIDE))], 0), expand
    )
    direct = sums[:CHUNK]
    gcum = sums[CHUNK : 2 * CHUNK] - dt * direct
    gld = dot_exact(jnp.where(t >= u, 1.0, 0.0), gcum) + sums[2 * CHUNK : 2 * CHUNK + 1]
    a = a_ref[...]
    gstep = (direct + a * gld) * sg_ref[0]
    small_ref[0:1] += jnp.sum(dt * gld, 0, keepdims=True) * a
    small_ref[1:2] += jnp.sum(gstep, 0, keepdims=True)
    pre = pre_ref[0].astype(F32)
    sg = sigmoid(pre)
    gpre = gact[...] * (sg * (1.0 + pre * (1.0 - sg)))
    ext = jnp.concatenate([gpre, after[...]], 0)
    after[...] = gpre[:8]
    conv = cl_ref[0].astype(F32)
    gconv = cw_ref[3:4] * gpre
    gw_ref[3:4] += jnp.sum(conv * gpre, 0, keepdims=True)
    gw_ref[4:5] += jnp.sum(gpre, 0, keepdims=True)
    for ahead in range(1, 4):
        moved = pltpu.roll(ext, CHUNK + 8 - ahead, 0)[:CHUNK]
        gconv = gconv + cw_ref[3 - ahead : 4 - ahead] * moved
        gw_ref[3 - ahead : 4 - ahead] += jnp.sum(conv * moved, 0, keepdims=True)
    everything = jnp.concatenate([low(gconv), low(gstep), jnp.zeros((CHUNK, 128), BF16)], 1)
    halves_out(core_ref[0], (everything,), gc_m, gc_y)

    @pl.when(c == 0)
    def _():
        tail_ref[0, :, :conv_width] = gconv[CHUNK - 8 :]
        tail_ref[0, :, conv_width : conv_width + 128] = gstep[CHUNK - 8 :]
        tail_ref[0, :, conv_width + 128 :] = jnp.zeros((8, 128), F32)

    @pl.when(c == chunks - 1)
    def _():
        head_ref[0] = gpre[:8]


def scan_backward(x, bk, cq, dt, sg, cum, cumt, dy, mixed, states, pre, conv, skip, a, cw, expand, core, adjoints):
    seqs, span, _ = x.shape
    chunks = span // CHUNK
    conv_width = pre.shape[2]

    def row(n):
        return pl.BlockSpec((1, CHUNK, n), lambda s, c: (s, chunks - 1 - c, 0))

    def once(m, n):
        return pl.BlockSpec((m, n), lambda s, c: (0, 0))

    edge = pl.BlockSpec((1, 8, conv_width), lambda s, c: (s, 0, 0))
    return pl.pallas_call(
        functools.partial(scan_back_body, chunks=chunks, conv_width=conv_width),
        grid=(seqs, chunks),
        in_specs=[
            row(WIDE), row(STATE), row(STATE), row(128), row(128), row(128),
            pl.BlockSpec((1, 32, CHUNK), lambda s, c: (s, 0, chunks - 1 - c)),
            row(WIDE), row(WIDE),
            pl.BlockSpec((1, 1, STATE, WIDE), lambda s, c: (s, chunks - 1 - c, 0, 0)),
            row(conv_width), row(conv_width),
            full_spec(skip.shape), full_spec(a.shape), full_spec(cw.shape), full_spec(expand.shape), SCALARS,
        ]
        + [
            pl.BlockSpec((1, STATE + 16, WIDE), lambda s, c: (s, 0, 0), pipeline_mode=pl.Buffered(1))
            for _ in adjoints
        ],
        out_specs=[
            row((conv_width + 256) // 2), row((conv_width + 256) // 2),
            pl.BlockSpec((1, 8, conv_width + 256), lambda s, c: (s, 0, 0)), edge, once(8, conv_width), once(1, WIDE), once(8, 128),
        ],
        out_shape=[
            jax.ShapeDtypeStruct((seqs, span, (conv_width + 256) // 2), BF16),
            jax.ShapeDtypeStruct((seqs, span, (conv_width + 256) // 2), BF16),
            jax.ShapeDtypeStruct((seqs, 8, conv_width + 256), F32),
            jax.ShapeDtypeStruct((seqs, 8, conv_width), F32),
            jax.ShapeDtypeStruct((8, conv_width), F32),
            jax.ShapeDtypeStruct((1, WIDE), F32),
            jax.ShapeDtypeStruct((8, 128), F32),
        ],
        scratch_shapes=[
            pltpu.VMEM((STATE, WIDE), F32), pltpu.VMEM((8, conv_width), F32), pltpu.VMEM((CHUNK, conv_width), F32),
        ],
        compiler_params=params(),
        cost_estimate=cost(4),
        name="scan_backward",
    )(x, bk, cq, dt, sg, cum, cumt, dy, mixed, states, pre, conv, skip, a, cw, expand, core, *adjoints)


def leave_mixer_body(core_ref, gz_m, gz_y, gc_m, gc_y, wz_ref, wc_ref, ws_ref, gh_ref, *, conv_width):
    core = core_ref[0]
    gz = halves_in(core, gz_m[0], gz_y[0])
    gc = halves_in(core, gc_m[0], gc_y[0])
    gh = dot(gz, wz_ref[...], NT) + dot(gc[:, :conv_width], wc_ref[...], NT)
    gh_ref[0] = gh + dot(gc[:, conv_width : conv_width + 128], ws_ref[...], NT)


def leave_mixer(core, gz, gc, wz, wc, ws):
    seqs, span, _ = gz[0].shape
    rows = min(256, span)

    def row(n):
        return pl.BlockSpec((1, rows, n), lambda s, b: (s, b, 0))

    width = wz.shape[0]
    return pl.pallas_call(
        functools.partial(leave_mixer_body, conv_width=wc.shape[1]),
        grid=(seqs, span // rows),
        in_specs=[SCALARS]
        + [row(v.shape[2]) for v in (*gz, *gc)]
        + [full_spec(v.shape) for v in (wz, wc, ws)],
        out_specs=row(width),
        out_shape=jax.ShapeDtypeStruct((seqs, span, width), F32),
        compiler_params=params(),
        cost_estimate=cost(0),
        name="leave_mixer",
    )(core, *gz, *gc, wz, wc, ws)


def heads_body(core_ref, cos_ref, sin_ref, *rest, blocks, count):
    near, far = rest[:2], rest[2:4]
    pieces = rest[4 : 4 + 2 * count]
    gq_m, gq_y, gkv_m, gkv_y = rest[4 + 2 * count :]
    core = core_ref[0]
    b = pl.program_id(1)
    halves_out(core, (jnp.concatenate([jnp.where(b < blocks // 2, near[j][0], far[j][0]) for j in range(2)], 1),), gq_m, gq_y)
    sums = []
    for j in range(2):
        t = pieces[j * count][0].astype(F32)
        for r in range(1, count):
            t = t + pieces[j * count + r][0].astype(F32)
        sums.append(t)
    lane = lax.broadcasted_iota(jnp.int32, sums[0].shape, 1)
    gk = jnp.where(lane < 64, sums[0], pltpu.roll(sums[1], 64, 1))
    gv = low(jnp.where(lane < 64, pltpu.roll(sums[0], 64, 1), sums[1]))
    gk = low(gk * cos_ref[...] - swap_halves(gk) * sin_ref[...])
    halves_out(core, (jnp.concatenate([gk, gv], 1),), gkv_m, gkv_y)


def heads_back(core, cosine, sine, near, far, pieces):
    seqs, half, _ = near[0].shape
    span = 2 * half
    rows = min(256, half)
    blocks = span // rows
    table = pl.BlockSpec((rows, 128), lambda s, b: (b, 0))
    lower = pl.BlockSpec((1, rows, 256), lambda s, b: (s, jnp.minimum(b, blocks // 2 - 1), 0))
    upper = pl.BlockSpec((1, rows, 256), lambda s, b: (s, jnp.maximum(b - blocks // 2, 0), 0))

    def row(n):
        return pl.BlockSpec((1, rows, n), lambda s, b: (s, b, 0))

    return pl.pallas_call(
        functools.partial(heads_body, blocks=blocks, count=len(pieces) // 2),
        grid=(seqs, blocks),
        in_specs=[SCALARS, table, table, lower, lower, upper, upper] + [row(128)] * len(pieces),
        out_specs=[row(256), row(256), row(128), row(128)],
        out_shape=[jax.ShapeDtypeStruct((seqs, span, n), BF16) for n in (256, 256, 128, 128)],
        compiler_params=params(),
        cost_estimate=cost(0),
        name="heads_back",
    )(core, cosine, sine, *near, *far, *pieces)


def leave_body(
    core_ref, tok_ref, gmid_ref, gh_ref, gq_m, gq_y, gkv_m, gkv_y, gain_ref, wq_ref, wk_ref, wv_ref, gt_ref, gn_ref
):
    @pl.when((pl.program_id(0) == 0) & (pl.program_id(1) == 0))
    def _():
        gn_ref[...] = jnp.zeros_like(gn_ref)

    core = core_ref[0]
    gh = gh_ref[0] + dot(halves_in(core, gq_m[0], gq_y[0]), wq_ref[...], NT)
    gkv = halves_in(core, gkv_m[0], gkv_y[0])
    gh = gh + dot(gkv[:, :128], wk_ref[...], NT) + dot(gkv[:, 128:], wv_ref[...], NT)
    v = tok_ref[0].astype(F32)
    scale = lax.rsqrt(jnp.mean(v * v, -1, keepdims=True) + EPS)
    unit = v * scale
    gn_ref[...] += jnp.sum(gh * unit, 0, keepdims=True)
    g = gh * gain_ref[...]
    gt_ref[0] = gmid_ref[0] + scale * (g - unit * jnp.mean(g * unit, -1, keepdims=True))


def leave(core, tokens, gmid, gh, heads, gain, wq, wk, wv):
    seqs, span, width = tokens.shape
    rows = min(256, span)

    def row(n):
        return pl.BlockSpec((1, rows, n), lambda s, b: (s, b, 0))

    return pl.pallas_call(
        leave_body,
        grid=(seqs, span // rows),
        in_specs=[SCALARS] + [row(width)] * 3 + [row(v.shape[2]) for v in heads] + [full_spec(v.shape) for v in (gain, wq, wk, wv)],
        out_specs=[row(width), pl.BlockSpec((1, width), lambda s, b: (0, 0))],
        out_shape=[jax.ShapeDtypeStruct((seqs, span, width), F32), jax.ShapeDtypeStruct((1, width), F32)],
        compiler_params=params(),
        cost_estimate=cost(0),
        name="leave",
    )(core, tokens, gmid, gh, *heads, gain, wq, wk, wv)


def dup_halves(v):
    lane = lax.broadcasted_iota(jnp.int32, v.shape, 1)
    other = pltpu.roll(v, 64, 1)
    return low(jnp.where(lane < 64, v, other)), low(jnp.where(lane < 64, other, v))


def head_rows(v):
    lane = lax.broadcasted_iota(jnp.int32, (v.shape[0], 128), 1)
    heads = []
    for h in range(v.shape[1] // HEAD):
        t = v[:, (h // 2) * 128 : (h // 2) * 128 + 128]
        heads.append(jnp.where((lane < 64) if h % 2 == 0 else (lane >= 64), t, jnp.zeros_like(t)))
    return heads


def key_range(first, length, rows, keys):
    whole = jnp.minimum((first + 1) // keys, length // keys)
    some = jnp.minimum((first + rows + keys - 1) // keys, (length + keys - 1) // keys)
    return whole, some


def seen(i, first, length, rows, keys):
    key_at = i * keys + lax.broadcasted_iota(jnp.int32, (keys, rows), 0)
    query_at = first + lax.broadcasted_iota(jnp.int32, (keys, rows), 1)
    return (key_at <= query_at) & (key_at < length)


def attend_body(
    pos_ref, len_ref, from_ref, q_ref, other_ref, *rest, rows, keys, blocks, count, span,
):
    kv_refs = rest[:count]
    near_ref, far_ref, lse_ref, kd, vt, top, acc, score_a, score_b, top_a, top_b = rest[count:]
    s = pl.program_id(0)
    b = pl.program_id(1)
    prep = min(512, span)

    @pl.when(b == 0)
    def _():
        ones = jnp.ones((16, prep), F32)
        for r, kv_ref in enumerate(kv_refs):
            for i in range(span // prep):
                here = slice(i * prep, (i + 1) * prep)
                at = pl.ds(pl.multiple_of(from_ref[r] * span + i * prep, prep), prep)
                kd[0, at, :], kd[1, at, :] = dup_halves(kv_ref[0, here, :128].astype(F32))
                t = kv_ref[0, here, 128:].astype(F32).T
                vt[0, :, at] = low(jnp.concatenate([t[:64], ones], 0))
                vt[1, :, at] = low(jnp.concatenate([t[64:], ones], 0))

    first = pos_ref[b]
    length = len_ref[s]
    heads = head_rows(jnp.where(b < blocks // 2, q_ref[0], other_ref[0]))
    top[...] = jnp.full_like(top, LOWEST)
    acc[...] = jnp.zeros_like(acc)
    whole, some = key_range(first, length, rows, keys)

    def scores(i, buffer, tops, h, mask=None):
        at = pl.ds(pl.multiple_of(i * keys, keys), keys)
        t = dot(kd[h // 4, at, :], heads[h], NT)
        if mask is not None:
            t = jnp.where(mask, t, LOWEST)
        buffer[h] = t
        tops[h] = jnp.max(t, 0, keepdims=True)

    def add(i, buffer, tops, h):
        at = pl.ds(pl.multiple_of(i * keys, keys), keys)
        before = top[h]
        now = jnp.maximum(before, tops[h])
        p = low(jnp.exp2((buffer[h] - now) * SCORE2))
        acc[h] = acc[h] * jnp.exp2((before - now) * SCORE2) + dot(vt[h // 4, :, at], p)
        top[h] = now

    def edge(i, _):
        mask = seen(i, first, length, rows, keys)
        for h in range(HEADS):
            scores(i, score_a, top_a, h, mask)
        for h in range(HEADS):
            add(i, score_a, top_a, h)
        return 0

    lax.fori_loop(whole, some, edge, 0)
    last = jnp.maximum(whole - 1, 0)
    for h in range(HEADS):
        scores(0, score_a, top_a, h)

    def two(i, _):
        for h in range(HEADS):
            scores(2 * i + 1, score_b, top_b, h)
            add(2 * i, score_a, top_a, h)
        following = jnp.minimum(2 * i + 2, last)
        for h in range(HEADS):
            scores(following, score_a, top_a, h)
            add(2 * i + 1, score_b, top_b, h)
        return 0

    lax.fori_loop(0, whole // 2, two, 0)

    @pl.when(whole % 2 == 1)
    def _():
        for h in range(HEADS):
            add(last, score_a, top_a, h)

    outs = []
    for h in range(HEADS):
        t = acc[h]
        weight = t[64:65]
        outs.append(t[:64] / weight)
        lse_ref[0, h : h + 1, :] = top[h] * SCORE2 + jnp.log2(weight)
    result = low(jnp.concatenate(outs, 0).T)

    @pl.when(b < blocks // 2)
    def _():
        near_ref[0] = result

    @pl.when(b >= blocks // 2)
    def _():
        far_ref[0] = result


def halves_specs(rows, blocks, columns):
    lower = pl.BlockSpec((1, rows, columns), lambda s, b, *_: (s, jnp.minimum(b, blocks // 2 - 1), 0))
    upper = pl.BlockSpec((1, rows, columns), lambda s, b, *_: (s, jnp.maximum(b - blocks // 2, 0), 0))
    return lower, upper


def attend(pos, lens, sources, q, other, kvs):
    seqs, span, _ = q.shape
    count = len(kvs)
    total = count * span
    rows = min(256, span // 2)
    keys = 256
    blocks = span // rows
    lower, upper = halves_specs(rows, blocks, 512)
    half = jax.ShapeDtypeStruct((seqs, span // 2, 512), BF16)
    return pl.pallas_call(
        functools.partial(attend_body, rows=rows, keys=keys, blocks=blocks, count=count, span=span),
        grid_spec=pltpu.PrefetchScalarGridSpec(
            num_scalar_prefetch=3,
            grid=(seqs, blocks),
            in_specs=[lower, upper]
            + [pl.BlockSpec((1, span, 256), lambda s, b, *_: (s, 0, 0), pipeline_mode=pl.Buffered(1))] * count,
            out_specs=[lower, upper, pl.BlockSpec((1, 8, rows), lambda s, b, *_: (s, 0, b))],
            scratch_shapes=[
                pltpu.VMEM((2, total, 128), BF16), pltpu.VMEM((2, 80, total), BF16),
                pltpu.VMEM((8, 1, rows), F32), pltpu.VMEM((8, 80, rows), F32),
                pltpu.VMEM((8, keys, rows), F32), pltpu.VMEM((8, keys, rows), F32),
                pltpu.VMEM((8, 1, rows), F32), pltpu.VMEM((8, 1, rows), F32),
            ],
        ),
        out_shape=[half, half, jax.ShapeDtypeStruct((seqs, 8, span), F32)],
        compiler_params=params(),
        cost_estimate=cost(26),
        name="attend",
    )(pos, lens, sources, q, other, *kvs)


def attend_back_body(
    pos_ref, len_ref, from_ref, q_ref, other_ref, do_near_ref, do_far_ref, o_near_ref, o_far_ref, lse_ref,
    cos_ref, sin_ref, *rest, rows, keys, blocks, count, span, group,
):
    kv_refs = rest[:count]
    dq_near_ref, dq_far_ref = rest[count : count + 2]
    dkv_refs = rest[count + 2 : 2 * count + 2]
    kd, vd, kt, dk, dv, dq = rest[2 * count + 2 :]
    s = pl.program_id(0)
    b = pl.program_id(1)
    prep = min(512, span)

    @pl.when(b == 0)
    def _():
        for r, kv_ref in enumerate(kv_refs):
            for i in range(span // prep):
                here = slice(i * prep, (i + 1) * prep)
                at = pl.ds(pl.multiple_of(from_ref[r] * span + i * prep, prep), prep)
                k = kv_ref[0, here, :128].astype(F32)
                kd[at, :] = dup_halves(k)[group]
                vd[at, :] = dup_halves(kv_ref[0, here, 128:].astype(F32))[group]
                kt[:, at] = low(k.T[64 * group : 64 * group + 64])
        dk[...] = jnp.zeros_like(dk)
        dv[...] = jnp.zeros_like(dv)

    first = pos_ref[b]
    length = len_ref[s]
    is_near = b < blocks // 2
    heads = head_rows(jnp.where(is_near, q_ref[0], other_ref[0]))
    do = jnp.where(is_near, do_near_ref[0], do_far_ref[0])
    grads = head_rows(do)
    prod = do.astype(F32) * jnp.where(is_near, o_near_ref[0], o_far_ref[0]).astype(F32)
    col = lax.broadcasted_iota(jnp.int32, (8, 256), 1) // HEAD
    ones = low(jnp.where(col == lax.broadcasted_iota(jnp.int32, (8, 256), 0), 1.0, 0.0))
    high, remain = split_low(prod)
    delta = dot(ones, high, NT) + dot(ones, remain, NT)
    dq[...] = jnp.zeros_like(dq)
    whole, some = key_range(first, length, rows, keys)

    def step(i, masked):
        at = pl.ds(pl.multiple_of(i * keys, keys), keys)
        mask = seen(i, first, length, rows, keys) if masked else None
        dv_sum = dk_sum = None
        for h in range(4):
            x = dot(kd[at, :], heads[h], NT) * SCORE2 - lse_ref[0, 4 * group + h : 4 * group + h + 1, :]
            dp = dot(vd[at, :], grads[h], NT)
            if masked:
                x = jnp.where(mask, x, LOWEST)
            p = jnp.exp2(x)
            ds = low(p * (dp - delta[h : h + 1]))
            dv_part = dot(low(p), grads[h])
            dk_part = dot(ds, heads[h])
            dv_sum = dv_part if dv_sum is None else dv_sum + dv_part
            dk_sum = dk_part if dk_sum is None else dk_sum + dk_part
            dq[h] += dot(kt[:, at], ds)
        dv[at, :] += dv_sum
        dk[at, :] += dk_sum

    lax.fori_loop(0, whole, lambda i, _: (step(i, False), 0)[1], 0)
    lax.fori_loop(whole, some, lambda i, _: (step(i, True), 0)[1], 0)
    cosine, sine = cos_ref[...], sin_ref[...]
    parts = []
    for h in range(4):
        t = dq[h] * 0.125
        former, latter = t[:32], t[32:]
        parts += [former * cosine + latter * sine, latter * cosine - former * sine]
    result = low(jnp.concatenate(parts, 0).T)

    @pl.when(is_near)
    def _():
        dq_near_ref[0] = result

    @pl.when(jnp.logical_not(is_near))
    def _():
        dq_far_ref[0] = result

    @pl.when(b == blocks - 1)
    def _():
        lane = lax.broadcasted_iota(jnp.int32, (prep, 128), 1)
        for r, dkv_ref in enumerate(dkv_refs):
            for i in range(span // prep):
                at = pl.ds(pl.multiple_of(from_ref[r] * span + i * prep, prep), prep)
                k, v = dk[at, :], dv[at, :]
                k = (k + pltpu.roll(k, 64, 1)) * 0.125
                v = v + pltpu.roll(v, 64, 1)
                dkv_ref[0, i * prep : (i + 1) * prep] = low(jnp.where(lane < 64, k, v))


def attend_backward(group, pos, lens, sources, q, other, do_near, do_far, o_near, o_far, lse, cosine, sine, kvs):
    seqs, span, _ = q.shape
    count = len(kvs)
    total = count * span
    rows = min(256, span // 2)
    keys = 512
    blocks = span // rows
    lower = pl.BlockSpec((1, rows, 256), lambda s, b, *_: (s, jnp.minimum(b, blocks // 2 - 1), group))
    upper = pl.BlockSpec((1, rows, 256), lambda s, b, *_: (s, jnp.maximum(b - blocks // 2, 0), group))
    out_lower, out_upper = halves_specs(rows, blocks, 256)
    stat = pl.BlockSpec((1, 8, rows), lambda s, b, *_: (s, 0, b))
    table = pl.BlockSpec((32, rows), lambda s, b, *_: (0, b))
    half = jax.ShapeDtypeStruct((seqs, span // 2, 256), BF16)
    outs = pl.pallas_call(
        functools.partial(
            attend_back_body, rows=rows, keys=keys, blocks=blocks, count=count, span=span, group=group
        ),
        grid_spec=pltpu.PrefetchScalarGridSpec(
            num_scalar_prefetch=3,
            grid=(seqs, blocks),
            in_specs=[lower, upper, lower, upper, lower, upper, stat, table, table]
            + [pl.BlockSpec((1, span, 256), lambda s, b, *_: (s, 0, 0), pipeline_mode=pl.Buffered(1))] * count,
            out_specs=[out_lower, out_upper]
            + [pl.BlockSpec((1, span, 128), lambda s, b, *_: (s, 0, 0))] * count,
            scratch_shapes=[
                pltpu.VMEM((total, 128), BF16), pltpu.VMEM((total, 128), BF16), pltpu.VMEM((64, total), BF16),
                pltpu.VMEM((total, 128), F32), pltpu.VMEM((total, 128), F32), pltpu.VMEM((4, 64, rows), F32),
            ],
        ),
        out_shape=[half, half] + [jax.ShapeDtypeStruct((seqs, span, 128), BF16)] * count,
        compiler_params=params(),
        cost_estimate=cost(1 if group else 20),
        name="attend_backward",
    )(pos, lens, sources, q, other, do_near, do_far, o_near, o_far, lse, cosine, sine, *kvs)
    return outs[0], outs[1], outs[2:]


def in_hbm(shape):
    return pltpu.HBM(shape, BF16)


def both(left, right):
    return dot(left[0][...], right[0][...], TN) + dot(left[1][...], right[1][...], TN)


def tall_body(place_ref, left_a, left_b, *rest, n, widths, square):
    rights = [rest[2 * k : 2 * k + 2] for k in range(len(widths))]
    outs = rest[2 * len(widths) :]
    rows = left_a.shape[1] // n
    i = pl.program_id(0)
    start = 0
    for part, (right, steps) in enumerate(zip(rights, widths)):

        @pl.when((i >= start) & (i < start + steps))
        def _(part=part, right=right):
            if square:
                if square == "hops":
                    own, to_x, keep_x, to_y, keep_y = outs
                    first, keep = ((to_x, keep_x), (to_y, keep_y))[part]
                for k in range(4):
                    block = jnp.bitwise_xor(place_ref[0], k)
                    columns = pl.ds(pl.multiple_of(block * rows, rows), rows)
                    value = low(both((left_a.at[:, columns], left_b.at[:, columns]), right))
                    if square == "direct":
                        outs[k][...] = value
                    elif k == 0:
                        own[...] = value
                    elif k == 3:
                        first[1] = value
                    elif k == part + 1:
                        first[0] = value
                    else:
                        keep[...] = value
            else:
                value = low(both((left_a, left_b), right))
                for j in range(n):
                    outs[0][j] = value[j * rows : (j + 1) * rows]

        start += steps


def tall_grad(place, left, rights, chunk, n, square="", micros=0.0, name="grad"):
    tokens, width = left[0].shape[0], left[3]
    widths = [v[3] // chunk for v in rights]
    steps = sum(widths)
    rows = width // n
    starts = [0, widths[0]]
    parts = range(len(rights))

    def within(k, i):
        return jnp.clip(i - starts[k], 0, widths[k] - 1)

    def right_spec(k):
        return pl.BlockSpec((tokens, chunk), lambda i, place: (0, rights[k][2] // chunk + within(k, i)))

    left_spec = pl.BlockSpec(
        (tokens, width), lambda i, place: (0, left[2] // width), pipeline_mode=pl.Buffered(1)
    )

    if square == "direct":
        out_specs = [pl.BlockSpec((rows, chunk), lambda i, place: (i, 0))] * 4
        out_shape = [in_hbm((steps * rows, chunk))] * 4
    elif square:
        out_specs = [pl.BlockSpec((rows, chunk), lambda i, place: (i, 0))]
        out_shape = [jax.ShapeDtypeStruct((steps * rows, chunk), BF16)]
        for k in parts:
            out_specs.append(pl.BlockSpec((2, rows, chunk), lambda i, place, k=k: (0, within(k, i), 0)))
            out_specs.append(pl.BlockSpec((rows, chunk), lambda i, place, k=k: (within(k, i), 0)))
            out_shape.append(in_hbm((2, widths[k] * rows, chunk)))
            out_shape.append(jax.ShapeDtypeStruct((widths[k] * rows, chunk), BF16))
    else:
        out_specs = pl.BlockSpec((n, rows, chunk), lambda i, place: (0, i, 0))
        out_shape = jax.ShapeDtypeStruct((n, steps * rows, chunk), BF16)
    return pl.pallas_call(
        functools.partial(tall_body, n=n, widths=widths, square=square),
        grid_spec=pltpu.PrefetchScalarGridSpec(
            num_scalar_prefetch=1,
            grid=(steps,),
            in_specs=[left_spec] * 2 + [right_spec(k) for k in parts for _ in range(2)],
            out_specs=out_specs,
        ),
        out_shape=out_shape,
        compiler_params=pltpu.CompilerParams(vmem_limit_bytes=VMEM_LIMIT),
        cost_estimate=cost(micros),
        name=name,
    )(place, *left[:2], *[v for right in rights for v in right[:2]])


PIECE = 256


def wide_body(place_ref, *rest, parts, group, square, split):
    lefts = [rest[2 * k : 2 * k + 2] for k in range(parts)]
    rights = [rest[2 * k : 2 * k + 2] for k in range(parts, 2 * parts)]
    outs = rest[4 * parts :]
    values = [low(both(left, right)) for left, right in zip(lefts, rights)]
    values = [v[:, c : c + PIECE] for v in values for c in range(0, v.shape[1], PIECE)]
    if square:
        own, to_x, keep_x, to_y, keep_y = outs
        value = jnp.concatenate(values, 0)
        for k in range(4):

            @pl.when(pl.program_id(0) == k)
            def _(k=k):
                if k == 0:
                    own[...] = value
                    return
                for part, (first, keep) in enumerate(((to_x, keep_x), (to_y, keep_y))):
                    here = value[split:] if part else value[:split]
                    if k == 3:
                        first[1] = here
                    elif k == part + 1:
                        first[0] = here
                    else:
                        keep[...] = here
    else:
        for j in range(group):
            start = 0
            for v in values:
                rows = v.shape[0] // group
                outs[0][j, start : start + rows] = v[j * rows : (j + 1) * rows]
                start += rows


def wide_grad(place, lefts, rights, n, square="", micros=0.0, name="grad"):
    tokens = lefts[0][0].shape[0]
    steps = min(n, 4)
    rows = [v[3] // n * (g[3] // PIECE) for v, g in zip(lefts, rights)]
    total = sum(rows)
    split = sum(rows[:2])

    def turn(i, place):
        return jnp.bitwise_xor(place[0], i) if square else i

    def once(*dims):
        return pl.BlockSpec(dims, lambda i, place: (0,) * len(dims), pipeline_mode=pl.Buffered(1))

    def left_spec(v):
        size = v[3] // steps
        return pl.BlockSpec((tokens, size), lambda i, place: (0, v[2] // size + turn(i, place)))

    def right_spec(v):
        return pl.BlockSpec((tokens, v[3]), lambda i, place: (0, v[2] // v[3]), pipeline_mode=pl.Buffered(1))

    if square:
        dims = [(total, PIECE)]
        for size in (split, total - split):
            dims += [(2, size, PIECE), (size, PIECE)]
        out_specs = [once(*d) for d in dims]
        out_shape = [in_hbm(d) for d in dims]
    else:
        out_specs = pl.BlockSpec((n // steps, total, PIECE), lambda i, place: (i, 0, 0))
        out_shape = jax.ShapeDtypeStruct((n, total, PIECE), BF16)
    return pl.pallas_call(
        functools.partial(wide_body, parts=len(lefts), group=n // steps, square=square, split=split),
        grid_spec=pltpu.PrefetchScalarGridSpec(
            num_scalar_prefetch=1,
            grid=(steps,),
            in_specs=[left_spec(v) for v in lefts for _ in range(2)] + [right_spec(v) for v in rights for _ in range(2)],
            out_specs=out_specs,
        ),
        out_shape=out_shape,
        compiler_params=pltpu.CompilerParams(vmem_limit_bytes=VMEM_LIMIT),
        cost_estimate=cost(micros),
        name=name,
    )(place, *[v for left in lefts for v in left[:2]], *[v for right in rights for v in right[:2]])


def in_place(body, args, outs, name, micros=0):
    return pl.pallas_call(
        body,
        grid=(1,),
        in_specs=[SCALARS if v.ndim == 1 else full_spec(v.shape) for v in args],
        out_specs=[full_spec(v.shape) for v in outs],
        out_shape=outs,
        compiler_params=pltpu.CompilerParams(vmem_limit_bytes=VMEM_LIMIT),
        cost_estimate=cost(micros),
        name=name,
    )(*args)


def like(v):
    return in_hbm(v.shape)


def first_body(keep_x, keep_y, from_x, from_y, to_y, to_x):
    to_y[...] = low(keep_x[...].astype(F32) + from_x[1].astype(F32))
    to_x[...] = low(keep_y[...].astype(F32) + from_y[1].astype(F32))


def second_body(own, from_x, from_y, late_y, late_x, out):
    split = late_y.shape[0]
    for at, first, last in ((slice(0, split), from_x, late_y), (slice(split, None), from_y, late_x)):
        out[at] = low(own[at].astype(F32) + first[0].astype(F32) + last[...].astype(F32))


def sum_body(*refs):
    total = refs[0][...].astype(F32)
    for ref in refs[1:-1]:
        total = total + ref[...].astype(F32)
    refs[-1][...] = low(total)


def square_body(own, one, two, three, out):
    near = own[...].astype(F32) + one[...].astype(F32)
    out[...] = low(near + (two[...].astype(F32) + three[...].astype(F32)))


def unpack_body(core_ref, own, other, *outs, plan):
    first = core_ref[0] == 0
    for out, column, columns, half, start, rows in plan:
        at = slice(start, start + rows)
        a, b = (own, other) if half == 0 else (other, own)
        value = jnp.where(first, a[at], b[at])
        outs[out][:, column : column + columns] = value[:, :columns].astype(F32)


def unpack(core, own, other, matrices):
    piece = own.shape[1]
    plan, shapes, start = [], [], 0
    for rows, pieces, columns in matrices:
        ends = np.cumsum([0] + list(columns))
        for half in range(2):
            for i in range(pieces):
                column = (half * pieces + i) * piece
                for k, size in enumerate(columns):
                    if ends[k] <= column < ends[k + 1]:
                        offset = int(column - ends[k])
                        plan.append(
                            (len(shapes) + k, offset, min(piece, size - offset), half, start + i * rows, rows)
                        )
        shapes += [jax.ShapeDtypeStruct((rows, size), F32) for size in columns]
        start += pieces * rows
    return in_place(functools.partial(unpack_body, plan=plan), (core, own, other), shapes, "unpack")


def ring(value, steps):
    n = lax.axis_size("seq")
    return lax.ppermute(value, "seq", [(i, (i + steps) % n) for i in range(n)])


def along(value, steps):
    n = lax.axis_size("seq")
    return lax.ppermute(value, "seq", [(i, i + steps) for i in range(n) if 0 <= i + steps < n])


def mirror(value):
    n = lax.axis_size("seq")
    return lax.ppermute(value, "seq", [(i, n - 1 - i) for i in range(n)])


def flip_dp(value, bit):
    n = lax.axis_size("dp")
    return lax.ppermute(value, "dp", [(i, i ^ bit) for i in range(n)])


def other_core(value):
    return flip_dp(value, 1)


def after(value, *done):
    return lax.optimization_barrier((value, done))[0]


def scatter_seq(value):
    return lax.psum_scatter(value, "seq", scatter_dimension=0, tiled=True)[0]


def flip_seq(value, bit):
    n = lax.axis_size("seq")
    return lax.ppermute(value, "seq", [(i, i ^ bit) for i in range(n)])


def add_low(*values):
    return in_place(sum_body, values, [like(values[0])], "add")[0]


def direct_sum(pieces):
    return add_low(pieces[0], *[flip_seq(v, k) for k, v in enumerate(pieces) if k])


def first_hop(pieces, *done):
    own, to_x, keep_x, to_y, keep_y = pieces
    from_x, from_y = flip_seq(to_x, 1), flip_seq(to_y, 2)
    held = in_place(
        first_body, (after(keep_x, *done), keep_y, from_x, from_y), [like(keep_x), like(keep_y)], "first_hop"
    )
    return (*held, own, from_x, from_y)


def with_rows(pieces, place, rows):
    own, to_x, keep_x, to_y, keep_y = pieces
    split = keep_x.shape[0]
    mine, beside, below, across = [rows[jnp.bitwise_xor(place, k)] for k in range(4)]
    own = jnp.concatenate([own[:split], mine, own[split:]], 0)
    to_x = jnp.concatenate([to_x, jnp.stack([beside, across])], 1)
    return own, to_x, jnp.concatenate([keep_x, below], 0), to_y, keep_y


def second_hop(held, *done):
    to_y, to_x, own, from_x, from_y = held
    args = (after(own, *done), from_x, from_y, flip_seq(to_y, 2), flip_seq(to_x, 1))
    return in_place(second_body, args, [like(own)], "second_hop")[0]


def offloaded_sum_z(value, which):
    n = lax.axis_size("dp")
    groups = [list(range(c, n, 2))[:: -1 if which & 1 else 1] for c in range(2)]
    return lax.psum(value, "dp", axis_index_groups=groups[:: -1 if which & 2 else 1])


def sum_four(value, *done):
    got = [flip_dp(value, bit) for bit in (2, 4, 6)]
    return in_place(square_body, (after(value, *done), *got), [like(value)], "add")[0]


def sum_z(value, first=2, last=None):
    bit = first
    while bit < (last or lax.axis_size("dp")):
        value = add_low(value, flip_dp(value, bit))
        bit *= 2
    return value


def on_device(
    tokens, cotangent, lengths, norm_one, w_query, w_key, w_value, w_gatez, w_conv_in, w_step, conv_weight,
    conv_bias, step_bias, decay_log, skip_gain, gated_gain, w_attn_out, w_mix_out, norm_two, w_gate, w_up, w_down,
):
    seqs, span, width = tokens.shape
    half = span // 2
    taps, conv_width = conv_weight.shape
    count = lax.axis_size("seq")
    place = lax.axis_index("seq").astype(jnp.int32)
    core = (lax.axis_index("dp") % 2).astype(jnp.int32)
    first = place * span
    mirrored = (count - 1 - place) * span + half
    inverse = 1.0 / ROPE_BASE ** (jnp.arange(0, HEAD, 2).astype(F32) / HEAD)

    def tables(positions):
        angles = positions.astype(F32)[:, None] * inverse[None, :]
        return jnp.cos(angles), jnp.sin(angles)

    cosine, sine = tables(first + jnp.arange(span))
    cos_row = jnp.concatenate([cosine] * 4, 1)
    sin_row = jnp.concatenate([-sine, sine] * 2, 1)
    cos_back, sin_back = tables(jnp.concatenate([first + jnp.arange(half), mirrored + jnp.arange(half)]))
    rate = -jnp.exp(decay_log)
    pad = (0, 128 - SSM_HEADS)
    rate_row = jnp.pad(rate, pad)[None]
    step_row = jnp.pad(step_bias, pad)[None]
    w_step_wide = jnp.pad(w_step, ((0, 0), pad))
    skip_row = jnp.repeat(skip_gain, SSM_HEAD)[None]
    ones = (np.arange(WIDE)[None, :] // SSM_HEAD == np.arange(128)[:, None]).astype(np.float32)
    expand = jnp.asarray(np.concatenate([ones, ones], 0), BF16)
    pos = jnp.stack([first, core])
    core_here = core[None]
    rows = min(256, half)
    blocks = jnp.concatenate([base + jnp.arange(0, half, rows, dtype=jnp.int32) for base in (first, mirrored)])
    sources = lax.rem(place - jnp.arange(count, dtype=jnp.int32) + count, count)
    here = place[None]

    def flat(v):
        return v.reshape(seqs * span, v.shape[2])

    def with_other(mine, yours=None):
        mine, yours = flat(mine), flat(mine if yours is None else yours)
        return mine, other_core(yours), 0, mine.shape[1]

    halo = along(tokens[:, span - 16 :], 1)
    hidden, q, kv = enter(after(tokens, halo), norm_one[None], w_query, w_key, w_value, cos_row, sin_row)
    kvs = [kv] + [ring(kv, r) for r in range(1, count)]
    q_other = mirror(q[:, half:])
    z, conv, pre, x, bk, cq, dt, sg, cum, cumt, state = mixer(
        pos, lengths, hidden, halo, norm_one[None], w_gatez, w_conv_in, w_step_wide, conv_weight, conv_bias[None],
        step_row, rate_row * LOG2E, expand,
    )
    states = lax.all_gather(state, "seq")
    o_near, o_far, lse = attend(blocks, lengths, sources, after(q, state), q_other, kvs)
    o_back = mirror(o_far)
    mixed, mix_low, held = scan_forward(
        here, after(x, o_near), bk, cq, dt, cum, cumt, skip_row, z, gated_gain[None], expand, states
    )
    hid = with_other(hidden)
    mix_pair = with_other(mix_low)
    output, lefts, mine, yours, grad_mid, g_norm_two = middle(
        pos, lengths, o_near, o_back, after(mix_low, hid[1]), tokens, cotangent, w_attn_out, w_mix_out, w_gate, w_up, w_down,
        norm_two[None],
    )
    square = "hops" if count == 4 else ""
    ff = w_gate.shape[1]
    lefts, rights = with_other(lefts), with_other(mine, yours)
    ffn_left = (*lefts[:2], 0, width)
    ffn_rights = [(*rights[:2], k * ff // 2, ff // 2) for k in range(2)]
    grad_ffn, grad_branch = [(*rights[:2], ff + k * width // 2, width // 2) for k in range(2)]
    out_lefts = ((*lefts[:2], width, ff), (*lefts[:2], width + ff, w_attn_out.shape[0]), mix_pair, hid)
    do_near, do_far, grad_mixed, gz_m, gz_y, g_gated, adjoint = branch_back(
        core_here, mine, yours, mixed, z, cq, cum, w_attn_out, w_mix_out, gated_gain[None], expand
    )
    adjoints = [along(adjoint, -r) for r in range(1, count)]
    do_other = mirror(do_far)
    part_ffn = tall_grad(after(here, do_near), ffn_left, ffn_rights, 512, count, square, name="grad_ffn_in")
    part_out = wide_grad(
        after(here, part_ffn[0], *adjoints), out_lefts, (grad_ffn, grad_branch, grad_branch, with_other(gz_m, gz_y)), count,
        square, micros=16, name="grad_outs",
    )
    ffn_held = first_hop(part_ffn, part_out[0]) if square else scatter_seq(part_ffn)
    gc_m, gc_y, tail, head, g_conv_small, g_skip, g_small = scan_backward(
        after(x, part_out[0]), bk, cq, dt, sg, cum, cumt, grad_mixed, mixed, held, pre, conv, skip_row, rate_row,
        conv_weight, expand, core_here, adjoints,
    )
    out_held = first_hop(part_out) if square else scatter_seq(part_out)
    ffn_sum = second_hop(ffn_held) if square else ffn_held
    head = after(head, out_held, ffn_sum)
    returned = along(low(head), -1).astype(F32)[:, : taps - 1]
    g_conv_weight = g_conv_small[:taps]
    beside = ((0, 0), (0, 0), (0, tail.shape[2] - conv_width))
    for ahead in range(1, taps):
        tap = taps - 1 - ahead
        fill = jnp.pad(returned[:, :ahead], ((0, 0), (8 - ahead, 0), (0, 0)))
        tail = tail + jnp.pad(conv_weight[tap] * fill, beside)
        g_conv_weight = g_conv_weight.at[tap].add(jnp.sum(fill * conv[:, span - 8 :].astype(F32), (0, 1)))
    tail = low(tail)
    size = tail.shape[2] // 2
    tails = tail[:, :, :size], tail[:, :, size:]
    gc_m, gc_y = [
        lax.dynamic_update_slice(v, jnp.where(core == i, *tails), (0, span - 8, 0)) for i, v in enumerate((gc_m, gc_y))
    ]
    part_in = tall_grad(
        here, hid, (with_other(gc_m, gc_y),), 256, count, "direct" if square else "", name="grad_conv_in"
    )
    ffn_sum = offloaded_sum_z(ffn_sum, 0)
    out_sum = second_hop(out_held, part_in[0]) if square else out_held
    order = (part_in[0], out_sum)
    out_sum = offloaded_sum_z(out_sum, 1)

    small = [
        g_norm_two[0], g_gated[0], g_conv_weight.reshape(-1), g_conv_small[taps], g_skip[0],
        g_small[0], g_small[1],
    ]
    sizes = [v.shape[0] for v in small]
    total = jnp.concatenate(small)
    total = jnp.pad(total, (0, -total.shape[0] % 1024)).reshape(-1, 128)
    hops = [("seq", 1 << k) for k in range(count.bit_length() - 1)]
    hops += [("dp", 2 << k) for k in range(lax.axis_size("dp").bit_length() - 2)] + [("dp", 1)]

    def flip(value, axis, bit):
        return flip_seq(value, bit) if axis == "seq" else flip_dp(value, bit)

    def small_step(total):
        axis, bit = hops.pop(0)
        return total + flip(total, axis, bit)

    def back(group, order):
        near, far, parts = attend_backward(
            group, blocks, lengths, sources, after(q, *order), q_other, do_near, do_other, o_near, o_far, lse,
            cos_back.T, sin_back.T, kvs,
        )
        return near, mirror(far), [parts[0]] + [ring(parts[r], -r) for r in range(1, count)]

    dq_near, dq_far, pieces = back(0, order)
    in_sum = direct_sum([after(part_in[0], dq_near), *part_in[1:]]) if square else scatter_seq(part_in)
    total = small_step(total)
    results = back(1, (dq_near, in_sum, ffn_sum, total))
    four = lax.axis_size("dp") == 8
    in_sum = offloaded_sum_z(in_sum, 2)
    total = small_step(after(total, dq_near))
    gh = leave_mixer(
        core_here, (after(gz_m, results[0], dq_far, total, *pieces), gz_y), (gc_m, gc_y), w_gatez, w_conv_in, w_step_wide
    )
    total = small_step(after(total, results[0]))
    heads = heads_back(
        core_here, after(cos_row, gh, total), sin_row, (dq_near, results[0]), (dq_far, results[1]), pieces + results[2]
    )
    heads_pairs = with_other(*heads[:2]), with_other(*heads[2:])
    grad_tokens, g_norm_one = leave(
        core_here, tokens, grad_mid, gh, heads, norm_one[None], w_query, w_key, w_value
    )
    total = small_step(after(total, gh))
    part_qkv = tall_grad(
        after(here, grad_tokens, out_sum, total), hid, heads_pairs, 128, count, square, name="grad_qkv"
    )
    norm_rows = low(g_norm_one.reshape(count, -1))
    columns = min(128, norm_rows.shape[1])
    norm_rows = norm_rows.reshape(count, -1, columns)
    norm_shape = norm_rows.shape[1:]
    norm_rows = jnp.pad(norm_rows, ((0, 0), (0, -norm_shape[0] % 16), (0, 128 - columns)))
    norm_at = 2 * width // count if square else part_qkv.shape[1]
    if square:
        part_qkv = with_rows(part_qkv, place, norm_rows)
    else:
        part_qkv = jnp.concatenate([part_qkv, norm_rows], 1)
    while hops:
        total = small_step(total)
    qkv_held = first_hop(part_qkv, out_sum, in_sum, total) if square else scatter_seq(part_qkv)
    qkv_sum = second_hop(qkv_held, total) if square else qkv_held
    ffn_sum, out_sum, in_sum = [after(v, qkv_sum) for v in (ffn_sum, out_sum, in_sum)]
    block = width // count

    def rows_of(*weights):
        return [(v.shape[0] // count, v.shape[1] // 2 // PIECE, (v.shape[1],)) for v in weights]

    s_gate, s_up = unpack(core_here, ffn_sum, other_core(ffn_sum), [(block, 2, (v.shape[1],)) for v in (w_gate, w_up)])
    s_down, s_attn_out, s_mix_out, s_gatez = unpack(
        core_here, out_sum, other_core(out_sum), rows_of(w_down, w_attn_out, w_mix_out, w_gatez)
    )
    s_conv, s_step = unpack(
        core_here, in_sum, other_core(in_sum),
        [(block, (conv_width + 256) // 2 // PIECE, (conv_width, SSM_HEADS))],
    )
    if four:
        qkv_sum = sum_four(qkv_sum, s_gate, s_down, s_conv)
    else:
        qkv_sum = sum_z(qkv_sum)
    got = other_core(qkv_sum)
    norm_parts = [v[norm_at : norm_at + norm_shape[0], : norm_shape[1]].astype(F32) for v in (qkv_sum, got)]
    s_norm_one = (norm_parts[0] + norm_parts[1]).reshape(-1)
    qkv_sum, got = [
        jnp.concatenate([v[:norm_at], v[norm_at + norm_rows.shape[1] :]], 0) for v in (qkv_sum, got)
    ]
    s_query, s_key, s_value = unpack(
        core_here, qkv_sum, got, [(block, 2, (w_query.shape[1],)), (block, 1, (w_key.shape[1], w_value.shape[1]))]
    )
    total = total.reshape(-1)
    starts = np.cumsum([0] + sizes)
    small = [total[a:b] for a, b in zip(starts[:-1], starts[1:])]

    def own(v):
        n = v.shape[0] // count
        return lax.dynamic_slice(v, (place * n,), (n,))

    s_norm_two, s_gated = [own(v) for v in small[:2]]
    s_skip = jnp.sum(small[4].reshape(SSM_HEADS, SSM_HEAD), 1)
    return (
        output,
        grad_tokens,
        s_norm_one,
        s_query,
        s_key,
        s_value,
        s_gatez,
        s_conv,
        s_step,
        small[2].reshape(taps, -1),
        small[3],
        small[6][:SSM_HEADS],
        small[5][:SSM_HEADS],
        s_skip,
        s_gated,
        s_attn_out,
        s_mix_out,
        s_norm_two,
        s_gate,
        s_up,
        s_down,
    )


def solution(mesh):
    copied = (P(),) * 19
    return jax.shard_map(
        on_device,
        mesh=mesh,
        in_specs=(P("dp", "seq", None), P("dp", "seq", None), P("dp")) + copied,
        out_specs=(
            P("dp", "seq", None), P("dp", "seq", None), P("seq"),
            P("seq", None), P("seq", None), P("seq", None), P("seq", None), P("seq", None), P("seq", None),
            P(), P(), P(), P(), P(),
            P("seq"), P("seq", None), P("seq", None), P("seq"), P("seq", None), P("seq", None), P("seq", None),
        ),
        check_vma=False,
    )
```

```python
import functools

import jax
import jax.numpy as jnp
import numpy as np
from jax import lax
from jax.experimental import pallas as pl
from jax.experimental.pallas import tpu as pltpu
from jax.sharding import PartitionSpec as P

HEADS = 8
KV_HEADS = 2
HEAD = 64
SSM_HEADS = 24
SSM_HEAD = 64
STATE = 128
WIDE = SSM_HEADS * SSM_HEAD
CHUNK = 128
EPS = 1e-05
ROPE_BASE = 100000000000.0
LOG2E = 1.4426950408889634
SCORE2 = 0.125 * LOG2E
LOWEST = -1e30
F32 = jnp.float32
BF16 = jnp.bfloat16
NN = (((1,), (0,)), ((), ()))
NT = (((1,), (1,)), ((), ()))
TN = (((0,), (0,)), ((), ()))
VMEM_LIMIT = 127 << 19


def dot(a, b, dims=NN):
    return lax.dot_general(a, b, dims, preferred_element_type=F32)


def dot_exact(a, b, dims=NN):
    return lax.dot_general(a, b, dims, precision=lax.Precision.HIGHEST, preferred_element_type=F32)


def low(v):
    return v.astype(BF16)


def sigmoid(v):
    return jax.nn.sigmoid(v)


def softplus(v):
    e = jnp.exp(-jnp.abs(v))
    tail = jnp.where(e < 1e-2, e * (1.0 - e * (0.5 - e * (1.0 / 3.0))), jnp.log(1.0 + e))
    return jnp.maximum(v, 0.0) + tail


def split_low(v):
    high = low(v)
    return high, low(v - high.astype(F32))


def widen(v, expand):
    return dot(jnp.concatenate(split_low(v), 1), expand)


def head_sums(v, expand):
    high, rest = split_low(v)
    ones = expand[:128]
    return dot(high, ones, NT) + dot(rest, ones, NT)


def cost(micros):
    return pl.CostEstimate(flops=int(micros * 3e9), bytes_accessed=int(micros * 1e5), transcendentals=0)


def full_spec(shape):
    return pl.BlockSpec(shape, lambda *_: (0,) * len(shape), pipeline_mode=pl.Buffered(1))


def params(limit=VMEM_LIMIT):
    return pltpu.CompilerParams(
        vmem_limit_bytes=limit, dimension_semantics=("arbitrary", "arbitrary")
    )


SCALARS = pl.BlockSpec(memory_space=pltpu.SMEM)


def halves_out(core, values, mine_ref, yours_ref):
    first = core == 0
    start = 0
    for value in values:
        size = value.shape[1] // 2
        lower, upper = value[:, :size], value[:, size:]
        mine_ref[0, :, start : start + size] = jnp.where(first, lower, upper)
        yours_ref[0, :, start : start + size] = jnp.where(first, upper, lower)
        start += size


def halves_in(core, mine, yours):
    first = core == 0
    return jnp.concatenate([jnp.where(first, mine, yours), jnp.where(first, yours, mine)], 1)


def low_rows(rows):
    t = lax.broadcasted_iota(jnp.int32, (rows, rows), 0)
    u = lax.broadcasted_iota(jnp.int32, (rows, rows), 1)
    return t >= u


def rotation(span, count, order):
    inverse = (1.0 / np.float64(ROPE_BASE) ** (np.arange(0, HEAD, 2) / HEAD)).astype(np.float32).astype(np.float64)
    steps = np.arange(span)[:, None] * inverse
    starts = (np.arange(count) * span)[:, None] * inverse
    if order == "rows":
        sign = np.tile(np.repeat([-1.0, 1.0], HEAD // 2), 2)
        made = [np.tile(np.cos(steps), 4), np.tile(np.sin(steps), 4) * sign]
        made += [np.tile(np.cos(starts), 4)[:, None], (np.tile(np.sin(starts), 4) * sign)[:, None]]
    else:
        made = [np.cos(steps).T, np.sin(steps).T]
        made += [np.repeat(f(starts)[:, :, None], 128, 2) for f in (np.cos, np.sin)]
    return [jnp.asarray(v.astype(np.float32)) for v in made]


def turned(step_cos, step_sin, start_cos, start_sin):
    return start_cos * step_cos - start_sin * step_sin, start_sin * step_cos + start_cos * step_sin


def swap_halves(v):
    lane = lax.broadcasted_iota(jnp.int32, v.shape, 1)
    return jnp.where((lane & 63) < 32, pltpu.roll(v, 96, 1), pltpu.roll(v, 32, 1))


def pair_rows(v):
    lane = lax.broadcasted_iota(jnp.int32, v.shape, 1)
    none = jnp.zeros_like(v)
    return jnp.concatenate([jnp.where(lane < 64, v, none), jnp.where(lane >= 64, v, none)], 0)


def first_norm(v, gain):
    v = v.astype(F32)
    return low(v * lax.rsqrt(jnp.mean(v * v, -1, keepdims=True) + EPS) * gain)


def enter_body(
    place_ref, tok_ref, gain_ref, wq_ref, wk_ref, wv_ref, cos_ref, sin_ref, cos0_ref, sin0_ref, hid_ref, q_ref, kv_ref
):
    hid = first_norm(tok_ref[0], gain_ref[...])
    hid_ref[0] = hid
    place = place_ref[0]
    cosine, sine = turned(cos_ref[...], sin_ref[...], cos0_ref[place], sin0_ref[place])
    t = dot(hid, wk_ref[...])
    kv_ref[0, :, :128] = low(t * cosine + swap_halves(t) * sine)
    kv_ref[0, :, 128:] = low(dot(hid, wv_ref[...]))
    q = dot(hid, wq_ref[...])
    for g in range(4):
        t = q[:, g * 128 : g * 128 + 128]
        q_ref[0, :, g * 128 : g * 128 + 128] = low(t * cosine + swap_halves(t) * sine)


def enter(place, tokens, gain, wq, wk, wv, tables):
    seqs, span, width = tokens.shape
    rows = min(256, span)

    def row(n):
        return pl.BlockSpec((1, rows, n), lambda s, b: (s, b, 0))

    table = pl.BlockSpec((rows, 128), lambda s, b: (b, 0))
    return pl.pallas_call(
        enter_body,
        grid=(seqs, span // rows),
        in_specs=[SCALARS, row(width)]
        + [full_spec(v.shape) for v in (gain, wq, wk, wv)]
        + [table, table]
        + [full_spec(v.shape) for v in tables[2:]],
        out_specs=[row(width), row(512), row(256)],
        out_shape=[jax.ShapeDtypeStruct((seqs, span, n), BF16) for n in (width, 512, 256)],
        compiler_params=params(),
        cost_estimate=cost(8),
        name="enter",
    )(place, tokens, gain, wq, wk, wv, *tables)


def mixer_body(
    pos_ref, len_ref, hid_ref, halo_ref, gain_ref, wz_ref, wc_ref, ws_ref, cw_ref, cb_ref, sb_ref, a_ref, exp_ref,
    z_ref, cl_ref, pre_ref, x_ref, bk_ref, cq_ref, dt_ref, sg_ref, cum_ref, cumt_ref, st_ref,
    prev, state, total, *, rows, blocks,
):
    s = pl.program_id(0)
    b = pl.program_id(1)

    @pl.when(b == 0)
    def _():
        prev[...] = dot(first_norm(halo_ref[0], gain_ref[...]), wc_ref[...])[8:]
        state[...] = jnp.zeros_like(state)
        total[...] = jnp.zeros_like(total)

    hid = hid_ref[0]
    conv = dot(hid, wc_ref[...])
    raw = dot(hid, ws_ref[...]) + sb_ref[...]
    z_ref[0] = low(dot(hid, wz_ref[...]))
    cl_ref[0] = low(conv)
    ext = jnp.concatenate([prev[...], conv], 0)
    prev[...] = conv[rows - 8 :]
    pre = cb_ref[...] + cw_ref[3:4] * conv
    for back in range(1, 4):
        pre = pre + cw_ref[3 - back : 4 - back] * pltpu.roll(ext, back, 0)[8:]
    pre_ref[0] = low(pre)
    act = low(pre * sigmoid(pre))
    x = act[:, :WIDE]
    bk = act[:, WIDE : WIDE + STATE]
    x_ref[0] = x
    bk_ref[0] = bk
    cq_ref[0] = act[:, WIDE + STATE :]
    at = pos_ref[0] + b * rows + lax.broadcasted_iota(jnp.int32, raw.shape, 0)
    live = jnp.where(at < len_ref[s], 1.0, 0.0)
    dt = softplus(raw) * live
    dt_ref[0] = dt
    sg_ref[0] = sigmoid(raw) * live
    log_decay = dt * a_ref[...]
    tri = jnp.where(low_rows(CHUNK), 1.0, 0.0)
    for c in range(rows // CHUNK):
        here = slice(c * CHUNK, (c + 1) * CHUNK)
        cum = dot_exact(tri, log_decay[here])
        cum_ref[0, here] = cum
        cumt_ref[0, :, here] = cum.T[:32]
        last = cum[CHUNK - 1 :]
        weight = dt[here] * jnp.exp2(last - cum)
        wide = widen(
            jnp.concatenate([weight, jnp.broadcast_to(jnp.exp2(last), (16, 128))], 0), exp_ref[...]
        )
        xw = low(x[here].astype(F32) * wide[:CHUNK])
        state[...] = state[...] * wide[CHUNK : CHUNK + 1] + dot(bk[here], xw, TN)
        total[...] = total[...] + last

    @pl.when(b == blocks - 1)
    def _():
        st_ref[0, :STATE] = low(state[...])
        st_ref[0, STATE:] = total_rows(total[...], exp_ref[...])


def total_rows(total, expand):
    wide = widen(jnp.broadcast_to(total, (8, 128)), expand)
    high = wide.astype(BF16).astype(F32)
    return low(jnp.concatenate([high, wide - high], 0))


def mixer(pos, lens, hid, halo, gain, wz, wc, ws, cw, cb, sb, a, expand):
    seqs, span, width = hid.shape
    rows = min(256, span)
    blocks = span // rows
    conv_width = wc.shape[1]

    def row(n):
        return pl.BlockSpec((1, rows, n), lambda s, b, *_: (s, b, 0))

    def shape(n, kind):
        return jax.ShapeDtypeStruct((seqs, span, n), kind)

    return pl.pallas_call(
        functools.partial(mixer_body, rows=rows, blocks=blocks),
        grid_spec=pltpu.PrefetchScalarGridSpec(
            num_scalar_prefetch=2,
            grid=(seqs, blocks),
            in_specs=[row(width), pl.BlockSpec((1, 16, width), lambda s, b, *_: (s, 0, 0))]
            + [full_spec(v.shape) for v in (gain, wz, wc, ws, cw, cb, sb, a, expand)],
            out_specs=[
                row(WIDE), row(conv_width), row(conv_width), row(WIDE), row(STATE), row(STATE),
                row(128), row(128), row(128),
                pl.BlockSpec((1, 32, rows), lambda s, b, *_: (s, 0, b)),
                pl.BlockSpec((1, STATE + 16, WIDE), lambda s, b, *_: (s, 0, 0)),
            ],
            scratch_shapes=[
                pltpu.VMEM((8, conv_width), F32), pltpu.VMEM((STATE, WIDE), F32), pltpu.VMEM((1, 128), F32),
            ],
        ),
        out_shape=[
            shape(WIDE, BF16), shape(conv_width, BF16), shape(conv_width, BF16), shape(WIDE, BF16),
            shape(STATE, BF16), shape(STATE, BF16), shape(128, F32), shape(128, F32), shape(128, F32),
            jax.ShapeDtypeStruct((seqs, 32, span), F32),
            jax.ShapeDtypeStruct((seqs, STATE + 16, WIDE), BF16),
        ],
        compiler_params=params(),
        cost_estimate=cost(20),
        name="mixer",
    )(pos, lens, hid, halo, gain, wz, wc, ws, cw, cb, sb, a, expand)


def joined(place, ref):
    state = jnp.zeros((STATE, WIDE), F32)
    for i in range(ref.shape[0]):
        logs = ref[i, 0, STATE : STATE + 1].astype(F32) + ref[i, 0, STATE + 8 : STATE + 9].astype(F32)
        state = jnp.where(i < place, state * jnp.exp2(logs) + ref[i, 0, :STATE].astype(F32), state)
    return state


def joined_later(refs):
    state = jnp.zeros((STATE, WIDE), F32)
    for ref in reversed(refs):
        logs = ref[0, STATE : STATE + 1].astype(F32) + ref[0, STATE + 8 : STATE + 9].astype(F32)
        state = state * jnp.exp2(logs) + ref[0, :STATE].astype(F32)
    return state


def gathered_spec(states):
    return pl.BlockSpec((states.shape[0], 1) + states.shape[2:], lambda s, c: (0, s, 0, 0), pipeline_mode=pl.Buffered(1))


def scan_body(
    place_ref, x_ref, bk_ref, cq_ref, dt_ref, cum_ref, cumt_ref, skip_ref, z_ref, gain_ref, exp_ref, all_ref,
    mix_ref, low_ref, st_ref, state, y,
):
    c = pl.program_id(1)

    @pl.when(c == 0)
    def _():
        state[...] = joined(place_ref[0], all_ref)

    x = x_ref[0].astype(F32)
    bk, cq = bk_ref[0], cq_ref[0]
    cum = cum_ref[0]
    last = cum[CHUNK - 1 :]
    expand = exp_ref[...]
    xdt = x * widen(dt_ref[0], expand)
    ends = widen(
        jnp.concatenate([jnp.exp2(cum), jnp.exp2(last - cum), jnp.broadcast_to(jnp.exp2(last), (16, 128))], 0),
        expand,
    )
    inter = jnp.where(low_rows(CHUNK), dot(cq, bk, NT), 0.0)
    held = low(state[...])
    st_ref[0, 0] = held
    y[...] = dot(cq, held) * ends[:CHUNK] + skip_ref[...] * x
    state[...] = state[...] * ends[2 * CHUNK : 2 * CHUNK + 1] + dot(bk, low(xdt * ends[CHUNK : 2 * CHUNK]), TN)
    xdt = low(xdt)
    for p in range(SSM_HEADS // 2):
        parts = []
        for h in (2 * p, 2 * p + 1):
            differ = jnp.minimum(cum[:, h : h + 1] - cumt_ref[0, h : h + 1, :], 0.0)
            parts.append(low(inter * jnp.exp2(differ)))
        cols = slice(p * 128, p * 128 + 128)
        y[:, cols] += dot(jnp.concatenate(parts, 1), pair_rows(xdt[:, cols]))
    mixed = y[...]
    mix_ref[0] = mixed
    z = z_ref[0].astype(F32)
    v = mixed * (z * sigmoid(z))
    low_ref[0] = low(v * lax.rsqrt(jnp.mean(v * v, -1, keepdims=True) + EPS) * gain_ref[...])


def scan_forward(place, x, bk, cq, dt, cum, cumt, skip, z, gain, expand, states):
    seqs, span, _ = x.shape
    chunks = span // CHUNK

    def row(n):
        return pl.BlockSpec((1, CHUNK, n), lambda s, c: (s, c, 0))

    return pl.pallas_call(
        scan_body,
        grid=(seqs, chunks),
        in_specs=[
            SCALARS, row(WIDE), row(STATE), row(STATE), row(128), row(128),
            pl.BlockSpec((1, 32, CHUNK), lambda s, c: (s, 0, c)),
            full_spec(skip.shape), row(WIDE), full_spec(gain.shape), full_spec(expand.shape), gathered_spec(states),
        ],
        out_specs=[row(WIDE), row(WIDE), pl.BlockSpec((1, 1, STATE, WIDE), lambda s, c: (s, c, 0, 0))],
        out_shape=[
            jax.ShapeDtypeStruct((seqs, span, WIDE), F32),
            jax.ShapeDtypeStruct((seqs, span, WIDE), BF16),
            jax.ShapeDtypeStruct((seqs, chunks, STATE, WIDE), BF16),
        ],
        scratch_shapes=[pltpu.VMEM((STATE, WIDE), F32), pltpu.VMEM((CHUNK, WIDE), F32)],
        compiler_params=params(),
        cost_estimate=cost(16),
        name="scan_forward",
    )(place, x, bk, cq, dt, cum, cumt, skip, z, gain, expand, states)


def live_rows(pos_ref, len_ref, rows):
    at = pos_ref[0] + pl.program_id(1) * rows + lax.broadcasted_iota(jnp.int32, (rows, 1), 0)
    return jnp.where(at < len_ref[pl.program_id(0)], 1.0, 0.0)


def grad_act_body(pos_ref, len_ref, cot_ref, wd_ref, out_ref, *, rows):
    gffn = low(live_rows(pos_ref, len_ref, rows) * cot_ref[0].astype(F32))
    out_ref[0] = low(dot(gffn, wd_ref[...], NT))


def grad_act(pos, lens, cot, wd):
    seqs, span, width = cot.shape
    rows = min(256, span)
    ff = wd.shape[0]
    return pl.pallas_call(
        functools.partial(grad_act_body, rows=rows),
        grid_spec=pltpu.PrefetchScalarGridSpec(
            num_scalar_prefetch=2,
            grid=(seqs, span // rows),
            in_specs=[pl.BlockSpec((1, rows, width), lambda s, b, *_: (s, b, 0)), full_spec(wd.shape)],
            out_specs=pl.BlockSpec((1, rows, ff), lambda s, b, *_: (s, b, 0)),
        ),
        out_shape=jax.ShapeDtypeStruct((seqs, span, ff), BF16),
        compiler_params=params(),
        cost_estimate=cost(0),
        name="grad_act",
    )(pos, lens, cot, wd)


def middle_body(
    pos_ref, len_ref, near_ref, far_ref, mix_ref, tok_ref, cot_ref, gact_ref,
    wao_ref, wmo_ref, wg_ref, wu_ref, wd_ref, gain2_ref,
    out_ref, left_ref, mine_ref, yours_ref, gmid_ref, *, rows, blocks,
):
    b = pl.program_id(1)
    live = live_rows(pos_ref, len_ref, rows)
    attn = jnp.where(b < blocks // 2, near_ref[0], far_ref[0])
    width, ff = wd_ref.shape[1], wd_ref.shape[0]
    left_ref[0, :, width + ff :] = attn
    branch = dot(attn, wao_ref[...]) + dot(mix_ref[0], wmo_ref[...])
    after = tok_ref[0].astype(F32) + live * branch
    scale = lax.rsqrt(jnp.mean(after * after, -1, keepdims=True) + EPS)
    unit = after * scale
    gain = gain2_ref[...]
    h2 = low(unit * gain)
    left_ref[0, :, :width] = h2
    gate = dot(h2, wg_ref[...])
    up = dot(h2, wu_ref[...])
    sg = sigmoid(gate)
    silu = gate * sg
    act = low(silu * up)
    left_ref[0, :, width : width + ff] = act
    out_ref[0] = low(after + live * dot(act, wd_ref[...]))
    cot = cot_ref[0].astype(F32)
    gffn = low(live * cot)
    gact = gact_ref[0].astype(F32)
    gg = low(gact * up * (sg * (1.0 + gate * (1.0 - sg))))
    gu = low(gact * silu)
    gh2 = dot(gg, wg_ref[...], NT) + dot(gu, wu_ref[...], NT)
    g = gh2 * gain
    gmid = cot + scale * (g - unit * jnp.mean(g * unit, -1, keepdims=True))
    gmid_ref[0] = gmid
    halves_out(pos_ref[1], (gg, gu, gffn, low(live * gmid)), mine_ref, yours_ref)


def middle(pos, lens, near, far, mix, tokens, cot, gact, wao, wmo, wg, wu, wd, gain2):
    seqs, span, width = tokens.shape
    rows = min(256, span // 2)
    blocks = span // rows
    ff = wg.shape[1]
    lower = pl.BlockSpec((1, rows, 512), lambda s, b, *_: (s, jnp.minimum(b, blocks // 2 - 1), 0))
    upper = pl.BlockSpec((1, rows, 512), lambda s, b, *_: (s, jnp.maximum(b - blocks // 2, 0), 0))

    def row(n):
        return pl.BlockSpec((1, rows, n), lambda s, b, *_: (s, b, 0))

    def shape(n, kind):
        return jax.ShapeDtypeStruct((seqs, span, n), kind)

    return pl.pallas_call(
        functools.partial(middle_body, rows=rows, blocks=blocks),
        grid_spec=pltpu.PrefetchScalarGridSpec(
            num_scalar_prefetch=2,
            grid=(seqs, blocks),
            in_specs=[lower, upper, row(WIDE), row(width), row(width), row(ff)]
            + [full_spec(v.shape) for v in (wao, wmo, wg, wu, wd, gain2)],
            out_specs=[
                row(width), row(width + ff + 512), row(width + ff), row(width + ff), row(width),
            ],
        ),
        out_shape=[
            shape(width, BF16), shape(width + ff + 512, BF16), shape(width + ff, BF16), shape(width + ff, BF16),
            shape(width, F32),
        ],
        compiler_params=params(),
        cost_estimate=cost(45),
        name="middle",
    )(pos, lens, near, far, mix, tokens, cot, gact, wao, wmo, wg, wu, wd, gain2)


def branch_body(
    core_ref, gb_m, gb_y, mixed_ref, z_ref, cq_ref, cum_ref, wao_ref, wmo_ref, gated_ref, exp_ref,
    gnear_ref, gfar_ref, gmixed_ref, gz_m, gz_y, adj_ref, adj, offset, *, rows, blocks,
):
    b = pl.program_id(1)

    @pl.when(b == 0)
    def _():
        adj[...] = jnp.zeros_like(adj)
        offset[...] = jnp.zeros_like(offset)

    core = core_ref[0]
    gb = halves_in(core, gb_m[0], gb_y[0])
    gattn = low(dot(gb, wao_ref[...], NT))

    @pl.when(b < blocks // 2)
    def _():
        gnear_ref[0] = gattn

    @pl.when(b >= blocks // 2)
    def _():
        gfar_ref[0] = gattn

    gn = low(dot(gb, wmo_ref[...], NT)).astype(F32)
    mixed = mixed_ref[0]
    z = z_ref[0].astype(F32)
    sg = sigmoid(z)
    silu = z * sg
    v = mixed * silu
    scale = lax.rsqrt(jnp.mean(v * v, -1, keepdims=True) + EPS)
    unit = v * scale
    g = gn * gated_ref[...]
    g = scale * (g - unit * jnp.mean(g * unit, -1, keepdims=True))
    gmixed = g * silu
    gmixed_ref[0] = low(gmixed)
    halves_out(core, (low(g * mixed * (sg * (1.0 + z * (1.0 - sg)))),), gz_m, gz_y)
    cum = cum_ref[0]
    logs = []
    for c in range(rows // CHUNK):
        here = cum[c * CHUNK : (c + 1) * CHUNK]
        logs.append(here + offset[...])
        offset[...] += here[CHUNK - 1 :]
    wide = widen(jnp.exp2(jnp.concatenate(logs, 0)), exp_ref[...])
    adj[...] += dot(cq_ref[0], low(gmixed * wide), TN)

    @pl.when(b == blocks - 1)
    def _():
        adj_ref[0, :STATE] = low(adj[...])
        adj_ref[0, STATE:] = total_rows(offset[...], exp_ref[...])


def branch_back(core, mine, yours, mixed, z, cq, cum, wao, wmo, gated, expand):
    seqs, span, packed = mine.shape
    half_width = wao.shape[1] // 2
    gb = pl.BlockSpec((1, min(256, span // 2), half_width), lambda s, b: (s, b, packed // half_width - 1))
    rows = min(256, span // 2)
    blocks = span // rows
    lower = pl.BlockSpec((1, rows, 512), lambda s, b: (s, jnp.minimum(b, blocks // 2 - 1), 0))
    upper = pl.BlockSpec((1, rows, 512), lambda s, b: (s, jnp.maximum(b - blocks // 2, 0), 0))

    def row(n):
        return pl.BlockSpec((1, rows, n), lambda s, b: (s, b, 0))

    def shape(n, kind):
        return jax.ShapeDtypeStruct((seqs, span, n), kind)

    half = jax.ShapeDtypeStruct((seqs, span // 2, 512), BF16)
    return pl.pallas_call(
        functools.partial(branch_body, rows=rows, blocks=blocks),
        grid=(seqs, blocks),
        in_specs=[SCALARS, gb, gb, row(WIDE), row(WIDE), row(STATE), row(128)]
        + [full_spec(v.shape) for v in (wao, wmo, gated, expand)],
        out_specs=[
            lower, upper, row(WIDE), row(WIDE // 2), row(WIDE // 2),
            pl.BlockSpec((1, STATE + 16, WIDE), lambda s, b: (s, 0, 0)),
        ],
        out_shape=[
            half, half, shape(WIDE, BF16), shape(WIDE // 2, BF16), shape(WIDE // 2, BF16),
            jax.ShapeDtypeStruct((seqs, STATE + 16, WIDE), BF16),
        ],
        scratch_shapes=[pltpu.VMEM((STATE, WIDE), F32), pltpu.VMEM((1, 128), F32)],
        compiler_params=params(),
        cost_estimate=cost(6),
        name="branch_back",
    )(core, mine, yours, mixed, z, cq, cum, wao, wmo, gated, expand)


def scan_back_body(
    x_ref, bk_ref, cq_ref, dt_ref, sg_ref, cum_ref, cumt_ref, dy_ref, mix_ref, st_ref, pre_ref, cl_ref,
    skip_ref, a_ref, cw_ref, exp_ref, core_ref, *rest, chunks, conv_width,
):
    *later, gc_m, gc_y, tail_ref, head_ref, gw_ref, gskip_ref, small_ref, adj, after, gact = rest
    s = pl.program_id(0)
    c = pl.program_id(1)

    @pl.when((s == 0) & (c == 0))
    def _():
        gw_ref[...] = jnp.zeros_like(gw_ref)
        gskip_ref[...] = jnp.zeros_like(gskip_ref)
        small_ref[...] = jnp.zeros_like(small_ref)

    @pl.when(c == 0)
    def _():
        adj[...] = joined_later(later)
        after[...] = jnp.zeros_like(after)

    x = x_ref[0].astype(F32)
    bk, cq = bk_ref[0], cq_ref[0]
    dt = dt_ref[0]
    cum = cum_ref[0]
    last = cum[CHUNK - 1 :]
    expand = exp_ref[...]
    dt_wide = widen(dt, expand)
    ends = widen(
        jnp.concatenate([jnp.exp2(cum), jnp.exp2(last - cum), jnp.broadcast_to(jnp.exp2(last), (16, 128))], 0),
        expand,
    )
    to_end = ends[CHUNK : 2 * CHUNK]
    all_wide = ends[2 * CHUNK : 2 * CHUNK + 1]
    xdt = x * dt_wide
    dy_low = dy_ref[0]
    dy = dy_low.astype(F32)
    dy_in = low(dy * ends[:CHUNK])
    state = st_ref[0, 0]
    gstate = adj[...]
    gstate_low = low(gstate)
    from_end = dot(bk, gstate_low) * to_end
    gb = dot(low(xdt * to_end), gstate_low, NT)
    gc = dot(dy_in, state, NT)
    gfinal = all_wide * jnp.sum(gstate * state.astype(F32), 0, keepdims=True) + jnp.sum(
        xdt * from_end, 0, keepdims=True
    )
    adj[...] = gstate * all_wide + dot(cq, dy_in, TN)
    xdt_low = low(xdt)
    u = lax.broadcasted_iota(jnp.int32, (CHUNK, CHUNK), 0)
    t = lax.broadcasted_iota(jnp.int32, (CHUNK, CHUNK), 1)
    inter = jnp.where(t >= u, dot(bk, cq, NT), 0.0)
    ginter = jnp.zeros((CHUNK, CHUNK), F32)
    for p in range(SSM_HEADS // 2):
        cols = slice(p * 128, p * 128 + 128)
        dy_rows = pair_rows(dy_low[:, cols])
        gmix = dot(xdt_low[:, cols], dy_rows, NT)
        parts = []
        for n, h in enumerate((2 * p, 2 * p + 1)):
            decay = jnp.exp2(jnp.minimum(cumt_ref[0, h : h + 1, :] - cum[:, h : h + 1], 0.0))
            parts.append(low(inter * decay))
            ginter = ginter + gmix[:, n * CHUNK : (n + 1) * CHUNK] * decay
        gact[:, cols] = dot(jnp.concatenate(parts, 1), dy_rows)
    ginter = low(jnp.where(t >= u, ginter, 0.0))
    gact[:, WIDE : WIDE + STATE] = gb + dot(ginter, cq)
    gact[:, WIDE + STATE :] = gc + dot(ginter, bk, TN)
    gxdt = gact[:, :WIDE] + from_end
    skip = skip_ref[...]
    gact[:, :WIDE] = dt_wide * gxdt + skip * dy
    gskip_ref[...] += jnp.sum(dy * x, 0, keepdims=True)
    sums = head_sums(
        jnp.concatenate([x * gxdt, dy * (mix_ref[0] - skip * x), jnp.broadcast_to(gfinal, (16, WIDE))], 0), expand
    )
    direct = sums[:CHUNK]
    gcum = sums[CHUNK : 2 * CHUNK] - dt * direct
    gld = dot_exact(jnp.where(t >= u, 1.0, 0.0), gcum) + sums[2 * CHUNK : 2 * CHUNK + 1]
    a = a_ref[...]
    gstep = (direct + a * gld) * sg_ref[0]
    small_ref[0:1] += jnp.sum(dt * gld, 0, keepdims=True) * a
    small_ref[1:2] += jnp.sum(gstep, 0, keepdims=True)
    pre = pre_ref[0].astype(F32)
    sg = sigmoid(pre)
    gpre = gact[...] * (sg * (1.0 + pre * (1.0 - sg)))
    ext = jnp.concatenate([gpre, after[...]], 0)
    after[...] = gpre[:8]
    conv = cl_ref[0].astype(F32)
    gconv = cw_ref[3:4] * gpre
    gw_ref[3:4] += jnp.sum(conv * gpre, 0, keepdims=True)
    gw_ref[4:5] += jnp.sum(gpre, 0, keepdims=True)
    for ahead in range(1, 4):
        moved = pltpu.roll(ext, CHUNK + 8 - ahead, 0)[:CHUNK]
        gconv = gconv + cw_ref[3 - ahead : 4 - ahead] * moved
        gw_ref[3 - ahead : 4 - ahead] += jnp.sum(conv * moved, 0, keepdims=True)
    everything = jnp.concatenate([low(gconv), low(gstep), jnp.zeros((CHUNK, 128), BF16)], 1)
    halves_out(core_ref[0], (everything,), gc_m, gc_y)

    @pl.when(c == 0)
    def _():
        tail_ref[0, :, :conv_width] = gconv[CHUNK - 8 :]
        tail_ref[0, :, conv_width : conv_width + 128] = gstep[CHUNK - 8 :]
        tail_ref[0, :, conv_width + 128 :] = jnp.zeros((8, 128), F32)

    @pl.when(c == chunks - 1)
    def _():
        head_ref[0] = gpre[:8]


def scan_backward(x, bk, cq, dt, sg, cum, cumt, dy, mixed, states, pre, conv, skip, a, cw, expand, core, adjoints):
    seqs, span, _ = x.shape
    chunks = span // CHUNK
    conv_width = pre.shape[2]

    def row(n):
        return pl.BlockSpec((1, CHUNK, n), lambda s, c: (s, chunks - 1 - c, 0))

    def once(m, n):
        return pl.BlockSpec((m, n), lambda s, c: (0, 0))

    edge = pl.BlockSpec((1, 8, conv_width), lambda s, c: (s, 0, 0))
    return pl.pallas_call(
        functools.partial(scan_back_body, chunks=chunks, conv_width=conv_width),
        grid=(seqs, chunks),
        in_specs=[
            row(WIDE), row(STATE), row(STATE), row(128), row(128), row(128),
            pl.BlockSpec((1, 32, CHUNK), lambda s, c: (s, 0, chunks - 1 - c)),
            row(WIDE), row(WIDE),
            pl.BlockSpec((1, 1, STATE, WIDE), lambda s, c: (s, chunks - 1 - c, 0, 0)),
            row(conv_width), row(conv_width),
            full_spec(skip.shape), full_spec(a.shape), full_spec(cw.shape), full_spec(expand.shape), SCALARS,
        ]
        + [
            pl.BlockSpec((1, STATE + 16, WIDE), lambda s, c: (s, 0, 0), pipeline_mode=pl.Buffered(1))
            for _ in adjoints
        ],
        out_specs=[
            row((conv_width + 256) // 2), row((conv_width + 256) // 2),
            pl.BlockSpec((1, 8, conv_width + 256), lambda s, c: (s, 0, 0)), edge, once(8, conv_width), once(1, WIDE), once(8, 128),
        ],
        out_shape=[
            jax.ShapeDtypeStruct((seqs, span, (conv_width + 256) // 2), BF16),
            jax.ShapeDtypeStruct((seqs, span, (conv_width + 256) // 2), BF16),
            jax.ShapeDtypeStruct((seqs, 8, conv_width + 256), F32),
            jax.ShapeDtypeStruct((seqs, 8, conv_width), F32),
            jax.ShapeDtypeStruct((8, conv_width), F32),
            jax.ShapeDtypeStruct((1, WIDE), F32),
            jax.ShapeDtypeStruct((8, 128), F32),
        ],
        scratch_shapes=[
            pltpu.VMEM((STATE, WIDE), F32), pltpu.VMEM((8, conv_width), F32), pltpu.VMEM((CHUNK, conv_width), F32),
        ],
        compiler_params=params(),
        cost_estimate=cost(4),
        name="scan_backward",
    )(x, bk, cq, dt, sg, cum, cumt, dy, mixed, states, pre, conv, skip, a, cw, expand, core, *adjoints)


def leave_mixer_body(core_ref, gz_m, gz_y, gc_m, gc_y, wz_ref, wc_ref, ws_ref, gh_ref, *, conv_width):
    core = core_ref[0]
    gz = halves_in(core, gz_m[0], gz_y[0])
    gc = halves_in(core, gc_m[0], gc_y[0])
    gh = dot(gz, wz_ref[...], NT) + dot(gc[:, :conv_width], wc_ref[...], NT)
    gh_ref[0] = gh + dot(gc[:, conv_width : conv_width + 128], ws_ref[...], NT)


def leave_mixer(core, gz, gc, wz, wc, ws):
    seqs, span, _ = gz[0].shape
    rows = min(256, span)

    def row(n):
        return pl.BlockSpec((1, rows, n), lambda s, b: (s, b, 0))

    width = wz.shape[0]
    return pl.pallas_call(
        functools.partial(leave_mixer_body, conv_width=wc.shape[1]),
        grid=(seqs, span // rows),
        in_specs=[SCALARS]
        + [row(v.shape[2]) for v in (*gz, *gc)]
        + [full_spec(v.shape) for v in (wz, wc, ws)],
        out_specs=row(width),
        out_shape=jax.ShapeDtypeStruct((seqs, span, width), F32),
        compiler_params=params(),
        cost_estimate=cost(0),
        name="leave_mixer",
    )(core, *gz, *gc, wz, wc, ws)


def heads_body(core_ref, place_ref, cos_ref, sin_ref, cos0_ref, sin0_ref, *rest, blocks, count):
    near, far = rest[:2], rest[2:4]
    pieces = rest[4 : 4 + 2 * count]
    gq_m, gq_y, gkv_m, gkv_y = rest[4 + 2 * count :]
    core = core_ref[0]
    b = pl.program_id(1)
    halves_out(core, (jnp.concatenate([jnp.where(b < blocks // 2, near[j][0], far[j][0]) for j in range(2)], 1),), gq_m, gq_y)
    sums = []
    for j in range(2):
        t = pieces[j * count][0].astype(F32)
        for r in range(1, count):
            t = t + pieces[j * count + r][0].astype(F32)
        sums.append(t)
    lane = lax.broadcasted_iota(jnp.int32, sums[0].shape, 1)
    gk = jnp.where(lane < 64, sums[0], pltpu.roll(sums[1], 64, 1))
    gv = low(jnp.where(lane < 64, pltpu.roll(sums[0], 64, 1), sums[1]))
    place = place_ref[0]
    cosine, sine = turned(cos_ref[...], sin_ref[...], cos0_ref[place], sin0_ref[place])
    gk = low(gk * cosine - swap_halves(gk) * sine)
    halves_out(core, (jnp.concatenate([gk, gv], 1),), gkv_m, gkv_y)


def heads_back(core, place, tables, near, far, pieces):
    seqs, half, _ = near[0].shape
    span = 2 * half
    rows = min(256, half)
    blocks = span // rows
    table = pl.BlockSpec((rows, 128), lambda s, b: (b, 0))
    lower = pl.BlockSpec((1, rows, 256), lambda s, b: (s, jnp.minimum(b, blocks // 2 - 1), 0))
    upper = pl.BlockSpec((1, rows, 256), lambda s, b: (s, jnp.maximum(b - blocks // 2, 0), 0))

    def row(n):
        return pl.BlockSpec((1, rows, n), lambda s, b: (s, b, 0))

    return pl.pallas_call(
        functools.partial(heads_body, blocks=blocks, count=len(pieces) // 2),
        grid=(seqs, blocks),
        in_specs=[SCALARS, SCALARS, table, table]
        + [full_spec(v.shape) for v in tables[2:]]
        + [lower, lower, upper, upper] + [row(128)] * len(pieces),
        out_specs=[row(256), row(256), row(128), row(128)],
        out_shape=[jax.ShapeDtypeStruct((seqs, span, n), BF16) for n in (256, 256, 128, 128)],
        compiler_params=params(),
        cost_estimate=cost(0),
        name="heads_back",
    )(core, place, *tables, *near, *far, *pieces)


def leave_body(
    core_ref, tok_ref, gmid_ref, gh_ref, gq_m, gq_y, gkv_m, gkv_y, gain_ref, wq_ref, wk_ref, wv_ref, gt_ref
):
    core = core_ref[0]
    gh = gh_ref[0] + dot(halves_in(core, gq_m[0], gq_y[0]), wq_ref[...], NT)
    gkv = halves_in(core, gkv_m[0], gkv_y[0])
    gh = gh + dot(gkv[:, :128], wk_ref[...], NT) + dot(gkv[:, 128:], wv_ref[...], NT)
    v = tok_ref[0].astype(F32)
    scale = lax.rsqrt(jnp.mean(v * v, -1, keepdims=True) + EPS)
    unit = v * scale
    g = gh * gain_ref[...]
    gt_ref[0] = gmid_ref[0] + scale * (g - unit * jnp.mean(g * unit, -1, keepdims=True))


def leave(core, tokens, gmid, gh, heads, gain, wq, wk, wv):
    seqs, span, width = tokens.shape
    rows = min(256, span)

    def row(n):
        return pl.BlockSpec((1, rows, n), lambda s, b: (s, b, 0))

    return pl.pallas_call(
        leave_body,
        grid=(seqs, span // rows),
        in_specs=[SCALARS] + [row(width)] * 3 + [row(v.shape[2]) for v in heads] + [full_spec(v.shape) for v in (gain, wq, wk, wv)],
        out_specs=row(width),
        out_shape=jax.ShapeDtypeStruct((seqs, span, width), F32),
        compiler_params=params(),
        cost_estimate=cost(0),
        name="leave",
    )(core, tokens, gmid, gh, *heads, gain, wq, wk, wv)


def dup_halves(v):
    lane = lax.broadcasted_iota(jnp.int32, v.shape, 1)
    other = pltpu.roll(v, 64, 1)
    return low(jnp.where(lane < 64, v, other)), low(jnp.where(lane < 64, other, v))


def head_rows(v):
    lane = lax.broadcasted_iota(jnp.int32, (v.shape[0], 128), 1)
    heads = []
    for h in range(v.shape[1] // HEAD):
        t = v[:, (h // 2) * 128 : (h // 2) * 128 + 128]
        heads.append(jnp.where((lane < 64) if h % 2 == 0 else (lane >= 64), t, jnp.zeros_like(t)))
    return heads


def key_range(first, length, rows, keys):
    whole = jnp.minimum((first + 1) // keys, length // keys)
    some = jnp.minimum((first + rows + keys - 1) // keys, (length + keys - 1) // keys)
    return whole, some


def seen(i, first, length, rows, keys):
    key_at = i * keys + lax.broadcasted_iota(jnp.int32, (keys, rows), 0)
    query_at = first + lax.broadcasted_iota(jnp.int32, (keys, rows), 1)
    return (key_at <= query_at) & (key_at < length)


def attend_body(
    pos_ref, len_ref, from_ref, q_ref, other_ref, *rest, rows, keys, blocks, count, span,
):
    kv_refs = rest[:count]
    near_ref, far_ref, lse_ref, kd, vt, top, acc, score_a, score_b, top_a, top_b = rest[count:]
    s = pl.program_id(0)
    b = pl.program_id(1)
    prep = min(512, span)

    @pl.when(b == 0)
    def _():
        ones = jnp.ones((16, prep), F32)
        for r, kv_ref in enumerate(kv_refs):
            for i in range(span // prep):
                here = slice(i * prep, (i + 1) * prep)
                at = pl.ds(pl.multiple_of(from_ref[r] * span + i * prep, prep), prep)
                kd[0, at, :], kd[1, at, :] = dup_halves(kv_ref[0, here, :128].astype(F32))
                t = kv_ref[0, here, 128:].astype(F32).T
                vt[0, :, at] = low(jnp.concatenate([t[:64], ones], 0))
                vt[1, :, at] = low(jnp.concatenate([t[64:], ones], 0))

    first = pos_ref[b]
    length = len_ref[s]
    heads = head_rows(jnp.where(b < blocks // 2, q_ref[0], other_ref[0]))
    top[...] = jnp.full_like(top, LOWEST)
    acc[...] = jnp.zeros_like(acc)
    whole, some = key_range(first, length, rows, keys)

    def scores(i, buffer, tops, h, mask=None):
        at = pl.ds(pl.multiple_of(i * keys, keys), keys)
        t = dot(kd[h // 4, at, :], heads[h], NT)
        if mask is not None:
            t = jnp.where(mask, t, LOWEST)
        buffer[h] = t
        tops[h] = jnp.max(t, 0, keepdims=True)

    def add(i, buffer, tops, h):
        at = pl.ds(pl.multiple_of(i * keys, keys), keys)
        before = top[h]
        now = jnp.maximum(before, tops[h])
        p = low(jnp.exp2((buffer[h] - now) * SCORE2))
        acc[h] = acc[h] * jnp.exp2((before - now) * SCORE2) + dot(vt[h // 4, :, at], p)
        top[h] = now

    def edge(i, _):
        mask = seen(i, first, length, rows, keys)
        for h in range(HEADS):
            scores(i, score_a, top_a, h, mask)
        for h in range(HEADS):
            add(i, score_a, top_a, h)
        return 0

    lax.fori_loop(whole, some, edge, 0)
    last = jnp.maximum(whole - 1, 0)
    for h in range(HEADS):
        scores(0, score_a, top_a, h)

    def two(i, _):
        for h in range(HEADS):
            scores(2 * i + 1, score_b, top_b, h)
            add(2 * i, score_a, top_a, h)
        following = jnp.minimum(2 * i + 2, last)
        for h in range(HEADS):
            scores(following, score_a, top_a, h)
            add(2 * i + 1, score_b, top_b, h)
        return 0

    lax.fori_loop(0, whole // 2, two, 0)

    @pl.when(whole % 2 == 1)
    def _():
        for h in range(HEADS):
            add(last, score_a, top_a, h)

    outs = []
    for h in range(HEADS):
        t = acc[h]
        weight = t[64:65]
        outs.append(t[:64] / weight)
        lse_ref[0, h : h + 1, :] = top[h] * SCORE2 + jnp.log2(weight)
    result = low(jnp.concatenate(outs, 0).T)

    @pl.when(b < blocks // 2)
    def _():
        near_ref[0] = result

    @pl.when(b >= blocks // 2)
    def _():
        far_ref[0] = result


def halves_specs(rows, blocks, columns):
    lower = pl.BlockSpec((1, rows, columns), lambda s, b, *_: (s, jnp.minimum(b, blocks // 2 - 1), 0))
    upper = pl.BlockSpec((1, rows, columns), lambda s, b, *_: (s, jnp.maximum(b - blocks // 2, 0), 0))
    return lower, upper


def attend(pos, lens, sources, q, other, kvs):
    seqs, span, _ = q.shape
    count = len(kvs)
    total = count * span
    rows = min(256, span // 2)
    keys = 256
    blocks = span // rows
    lower, upper = halves_specs(rows, blocks, 512)
    half = jax.ShapeDtypeStruct((seqs, span // 2, 512), BF16)
    return pl.pallas_call(
        functools.partial(attend_body, rows=rows, keys=keys, blocks=blocks, count=count, span=span),
        grid_spec=pltpu.PrefetchScalarGridSpec(
            num_scalar_prefetch=3,
            grid=(seqs, blocks),
            in_specs=[lower, upper]
            + [pl.BlockSpec((1, span, 256), lambda s, b, *_: (s, 0, 0), pipeline_mode=pl.Buffered(1))] * count,
            out_specs=[lower, upper, pl.BlockSpec((1, 8, rows), lambda s, b, *_: (s, 0, b))],
            scratch_shapes=[
                pltpu.VMEM((2, total, 128), BF16), pltpu.VMEM((2, 80, total), BF16),
                pltpu.VMEM((8, 1, rows), F32), pltpu.VMEM((8, 80, rows), F32),
                pltpu.VMEM((8, keys, rows), F32), pltpu.VMEM((8, keys, rows), F32),
                pltpu.VMEM((8, 1, rows), F32), pltpu.VMEM((8, 1, rows), F32),
            ],
        ),
        out_shape=[half, half, jax.ShapeDtypeStruct((seqs, 8, span), F32)],
        compiler_params=params(),
        cost_estimate=cost(26),
        name="attend",
    )(pos, lens, sources, q, other, *kvs)


def attend_back_body(
    pos_ref, len_ref, from_ref, q_ref, other_ref, do_near_ref, do_far_ref, o_near_ref, o_far_ref, lse_ref,
    cos_ref, sin_ref, cos0_ref, sin0_ref, *rest, rows, keys, blocks, count, span, group,
):
    kv_refs = rest[:count]
    dq_near_ref, dq_far_ref = rest[count : count + 2]
    dkv_refs = rest[count + 2 : 2 * count + 2]
    kd, vd, kt, dk, dv, dq, score_a, grad_a, score_b, grad_b = rest[2 * count + 2 :]
    s = pl.program_id(0)
    b = pl.program_id(1)
    prep = min(512, span)

    @pl.when(b == 0)
    def _():
        for r, kv_ref in enumerate(kv_refs):
            for i in range(span // prep):
                here = slice(i * prep, (i + 1) * prep)
                at = pl.ds(pl.multiple_of(from_ref[r] * span + i * prep, prep), prep)
                k = kv_ref[0, here, :128].astype(F32)
                kd[at, :] = dup_halves(k)[group]
                vd[at, :] = dup_halves(kv_ref[0, here, 128:].astype(F32))[group]
                kt[:, at] = low(k.T[64 * group : 64 * group + 64])
        dk[...] = jnp.zeros_like(dk)
        dv[...] = jnp.zeros_like(dv)

    first = pos_ref[b]
    length = len_ref[s]
    is_near = b < blocks // 2
    heads = head_rows(jnp.where(is_near, q_ref[0], other_ref[0]))
    do = jnp.where(is_near, do_near_ref[0], do_far_ref[0])
    grads = head_rows(do)
    prod = do.astype(F32) * jnp.where(is_near, o_near_ref[0], o_far_ref[0]).astype(F32)
    col = lax.broadcasted_iota(jnp.int32, (8, 256), 1) // HEAD
    ones = low(jnp.where(col == lax.broadcasted_iota(jnp.int32, (8, 256), 0), 1.0, 0.0))
    high, remain = split_low(prod)
    delta = dot(ones, high, NT) + dot(ones, remain, NT)
    dq[...] = jnp.zeros_like(dq)
    whole, some = key_range(first, length, rows, keys)

    def scores(i, buffers, h):
        at = pl.ds(pl.multiple_of(i * keys, keys), keys)
        buffers[0][h] = dot(kd[at, :], heads[h], NT)
        buffers[1][h] = dot(vd[at, :], grads[h], NT)

    def add(i, buffers, h, sums, mask=None):
        at = pl.ds(pl.multiple_of(i * keys, keys), keys)
        x = buffers[0][h] * SCORE2 - lse_ref[0, 4 * group + h : 4 * group + h + 1, :]
        if mask is not None:
            x = jnp.where(mask, x, LOWEST)
        p = jnp.exp2(x)
        ds = low(p * (buffers[1][h] - delta[h : h + 1]))
        parts = dot(low(p), grads[h]), dot(ds, heads[h])
        dq[h] += dot(kt[:, at], ds)
        sums = parts if sums is None else (sums[0] + parts[0], sums[1] + parts[1])
        if h == 3:
            dv[at, :] += sums[0]
            dk[at, :] += sums[1]
        return sums

    early, late = (score_a, grad_a), (score_b, grad_b)

    def edge(i, _):
        mask = seen(i, first, length, rows, keys)
        for h in range(4):
            scores(i, early, h)
        sums = None
        for h in range(4):
            sums = add(i, early, h, sums, mask)
        return 0

    lax.fori_loop(whole, some, edge, 0)
    last = jnp.maximum(whole - 1, 0)
    for h in range(4):
        scores(0, early, h)

    def two(i, _):
        sums = None
        for h in range(4):
            scores(2 * i + 1, late, h)
            sums = add(2 * i, early, h, sums)
        following = jnp.minimum(2 * i + 2, last)
        sums = None
        for h in range(4):
            scores(following, early, h)
            sums = add(2 * i + 1, late, h, sums)
        return 0

    lax.fori_loop(0, whole // 2, two, 0)

    @pl.when(whole % 2 == 1)
    def _():
        sums = None
        for h in range(4):
            sums = add(last, early, h, sums)

    owner = jnp.where(is_near, from_ref[0], count - 1 - from_ref[0])
    cosine, sine = turned(cos_ref[...], sin_ref[...], cos0_ref[owner][:, :1], sin0_ref[owner][:, :1])
    parts = []
    for h in range(4):
        t = dq[h] * 0.125
        former, latter = t[:32], t[32:]
        parts += [former * cosine + latter * sine, latter * cosine - former * sine]
    result = low(jnp.concatenate(parts, 0).T)

    @pl.when(is_near)
    def _():
        dq_near_ref[0] = result

    @pl.when(jnp.logical_not(is_near))
    def _():
        dq_far_ref[0] = result

    @pl.when(b == blocks - 1)
    def _():
        lane = lax.broadcasted_iota(jnp.int32, (prep, 128), 1)
        for r, dkv_ref in enumerate(dkv_refs):
            for i in range(span // prep):
                at = pl.ds(pl.multiple_of(from_ref[r] * span + i * prep, prep), prep)
                k, v = dk[at, :], dv[at, :]
                k = (k + pltpu.roll(k, 64, 1)) * 0.125
                v = v + pltpu.roll(v, 64, 1)
                dkv_ref[0, i * prep : (i + 1) * prep] = low(jnp.where(lane < 64, k, v))


def attend_backward(group, pos, lens, sources, q, other, do_near, do_far, o_near, o_far, lse, tables, kvs):
    seqs, span, _ = q.shape
    count = len(kvs)
    total = count * span
    rows = min(256, span // 2)
    keys = 256
    blocks = span // rows
    lower = pl.BlockSpec((1, rows, 256), lambda s, b, *_: (s, jnp.minimum(b, blocks // 2 - 1), group))
    upper = pl.BlockSpec((1, rows, 256), lambda s, b, *_: (s, jnp.maximum(b - blocks // 2, 0), group))
    out_lower, out_upper = halves_specs(rows, blocks, 256)
    stat = pl.BlockSpec((1, 8, rows), lambda s, b, *_: (s, 0, b))
    table = pl.BlockSpec((32, rows), lambda s, b, *_: (0, b))
    half = jax.ShapeDtypeStruct((seqs, span // 2, 256), BF16)
    outs = pl.pallas_call(
        functools.partial(
            attend_back_body, rows=rows, keys=keys, blocks=blocks, count=count, span=span, group=group
        ),
        grid_spec=pltpu.PrefetchScalarGridSpec(
            num_scalar_prefetch=3,
            grid=(seqs, blocks),
            in_specs=[lower, upper, lower, upper, lower, upper, stat, table, table]
            + [full_spec(v.shape) for v in tables[2:]]
            + [pl.BlockSpec((1, span, 256), lambda s, b, *_: (s, 0, 0), pipeline_mode=pl.Buffered(1))] * count,
            out_specs=[out_lower, out_upper]
            + [pl.BlockSpec((1, span, 128), lambda s, b, *_: (s, 0, 0))] * count,
            scratch_shapes=[
                pltpu.VMEM((total, 128), BF16), pltpu.VMEM((total, 128), BF16), pltpu.VMEM((64, total), BF16),
                pltpu.VMEM((total, 128), F32), pltpu.VMEM((total, 128), F32), pltpu.VMEM((4, 64, rows), F32),
            ]
            + [pltpu.VMEM((4, keys, rows), F32)] * 4,
        ),
        out_shape=[half, half] + [jax.ShapeDtypeStruct((seqs, span, 128), BF16)] * count,
        compiler_params=params(),
        cost_estimate=cost(1 if group else 20),
        name="attend_backward",
    )(pos, lens, sources, q, other, do_near, do_far, o_near, o_far, lse, *tables, *kvs)
    return outs[0], outs[1], outs[2:]


def in_hbm(shape):
    return pltpu.HBM(shape, BF16)


def both(left, right):
    return dot(left[0][...], right[0][...], TN) + dot(left[1][...], right[1][...], TN)


def tall_body(place_ref, left_a, left_b, *rest, n, widths, square):
    rights = [rest[2 * k : 2 * k + 2] for k in range(len(widths))]
    outs = rest[2 * len(widths) :]
    rows = left_a.shape[1] // n
    i = pl.program_id(0)
    start = 0
    for part, (right, steps) in enumerate(zip(rights, widths)):

        @pl.when((i >= start) & (i < start + steps))
        def _(part=part, right=right):
            if square:
                if square == "hops":
                    own, to_x, keep_x, to_y, keep_y = outs
                    first, keep = ((to_x, keep_x), (to_y, keep_y))[part]
                for k in range(4):
                    block = jnp.bitwise_xor(place_ref[0], k)
                    columns = pl.ds(pl.multiple_of(block * rows, rows), rows)
                    value = low(both((left_a.at[:, columns], left_b.at[:, columns]), right))
                    if square == "direct":
                        outs[k][...] = value
                    elif k == 0:
                        own[...] = value
                    elif k == 3:
                        first[1] = value
                    elif k == part + 1:
                        first[0] = value
                    else:
                        keep[...] = value
            else:
                value = low(both((left_a, left_b), right))
                for j in range(n):
                    outs[0][j] = value[j * rows : (j + 1) * rows]

        start += steps


def tall_grad(place, left, rights, chunk, n, square="", micros=0.0, name="grad"):
    tokens, width = left[0].shape[0], left[3]
    widths = [v[3] // chunk for v in rights]
    steps = sum(widths)
    rows = width // n
    starts = [0, widths[0]]
    parts = range(len(rights))

    def within(k, i):
        return jnp.clip(i - starts[k], 0, widths[k] - 1)

    def right_spec(k):
        return pl.BlockSpec((tokens, chunk), lambda i, place: (0, rights[k][2] // chunk + within(k, i)))

    left_spec = pl.BlockSpec(
        (tokens, width), lambda i, place: (0, left[2] // width), pipeline_mode=pl.Buffered(1)
    )

    if square == "direct":
        out_specs = [pl.BlockSpec((rows, chunk), lambda i, place: (i, 0))] * 4
        out_shape = [in_hbm((steps * rows, chunk))] * 4
    elif square:
        out_specs = [pl.BlockSpec((rows, chunk), lambda i, place: (i, 0))]
        out_shape = [jax.ShapeDtypeStruct((steps * rows, chunk), BF16)]
        for k in parts:
            out_specs.append(pl.BlockSpec((2, rows, chunk), lambda i, place, k=k: (0, within(k, i), 0)))
            out_specs.append(pl.BlockSpec((rows, chunk), lambda i, place, k=k: (within(k, i), 0)))
            out_shape.append(in_hbm((2, widths[k] * rows, chunk)))
            out_shape.append(jax.ShapeDtypeStruct((widths[k] * rows, chunk), BF16))
    else:
        out_specs = pl.BlockSpec((n, rows, chunk), lambda i, place: (0, i, 0))
        out_shape = jax.ShapeDtypeStruct((n, steps * rows, chunk), BF16)
    return pl.pallas_call(
        functools.partial(tall_body, n=n, widths=widths, square=square),
        grid_spec=pltpu.PrefetchScalarGridSpec(
            num_scalar_prefetch=1,
            grid=(steps,),
            in_specs=[left_spec] * 2 + [right_spec(k) for k in parts for _ in range(2)],
            out_specs=out_specs,
        ),
        out_shape=out_shape,
        compiler_params=pltpu.CompilerParams(vmem_limit_bytes=VMEM_LIMIT),
        cost_estimate=cost(micros),
        name=name,
    )(place, *left[:2], *[v for right in rights for v in right[:2]])


PIECE = 256


def wide_body(place_ref, *rest, parts, group, square, split):
    lefts = [rest[2 * k : 2 * k + 2] for k in range(parts)]
    rights = [rest[2 * k : 2 * k + 2] for k in range(parts, 2 * parts)]
    outs = rest[4 * parts :]
    values = [low(both(left, right)) for left, right in zip(lefts, rights)]
    values = [v[:, c : c + PIECE] for v in values for c in range(0, v.shape[1], PIECE)]
    if square:
        own, to_x, keep_x, to_y, keep_y = outs
        value = jnp.concatenate(values, 0)
        for k in range(4):

            @pl.when(pl.program_id(0) == k)
            def _(k=k):
                if k == 0:
                    own[...] = value
                    return
                for part, (first, keep) in enumerate(((to_x, keep_x), (to_y, keep_y))):
                    here = value[split:] if part else value[:split]
                    if k == 3:
                        first[1] = here
                    elif k == part + 1:
                        first[0] = here
                    else:
                        keep[...] = here
    else:
        for j in range(group):
            start = 0
            for v in values:
                rows = v.shape[0] // group
                outs[0][j, start : start + rows] = v[j * rows : (j + 1) * rows]
                start += rows


def wide_grad(place, lefts, rights, n, square="", micros=0.0, name="grad"):
    tokens = lefts[0][0].shape[0]
    steps = min(n, 4)
    rows = [v[3] // n * (g[3] // PIECE) for v, g in zip(lefts, rights)]
    total = sum(rows)
    split = sum(rows[:2])

    def turn(i, place):
        return jnp.bitwise_xor(place[0], i) if square else i

    def once(*dims):
        return pl.BlockSpec(dims, lambda i, place: (0,) * len(dims), pipeline_mode=pl.Buffered(1))

    def left_spec(v):
        size = v[3] // steps
        return pl.BlockSpec((tokens, size), lambda i, place: (0, v[2] // size + turn(i, place)))

    def right_spec(v):
        return pl.BlockSpec((tokens, v[3]), lambda i, place: (0, v[2] // v[3]), pipeline_mode=pl.Buffered(1))

    if square:
        dims = [(total, PIECE)]
        for size in (split, total - split):
            dims += [(2, size, PIECE), (size, PIECE)]
        out_specs = [once(*d) for d in dims]
        out_shape = [in_hbm(d) for d in dims]
    else:
        out_specs = pl.BlockSpec((n // steps, total, PIECE), lambda i, place: (i, 0, 0))
        out_shape = jax.ShapeDtypeStruct((n, total, PIECE), BF16)
    return pl.pallas_call(
        functools.partial(wide_body, parts=len(lefts), group=n // steps, square=square, split=split),
        grid_spec=pltpu.PrefetchScalarGridSpec(
            num_scalar_prefetch=1,
            grid=(steps,),
            in_specs=[left_spec(v) for v in lefts for _ in range(2)] + [right_spec(v) for v in rights for _ in range(2)],
            out_specs=out_specs,
        ),
        out_shape=out_shape,
        compiler_params=pltpu.CompilerParams(vmem_limit_bytes=VMEM_LIMIT),
        cost_estimate=cost(micros),
        name=name,
    )(place, *[v for left in lefts for v in left[:2]], *[v for right in rights for v in right[:2]])


def in_place(body, args, outs, name, columns=None):
    def spec(shape):
        if columns is None:
            return full_spec(shape)
        return pl.BlockSpec((*shape[:-1], columns), lambda i: (0,) * (len(shape) - 1) + (i,))

    return pl.pallas_call(
        body,
        grid=(1 if columns is None else outs[0].shape[-1] // columns,),
        in_specs=[SCALARS if v.ndim == 1 else spec(v.shape) for v in args],
        out_specs=[spec(v.shape) for v in outs],
        out_shape=outs,
        compiler_params=pltpu.CompilerParams(vmem_limit_bytes=VMEM_LIMIT),
        cost_estimate=cost(0),
        name=name,
    )(*args)


def like(v):
    return in_hbm(v.shape)


def first_body(keep_x, keep_y, from_x, from_y, to_y, to_x):
    to_y[...] = low(keep_x[...].astype(F32) + from_x[1].astype(F32))
    to_x[...] = low(keep_y[...].astype(F32) + from_y[1].astype(F32))


def second_body(own, from_x, from_y, late_y, late_x, out):
    split = late_y.shape[0]
    for at, first, last in ((slice(0, split), from_x, late_y), (slice(split, None), from_y, late_x)):
        out[at] = low(own[at].astype(F32) + first[0].astype(F32) + last[...].astype(F32))


def sum_body(*refs):
    total = refs[0][...].astype(F32)
    for ref in refs[1:-1]:
        total = total + ref[...].astype(F32)
    refs[-1][...] = low(total)


def square_body(own, one, two, three, out):
    near = own[...].astype(F32) + one[...].astype(F32)
    out[...] = low(near + (two[...].astype(F32) + three[...].astype(F32)))


def unpack_body(at_ref, own, other, *rest, plan, summed, grads):
    weights = dict(zip(summed, rest))
    outs = rest[len(summed) : len(summed) + grads]
    sums = dict(zip(summed, rest[len(summed) + grads :]))
    first = at_ref[0] == 0
    totals = {}
    for out, column, columns, half, start, rows in plan:
        at = slice(start, start + rows)
        a, b = (own, other) if half == 0 else (other, own)
        value = jnp.where(first, a[at], b[at])[:, :columns].astype(F32)
        here = slice(column, column + columns)
        outs[out][:, here] = value
        if out in weights:
            part = jnp.sum(value * weights[out][:, here].astype(F32), 1, keepdims=True)
            totals[out] = totals[out] + part if out in totals else part
    for out, ref in sums.items():
        ref[...] = jnp.broadcast_to(totals[out], ref.shape)


def unpack(at, own, other, matrices):
    piece = own.shape[1]
    plan, shapes, weights, start = [], [], {}, 0
    for rows, pieces, parts in matrices:
        ends = np.cumsum([0] + [w.shape[1] for w, _ in parts])
        for half in range(2):
            for i in range(pieces):
                column = (half * pieces + i) * piece
                for k, (w, _) in enumerate(parts):
                    if ends[k] <= column < ends[k + 1]:
                        offset = int(column - ends[k])
                        plan.append(
                            (len(shapes) + k, offset, min(piece, w.shape[1] - offset), half, start + i * rows, rows)
                        )
        for w, wanted in parts:
            if wanted:
                weights[len(shapes)] = w
            shapes.append(jax.ShapeDtypeStruct((rows, w.shape[1]), F32))
        start += pieces * rows
    grads = len(shapes)
    summed = list(weights)
    shapes += [jax.ShapeDtypeStruct((shapes[k].shape[0], 128), F32) for k in summed]

    def whole(shape):
        return pl.BlockSpec(shape, lambda i, at: (0, 0))

    outs = pl.pallas_call(
        functools.partial(unpack_body, plan=plan, summed=summed, grads=grads),
        grid_spec=pltpu.PrefetchScalarGridSpec(
            num_scalar_prefetch=1,
            grid=(1,),
            in_specs=[whole(own.shape), whole(other.shape)]
            + [pl.BlockSpec(shapes[k].shape, lambda i, at: (at[1], 0)) for k in summed],
            out_specs=[whole(v.shape) for v in shapes],
        ),
        out_shape=shapes,
        compiler_params=pltpu.CompilerParams(vmem_limit_bytes=VMEM_LIMIT),
        cost_estimate=cost(0),
        name="unpack",
    )(at, own, other, *weights.values())
    return outs[:grads], [v[:, 0] for v in outs[grads:]]


def ring(value, steps):
    n = lax.axis_size("seq")
    return lax.ppermute(value, "seq", [(i, (i + steps) % n) for i in range(n)])


def along(value, steps):
    n = lax.axis_size("seq")
    return lax.ppermute(value, "seq", [(i, i + steps) for i in range(n) if 0 <= i + steps < n])


def mirror(value):
    n = lax.axis_size("seq")
    return lax.ppermute(value, "seq", [(i, n - 1 - i) for i in range(n)])


def flip_dp(value, bit):
    n = lax.axis_size("dp")
    return lax.ppermute(value, "dp", [(i, i ^ bit) for i in range(n)])


def other_core(value):
    return flip_dp(value, 1)


def after(value, *done):
    return lax.optimization_barrier((value, done))[0]


def scatter_seq(value):
    return lax.psum_scatter(value, "seq", scatter_dimension=0, tiled=True)[0]


def flip_seq(value, bit):
    n = lax.axis_size("seq")
    return lax.ppermute(value, "seq", [(i, i ^ bit) for i in range(n)])


def add_low(*values):
    return in_place(sum_body, values, [like(values[0])], "add")[0]


def direct_sum(pieces):
    return add_low(pieces[0], *[flip_seq(v, k) for k, v in enumerate(pieces) if k])


def first_hop(pieces, *done):
    own, to_x, keep_x, to_y, keep_y = pieces
    from_x, from_y = flip_seq(to_x, 1), flip_seq(to_y, 2)
    held = in_place(
        first_body, (after(keep_x, *done), keep_y, from_x, from_y), [like(keep_x), like(keep_y)], "first_hop"
    )
    return (*held, own, from_x, from_y)


def second_hop(held, *done):
    to_y, to_x, own, from_x, from_y = held
    args = (after(own, *done), from_x, from_y, flip_seq(to_y, 2), flip_seq(to_x, 1))
    return in_place(second_body, args, [like(own)], "second_hop")[0]


def offloaded_sum_z(value, which):
    n = lax.axis_size("dp")
    groups = [list(range(c, n, 2))[:: -1 if which & 1 else 1] for c in range(2)]
    return lax.psum(value, "dp", axis_index_groups=groups[:: -1 if which & 2 else 1])


def sum_four(value, *done):
    got = [flip_dp(value, bit) for bit in (2, 4, 6)]
    return in_place(square_body, (after(value, *done), *got), [like(value)], "add")[0]


def sum_z(value, first=2, last=None):
    bit = first
    while bit < (last or lax.axis_size("dp")):
        value = add_low(value, flip_dp(value, bit))
        bit *= 2
    return value


def on_device(
    tokens, cotangent, lengths, norm_one, w_query, w_key, w_value, w_gatez, w_conv_in, w_step, conv_weight,
    conv_bias, step_bias, decay_log, skip_gain, gated_gain, w_attn_out, w_mix_out, norm_two, w_gate, w_up, w_down,
):
    seqs, span, width = tokens.shape
    half = span // 2
    taps, conv_width = conv_weight.shape
    count = lax.axis_size("seq")
    place = lax.axis_index("seq").astype(jnp.int32)
    core = (lax.axis_index("dp") % 2).astype(jnp.int32)
    first = place * span
    mirrored = (count - 1 - place) * span + half
    row_tables = rotation(span, count, "rows")
    column_tables = rotation(span, count, "columns")
    rate = -jnp.exp(decay_log)
    pad = (0, 128 - SSM_HEADS)
    rate_row = jnp.pad(rate, pad)[None]
    step_row = jnp.pad(step_bias, pad)[None]
    w_step_wide = jnp.pad(w_step, ((0, 0), pad))
    skip_row = jnp.repeat(skip_gain, SSM_HEAD)[None]
    ones = (np.arange(WIDE)[None, :] // SSM_HEAD == np.arange(128)[:, None]).astype(np.float32)
    expand = jnp.asarray(np.concatenate([ones, ones], 0), BF16)
    pos = jnp.stack([first, core])
    core_here = core[None]
    rows = min(256, half)
    blocks = jnp.concatenate([base + jnp.arange(0, half, rows, dtype=jnp.int32) for base in (first, mirrored)])
    sources = lax.rem(place - jnp.arange(count, dtype=jnp.int32) + count, count)
    here = place[None]

    def flat(v):
        return v.reshape(seqs * span, v.shape[2])

    def with_other(mine, yours=None):
        mine, yours = flat(mine), flat(mine if yours is None else yours)
        return mine, other_core(yours), 0, mine.shape[1]

    halo = along(tokens[:, span - 16 :], 1)
    hidden, q, kv = enter(here, after(tokens, halo), norm_one[None], w_query, w_key, w_value, row_tables)
    kvs = [kv] + [ring(kv, r) for r in range(1, count)]
    q_other = mirror(q[:, half:])
    z, conv, pre, x, bk, cq, dt, sg, cum, cumt, state = mixer(
        pos, lengths, hidden, halo, norm_one[None], w_gatez, w_conv_in, w_step_wide, conv_weight, conv_bias[None],
        step_row, rate_row * LOG2E, expand,
    )
    states = lax.all_gather(state, "seq")
    skip_row, blocks, sources = [after(v, state) for v in (skip_row, blocks, sources)]
    gated_row = after(gated_gain, state)[None]
    gact = grad_act(pos, lengths, after(cotangent, state), w_down)
    o_near, o_far, lse = attend(blocks, lengths, sources, after(q, gact), q_other, kvs)
    o_back = mirror(o_far)
    mixed, mix_low, held = scan_forward(
        here, after(x, o_near), bk, cq, dt, cum, cumt, skip_row, z, gated_row, expand, states
    )
    hid = with_other(hidden)
    mix_pair = with_other(mix_low)
    output, lefts, mine, yours, grad_mid = middle(
        pos, lengths, o_near, o_back, after(mix_low, hid[1]), tokens, cotangent, gact, w_attn_out, w_mix_out, w_gate, w_up, w_down,
        norm_two[None],
    )
    square = "hops" if count == 4 else ""
    ff = w_gate.shape[1]
    lefts, rights = with_other(lefts), with_other(mine, yours)
    ffn_left = (*lefts[:2], 0, width)
    ffn_rights = [(*rights[:2], k * ff // 2, ff // 2) for k in range(2)]
    grad_ffn, grad_branch = [(*rights[:2], ff + k * width // 2, width // 2) for k in range(2)]
    out_lefts = ((*lefts[:2], width, ff), (*lefts[:2], width + ff, w_attn_out.shape[0]), mix_pair, hid)
    do_near, do_far, grad_mixed, gz_m, gz_y, adjoint = branch_back(
        core_here, mine, yours, mixed, z, cq, cum, w_attn_out, w_mix_out, gated_row, expand
    )
    adjoints = [along(adjoint, -r) for r in range(1, count)]
    part_ffn = tall_grad(after(here, do_near), ffn_left, ffn_rights, 512, count, square, name="grad_ffn_in")
    part_out = wide_grad(
        after(here, part_ffn[0], *adjoints), out_lefts, (grad_ffn, grad_branch, grad_branch, with_other(gz_m, gz_y)), count,
        square, micros=16, name="grad_outs",
    )
    ffn_held = first_hop(part_ffn, part_out[0]) if square else scatter_seq(part_ffn)
    gc_m, gc_y, tail, head, g_conv_small, g_skip, g_small = scan_backward(
        after(x, part_out[0], ffn_held), bk, cq, dt, sg, cum, cumt, grad_mixed, mixed, held, pre, conv, skip_row, rate_row,
        conv_weight, expand, core_here, adjoints,
    )
    do_other = mirror(after(do_far, head))
    ffn_sum = second_hop(ffn_held) if square else ffn_held
    out_held = first_hop([after(v, ffn_held) for v in part_out]) if square else scatter_seq(part_out)
    head = after(head, ffn_sum, out_held)
    ffn_sum = offloaded_sum_z(ffn_sum, 0)
    returned = along(low(head), -1).astype(F32)[:, : taps - 1]
    g_conv_weight = g_conv_small[:taps]
    beside = ((0, 0), (0, 0), (0, tail.shape[2] - conv_width))
    for ahead in range(1, taps):
        tap = taps - 1 - ahead
        fill = jnp.pad(returned[:, :ahead], ((0, 0), (8 - ahead, 0), (0, 0)))
        tail = tail + jnp.pad(conv_weight[tap] * fill, beside)
        g_conv_weight = g_conv_weight.at[tap].add(jnp.sum(fill * conv[:, span - 8 :].astype(F32), (0, 1)))
    tail = low(tail)
    size = tail.shape[2] // 2
    tails = tail[:, :, :size], tail[:, :, size:]
    gc_m, gc_y = [
        lax.dynamic_update_slice(v, jnp.where(core == i, *tails), (0, span - 8, 0)) for i, v in enumerate((gc_m, gc_y))
    ]
    part_in = tall_grad(
        here, hid, (with_other(gc_m, gc_y),), 256, count, "direct" if square else "", name="grad_conv_in"
    )
    small = [
        g_conv_weight.reshape(-1), g_conv_small[taps], g_skip[0],
        g_small[0], g_small[1],
    ]
    sizes = [v.shape[0] for v in small]
    total = jnp.concatenate(small)
    total = jnp.pad(total, (0, -total.shape[0] % 1024)).reshape(-1, 128)
    hops = [("seq", 1 << k) for k in range(count.bit_length() - 1)]
    hops += [("dp", 2 << k) for k in range(lax.axis_size("dp").bit_length() - 2)] + [("dp", 1)]

    def flip(value, axis, bit):
        return flip_seq(value, bit) if axis == "seq" else flip_dp(value, bit)

    def small_step(total):
        axis, bit = hops.pop(0)
        return total + flip(total, axis, bit)

    def back(group, order):
        near, far, parts = attend_backward(
            group, blocks, lengths, sources, after(q, *order), q_other, do_near, do_other, o_near, o_far, lse,
            column_tables, kvs,
        )
        return near, mirror(far), [parts[0]] + [ring(parts[r], -r) for r in range(1, count)]

    dq_near, dq_far, pieces = back(0, (part_in[0],))
    out_sum = second_hop(out_held, dq_near) if square else out_held
    in_sum = direct_sum([after(part_in[0], dq_near), *part_in[1:]]) if square else scatter_seq(part_in)
    total = small_step(total)
    results = back(1, (dq_near, in_sum, ffn_sum, out_sum, total))
    out_sum = offloaded_sum_z(out_sum, 1)
    four = lax.axis_size("dp") == 8
    in_sum = offloaded_sum_z(in_sum, 2)
    total = small_step(after(total, dq_near))
    gh = leave_mixer(
        core_here, (after(gz_m, results[0], dq_far, total, *pieces), gz_y), (gc_m, gc_y), w_gatez, w_conv_in, w_step_wide
    )
    total = small_step(after(total, results[0]))
    heads = heads_back(
        core_here, after(here, gh, total), row_tables, (dq_near, results[0]), (dq_far, results[1]), pieces + results[2]
    )
    heads_pairs = with_other(*heads[:2]), with_other(*heads[2:])
    total = small_step(after(total, gh))
    part_qkv = tall_grad(after(here, out_sum, total), hid, heads_pairs, 128, count, square, name="grad_qkv")
    grad_tokens = leave(
        core_here, tokens, grad_mid, after(gh, part_qkv[0]), heads, norm_one[None], w_query, w_key, w_value
    )
    while hops:
        total = small_step(total)
    qkv_held = first_hop(part_qkv, out_sum, total, grad_tokens) if square else scatter_seq(part_qkv)
    qkv_sum = second_hop(qkv_held, total, in_sum) if square else qkv_held
    ffn_sum, out_sum, in_sum = [after(v, qkv_sum) for v in (ffn_sum, out_sum, in_sum)]
    at = jnp.stack([core, place])

    def matrix(pieces, *weights, wanted=True):
        return weights[0].shape[0] // count, pieces, [(w, wanted) for w in weights]

    (s_gate, s_up), two_sums = unpack(at, ffn_sum, other_core(ffn_sum), [matrix(2, w_gate), matrix(2, w_up)])
    (s_down, s_attn_out, s_mix_out, s_gatez), (gated_sum, z_sum) = unpack(
        at, out_sum, other_core(out_sum),
        [matrix(2, w_down, wanted=False), matrix(2, w_attn_out, wanted=False), matrix(2, w_mix_out), matrix(3, w_gatez)],
    )
    (s_conv, s_step), in_sums = unpack(at, in_sum, other_core(in_sum), [matrix(4, w_conv_in, w_step)])
    if four:
        qkv_sum = sum_four(qkv_sum, s_gate, s_down, s_conv)
    else:
        qkv_sum = sum_z(qkv_sum)
    got = other_core(qkv_sum)
    (s_query, s_key, s_value), qkv_sums = unpack(at, qkv_sum, got, [matrix(2, w_query), matrix(1, w_key, w_value)])
    total = total.reshape(-1)
    starts = np.cumsum([0] + sizes)
    small = [total[a:b] for a, b in zip(starts[:-1], starts[1:])]

    def own(v):
        n = v.shape[0] // count
        return lax.dynamic_slice(v, (place * n,), (n,))

    s_norm_one = (z_sum + in_sums[0] + in_sums[1] + qkv_sums[0] + qkv_sums[1] + qkv_sums[2]) / own(norm_one)
    s_norm_two = (two_sums[0] + two_sums[1]) / own(norm_two)
    s_gated = gated_sum / own(gated_gain)
    s_skip = jnp.sum(small[2].reshape(SSM_HEADS, SSM_HEAD), 1)
    return (
        output,
        grad_tokens,
        s_norm_one,
        s_query,
        s_key,
        s_value,
        s_gatez,
        s_conv,
        s_step,
        small[0].reshape(taps, -1),
        small[1],
        small[4][:SSM_HEADS],
        small[3][:SSM_HEADS],
        s_skip,
        s_gated,
        s_attn_out,
        s_mix_out,
        s_norm_two,
        s_gate,
        s_up,
        s_down,
    )


def solution(mesh):
    copied = (P(),) * 19
    return jax.shard_map(
        on_device,
        mesh=mesh,
        in_specs=(P("dp", "seq", None), P("dp", "seq", None), P("dp")) + copied,
        out_specs=(
            P("dp", "seq", None), P("dp", "seq", None), P("seq"),
            P("seq", None), P("seq", None), P("seq", None), P("seq", None), P("seq", None), P("seq", None),
            P(), P(), P(), P(), P(),
            P("seq"), P("seq", None), P("seq", None), P("seq"), P("seq", None), P("seq", None), P("seq", None),
        ),
        check_vma=False,
    )
```

```python
import functools

import jax
import jax.numpy as jnp
import numpy as np
from jax import lax
from jax.experimental import pallas as pl
from jax.experimental.pallas import tpu as pltpu
from jax.sharding import PartitionSpec as P

HEADS = 8
KV_HEADS = 2
HEAD = 64
SSM_HEADS = 24
SSM_HEAD = 64
STATE = 128
WIDE = SSM_HEADS * SSM_HEAD
CHUNK = 128
EPS = 1e-05
ROPE_BASE = 100000000000.0
LOG2E = 1.4426950408889634
SCORE2 = 0.125 * LOG2E
LOWEST = -1e30
F32 = jnp.float32
BF16 = jnp.bfloat16
NN = (((1,), (0,)), ((), ()))
NT = (((1,), (1,)), ((), ()))
TN = (((0,), (0,)), ((), ()))
VMEM_LIMIT = 127 << 19


def dot(a, b, dims=NN):
    return lax.dot_general(a, b, dims, preferred_element_type=F32)


def dot_exact(a, b, dims=NN):
    return lax.dot_general(a, b, dims, precision=lax.Precision.HIGHEST, preferred_element_type=F32)


def low(v):
    return v.astype(BF16)


def sigmoid(v):
    return jax.nn.sigmoid(v)


def softplus(v):
    e = jnp.exp(-jnp.abs(v))
    tail = jnp.where(e < 1e-2, e * (1.0 - e * (0.5 - e * (1.0 / 3.0))), jnp.log(1.0 + e))
    return jnp.maximum(v, 0.0) + tail


def split_low(v):
    high = low(v)
    return high, low(v - high.astype(F32))


def widen(v, expand):
    return dot(jnp.concatenate(split_low(v), 1), expand)


def head_sums(v, expand):
    high, rest = split_low(v)
    ones = expand[:128]
    return dot(high, ones, NT) + dot(rest, ones, NT)


def cost(micros):
    return pl.CostEstimate(flops=int(micros * 3e9), bytes_accessed=int(micros * 1e5), transcendentals=0)


def full_spec(shape):
    return pl.BlockSpec(shape, lambda *_: (0,) * len(shape), pipeline_mode=pl.Buffered(1))


def params(limit=VMEM_LIMIT):
    return pltpu.CompilerParams(
        vmem_limit_bytes=limit, dimension_semantics=("arbitrary", "arbitrary")
    )


SCALARS = pl.BlockSpec(memory_space=pltpu.SMEM)


def halves_out(core, values, mine_ref, yours_ref):
    first = core == 0
    start = 0
    for value in values:
        size = value.shape[1] // 2
        lower, upper = value[:, :size], value[:, size:]
        mine_ref[0, :, start : start + size] = jnp.where(first, lower, upper)
        yours_ref[0, :, start : start + size] = jnp.where(first, upper, lower)
        start += size


def halves_in(core, mine, yours):
    first = core == 0
    return jnp.concatenate([jnp.where(first, mine, yours), jnp.where(first, yours, mine)], 1)


def low_rows(rows):
    t = lax.broadcasted_iota(jnp.int32, (rows, rows), 0)
    u = lax.broadcasted_iota(jnp.int32, (rows, rows), 1)
    return t >= u


def rotation(span, count, order):
    inverse = (1.0 / np.float64(ROPE_BASE) ** (np.arange(0, HEAD, 2) / HEAD)).astype(np.float32).astype(np.float64)
    steps = np.arange(span)[:, None] * inverse
    starts = (np.arange(count) * span)[:, None] * inverse
    if order == "rows":
        sign = np.tile(np.repeat([-1.0, 1.0], HEAD // 2), 2)
        made = [np.tile(np.cos(steps), 4), np.tile(np.sin(steps), 4) * sign]
        made += [np.tile(np.cos(starts), 4)[:, None], (np.tile(np.sin(starts), 4) * sign)[:, None]]
    else:
        made = [np.cos(steps).T, np.sin(steps).T]
        made += [np.repeat(f(starts)[:, :, None], 128, 2) for f in (np.cos, np.sin)]
    return [jnp.asarray(v.astype(np.float32)) for v in made]


def turned(step_cos, step_sin, start_cos, start_sin):
    return start_cos * step_cos - start_sin * step_sin, start_sin * step_cos + start_cos * step_sin


def swap_halves(v):
    lane = lax.broadcasted_iota(jnp.int32, v.shape, 1)
    return jnp.where((lane & 63) < 32, pltpu.roll(v, 96, 1), pltpu.roll(v, 32, 1))


def pair_rows(v):
    lane = lax.broadcasted_iota(jnp.int32, v.shape, 1)
    none = jnp.zeros_like(v)
    return jnp.concatenate([jnp.where(lane < 64, v, none), jnp.where(lane >= 64, v, none)], 0)


def first_norm(v, gain):
    v = v.astype(F32)
    return low(v * lax.rsqrt(jnp.mean(v * v, -1, keepdims=True) + EPS) * gain)


def enter_body(
    place_ref, tok_ref, gain_ref, wq_ref, wk_ref, wv_ref, cos_ref, sin_ref, cos0_ref, sin0_ref, hid_ref, q_ref, kv_ref
):
    hid = first_norm(tok_ref[0], gain_ref[...])
    hid_ref[0] = hid
    place = place_ref[0]
    cosine, sine = turned(cos_ref[...], sin_ref[...], cos0_ref[place], sin0_ref[place])
    t = dot(hid, wk_ref[...])
    kv_ref[0, :, :128] = low(t * cosine + swap_halves(t) * sine)
    kv_ref[0, :, 128:] = low(dot(hid, wv_ref[...]))
    q = dot(hid, wq_ref[...])
    for g in range(4):
        t = q[:, g * 128 : g * 128 + 128]
        q_ref[0, :, g * 128 : g * 128 + 128] = low(t * cosine + swap_halves(t) * sine)


def enter(place, tokens, gain, wq, wk, wv, tables):
    seqs, span, width = tokens.shape
    rows = min(256, span)

    def row(n):
        return pl.BlockSpec((1, rows, n), lambda s, b: (s, b, 0))

    table = pl.BlockSpec((rows, 128), lambda s, b: (b, 0))
    return pl.pallas_call(
        enter_body,
        grid=(seqs, span // rows),
        in_specs=[SCALARS, row(width)]
        + [full_spec(v.shape) for v in (gain, wq, wk, wv)]
        + [table, table]
        + [full_spec(v.shape) for v in tables[2:]],
        out_specs=[row(width), row(512), row(256)],
        out_shape=[jax.ShapeDtypeStruct((seqs, span, n), BF16) for n in (width, 512, 256)],
        compiler_params=params(),
        cost_estimate=cost(8),
        name="enter",
    )(place, tokens, gain, wq, wk, wv, *tables)


def mixer_body(
    pos_ref, len_ref, hid_ref, halo_ref, gain_ref, wz_ref, wc_ref, ws_ref, cw_ref, cb_ref, sb_ref, a_ref, exp_ref,
    z_ref, cl_ref, pre_ref, x_ref, bk_ref, cq_ref, dt_ref, sg_ref, cum_ref, cumt_ref, st_ref,
    prev, state, total, *, rows, blocks,
):
    s = pl.program_id(0)
    b = pl.program_id(1)

    @pl.when(b == 0)
    def _():
        prev[...] = dot(first_norm(halo_ref[0], gain_ref[...]), wc_ref[...])[8:]
        state[...] = jnp.zeros_like(state)
        total[...] = jnp.zeros_like(total)

    hid = hid_ref[0]
    conv = dot(hid, wc_ref[...])
    raw = dot(hid, ws_ref[...]) + sb_ref[...]
    z_ref[0] = low(dot(hid, wz_ref[...]))
    cl_ref[0] = low(conv)
    ext = jnp.concatenate([prev[...], conv], 0)
    prev[...] = conv[rows - 8 :]
    pre = cb_ref[...] + cw_ref[3:4] * conv
    for back in range(1, 4):
        pre = pre + cw_ref[3 - back : 4 - back] * pltpu.roll(ext, back, 0)[8:]
    pre_ref[0] = low(pre)
    act = low(pre * sigmoid(pre))
    x = act[:, :WIDE]
    bk = act[:, WIDE : WIDE + STATE]
    x_ref[0] = x
    bk_ref[0] = bk
    cq_ref[0] = act[:, WIDE + STATE :]
    at = pos_ref[0] + b * rows + lax.broadcasted_iota(jnp.int32, raw.shape, 0)
    live = jnp.where(at < len_ref[s], 1.0, 0.0)
    dt = softplus(raw) * live
    dt_ref[0] = dt
    sg_ref[0] = sigmoid(raw) * live
    log_decay = dt * a_ref[...]
    tri = jnp.where(low_rows(CHUNK), 1.0, 0.0)
    for c in range(rows // CHUNK):
        here = slice(c * CHUNK, (c + 1) * CHUNK)
        cum = dot_exact(tri, log_decay[here])
        cum_ref[0, here] = cum
        cumt_ref[0, :, here] = cum.T[:32]
        last = cum[CHUNK - 1 :]
        weight = dt[here] * jnp.exp2(last - cum)
        wide = widen(
            jnp.concatenate([weight, jnp.broadcast_to(jnp.exp2(last), (16, 128))], 0), exp_ref[...]
        )
        xw = low(x[here].astype(F32) * wide[:CHUNK])
        state[...] = state[...] * wide[CHUNK : CHUNK + 1] + dot(bk[here], xw, TN)
        total[...] = total[...] + last

    @pl.when(b == blocks - 1)
    def _():
        st_ref[0, :STATE] = low(state[...])
        st_ref[0, STATE:] = total_rows(total[...], exp_ref[...])


def total_rows(total, expand):
    wide = widen(jnp.broadcast_to(total, (8, 128)), expand)
    high = wide.astype(BF16).astype(F32)
    return low(jnp.concatenate([high, wide - high], 0))


def mixer(pos, lens, hid, halo, gain, wz, wc, ws, cw, cb, sb, a, expand):
    seqs, span, width = hid.shape
    rows = min(256, span)
    blocks = span // rows
    conv_width = wc.shape[1]

    def row(n):
        return pl.BlockSpec((1, rows, n), lambda s, b, *_: (s, b, 0))

    def shape(n, kind):
        return jax.ShapeDtypeStruct((seqs, span, n), kind)

    return pl.pallas_call(
        functools.partial(mixer_body, rows=rows, blocks=blocks),
        grid_spec=pltpu.PrefetchScalarGridSpec(
            num_scalar_prefetch=2,
            grid=(seqs, blocks),
            in_specs=[row(width), pl.BlockSpec((1, 16, width), lambda s, b, *_: (s, 0, 0))]
            + [full_spec(v.shape) for v in (gain, wz, wc, ws, cw, cb, sb, a, expand)],
            out_specs=[
                row(WIDE), row(conv_width), row(conv_width), row(WIDE), row(STATE), row(STATE),
                row(128), row(128), row(128),
                pl.BlockSpec((1, 32, rows), lambda s, b, *_: (s, 0, b)),
                pl.BlockSpec((1, STATE + 16, WIDE), lambda s, b, *_: (s, 0, 0)),
            ],
            scratch_shapes=[
                pltpu.VMEM((8, conv_width), F32), pltpu.VMEM((STATE, WIDE), F32), pltpu.VMEM((1, 128), F32),
            ],
        ),
        out_shape=[
            shape(WIDE, BF16), shape(conv_width, BF16), shape(conv_width, BF16), shape(WIDE, BF16),
            shape(STATE, BF16), shape(STATE, BF16), shape(128, F32), shape(128, F32), shape(128, F32),
            jax.ShapeDtypeStruct((seqs, 32, span), F32),
            jax.ShapeDtypeStruct((seqs, STATE + 16, WIDE), BF16),
        ],
        compiler_params=params(),
        cost_estimate=cost(20),
        name="mixer",
    )(pos, lens, hid, halo, gain, wz, wc, ws, cw, cb, sb, a, expand)


def joined(place, ref):
    state = jnp.zeros((STATE, WIDE), F32)
    for i in range(ref.shape[0]):
        logs = ref[i, 0, STATE : STATE + 1].astype(F32) + ref[i, 0, STATE + 8 : STATE + 9].astype(F32)
        state = jnp.where(i < place, state * jnp.exp2(logs) + ref[i, 0, :STATE].astype(F32), state)
    return state


def joined_later(refs):
    state = jnp.zeros((STATE, WIDE), F32)
    for ref in reversed(refs):
        logs = ref[0, STATE : STATE + 1].astype(F32) + ref[0, STATE + 8 : STATE + 9].astype(F32)
        state = state * jnp.exp2(logs) + ref[0, :STATE].astype(F32)
    return state


def gathered_spec(states):
    return pl.BlockSpec((states.shape[0], 1) + states.shape[2:], lambda s, c: (0, s, 0, 0), pipeline_mode=pl.Buffered(1))


def scan_body(
    place_ref, x_ref, bk_ref, cq_ref, dt_ref, cum_ref, cumt_ref, skip_ref, z_ref, gain_ref, exp_ref, all_ref,
    mix_ref, low_ref, st_ref, state, y,
):
    c = pl.program_id(1)

    @pl.when(c == 0)
    def _():
        state[...] = joined(place_ref[0], all_ref)

    x = x_ref[0].astype(F32)
    bk, cq = bk_ref[0], cq_ref[0]
    cum = cum_ref[0]
    last = cum[CHUNK - 1 :]
    expand = exp_ref[...]
    xdt = x * widen(dt_ref[0], expand)
    ends = widen(
        jnp.concatenate([jnp.exp2(cum), jnp.exp2(last - cum), jnp.broadcast_to(jnp.exp2(last), (16, 128))], 0),
        expand,
    )
    inter = jnp.where(low_rows(CHUNK), dot(cq, bk, NT), 0.0)
    held = low(state[...])
    st_ref[0, 0] = held
    y[...] = dot(cq, held) * ends[:CHUNK] + skip_ref[...] * x
    state[...] = state[...] * ends[2 * CHUNK : 2 * CHUNK + 1] + dot(bk, low(xdt * ends[CHUNK : 2 * CHUNK]), TN)
    xdt = low(xdt)
    for p in range(SSM_HEADS // 2):
        parts = []
        for h in (2 * p, 2 * p + 1):
            differ = jnp.minimum(cum[:, h : h + 1] - cumt_ref[0, h : h + 1, :], 0.0)
            parts.append(low(inter * jnp.exp2(differ)))
        cols = slice(p * 128, p * 128 + 128)
        y[:, cols] += dot(jnp.concatenate(parts, 1), pair_rows(xdt[:, cols]))
    mixed = y[...]
    mix_ref[0] = mixed
    z = z_ref[0].astype(F32)
    v = mixed * (z * sigmoid(z))
    low_ref[0] = low(v * lax.rsqrt(jnp.mean(v * v, -1, keepdims=True) + EPS) * gain_ref[...])


def scan_forward(place, x, bk, cq, dt, cum, cumt, skip, z, gain, expand, states):
    seqs, span, _ = x.shape
    chunks = span // CHUNK

    def row(n):
        return pl.BlockSpec((1, CHUNK, n), lambda s, c: (s, c, 0))

    return pl.pallas_call(
        scan_body,
        grid=(seqs, chunks),
        in_specs=[
            SCALARS, row(WIDE), row(STATE), row(STATE), row(128), row(128),
            pl.BlockSpec((1, 32, CHUNK), lambda s, c: (s, 0, c)),
            full_spec(skip.shape), row(WIDE), full_spec(gain.shape), full_spec(expand.shape), gathered_spec(states),
        ],
        out_specs=[row(WIDE), row(WIDE), pl.BlockSpec((1, 1, STATE, WIDE), lambda s, c: (s, c, 0, 0))],
        out_shape=[
            jax.ShapeDtypeStruct((seqs, span, WIDE), F32),
            jax.ShapeDtypeStruct((seqs, span, WIDE), BF16),
            jax.ShapeDtypeStruct((seqs, chunks, STATE, WIDE), BF16),
        ],
        scratch_shapes=[pltpu.VMEM((STATE, WIDE), F32), pltpu.VMEM((CHUNK, WIDE), F32)],
        compiler_params=params(),
        cost_estimate=cost(16),
        name="scan_forward",
    )(place, x, bk, cq, dt, cum, cumt, skip, z, gain, expand, states)


def live_rows(pos_ref, len_ref, rows):
    at = pos_ref[0] + pl.program_id(1) * rows + lax.broadcasted_iota(jnp.int32, (rows, 1), 0)
    return jnp.where(at < len_ref[pl.program_id(0)], 1.0, 0.0)


def grad_act_body(pos_ref, len_ref, cot_ref, wd_ref, out_ref, *, rows):
    gffn = low(live_rows(pos_ref, len_ref, rows) * cot_ref[0].astype(F32))
    out_ref[0] = low(dot(gffn, wd_ref[...], NT))


def grad_act(pos, lens, cot, wd):
    seqs, span, width = cot.shape
    rows = min(256, span)
    ff = wd.shape[0]
    return pl.pallas_call(
        functools.partial(grad_act_body, rows=rows),
        grid_spec=pltpu.PrefetchScalarGridSpec(
            num_scalar_prefetch=2,
            grid=(seqs, span // rows),
            in_specs=[pl.BlockSpec((1, rows, width), lambda s, b, *_: (s, b, 0)), full_spec(wd.shape)],
            out_specs=pl.BlockSpec((1, rows, ff), lambda s, b, *_: (s, b, 0)),
        ),
        out_shape=jax.ShapeDtypeStruct((seqs, span, ff), BF16),
        compiler_params=params(),
        cost_estimate=cost(0),
        name="grad_act",
    )(pos, lens, cot, wd)


def middle_body(
    pos_ref, len_ref, near_ref, far_ref, mix_ref, tok_ref, cot_ref, gact_ref,
    wao_ref, wmo_ref, wg_ref, wu_ref, wd_ref, gain2_ref,
    out_ref, left_ref, mine_ref, yours_ref, gmid_ref, *, rows, blocks,
):
    b = pl.program_id(1)
    live = live_rows(pos_ref, len_ref, rows)
    attn = jnp.where(b < blocks // 2, near_ref[0], far_ref[0])
    width, ff = wd_ref.shape[1], wd_ref.shape[0]
    left_ref[0, :, width + ff :] = attn
    branch = dot(attn, wao_ref[...]) + dot(mix_ref[0], wmo_ref[...])
    after = tok_ref[0].astype(F32) + live * branch
    scale = lax.rsqrt(jnp.mean(after * after, -1, keepdims=True) + EPS)
    unit = after * scale
    gain = gain2_ref[...]
    h2 = low(unit * gain)
    left_ref[0, :, :width] = h2
    gate = dot(h2, wg_ref[...])
    up = dot(h2, wu_ref[...])
    sg = sigmoid(gate)
    silu = gate * sg
    act = low(silu * up)
    left_ref[0, :, width : width + ff] = act
    out_ref[0] = low(after + live * dot(act, wd_ref[...]))
    cot = cot_ref[0].astype(F32)
    gffn = low(live * cot)
    gact = gact_ref[0].astype(F32)
    gg = low(gact * up * (sg * (1.0 + gate * (1.0 - sg))))
    gu = low(gact * silu)
    gh2 = dot(gg, wg_ref[...], NT) + dot(gu, wu_ref[...], NT)
    g = gh2 * gain
    gmid = cot + scale * (g - unit * jnp.mean(g * unit, -1, keepdims=True))
    gmid_ref[0] = low(gmid)
    halves_out(pos_ref[1], (gg, gu, gffn, low(live * gmid)), mine_ref, yours_ref)


def middle(pos, lens, near, far, mix, tokens, cot, gact, wao, wmo, wg, wu, wd, gain2):
    seqs, span, width = tokens.shape
    rows = min(256, span // 2)
    blocks = span // rows
    ff = wg.shape[1]
    lower = pl.BlockSpec((1, rows, 512), lambda s, b, *_: (s, jnp.minimum(b, blocks // 2 - 1), 0))
    upper = pl.BlockSpec((1, rows, 512), lambda s, b, *_: (s, jnp.maximum(b - blocks // 2, 0), 0))

    def row(n):
        return pl.BlockSpec((1, rows, n), lambda s, b, *_: (s, b, 0))

    def shape(n, kind):
        return jax.ShapeDtypeStruct((seqs, span, n), kind)

    return pl.pallas_call(
        functools.partial(middle_body, rows=rows, blocks=blocks),
        grid_spec=pltpu.PrefetchScalarGridSpec(
            num_scalar_prefetch=2,
            grid=(seqs, blocks),
            in_specs=[lower, upper, row(WIDE), row(width), row(width), row(ff)]
            + [full_spec(v.shape) for v in (wao, wmo, wg, wu, wd, gain2)],
            out_specs=[
                row(width), row(width + ff + 512), row(width + ff), row(width + ff), row(width),
            ],
        ),
        out_shape=[
            shape(width, BF16), shape(width + ff + 512, BF16), shape(width + ff, BF16), shape(width + ff, BF16),
            shape(width, BF16),
        ],
        compiler_params=params(),
        cost_estimate=cost(45),
        name="middle",
    )(pos, lens, near, far, mix, tokens, cot, gact, wao, wmo, wg, wu, wd, gain2)


def branch_body(
    core_ref, gb_m, gb_y, mixed_ref, z_ref, cq_ref, cum_ref, wao_ref, wmo_ref, gated_ref, exp_ref,
    gnear_ref, gfar_ref, gmixed_ref, gz_m, gz_y, adj_ref, adj, offset, *, rows, blocks,
):
    b = pl.program_id(1)

    @pl.when(b == 0)
    def _():
        adj[...] = jnp.zeros_like(adj)
        offset[...] = jnp.zeros_like(offset)

    core = core_ref[0]
    gb = halves_in(core, gb_m[0], gb_y[0])
    gattn = low(dot(gb, wao_ref[...], NT))

    @pl.when(b < blocks // 2)
    def _():
        gnear_ref[0] = gattn

    @pl.when(b >= blocks // 2)
    def _():
        gfar_ref[0] = gattn

    gn = low(dot(gb, wmo_ref[...], NT)).astype(F32)
    mixed = mixed_ref[0]
    z = z_ref[0].astype(F32)
    sg = sigmoid(z)
    silu = z * sg
    v = mixed * silu
    scale = lax.rsqrt(jnp.mean(v * v, -1, keepdims=True) + EPS)
    unit = v * scale
    g = gn * gated_ref[...]
    g = scale * (g - unit * jnp.mean(g * unit, -1, keepdims=True))
    gmixed = g * silu
    gmixed_ref[0] = low(gmixed)
    halves_out(core, (low(g * mixed * (sg * (1.0 + z * (1.0 - sg)))),), gz_m, gz_y)
    cum = cum_ref[0]
    logs = []
    for c in range(rows // CHUNK):
        here = cum[c * CHUNK : (c + 1) * CHUNK]
        logs.append(here + offset[...])
        offset[...] += here[CHUNK - 1 :]
    wide = widen(jnp.exp2(jnp.concatenate(logs, 0)), exp_ref[...])
    adj[...] += dot(cq_ref[0], low(gmixed * wide), TN)

    @pl.when(b == blocks - 1)
    def _():
        adj_ref[0, :STATE] = low(adj[...])
        adj_ref[0, STATE:] = total_rows(offset[...], exp_ref[...])


def branch_back(core, mine, yours, mixed, z, cq, cum, wao, wmo, gated, expand):
    seqs, span, packed = mine.shape
    half_width = wao.shape[1] // 2
    gb = pl.BlockSpec((1, min(256, span // 2), half_width), lambda s, b: (s, b, packed // half_width - 1))
    rows = min(256, span // 2)
    blocks = span // rows
    lower = pl.BlockSpec((1, rows, 512), lambda s, b: (s, jnp.minimum(b, blocks // 2 - 1), 0))
    upper = pl.BlockSpec((1, rows, 512), lambda s, b: (s, jnp.maximum(b - blocks // 2, 0), 0))

    def row(n):
        return pl.BlockSpec((1, rows, n), lambda s, b: (s, b, 0))

    def shape(n, kind):
        return jax.ShapeDtypeStruct((seqs, span, n), kind)

    half = jax.ShapeDtypeStruct((seqs, span // 2, 512), BF16)
    return pl.pallas_call(
        functools.partial(branch_body, rows=rows, blocks=blocks),
        grid=(seqs, blocks),
        in_specs=[SCALARS, gb, gb, row(WIDE), row(WIDE), row(STATE), row(128)]
        + [full_spec(v.shape) for v in (wao, wmo, gated, expand)],
        out_specs=[
            lower, upper, row(WIDE), row(WIDE // 2), row(WIDE // 2),
            pl.BlockSpec((1, STATE + 16, WIDE), lambda s, b: (s, 0, 0)),
        ],
        out_shape=[
            half, half, shape(WIDE, BF16), shape(WIDE // 2, BF16), shape(WIDE // 2, BF16),
            jax.ShapeDtypeStruct((seqs, STATE + 16, WIDE), BF16),
        ],
        scratch_shapes=[pltpu.VMEM((STATE, WIDE), F32), pltpu.VMEM((1, 128), F32)],
        compiler_params=params(),
        cost_estimate=cost(6),
        name="branch_back",
    )(core, mine, yours, mixed, z, cq, cum, wao, wmo, gated, expand)


def scan_back_body(
    x_ref, bk_ref, cq_ref, dt_ref, sg_ref, cum_ref, cumt_ref, dy_ref, mix_ref, st_ref, pre_ref, cl_ref,
    skip_ref, a_ref, cw_ref, exp_ref, core_ref, *rest, chunks, conv_width,
):
    *later, gc_m, gc_y, tail_ref, head_ref, gw_ref, gskip_ref, small_ref, adj, after, gact = rest
    s = pl.program_id(0)
    c = pl.program_id(1)

    @pl.when((s == 0) & (c == 0))
    def _():
        gw_ref[...] = jnp.zeros_like(gw_ref)
        gskip_ref[...] = jnp.zeros_like(gskip_ref)
        small_ref[...] = jnp.zeros_like(small_ref)

    @pl.when(c == 0)
    def _():
        adj[...] = joined_later(later)
        after[...] = jnp.zeros_like(after)

    x = x_ref[0].astype(F32)
    bk, cq = bk_ref[0], cq_ref[0]
    dt = dt_ref[0]
    cum = cum_ref[0]
    last = cum[CHUNK - 1 :]
    expand = exp_ref[...]
    dt_wide = widen(dt, expand)
    ends = widen(
        jnp.concatenate([jnp.exp2(cum), jnp.exp2(last - cum), jnp.broadcast_to(jnp.exp2(last), (16, 128))], 0),
        expand,
    )
    to_end = ends[CHUNK : 2 * CHUNK]
    all_wide = ends[2 * CHUNK : 2 * CHUNK + 1]
    xdt = x * dt_wide
    dy_low = dy_ref[0]
    dy = dy_low.astype(F32)
    dy_in = low(dy * ends[:CHUNK])
    state = st_ref[0, 0]
    gstate = adj[...]
    gstate_low = low(gstate)
    from_end = dot(bk, gstate_low) * to_end
    gb = dot(low(xdt * to_end), gstate_low, NT)
    gc = dot(dy_in, state, NT)
    gfinal = all_wide * jnp.sum(gstate * state.astype(F32), 0, keepdims=True) + jnp.sum(
        xdt * from_end, 0, keepdims=True
    )
    adj[...] = gstate * all_wide + dot(cq, dy_in, TN)
    xdt_low = low(xdt)
    u = lax.broadcasted_iota(jnp.int32, (CHUNK, CHUNK), 0)
    t = lax.broadcasted_iota(jnp.int32, (CHUNK, CHUNK), 1)
    inter = jnp.where(t >= u, dot(bk, cq, NT), 0.0)
    ginter = jnp.zeros((CHUNK, CHUNK), F32)
    for p in range(SSM_HEADS // 2):
        cols = slice(p * 128, p * 128 + 128)
        dy_rows = pair_rows(dy_low[:, cols])
        gmix = dot(xdt_low[:, cols], dy_rows, NT)
        parts = []
        for n, h in enumerate((2 * p, 2 * p + 1)):
            decay = jnp.exp2(jnp.minimum(cumt_ref[0, h : h + 1, :] - cum[:, h : h + 1], 0.0))
            parts.append(low(inter * decay))
            ginter = ginter + gmix[:, n * CHUNK : (n + 1) * CHUNK] * decay
        gact[:, cols] = dot(jnp.concatenate(parts, 1), dy_rows)
    ginter = low(jnp.where(t >= u, ginter, 0.0))
    gact[:, WIDE : WIDE + STATE] = gb + dot(ginter, cq)
    gact[:, WIDE + STATE :] = gc + dot(ginter, bk, TN)
    gxdt = gact[:, :WIDE] + from_end
    skip = skip_ref[...]
    gact[:, :WIDE] = dt_wide * gxdt + skip * dy
    gskip_ref[...] += jnp.sum(dy * x, 0, keepdims=True)
    sums = head_sums(
        jnp.concatenate([x * gxdt, dy * (mix_ref[0] - skip * x), jnp.broadcast_to(gfinal, (16, WIDE))], 0), expand
    )
    direct = sums[:CHUNK]
    gcum = sums[CHUNK : 2 * CHUNK] - dt * direct
    gld = dot_exact(jnp.where(t >= u, 1.0, 0.0), gcum) + sums[2 * CHUNK : 2 * CHUNK + 1]
    a = a_ref[...]
    gstep = (direct + a * gld) * sg_ref[0]
    small_ref[0:1] += jnp.sum(dt * gld, 0, keepdims=True) * a
    small_ref[1:2] += jnp.sum(gstep, 0, keepdims=True)
    pre = pre_ref[0].astype(F32)
    sg = sigmoid(pre)
    gpre = gact[...] * (sg * (1.0 + pre * (1.0 - sg)))
    ext = jnp.concatenate([gpre, after[...]], 0)
    after[...] = gpre[:8]
    conv = cl_ref[0].astype(F32)
    gconv = cw_ref[3:4] * gpre
    gw_ref[3:4] += jnp.sum(conv * gpre, 0, keepdims=True)
    gw_ref[4:5] += jnp.sum(gpre, 0, keepdims=True)
    for ahead in range(1, 4):
        moved = pltpu.roll(ext, CHUNK + 8 - ahead, 0)[:CHUNK]
        gconv = gconv + cw_ref[3 - ahead : 4 - ahead] * moved
        gw_ref[3 - ahead : 4 - ahead] += jnp.sum(conv * moved, 0, keepdims=True)
    everything = jnp.concatenate([low(gconv), low(gstep), jnp.zeros((CHUNK, 128), BF16)], 1)
    halves_out(core_ref[0], (everything,), gc_m, gc_y)

    @pl.when(c == 0)
    def _():
        tail_ref[0, :, :conv_width] = gconv[CHUNK - 8 :]
        tail_ref[0, :, conv_width : conv_width + 128] = gstep[CHUNK - 8 :]
        tail_ref[0, :, conv_width + 128 :] = jnp.zeros((8, 128), F32)

    @pl.when(c == chunks - 1)
    def _():
        head_ref[0] = gpre[:8]


def scan_backward(x, bk, cq, dt, sg, cum, cumt, dy, mixed, states, pre, conv, skip, a, cw, expand, core, adjoints):
    seqs, span, _ = x.shape
    chunks = span // CHUNK
    conv_width = pre.shape[2]

    def row(n):
        return pl.BlockSpec((1, CHUNK, n), lambda s, c: (s, chunks - 1 - c, 0))

    def once(m, n):
        return pl.BlockSpec((m, n), lambda s, c: (0, 0))

    edge = pl.BlockSpec((1, 8, conv_width), lambda s, c: (s, 0, 0))
    return pl.pallas_call(
        functools.partial(scan_back_body, chunks=chunks, conv_width=conv_width),
        grid=(seqs, chunks),
        in_specs=[
            row(WIDE), row(STATE), row(STATE), row(128), row(128), row(128),
            pl.BlockSpec((1, 32, CHUNK), lambda s, c: (s, 0, chunks - 1 - c)),
            row(WIDE), row(WIDE),
            pl.BlockSpec((1, 1, STATE, WIDE), lambda s, c: (s, chunks - 1 - c, 0, 0)),
            row(conv_width), row(conv_width),
            full_spec(skip.shape), full_spec(a.shape), full_spec(cw.shape), full_spec(expand.shape), SCALARS,
        ]
        + [
            pl.BlockSpec((1, STATE + 16, WIDE), lambda s, c: (s, 0, 0), pipeline_mode=pl.Buffered(1))
            for _ in adjoints
        ],
        out_specs=[
            row((conv_width + 256) // 2), row((conv_width + 256) // 2),
            pl.BlockSpec((1, 8, conv_width + 256), lambda s, c: (s, 0, 0)), edge, once(8, conv_width), once(1, WIDE), once(8, 128),
        ],
        out_shape=[
            jax.ShapeDtypeStruct((seqs, span, (conv_width + 256) // 2), BF16),
            jax.ShapeDtypeStruct((seqs, span, (conv_width + 256) // 2), BF16),
            jax.ShapeDtypeStruct((seqs, 8, conv_width + 256), F32),
            jax.ShapeDtypeStruct((seqs, 8, conv_width), F32),
            jax.ShapeDtypeStruct((8, conv_width), F32),
            jax.ShapeDtypeStruct((1, WIDE), F32),
            jax.ShapeDtypeStruct((8, 128), F32),
        ],
        scratch_shapes=[
            pltpu.VMEM((STATE, WIDE), F32), pltpu.VMEM((8, conv_width), F32), pltpu.VMEM((CHUNK, conv_width), F32),
        ],
        compiler_params=params(),
        cost_estimate=cost(4),
        name="scan_backward",
    )(x, bk, cq, dt, sg, cum, cumt, dy, mixed, states, pre, conv, skip, a, cw, expand, core, *adjoints)


def leave_mixer_body(core_ref, gz_m, gz_y, gc_m, gc_y, wz_ref, wc_ref, ws_ref, gh_ref, *, conv_width):
    core = core_ref[0]
    gz = halves_in(core, gz_m[0], gz_y[0])
    gc = halves_in(core, gc_m[0], gc_y[0])
    gh = dot(gz, wz_ref[...], NT) + dot(gc[:, :conv_width], wc_ref[...], NT)
    gh_ref[0] = low(gh + dot(gc[:, conv_width : conv_width + 128], ws_ref[...], NT))


def leave_mixer(core, gz, gc, wz, wc, ws):
    seqs, span, _ = gz[0].shape
    rows = min(256, span)

    def row(n):
        return pl.BlockSpec((1, rows, n), lambda s, b: (s, b, 0))

    width = wz.shape[0]
    return pl.pallas_call(
        functools.partial(leave_mixer_body, conv_width=wc.shape[1]),
        grid=(seqs, span // rows),
        in_specs=[SCALARS]
        + [row(v.shape[2]) for v in (*gz, *gc)]
        + [full_spec(v.shape) for v in (wz, wc, ws)],
        out_specs=row(width),
        out_shape=jax.ShapeDtypeStruct((seqs, span, width), BF16),
        compiler_params=params(),
        cost_estimate=cost(0),
        name="leave_mixer",
    )(core, *gz, *gc, wz, wc, ws)


def heads_body(core_ref, place_ref, cos_ref, sin_ref, cos0_ref, sin0_ref, *rest, blocks, count):
    near, far = rest[:2], rest[2:4]
    pieces = rest[4 : 4 + 2 * count]
    gq_m, gq_y, gkv_m, gkv_y = rest[4 + 2 * count :]
    core = core_ref[0]
    b = pl.program_id(1)
    halves_out(core, (jnp.concatenate([jnp.where(b < blocks // 2, near[j][0], far[j][0]) for j in range(2)], 1),), gq_m, gq_y)
    sums = []
    for j in range(2):
        t = pieces[j * count][0].astype(F32)
        for r in range(1, count):
            t = t + pieces[j * count + r][0].astype(F32)
        sums.append(t)
    lane = lax.broadcasted_iota(jnp.int32, sums[0].shape, 1)
    gk = jnp.where(lane < 64, sums[0], pltpu.roll(sums[1], 64, 1))
    gv = low(jnp.where(lane < 64, pltpu.roll(sums[0], 64, 1), sums[1]))
    place = place_ref[0]
    cosine, sine = turned(cos_ref[...], sin_ref[...], cos0_ref[place], sin0_ref[place])
    gk = low(gk * cosine - swap_halves(gk) * sine)
    halves_out(core, (jnp.concatenate([gk, gv], 1),), gkv_m, gkv_y)


def heads_back(core, place, tables, near, far, pieces):
    seqs, half, _ = near[0].shape
    span = 2 * half
    rows = min(256, half)
    blocks = span // rows
    table = pl.BlockSpec((rows, 128), lambda s, b: (b, 0))
    lower = pl.BlockSpec((1, rows, 256), lambda s, b: (s, jnp.minimum(b, blocks // 2 - 1), 0))
    upper = pl.BlockSpec((1, rows, 256), lambda s, b: (s, jnp.maximum(b - blocks // 2, 0), 0))

    def row(n):
        return pl.BlockSpec((1, rows, n), lambda s, b: (s, b, 0))

    return pl.pallas_call(
        functools.partial(heads_body, blocks=blocks, count=len(pieces) // 2),
        grid=(seqs, blocks),
        in_specs=[SCALARS, SCALARS, table, table]
        + [full_spec(v.shape) for v in tables[2:]]
        + [lower, lower, upper, upper] + [row(128)] * len(pieces),
        out_specs=[row(256), row(256), row(128), row(128)],
        out_shape=[jax.ShapeDtypeStruct((seqs, span, n), BF16) for n in (256, 256, 128, 128)],
        compiler_params=params(),
        cost_estimate=cost(0),
        name="heads_back",
    )(core, place, *tables, *near, *far, *pieces)


def leave_body(
    core_ref, tok_ref, gmid_ref, gh_ref, gq_m, gq_y, gkv_m, gkv_y, gain_ref, wq_ref, wk_ref, wv_ref, gt_ref
):
    core = core_ref[0]
    gh = gh_ref[0].astype(F32) + dot(halves_in(core, gq_m[0], gq_y[0]), wq_ref[...], NT)
    gkv = halves_in(core, gkv_m[0], gkv_y[0])
    gh = gh + dot(gkv[:, :128], wk_ref[...], NT) + dot(gkv[:, 128:], wv_ref[...], NT)
    v = tok_ref[0].astype(F32)
    scale = lax.rsqrt(jnp.mean(v * v, -1, keepdims=True) + EPS)
    unit = v * scale
    g = gh * gain_ref[...]
    gt_ref[0] = gmid_ref[0].astype(F32) + scale * (g - unit * jnp.mean(g * unit, -1, keepdims=True))


def leave(core, tokens, gmid, gh, heads, gain, wq, wk, wv):
    seqs, span, width = tokens.shape
    rows = min(256, span)

    def row(n):
        return pl.BlockSpec((1, rows, n), lambda s, b: (s, b, 0))

    return pl.pallas_call(
        leave_body,
        grid=(seqs, span // rows),
        in_specs=[SCALARS] + [row(width)] * 3 + [row(v.shape[2]) for v in heads] + [full_spec(v.shape) for v in (gain, wq, wk, wv)],
        out_specs=row(width),
        out_shape=jax.ShapeDtypeStruct((seqs, span, width), F32),
        compiler_params=params(),
        cost_estimate=cost(0),
        name="leave",
    )(core, tokens, gmid, gh, *heads, gain, wq, wk, wv)


def dup_halves(v):
    lane = lax.broadcasted_iota(jnp.int32, v.shape, 1)
    other = pltpu.roll(v, 64, 1)
    return low(jnp.where(lane < 64, v, other)), low(jnp.where(lane < 64, other, v))


def head_rows(v):
    lane = lax.broadcasted_iota(jnp.int32, (v.shape[0], 128), 1)
    heads = []
    for h in range(v.shape[1] // HEAD):
        t = v[:, (h // 2) * 128 : (h // 2) * 128 + 128]
        heads.append(jnp.where((lane < 64) if h % 2 == 0 else (lane >= 64), t, jnp.zeros_like(t)))
    return heads


def key_range(first, length, rows, keys):
    whole = jnp.minimum((first + 1) // keys, length // keys)
    some = jnp.minimum((first + rows + keys - 1) // keys, (length + keys - 1) // keys)
    return whole, some


def seen(i, first, length, rows, keys):
    key_at = i * keys + lax.broadcasted_iota(jnp.int32, (keys, rows), 0)
    query_at = first + lax.broadcasted_iota(jnp.int32, (keys, rows), 1)
    return (key_at <= query_at) & (key_at < length)


def attend_body(
    pos_ref, len_ref, from_ref, q_ref, other_ref, *rest, rows, keys, blocks, count, span,
):
    kv_refs = rest[:count]
    near_ref, far_ref, lse_ref, kd, vt, top, acc, score_a, score_b, top_a, top_b = rest[count:]
    s = pl.program_id(0)
    b = pl.program_id(1)
    prep = min(512, span)

    @pl.when(b == 0)
    def _():
        ones = jnp.ones((16, prep), F32)
        for r, kv_ref in enumerate(kv_refs):
            for i in range(span // prep):
                here = slice(i * prep, (i + 1) * prep)
                at = pl.ds(pl.multiple_of(from_ref[r] * span + i * prep, prep), prep)
                kd[0, at, :], kd[1, at, :] = dup_halves(kv_ref[0, here, :128].astype(F32))
                t = kv_ref[0, here, 128:].astype(F32).T
                vt[0, :, at] = low(jnp.concatenate([t[:64], ones], 0))
                vt[1, :, at] = low(jnp.concatenate([t[64:], ones], 0))

    first = pos_ref[b]
    length = len_ref[s]
    heads = head_rows(jnp.where(b < blocks // 2, q_ref[0], other_ref[0]))
    top[...] = jnp.full_like(top, LOWEST)
    acc[...] = jnp.zeros_like(acc)
    whole, some = key_range(first, length, rows, keys)

    def scores(i, buffer, tops, h, mask=None):
        at = pl.ds(pl.multiple_of(i * keys, keys), keys)
        t = dot(kd[h // 4, at, :], heads[h], NT)
        if mask is not None:
            t = jnp.where(mask, t, LOWEST)
        buffer[h] = t
        tops[h] = jnp.max(t, 0, keepdims=True)

    def add(i, buffer, tops, h):
        at = pl.ds(pl.multiple_of(i * keys, keys), keys)
        before = top[h]
        now = jnp.maximum(before, tops[h])
        p = low(jnp.exp2((buffer[h] - now) * SCORE2))
        acc[h] = acc[h] * jnp.exp2((before - now) * SCORE2) + dot(vt[h // 4, :, at], p)
        top[h] = now

    def edge(i, _):
        mask = seen(i, first, length, rows, keys)
        for h in range(HEADS):
            scores(i, score_a, top_a, h, mask)
        for h in range(HEADS):
            add(i, score_a, top_a, h)
        return 0

    lax.fori_loop(whole, some, edge, 0)
    last = jnp.maximum(whole - 1, 0)
    for h in range(HEADS):
        scores(0, score_a, top_a, h)

    def two(i, _):
        for h in range(HEADS):
            scores(2 * i + 1, score_b, top_b, h)
            add(2 * i, score_a, top_a, h)
        following = jnp.minimum(2 * i + 2, last)
        for h in range(HEADS):
            scores(following, score_a, top_a, h)
            add(2 * i + 1, score_b, top_b, h)
        return 0

    lax.fori_loop(0, whole // 2, two, 0)

    @pl.when(whole % 2 == 1)
    def _():
        for h in range(HEADS):
            add(last, score_a, top_a, h)

    outs = []
    for h in range(HEADS):
        t = acc[h]
        weight = t[64:65]
        outs.append(t[:64] / weight)
        lse_ref[0, h : h + 1, :] = top[h] * SCORE2 + jnp.log2(weight)
    result = low(jnp.concatenate(outs, 0).T)

    @pl.when(b < blocks // 2)
    def _():
        near_ref[0] = result

    @pl.when(b >= blocks // 2)
    def _():
        far_ref[0] = result


def halves_specs(rows, blocks, columns):
    lower = pl.BlockSpec((1, rows, columns), lambda s, b, *_: (s, jnp.minimum(b, blocks // 2 - 1), 0))
    upper = pl.BlockSpec((1, rows, columns), lambda s, b, *_: (s, jnp.maximum(b - blocks // 2, 0), 0))
    return lower, upper


def attend(pos, lens, sources, q, other, kvs):
    seqs, span, _ = q.shape
    count = len(kvs)
    total = count * span
    rows = min(256, span // 2)
    keys = 256
    blocks = span // rows
    lower, upper = halves_specs(rows, blocks, 512)
    half = jax.ShapeDtypeStruct((seqs, span // 2, 512), BF16)
    return pl.pallas_call(
        functools.partial(attend_body, rows=rows, keys=keys, blocks=blocks, count=count, span=span),
        grid_spec=pltpu.PrefetchScalarGridSpec(
            num_scalar_prefetch=3,
            grid=(seqs, blocks),
            in_specs=[lower, upper]
            + [pl.BlockSpec((1, span, 256), lambda s, b, *_: (s, 0, 0), pipeline_mode=pl.Buffered(1))] * count,
            out_specs=[lower, upper, pl.BlockSpec((1, 8, rows), lambda s, b, *_: (s, 0, b))],
            scratch_shapes=[
                pltpu.VMEM((2, total, 128), BF16), pltpu.VMEM((2, 80, total), BF16),
                pltpu.VMEM((8, 1, rows), F32), pltpu.VMEM((8, 80, rows), F32),
                pltpu.VMEM((8, keys, rows), F32), pltpu.VMEM((8, keys, rows), F32),
                pltpu.VMEM((8, 1, rows), F32), pltpu.VMEM((8, 1, rows), F32),
            ],
        ),
        out_shape=[half, half, jax.ShapeDtypeStruct((seqs, 8, span), F32)],
        compiler_params=params(),
        cost_estimate=cost(26),
        name="attend",
    )(pos, lens, sources, q, other, *kvs)


def attend_back_body(
    pos_ref, len_ref, from_ref, q_ref, other_ref, do_near_ref, do_far_ref, o_near_ref, o_far_ref, lse_ref,
    cos_ref, sin_ref, cos0_ref, sin0_ref, *rest, rows, keys, blocks, count, span, group,
):
    kv_refs = rest[:count]
    dq_near_ref, dq_far_ref = rest[count : count + 2]
    dkv_refs = rest[count + 2 : 2 * count + 2]
    kd, vd, kt, dk, dv, dq, score_a, grad_a, score_b, grad_b = rest[2 * count + 2 :]
    s = pl.program_id(0)
    b = pl.program_id(1)
    prep = min(512, span)

    @pl.when(b == 0)
    def _():
        for r, kv_ref in enumerate(kv_refs):
            for i in range(span // prep):
                here = slice(i * prep, (i + 1) * prep)
                at = pl.ds(pl.multiple_of(from_ref[r] * span + i * prep, prep), prep)
                k = kv_ref[0, here, :128].astype(F32)
                kd[at, :] = dup_halves(k)[group]
                vd[at, :] = dup_halves(kv_ref[0, here, 128:].astype(F32))[group]
                kt[:, at] = low(k.T[64 * group : 64 * group + 64])
        dk[...] = jnp.zeros_like(dk)
        dv[...] = jnp.zeros_like(dv)

    first = pos_ref[b]
    length = len_ref[s]
    is_near = b < blocks // 2
    heads = head_rows(jnp.where(is_near, q_ref[0], other_ref[0]))
    do = jnp.where(is_near, do_near_ref[0], do_far_ref[0])
    grads = head_rows(do)
    prod = do.astype(F32) * jnp.where(is_near, o_near_ref[0], o_far_ref[0]).astype(F32)
    col = lax.broadcasted_iota(jnp.int32, (8, 256), 1) // HEAD
    ones = low(jnp.where(col == lax.broadcasted_iota(jnp.int32, (8, 256), 0), 1.0, 0.0))
    high, remain = split_low(prod)
    delta = dot(ones, high, NT) + dot(ones, remain, NT)
    dq[...] = jnp.zeros_like(dq)
    whole, some = key_range(first, length, rows, keys)

    def scores(i, buffers, h):
        at = pl.ds(pl.multiple_of(i * keys, keys), keys)
        buffers[0][h] = dot(kd[at, :], heads[h], NT)
        buffers[1][h] = dot(vd[at, :], grads[h], NT)

    def add(i, buffers, h, sums, mask=None):
        at = pl.ds(pl.multiple_of(i * keys, keys), keys)
        x = buffers[0][h] * SCORE2 - lse_ref[0, 4 * group + h : 4 * group + h + 1, :]
        if mask is not None:
            x = jnp.where(mask, x, LOWEST)
        p = jnp.exp2(x)
        ds = low(p * (buffers[1][h] - delta[h : h + 1]))
        parts = dot(low(p), grads[h]), dot(ds, heads[h])
        dq[h] += dot(kt[:, at], ds)
        sums = parts if sums is None else (sums[0] + parts[0], sums[1] + parts[1])
        if h == 3:
            dv[at, :] += sums[0]
            dk[at, :] += sums[1]
        return sums

    early, late = (score_a, grad_a), (score_b, grad_b)

    def edge(i, _):
        mask = seen(i, first, length, rows, keys)
        for h in range(4):
            scores(i, early, h)
        sums = None
        for h in range(4):
            sums = add(i, early, h, sums, mask)
        return 0

    lax.fori_loop(whole, some, edge, 0)
    last = jnp.maximum(whole - 1, 0)
    for h in range(4):
        scores(0, early, h)

    def two(i, _):
        sums = None
        for h in range(4):
            scores(2 * i + 1, late, h)
            sums = add(2 * i, early, h, sums)
        following = jnp.minimum(2 * i + 2, last)
        sums = None
        for h in range(4):
            scores(following, early, h)
            sums = add(2 * i + 1, late, h, sums)
        return 0

    lax.fori_loop(0, whole // 2, two, 0)

    @pl.when(whole % 2 == 1)
    def _():
        sums = None
        for h in range(4):
            sums = add(last, early, h, sums)

    owner = jnp.where(is_near, from_ref[0], count - 1 - from_ref[0])
    cosine, sine = turned(cos_ref[...], sin_ref[...], cos0_ref[owner][:, :1], sin0_ref[owner][:, :1])
    parts = []
    for h in range(4):
        t = dq[h] * 0.125
        former, latter = t[:32], t[32:]
        parts += [former * cosine + latter * sine, latter * cosine - former * sine]
    result = low(jnp.concatenate(parts, 0).T)

    @pl.when(is_near)
    def _():
        dq_near_ref[0] = result

    @pl.when(jnp.logical_not(is_near))
    def _():
        dq_far_ref[0] = result

    @pl.when(b == blocks - 1)
    def _():
        lane = lax.broadcasted_iota(jnp.int32, (prep, 128), 1)
        for r, dkv_ref in enumerate(dkv_refs):
            for i in range(span // prep):
                at = pl.ds(pl.multiple_of(from_ref[r] * span + i * prep, prep), prep)
                k, v = dk[at, :], dv[at, :]
                k = (k + pltpu.roll(k, 64, 1)) * 0.125
                v = v + pltpu.roll(v, 64, 1)
                dkv_ref[0, i * prep : (i + 1) * prep] = low(jnp.where(lane < 64, k, v))


def attend_backward(group, pos, lens, sources, q, other, do_near, do_far, o_near, o_far, lse, tables, kvs):
    seqs, span, _ = q.shape
    count = len(kvs)
    total = count * span
    rows = min(256, span // 2)
    keys = 256
    blocks = span // rows
    lower = pl.BlockSpec((1, rows, 256), lambda s, b, *_: (s, jnp.minimum(b, blocks // 2 - 1), group))
    upper = pl.BlockSpec((1, rows, 256), lambda s, b, *_: (s, jnp.maximum(b - blocks // 2, 0), group))
    out_lower, out_upper = halves_specs(rows, blocks, 256)
    stat = pl.BlockSpec((1, 8, rows), lambda s, b, *_: (s, 0, b))
    table = pl.BlockSpec((32, rows), lambda s, b, *_: (0, b))
    half = jax.ShapeDtypeStruct((seqs, span // 2, 256), BF16)
    outs = pl.pallas_call(
        functools.partial(
            attend_back_body, rows=rows, keys=keys, blocks=blocks, count=count, span=span, group=group
        ),
        grid_spec=pltpu.PrefetchScalarGridSpec(
            num_scalar_prefetch=3,
            grid=(seqs, blocks),
            in_specs=[lower, upper, lower, upper, lower, upper, stat, table, table]
            + [full_spec(v.shape) for v in tables[2:]]
            + [pl.BlockSpec((1, span, 256), lambda s, b, *_: (s, 0, 0), pipeline_mode=pl.Buffered(1))] * count,
            out_specs=[out_lower, out_upper]
            + [pl.BlockSpec((1, span, 128), lambda s, b, *_: (s, 0, 0))] * count,
            scratch_shapes=[
                pltpu.VMEM((total, 128), BF16), pltpu.VMEM((total, 128), BF16), pltpu.VMEM((64, total), BF16),
                pltpu.VMEM((total, 128), F32), pltpu.VMEM((total, 128), F32), pltpu.VMEM((4, 64, rows), F32),
            ]
            + [pltpu.VMEM((4, keys, rows), F32)] * 4,
        ),
        out_shape=[half, half] + [jax.ShapeDtypeStruct((seqs, span, 128), BF16)] * count,
        compiler_params=params(),
        cost_estimate=cost(1 if group else 20),
        name="attend_backward",
    )(pos, lens, sources, q, other, do_near, do_far, o_near, o_far, lse, *tables, *kvs)
    return outs[0], outs[1], outs[2:]


def in_hbm(shape):
    return pltpu.HBM(shape, BF16)


def both(left, right):
    return dot(left[0][...], right[0][...], TN) + dot(left[1][...], right[1][...], TN)


def tall_body(place_ref, left_a, left_b, *rest, n, widths, square):
    rights = [rest[2 * k : 2 * k + 2] for k in range(len(widths))]
    outs = rest[2 * len(widths) :]
    rows = left_a.shape[1] // n
    i = pl.program_id(0)
    start = 0
    for part, (right, steps) in enumerate(zip(rights, widths)):

        @pl.when((i >= start) & (i < start + steps))
        def _(part=part, right=right):
            if square:
                if square == "hops":
                    own, to_x, keep_x, to_y, keep_y = outs
                    first, keep = ((to_x, keep_x), (to_y, keep_y))[part]
                for k in range(4):
                    block = jnp.bitwise_xor(place_ref[0], k)
                    columns = pl.ds(pl.multiple_of(block * rows, rows), rows)
                    value = low(both((left_a.at[:, columns], left_b.at[:, columns]), right))
                    if square == "direct":
                        outs[k][...] = value
                    elif k == 0:
                        own[...] = value
                    elif k == 3:
                        first[1] = value
                    elif k == part + 1:
                        first[0] = value
                    else:
                        keep[...] = value
            else:
                value = low(both((left_a, left_b), right))
                for j in range(n):
                    outs[0][j] = value[j * rows : (j + 1) * rows]

        start += steps


def tall_grad(place, left, rights, chunk, n, square="", micros=0.0, name="grad"):
    tokens, width = left[0].shape[0], left[3]
    widths = [v[3] // chunk for v in rights]
    steps = sum(widths)
    rows = width // n
    starts = [0, widths[0]]
    parts = range(len(rights))

    def within(k, i):
        return jnp.clip(i - starts[k], 0, widths[k] - 1)

    def right_spec(k):
        return pl.BlockSpec((tokens, chunk), lambda i, place: (0, rights[k][2] // chunk + within(k, i)))

    left_spec = pl.BlockSpec(
        (tokens, width), lambda i, place: (0, left[2] // width), pipeline_mode=pl.Buffered(1)
    )

    if square == "direct":
        out_specs = [pl.BlockSpec((rows, chunk), lambda i, place: (i, 0))] * 4
        out_shape = [in_hbm((steps * rows, chunk))] * 4
    elif square:
        out_specs = [pl.BlockSpec((rows, chunk), lambda i, place: (i, 0))]
        out_shape = [jax.ShapeDtypeStruct((steps * rows, chunk), BF16)]
        for k in parts:
            out_specs.append(pl.BlockSpec((2, rows, chunk), lambda i, place, k=k: (0, within(k, i), 0)))
            out_specs.append(pl.BlockSpec((rows, chunk), lambda i, place, k=k: (within(k, i), 0)))
            out_shape.append(in_hbm((2, widths[k] * rows, chunk)))
            out_shape.append(jax.ShapeDtypeStruct((widths[k] * rows, chunk), BF16))
    else:
        out_specs = pl.BlockSpec((n, rows, chunk), lambda i, place: (0, i, 0))
        out_shape = jax.ShapeDtypeStruct((n, steps * rows, chunk), BF16)
    return pl.pallas_call(
        functools.partial(tall_body, n=n, widths=widths, square=square),
        grid_spec=pltpu.PrefetchScalarGridSpec(
            num_scalar_prefetch=1,
            grid=(steps,),
            in_specs=[left_spec] * 2 + [right_spec(k) for k in parts for _ in range(2)],
            out_specs=out_specs,
        ),
        out_shape=out_shape,
        compiler_params=pltpu.CompilerParams(vmem_limit_bytes=VMEM_LIMIT),
        cost_estimate=cost(micros),
        name=name,
    )(place, *left[:2], *[v for right in rights for v in right[:2]])


PIECE = 256


def wide_body(place_ref, *rest, parts, group, square, split):
    lefts = [rest[2 * k : 2 * k + 2] for k in range(parts)]
    rights = [rest[2 * k : 2 * k + 2] for k in range(parts, 2 * parts)]
    outs = rest[4 * parts :]
    values = [low(both(left, right)) for left, right in zip(lefts, rights)]
    values = [v[:, c : c + PIECE] for v in values for c in range(0, v.shape[1], PIECE)]
    if square:
        own, to_x, keep_x, to_y, keep_y = outs
        value = jnp.concatenate(values, 0)
        for k in range(4):

            @pl.when(pl.program_id(0) == k)
            def _(k=k):
                if k == 0:
                    own[...] = value
                    return
                for part, (first, keep) in enumerate(((to_x, keep_x), (to_y, keep_y))):
                    here = value[split:] if part else value[:split]
                    if k == 3:
                        first[1] = here
                    elif k == part + 1:
                        first[0] = here
                    else:
                        keep[...] = here
    else:
        for j in range(group):
            start = 0
            for v in values:
                rows = v.shape[0] // group
                outs[0][j, start : start + rows] = v[j * rows : (j + 1) * rows]
                start += rows


def wide_grad(place, lefts, rights, n, square="", micros=0.0, name="grad"):
    tokens = lefts[0][0].shape[0]
    steps = min(n, 4)
    rows = [v[3] // n * (g[3] // PIECE) for v, g in zip(lefts, rights)]
    total = sum(rows)
    split = sum(rows[:2])

    def turn(i, place):
        return jnp.bitwise_xor(place[0], i) if square else i

    def once(*dims):
        return pl.BlockSpec(dims, lambda i, place: (0,) * len(dims), pipeline_mode=pl.Buffered(1))

    def left_spec(v):
        size = v[3] // steps
        return pl.BlockSpec((tokens, size), lambda i, place: (0, v[2] // size + turn(i, place)))

    def right_spec(v):
        return pl.BlockSpec((tokens, v[3]), lambda i, place: (0, v[2] // v[3]), pipeline_mode=pl.Buffered(1))

    if square:
        dims = [(total, PIECE)]
        for size in (split, total - split):
            dims += [(2, size, PIECE), (size, PIECE)]
        out_specs = [once(*d) for d in dims]
        out_shape = [in_hbm(d) for d in dims]
    else:
        out_specs = pl.BlockSpec((n // steps, total, PIECE), lambda i, place: (i, 0, 0))
        out_shape = jax.ShapeDtypeStruct((n, total, PIECE), BF16)
    return pl.pallas_call(
        functools.partial(wide_body, parts=len(lefts), group=n // steps, square=square, split=split),
        grid_spec=pltpu.PrefetchScalarGridSpec(
            num_scalar_prefetch=1,
            grid=(steps,),
            in_specs=[left_spec(v) for v in lefts for _ in range(2)] + [right_spec(v) for v in rights for _ in range(2)],
            out_specs=out_specs,
        ),
        out_shape=out_shape,
        compiler_params=pltpu.CompilerParams(vmem_limit_bytes=VMEM_LIMIT),
        cost_estimate=cost(micros),
        name=name,
    )(place, *[v for left in lefts for v in left[:2]], *[v for right in rights for v in right[:2]])


def in_place(body, args, outs, name, columns=None):
    def spec(shape):
        if columns is None:
            return full_spec(shape)
        return pl.BlockSpec((*shape[:-1], columns), lambda i: (0,) * (len(shape) - 1) + (i,))

    return pl.pallas_call(
        body,
        grid=(1 if columns is None else outs[0].shape[-1] // columns,),
        in_specs=[SCALARS if v.ndim == 1 else spec(v.shape) for v in args],
        out_specs=[spec(v.shape) for v in outs],
        out_shape=outs,
        compiler_params=pltpu.CompilerParams(vmem_limit_bytes=VMEM_LIMIT),
        cost_estimate=cost(0),
        name=name,
    )(*args)


def like(v):
    return in_hbm(v.shape)


def first_body(keep_x, keep_y, from_x, from_y, to_y, to_x):
    to_y[...] = low(keep_x[...].astype(F32) + from_x[1].astype(F32))
    to_x[...] = low(keep_y[...].astype(F32) + from_y[1].astype(F32))


def second_body(own, from_x, from_y, late_y, late_x, out):
    split = late_y.shape[0]
    for at, first, last in ((slice(0, split), from_x, late_y), (slice(split, None), from_y, late_x)):
        out[at] = low(own[at].astype(F32) + first[0].astype(F32) + last[...].astype(F32))


def sum_body(*refs):
    total = refs[0][...].astype(F32)
    for ref in refs[1:-1]:
        total = total + ref[...].astype(F32)
    refs[-1][...] = low(total)


def square_body(own, one, two, three, out):
    near = own[...].astype(F32) + one[...].astype(F32)
    out[...] = low(near + (two[...].astype(F32) + three[...].astype(F32)))


def unpack_body(at_ref, own, other, *rest, plan, summed, grads):
    weights = dict(zip(summed, rest))
    outs = rest[len(summed) : len(summed) + grads]
    sums = dict(zip(summed, rest[len(summed) + grads :]))
    first = at_ref[0] == 0
    totals = {}
    for out, column, columns, half, start, rows in plan:
        at = slice(start, start + rows)
        a, b = (own, other) if half == 0 else (other, own)
        value = jnp.where(first, a[at], b[at])[:, :columns].astype(F32)
        here = slice(column, column + columns)
        outs[out][:, here] = value
        if out in weights:
            part = jnp.sum(value * weights[out][:, here].astype(F32), 1, keepdims=True)
            totals[out] = totals[out] + part if out in totals else part
    for out, ref in sums.items():
        ref[...] = jnp.broadcast_to(totals[out], ref.shape)


def unpack(at, own, other, matrices):
    piece = own.shape[1]
    plan, shapes, weights, start = [], [], {}, 0
    for rows, pieces, parts in matrices:
        ends = np.cumsum([0] + [w.shape[1] for w, _ in parts])
        for half in range(2):
            for i in range(pieces):
                column = (half * pieces + i) * piece
                for k, (w, _) in enumerate(parts):
                    if ends[k] <= column < ends[k + 1]:
                        offset = int(column - ends[k])
                        plan.append(
                            (len(shapes) + k, offset, min(piece, w.shape[1] - offset), half, start + i * rows, rows)
                        )
        for w, wanted in parts:
            if wanted:
                weights[len(shapes)] = w
            shapes.append(jax.ShapeDtypeStruct((rows, w.shape[1]), F32))
        start += pieces * rows
    grads = len(shapes)
    summed = list(weights)
    shapes += [jax.ShapeDtypeStruct((shapes[k].shape[0], 128), F32) for k in summed]

    def whole(shape):
        return pl.BlockSpec(shape, lambda i, at: (0, 0))

    outs = pl.pallas_call(
        functools.partial(unpack_body, plan=plan, summed=summed, grads=grads),
        grid_spec=pltpu.PrefetchScalarGridSpec(
            num_scalar_prefetch=1,
            grid=(1,),
            in_specs=[whole(own.shape), whole(other.shape)]
            + [pl.BlockSpec(shapes[k].shape, lambda i, at: (at[1], 0)) for k in summed],
            out_specs=[whole(v.shape) for v in shapes],
        ),
        out_shape=shapes,
        compiler_params=pltpu.CompilerParams(vmem_limit_bytes=VMEM_LIMIT),
        cost_estimate=cost(0),
        name="unpack",
    )(at, own, other, *weights.values())
    return outs[:grads], [v[:, 0] for v in outs[grads:]]


def ring(value, steps):
    n = lax.axis_size("seq")
    return lax.ppermute(value, "seq", [(i, (i + steps) % n) for i in range(n)])


def along(value, steps):
    n = lax.axis_size("seq")
    return lax.ppermute(value, "seq", [(i, i + steps) for i in range(n) if 0 <= i + steps < n])


def mirror(value):
    n = lax.axis_size("seq")
    return lax.ppermute(value, "seq", [(i, n - 1 - i) for i in range(n)])


def flip_dp(value, bit):
    n = lax.axis_size("dp")
    return lax.ppermute(value, "dp", [(i, i ^ bit) for i in range(n)])


def other_core(value):
    return flip_dp(value, 1)


def after(value, *done):
    return lax.optimization_barrier((value, done))[0]


def scatter_seq(value):
    return lax.psum_scatter(value, "seq", scatter_dimension=0, tiled=True)[0]


def flip_seq(value, bit):
    n = lax.axis_size("seq")
    return lax.ppermute(value, "seq", [(i, i ^ bit) for i in range(n)])


def add_low(*values):
    return in_place(sum_body, values, [like(values[0])], "add")[0]


def direct_sum(pieces):
    return add_low(pieces[0], *[flip_seq(v, k) for k, v in enumerate(pieces) if k])


def first_hop(pieces, *done):
    own, to_x, keep_x, to_y, keep_y = pieces
    from_x, from_y = flip_seq(to_x, 1), flip_seq(to_y, 2)
    held = in_place(
        first_body, (after(keep_x, *done), keep_y, from_x, from_y), [like(keep_x), like(keep_y)], "first_hop"
    )
    return (*held, own, from_x, from_y)


def second_hop(held, *done):
    to_y, to_x, own, from_x, from_y = held
    args = (after(own, *done), from_x, from_y, flip_seq(to_y, 2), flip_seq(to_x, 1))
    return in_place(second_body, args, [like(own)], "second_hop")[0]


def offloaded_sum_z(value, which):
    n = lax.axis_size("dp")
    groups = [list(range(c, n, 2))[:: -1 if which & 1 else 1] for c in range(2)]
    return lax.psum(value, "dp", axis_index_groups=groups[:: -1 if which & 2 else 1])


def sum_four(value, *done):
    got = [flip_dp(value, bit) for bit in (2, 4, 6)]
    return in_place(square_body, (after(value, *done), *got), [like(value)], "add")[0]


def sum_z(value, first=2, last=None):
    bit = first
    while bit < (last or lax.axis_size("dp")):
        value = add_low(value, flip_dp(value, bit))
        bit *= 2
    return value


def on_device(
    tokens, cotangent, lengths, norm_one, w_query, w_key, w_value, w_gatez, w_conv_in, w_step, conv_weight,
    conv_bias, step_bias, decay_log, skip_gain, gated_gain, w_attn_out, w_mix_out, norm_two, w_gate, w_up, w_down,
):
    seqs, span, width = tokens.shape
    half = span // 2
    taps, conv_width = conv_weight.shape
    count = lax.axis_size("seq")
    place = lax.axis_index("seq").astype(jnp.int32)
    core = (lax.axis_index("dp") % 2).astype(jnp.int32)
    first = place * span
    mirrored = (count - 1 - place) * span + half
    row_tables = rotation(span, count, "rows")
    column_tables = rotation(span, count, "columns")
    rate = -jnp.exp(decay_log)
    pad = (0, 128 - SSM_HEADS)
    rate_row = jnp.pad(rate, pad)[None]
    step_row = jnp.pad(step_bias, pad)[None]
    w_step_wide = jnp.pad(w_step, ((0, 0), pad))
    skip_row = jnp.repeat(skip_gain, SSM_HEAD)[None]
    ones = (np.arange(WIDE)[None, :] // SSM_HEAD == np.arange(128)[:, None]).astype(np.float32)
    expand = jnp.asarray(np.concatenate([ones, ones], 0), BF16)
    pos = jnp.stack([first, core])
    core_here = core[None]
    rows = min(256, half)
    blocks = jnp.concatenate([base + jnp.arange(0, half, rows, dtype=jnp.int32) for base in (first, mirrored)])
    sources = lax.rem(place - jnp.arange(count, dtype=jnp.int32) + count, count)
    here = place[None]

    def flat(v):
        return v.reshape(seqs * span, v.shape[2])

    def with_other(mine, yours=None):
        mine, yours = flat(mine), flat(mine if yours is None else yours)
        return mine, other_core(yours), 0, mine.shape[1]

    halo = along(tokens[:, span - 16 :], 1)
    hidden, q, kv = enter(here, after(tokens, halo), norm_one[None], w_query, w_key, w_value, row_tables)
    kvs = [kv] + [ring(kv, r) for r in range(1, count)]
    q_other = mirror(q[:, half:])
    z, conv, pre, x, bk, cq, dt, sg, cum, cumt, state = mixer(
        pos, lengths, hidden, halo, norm_one[None], w_gatez, w_conv_in, w_step_wide, conv_weight, conv_bias[None],
        step_row, rate_row * LOG2E, expand,
    )
    states = lax.all_gather(state, "seq")
    skip_row, blocks, sources = [after(v, state) for v in (skip_row, blocks, sources)]
    gated_row = after(gated_gain, state)[None]
    gact = grad_act(pos, lengths, after(cotangent, state), w_down)
    o_near, o_far, lse = attend(blocks, lengths, sources, after(q, gact), q_other, kvs)
    o_back = mirror(o_far)
    mixed, mix_low, held = scan_forward(
        here, after(x, o_near), bk, cq, dt, cum, cumt, skip_row, z, gated_row, expand, states
    )
    hid = with_other(hidden)
    mix_pair = with_other(mix_low)
    output, lefts, mine, yours, grad_mid = middle(
        pos, lengths, o_near, o_back, after(mix_low, hid[1]), tokens, cotangent, gact, w_attn_out, w_mix_out, w_gate, w_up, w_down,
        norm_two[None],
    )
    square = "hops" if count == 4 else ""
    ff = w_gate.shape[1]
    lefts, rights = with_other(lefts), with_other(mine, yours)
    ffn_left = (*lefts[:2], 0, width)
    ffn_rights = [(*rights[:2], k * ff // 2, ff // 2) for k in range(2)]
    grad_ffn, grad_branch = [(*rights[:2], ff + k * width // 2, width // 2) for k in range(2)]
    out_lefts = ((*lefts[:2], width, ff), (*lefts[:2], width + ff, w_attn_out.shape[0]), mix_pair, hid)
    do_near, do_far, grad_mixed, gz_m, gz_y, adjoint = branch_back(
        core_here, mine, yours, mixed, z, cq, cum, w_attn_out, w_mix_out, gated_row, expand
    )
    adjoints = [along(adjoint, -r) for r in range(1, count)]
    part_ffn = tall_grad(after(here, do_near), ffn_left, ffn_rights, 512, count, square, name="grad_ffn_in")
    part_out = wide_grad(
        after(here, part_ffn[0], *adjoints), out_lefts, (grad_ffn, grad_branch, grad_branch, with_other(gz_m, gz_y)), count,
        square, micros=16, name="grad_outs",
    )
    ffn_held = first_hop(part_ffn, part_out[0]) if square else scatter_seq(part_ffn)
    gc_m, gc_y, tail, head, g_conv_small, g_skip, g_small = scan_backward(
        after(x, part_out[0], ffn_held), bk, cq, dt, sg, cum, cumt, grad_mixed, mixed, held, pre, conv, skip_row, rate_row,
        conv_weight, expand, core_here, adjoints,
    )
    do_other = mirror(after(do_far, head))
    ffn_sum = second_hop(ffn_held) if square else ffn_held
    out_held = first_hop([after(v, ffn_held) for v in part_out]) if square else scatter_seq(part_out)
    head = after(head, ffn_sum, out_held)
    ffn_sum = offloaded_sum_z(ffn_sum, 0)
    returned = along(low(head), -1).astype(F32)[:, : taps - 1]
    g_conv_weight = g_conv_small[:taps]
    beside = ((0, 0), (0, 0), (0, tail.shape[2] - conv_width))
    for ahead in range(1, taps):
        tap = taps - 1 - ahead
        fill = jnp.pad(returned[:, :ahead], ((0, 0), (8 - ahead, 0), (0, 0)))
        tail = tail + jnp.pad(conv_weight[tap] * fill, beside)
        g_conv_weight = g_conv_weight.at[tap].add(jnp.sum(fill * conv[:, span - 8 :].astype(F32), (0, 1)))
    tail = low(tail)
    size = tail.shape[2] // 2
    tails = tail[:, :, :size], tail[:, :, size:]
    gc_m, gc_y = [
        lax.dynamic_update_slice(v, jnp.where(core == i, *tails), (0, span - 8, 0)) for i, v in enumerate((gc_m, gc_y))
    ]
    part_in = tall_grad(
        here, hid, (with_other(gc_m, gc_y),), 256, count, "direct" if square else "", name="grad_conv_in"
    )
    small = [
        g_conv_weight.reshape(-1), g_conv_small[taps], g_skip[0],
        g_small[0], g_small[1],
    ]
    sizes = [v.shape[0] for v in small]
    total = jnp.concatenate(small)
    total = jnp.pad(total, (0, -total.shape[0] % 1024)).reshape(-1, 128)
    hops = [("seq", 1 << k) for k in range(count.bit_length() - 1)]
    hops += [("dp", 2 << k) for k in range(lax.axis_size("dp").bit_length() - 2)] + [("dp", 1)]

    def flip(value, axis, bit):
        return flip_seq(value, bit) if axis == "seq" else flip_dp(value, bit)

    def small_step(total):
        axis, bit = hops.pop(0)
        return total + flip(total, axis, bit)

    def back(group, order):
        near, far, parts = attend_backward(
            group, blocks, lengths, sources, after(q, *order), q_other, do_near, do_other, o_near, o_far, lse,
            column_tables, kvs,
        )
        return near, mirror(far), [parts[0]] + [ring(parts[r], -r) for r in range(1, count)]

    dq_near, dq_far, pieces = back(0, (part_in[0],))
    out_sum = second_hop(out_held, dq_near) if square else out_held
    in_sum = direct_sum([after(part_in[0], dq_near), *part_in[1:]]) if square else scatter_seq(part_in)
    results = back(1, (dq_near, in_sum, ffn_sum, out_sum))
    four = lax.axis_size("dp") == 8
    out_sum, in_sum = offloaded_sum_z((out_sum, in_sum), 1)
    total = small_step(after(total, dq_near))
    gh = leave_mixer(
        core_here, (after(gz_m, results[0], dq_far, total, *pieces), gz_y), (gc_m, gc_y), w_gatez, w_conv_in, w_step_wide
    )
    total = small_step(after(total, results[0]))
    heads = heads_back(
        core_here, after(here, gh, total), row_tables, (dq_near, results[0]), (dq_far, results[1]), pieces + results[2]
    )
    heads_pairs = with_other(*heads[:2]), with_other(*heads[2:])
    part_qkv = tall_grad(here, hid, heads_pairs, 128, count, square, name="grad_qkv")
    grad_tokens = leave(
        core_here, tokens, grad_mid, after(gh, part_qkv[0], out_sum, in_sum), heads, norm_one[None], w_query, w_key, w_value
    )
    total = small_step(after(total, part_qkv[0]))
    at = jnp.stack([core, place])

    def matrix(pieces, *weights, wanted=True):
        return weights[0].shape[0] // count, pieces, [(w, wanted) for w in weights]

    done = (total, grad_tokens)
    qkv_held = first_hop(part_qkv, *done) if square else scatter_seq(part_qkv)
    ffn_sum = after(ffn_sum, heads[0])
    (s_gate, s_up), two_sums = unpack(
        at, after(ffn_sum, qkv_held), other_core(ffn_sum), [matrix(2, w_gate), matrix(2, w_up)]
    )
    total = small_step(after(total, qkv_held))
    qkv_sum = second_hop(qkv_held, total, s_gate) if square else qkv_held
    out_sum, in_sum = [after(v, qkv_held) for v in (out_sum, in_sum)]
    (s_down, s_attn_out, s_mix_out, s_gatez), (gated_sum, z_sum) = unpack(
        at, after(out_sum, qkv_sum), other_core(out_sum),
        [matrix(2, w_down, wanted=False), matrix(2, w_attn_out, wanted=False), matrix(2, w_mix_out), matrix(3, w_gatez)],
    )
    (s_conv, s_step), in_sums = unpack(
        at, after(in_sum, qkv_sum), other_core(in_sum), [matrix(4, w_conv_in, w_step)]
    )
    if four:
        total = small_step(after(total, qkv_sum))
        qkv_sum = sum_four(qkv_sum, s_conv, s_down, total)
    else:
        qkv_sum = sum_z(qkv_sum)
    got = other_core(qkv_sum)
    while hops:
        total = small_step(total)
    (s_query, s_key, s_value), qkv_sums = unpack(at, qkv_sum, got, [matrix(2, w_query), matrix(1, w_key, w_value)])
    total = total.reshape(-1)
    starts = np.cumsum([0] + sizes)
    small = [total[a:b] for a, b in zip(starts[:-1], starts[1:])]

    def own(v):
        n = v.shape[0] // count
        return lax.dynamic_slice(v, (place * n,), (n,))

    s_norm_one = (z_sum + in_sums[0] + in_sums[1] + qkv_sums[0] + qkv_sums[1] + qkv_sums[2]) / own(norm_one)
    s_norm_two = (two_sums[0] + two_sums[1]) / own(norm_two)
    s_gated = gated_sum / own(gated_gain)
    s_skip = jnp.sum(small[2].reshape(SSM_HEADS, SSM_HEAD), 1)
    return (
        output,
        grad_tokens,
        s_norm_one,
        s_query,
        s_key,
        s_value,
        s_gatez,
        s_conv,
        s_step,
        small[0].reshape(taps, -1),
        small[1],
        small[4][:SSM_HEADS],
        small[3][:SSM_HEADS],
        s_skip,
        s_gated,
        s_attn_out,
        s_mix_out,
        s_norm_two,
        s_gate,
        s_up,
        s_down,
    )


def solution(mesh):
    copied = (P(),) * 19
    return jax.shard_map(
        on_device,
        mesh=mesh,
        in_specs=(P("dp", "seq", None), P("dp", "seq", None), P("dp")) + copied,
        out_specs=(
            P("dp", "seq", None), P("dp", "seq", None), P("seq"),
            P("seq", None), P("seq", None), P("seq", None), P("seq", None), P("seq", None), P("seq", None),
            P(), P(), P(), P(), P(),
            P("seq"), P("seq", None), P("seq", None), P("seq"), P("seq", None), P("seq", None), P("seq", None),
        ),
        check_vma=False,
    )
```

```python
import functools

import jax
import jax.numpy as jnp
import numpy as np
from jax import lax
from jax.experimental import pallas as pl
from jax.experimental.pallas import tpu as pltpu
from jax.sharding import PartitionSpec as P

HEADS = 8
KV_HEADS = 2
HEAD = 64
SSM_HEADS = 24
SSM_HEAD = 64
STATE = 128
WIDE = SSM_HEADS * SSM_HEAD
CHUNK = 128
EPS = 1e-05
ROPE_BASE = 100000000000.0
LOG2E = 1.4426950408889634
SCORE2 = 0.125 * LOG2E
LOWEST = -1e30
F32 = jnp.float32
BF16 = jnp.bfloat16
NN = (((1,), (0,)), ((), ()))
NT = (((1,), (1,)), ((), ()))
TN = (((0,), (0,)), ((), ()))
VMEM_LIMIT = 127 << 19


def dot(a, b, dims=NN):
    return lax.dot_general(a, b, dims, preferred_element_type=F32)


def dot_exact(a, b, dims=NN):
    return lax.dot_general(a, b, dims, precision=lax.Precision.HIGHEST, preferred_element_type=F32)


def low(v):
    return v.astype(BF16)


def sigmoid(v):
    return jax.nn.sigmoid(v)


def softplus(v):
    e = jnp.exp(-jnp.abs(v))
    tail = jnp.where(e < 1e-2, e * (1.0 - e * (0.5 - e * (1.0 / 3.0))), jnp.log(1.0 + e))
    return jnp.maximum(v, 0.0) + tail


def split_low(v):
    high = low(v)
    return high, low(v - high.astype(F32))


def widen(v, expand):
    return dot(jnp.concatenate(split_low(v), 1), expand)


def head_sums(v, expand):
    high, rest = split_low(v)
    ones = expand[:128]
    return dot(high, ones, NT) + dot(rest, ones, NT)


def cost(micros):
    return pl.CostEstimate(flops=int(micros * 3e9), bytes_accessed=int(micros * 1e5), transcendentals=0)


def full_spec(shape):
    return pl.BlockSpec(shape, lambda *_: (0,) * len(shape), pipeline_mode=pl.Buffered(1))


def params(limit=VMEM_LIMIT):
    return pltpu.CompilerParams(
        vmem_limit_bytes=limit, dimension_semantics=("arbitrary", "arbitrary")
    )


SCALARS = pl.BlockSpec(memory_space=pltpu.SMEM)


def halves_out(core, values, mine_ref, yours_ref):
    first = core == 0
    start = 0
    for value in values:
        size = value.shape[1] // 2
        lower, upper = value[:, :size], value[:, size:]
        mine_ref[0, :, start : start + size] = jnp.where(first, lower, upper)
        yours_ref[0, :, start : start + size] = jnp.where(first, upper, lower)
        start += size


def halves_in(core, mine, yours):
    first = core == 0
    return jnp.concatenate([jnp.where(first, mine, yours), jnp.where(first, yours, mine)], 1)


def low_rows(rows):
    t = lax.broadcasted_iota(jnp.int32, (rows, rows), 0)
    u = lax.broadcasted_iota(jnp.int32, (rows, rows), 1)
    return t >= u


def rotation(span, count, order):
    inverse = (1.0 / np.float64(ROPE_BASE) ** (np.arange(0, HEAD, 2) / HEAD)).astype(np.float32).astype(np.float64)
    steps = np.arange(span)[:, None] * inverse
    starts = (np.arange(count) * span)[:, None] * inverse
    if order == "rows":
        sign = np.tile(np.repeat([-1.0, 1.0], HEAD // 2), 2)
        made = [np.tile(np.cos(steps), 4), np.tile(np.sin(steps), 4) * sign]
        made += [np.tile(np.cos(starts), 4)[:, None], (np.tile(np.sin(starts), 4) * sign)[:, None]]
    else:
        made = [np.cos(steps).T, np.sin(steps).T]
        made += [np.repeat(f(starts)[:, :, None], 128, 2) for f in (np.cos, np.sin)]
    return [jnp.asarray(v.astype(np.float32)) for v in made]


def turned(step_cos, step_sin, start_cos, start_sin):
    return start_cos * step_cos - start_sin * step_sin, start_sin * step_cos + start_cos * step_sin


def swap_halves(v):
    lane = lax.broadcasted_iota(jnp.int32, v.shape, 1)
    return jnp.where((lane & 63) < 32, pltpu.roll(v, 96, 1), pltpu.roll(v, 32, 1))


def pair_rows(v):
    lane = lax.broadcasted_iota(jnp.int32, v.shape, 1)
    none = jnp.zeros_like(v)
    return jnp.concatenate([jnp.where(lane < 64, v, none), jnp.where(lane >= 64, v, none)], 0)


def first_norm(v, gain):
    v = v.astype(F32)
    return low(v * lax.rsqrt(jnp.mean(v * v, -1, keepdims=True) + EPS) * gain)


def enter_body(
    place_ref, tok_ref, gain_ref, wq_ref, wk_ref, wv_ref, cos_ref, sin_ref, cos0_ref, sin0_ref, hid_ref, q_ref, kv_ref
):
    hid = first_norm(tok_ref[0], gain_ref[...])
    hid_ref[0] = hid
    place = place_ref[0]
    cosine, sine = turned(cos_ref[...], sin_ref[...], cos0_ref[place], sin0_ref[place])
    t = dot(hid, wk_ref[...])
    kv_ref[0, :, :128] = low(t * cosine + swap_halves(t) * sine)
    kv_ref[0, :, 128:] = low(dot(hid, wv_ref[...]))
    q = dot(hid, wq_ref[...])
    for g in range(4):
        t = q[:, g * 128 : g * 128 + 128]
        q_ref[0, :, g * 128 : g * 128 + 128] = low(t * cosine + swap_halves(t) * sine)


def enter(place, tokens, gain, wq, wk, wv, tables):
    seqs, span, width = tokens.shape
    rows = min(512, span)

    def row(n):
        return pl.BlockSpec((1, rows, n), lambda s, b: (s, b, 0))

    table = pl.BlockSpec((rows, 128), lambda s, b: (b, 0))
    return pl.pallas_call(
        enter_body,
        grid=(seqs, span // rows),
        in_specs=[SCALARS, row(width)]
        + [full_spec(v.shape) for v in (gain, wq, wk, wv)]
        + [table, table]
        + [full_spec(v.shape) for v in tables[2:]],
        out_specs=[row(width), row(512), row(256)],
        out_shape=[jax.ShapeDtypeStruct((seqs, span, n), BF16) for n in (width, 512, 256)],
        compiler_params=params(),
        cost_estimate=cost(8),
        name="enter",
    )(place, tokens, gain, wq, wk, wv, *tables)


def mixer_body(
    pos_ref, len_ref, hid_ref, halo_ref, gain_ref, wz_ref, wc_ref, ws_ref, cw_ref, cb_ref, sb_ref, a_ref, exp_ref,
    z_ref, cl_ref, pre_ref, x_ref, bk_ref, cq_ref, dt_ref, sg_ref, cum_ref, cumt_ref, st_ref,
    prev, state, total, *, rows, blocks,
):
    s = pl.program_id(0)
    b = pl.program_id(1)

    @pl.when(b == 0)
    def _():
        prev[...] = dot(first_norm(halo_ref[0], gain_ref[...]), wc_ref[...])[8:]
        state[...] = jnp.zeros_like(state)
        total[...] = jnp.zeros_like(total)

    hid = hid_ref[0]
    conv = dot(hid, wc_ref[...])
    raw = dot(hid, ws_ref[...]) + sb_ref[...]
    z_ref[0] = low(dot(hid, wz_ref[...]))
    cl_ref[0] = low(conv)
    ext = jnp.concatenate([prev[...], conv], 0)
    prev[...] = conv[rows - 8 :]
    pre = cb_ref[...] + cw_ref[3:4] * conv
    for back in range(1, 4):
        pre = pre + cw_ref[3 - back : 4 - back] * pltpu.roll(ext, back, 0)[8:]
    pre_ref[0] = low(pre)
    act = low(pre * sigmoid(pre))
    x = act[:, :WIDE]
    bk = act[:, WIDE : WIDE + STATE]
    x_ref[0] = x
    bk_ref[0] = bk
    cq_ref[0] = act[:, WIDE + STATE :]
    at = pos_ref[0] + b * rows + lax.broadcasted_iota(jnp.int32, raw.shape, 0)
    live = jnp.where(at < len_ref[s], 1.0, 0.0)
    dt = softplus(raw) * live
    dt_ref[0] = dt
    sg_ref[0] = sigmoid(raw) * live
    log_decay = dt * a_ref[...]
    tri = jnp.where(low_rows(CHUNK), 1.0, 0.0)
    for c in range(rows // CHUNK):
        here = slice(c * CHUNK, (c + 1) * CHUNK)
        cum = dot_exact(tri, log_decay[here])
        cum_ref[0, here] = cum
        cumt_ref[0, :, here] = cum.T[:32]
        last = cum[CHUNK - 1 :]
        weight = dt[here] * jnp.exp2(last - cum)
        wide = widen(
            jnp.concatenate([weight, jnp.broadcast_to(jnp.exp2(last), (16, 128))], 0), exp_ref[...]
        )
        xw = low(x[here].astype(F32) * wide[:CHUNK])
        state[...] = state[...] * wide[CHUNK : CHUNK + 1] + dot(bk[here], xw, TN)
        total[...] = total[...] + last

    @pl.when(b == blocks - 1)
    def _():
        st_ref[0, :STATE] = low(state[...])
        st_ref[0, STATE:] = total_rows(total[...], exp_ref[...])


def total_rows(total, expand):
    wide = widen(jnp.broadcast_to(total, (8, 128)), expand)
    high = wide.astype(BF16).astype(F32)
    return low(jnp.concatenate([high, wide - high], 0))


def mixer(pos, lens, hid, halo, gain, wz, wc, ws, cw, cb, sb, a, expand):
    seqs, span, width = hid.shape
    rows = min(256, span)
    blocks = span // rows
    conv_width = wc.shape[1]

    def row(n):
        return pl.BlockSpec((1, rows, n), lambda s, b, *_: (s, b, 0))

    def shape(n, kind):
        return jax.ShapeDtypeStruct((seqs, span, n), kind)

    return pl.pallas_call(
        functools.partial(mixer_body, rows=rows, blocks=blocks),
        grid_spec=pltpu.PrefetchScalarGridSpec(
            num_scalar_prefetch=2,
            grid=(seqs, blocks),
            in_specs=[row(width), pl.BlockSpec((1, 16, width), lambda s, b, *_: (s, 0, 0))]
            + [full_spec(v.shape) for v in (gain, wz, wc, ws, cw, cb, sb, a, expand)],
            out_specs=[
                row(WIDE), row(conv_width), row(conv_width), row(WIDE), row(STATE), row(STATE),
                row(128), row(128), row(128),
                pl.BlockSpec((1, 32, rows), lambda s, b, *_: (s, 0, b)),
                pl.BlockSpec((1, STATE + 16, WIDE), lambda s, b, *_: (s, 0, 0)),
            ],
            scratch_shapes=[
                pltpu.VMEM((8, conv_width), F32), pltpu.VMEM((STATE, WIDE), F32), pltpu.VMEM((1, 128), F32),
            ],
        ),
        out_shape=[
            shape(WIDE, BF16), shape(conv_width, BF16), shape(conv_width, BF16), shape(WIDE, BF16),
            shape(STATE, BF16), shape(STATE, BF16), shape(128, F32), shape(128, F32), shape(128, F32),
            jax.ShapeDtypeStruct((seqs, 32, span), F32),
            jax.ShapeDtypeStruct((seqs, STATE + 16, WIDE), BF16),
        ],
        compiler_params=params(),
        cost_estimate=cost(20),
        name="mixer",
    )(pos, lens, hid, halo, gain, wz, wc, ws, cw, cb, sb, a, expand)


def joined(place, ref):
    state = jnp.zeros((STATE, WIDE), F32)
    for i in range(ref.shape[0]):
        logs = ref[i, 0, STATE : STATE + 1].astype(F32) + ref[i, 0, STATE + 8 : STATE + 9].astype(F32)
        state = jnp.where(i < place, state * jnp.exp2(logs) + ref[i, 0, :STATE].astype(F32), state)
    return state


def joined_later(refs):
    state = jnp.zeros((STATE, WIDE), F32)
    for ref in reversed(refs):
        logs = ref[0, STATE : STATE + 1].astype(F32) + ref[0, STATE + 8 : STATE + 9].astype(F32)
        state = state * jnp.exp2(logs) + ref[0, :STATE].astype(F32)
    return state


def gathered_spec(states):
    return pl.BlockSpec((states.shape[0], 1) + states.shape[2:], lambda s, c: (0, s, 0, 0), pipeline_mode=pl.Buffered(1))


def scan_body(
    place_ref, x_ref, bk_ref, cq_ref, dt_ref, cum_ref, cumt_ref, skip_ref, z_ref, gain_ref, exp_ref, all_ref,
    mix_ref, low_ref, st_ref, state, y,
):
    c = pl.program_id(1)

    @pl.when(c == 0)
    def _():
        state[...] = joined(place_ref[0], all_ref)

    x = x_ref[0].astype(F32)
    bk, cq = bk_ref[0], cq_ref[0]
    cum = cum_ref[0]
    last = cum[CHUNK - 1 :]
    expand = exp_ref[...]
    xdt = x * widen(dt_ref[0], expand)
    ends = widen(
        jnp.concatenate([jnp.exp2(cum), jnp.exp2(last - cum), jnp.broadcast_to(jnp.exp2(last), (16, 128))], 0),
        expand,
    )
    inter = jnp.where(low_rows(CHUNK), dot(cq, bk, NT), 0.0)
    held = low(state[...])
    st_ref[0, 0] = held
    y[...] = dot(cq, held) * ends[:CHUNK] + skip_ref[...] * x
    state[...] = state[...] * ends[2 * CHUNK : 2 * CHUNK + 1] + dot(bk, low(xdt * ends[CHUNK : 2 * CHUNK]), TN)
    xdt = low(xdt)
    for p in range(SSM_HEADS // 2):
        parts = []
        for h in (2 * p, 2 * p + 1):
            differ = jnp.minimum(cum[:, h : h + 1] - cumt_ref[0, h : h + 1, :], 0.0)
            parts.append(low(inter * jnp.exp2(differ)))
        cols = slice(p * 128, p * 128 + 128)
        y[:, cols] += dot(jnp.concatenate(parts, 1), pair_rows(xdt[:, cols]))
    mixed = y[...]
    mix_ref[0] = mixed
    z = z_ref[0].astype(F32)
    v = mixed * (z * sigmoid(z))
    low_ref[0] = low(v * lax.rsqrt(jnp.mean(v * v, -1, keepdims=True) + EPS) * gain_ref[...])


def scan_forward(place, x, bk, cq, dt, cum, cumt, skip, z, gain, expand, states):
    seqs, span, _ = x.shape
    chunks = span // CHUNK

    def row(n):
        return pl.BlockSpec((1, CHUNK, n), lambda s, c: (s, c, 0))

    return pl.pallas_call(
        scan_body,
        grid=(seqs, chunks),
        in_specs=[
            SCALARS, row(WIDE), row(STATE), row(STATE), row(128), row(128),
            pl.BlockSpec((1, 32, CHUNK), lambda s, c: (s, 0, c)),
            full_spec(skip.shape), row(WIDE), full_spec(gain.shape), full_spec(expand.shape), gathered_spec(states),
        ],
        out_specs=[row(WIDE), row(WIDE), pl.BlockSpec((1, 1, STATE, WIDE), lambda s, c: (s, c, 0, 0))],
        out_shape=[
            jax.ShapeDtypeStruct((seqs, span, WIDE), F32),
            jax.ShapeDtypeStruct((seqs, span, WIDE), BF16),
            jax.ShapeDtypeStruct((seqs, chunks, STATE, WIDE), BF16),
        ],
        scratch_shapes=[pltpu.VMEM((STATE, WIDE), F32), pltpu.VMEM((CHUNK, WIDE), F32)],
        compiler_params=params(),
        cost_estimate=cost(16),
        name="scan_forward",
    )(place, x, bk, cq, dt, cum, cumt, skip, z, gain, expand, states)


def live_rows(pos_ref, len_ref, rows):
    at = pos_ref[0] + pl.program_id(1) * rows + lax.broadcasted_iota(jnp.int32, (rows, 1), 0)
    return jnp.where(at < len_ref[pl.program_id(0)], 1.0, 0.0)


def grad_act_body(pos_ref, len_ref, cot_ref, wd_ref, out_ref, *, rows):
    gffn = low(live_rows(pos_ref, len_ref, rows) * cot_ref[0].astype(F32))
    out_ref[0] = low(dot(gffn, wd_ref[...], NT))


def grad_act(pos, lens, cot, wd):
    seqs, span, width = cot.shape
    rows = min(256, span)
    ff = wd.shape[0]
    return pl.pallas_call(
        functools.partial(grad_act_body, rows=rows),
        grid_spec=pltpu.PrefetchScalarGridSpec(
            num_scalar_prefetch=2,
            grid=(seqs, span // rows),
            in_specs=[pl.BlockSpec((1, rows, width), lambda s, b, *_: (s, b, 0)), full_spec(wd.shape)],
            out_specs=pl.BlockSpec((1, rows, ff), lambda s, b, *_: (s, b, 0)),
        ),
        out_shape=jax.ShapeDtypeStruct((seqs, span, ff), BF16),
        compiler_params=params(),
        cost_estimate=cost(0),
        name="grad_act",
    )(pos, lens, cot, wd)


def middle_body(
    pos_ref, len_ref, near_ref, far_ref, mix_ref, tok_ref, cot_ref, gact_ref,
    wao_ref, wmo_ref, wg_ref, wu_ref, wd_ref, gain2_ref,
    out_ref, left_ref, mine_ref, yours_ref, gmid_ref, *, rows, blocks,
):
    b = pl.program_id(1)
    live = live_rows(pos_ref, len_ref, rows)
    attn = jnp.where(b < blocks // 2, near_ref[0], far_ref[0])
    width, ff = wd_ref.shape[1], wd_ref.shape[0]
    left_ref[0, :, width + ff :] = attn
    branch = dot(attn, wao_ref[...]) + dot(mix_ref[0], wmo_ref[...])
    after = tok_ref[0].astype(F32) + live * branch
    scale = lax.rsqrt(jnp.mean(after * after, -1, keepdims=True) + EPS)
    unit = after * scale
    gain = gain2_ref[...]
    h2 = low(unit * gain)
    left_ref[0, :, :width] = h2
    gate = dot(h2, wg_ref[...])
    up = dot(h2, wu_ref[...])
    sg = sigmoid(gate)
    silu = gate * sg
    act = low(silu * up)
    left_ref[0, :, width : width + ff] = act
    out_ref[0] = low(after + live * dot(act, wd_ref[...]))
    cot = cot_ref[0].astype(F32)
    gffn = low(live * cot)
    gact = gact_ref[0].astype(F32)
    gg = low(gact * up * (sg * (1.0 + gate * (1.0 - sg))))
    gu = low(gact * silu)
    gh2 = dot(gg, wg_ref[...], NT) + dot(gu, wu_ref[...], NT)
    g = gh2 * gain
    gmid = cot + scale * (g - unit * jnp.mean(g * unit, -1, keepdims=True))
    gmid_ref[0] = low(gmid)
    halves_out(pos_ref[1], (gg, gu, gffn, low(live * gmid)), mine_ref, yours_ref)


def middle(pos, lens, near, far, mix, tokens, cot, gact, wao, wmo, wg, wu, wd, gain2):
    seqs, span, width = tokens.shape
    rows = min(256, span // 2)
    blocks = span // rows
    ff = wg.shape[1]
    lower = pl.BlockSpec((1, rows, 512), lambda s, b, *_: (s, jnp.minimum(b, blocks // 2 - 1), 0))
    upper = pl.BlockSpec((1, rows, 512), lambda s, b, *_: (s, jnp.maximum(b - blocks // 2, 0), 0))

    def row(n):
        return pl.BlockSpec((1, rows, n), lambda s, b, *_: (s, b, 0))

    def shape(n, kind):
        return jax.ShapeDtypeStruct((seqs, span, n), kind)

    return pl.pallas_call(
        functools.partial(middle_body, rows=rows, blocks=blocks),
        grid_spec=pltpu.PrefetchScalarGridSpec(
            num_scalar_prefetch=2,
            grid=(seqs, blocks),
            in_specs=[lower, upper, row(WIDE), row(width), row(width), row(ff)]
            + [full_spec(v.shape) for v in (wao, wmo, wg, wu, wd, gain2)],
            out_specs=[
                row(width), row(width + ff + 512), row(width + ff), row(width + ff), row(width),
            ],
        ),
        out_shape=[
            shape(width, BF16), shape(width + ff + 512, BF16), shape(width + ff, BF16), shape(width + ff, BF16),
            shape(width, BF16),
        ],
        compiler_params=params(),
        cost_estimate=cost(45),
        name="middle",
    )(pos, lens, near, far, mix, tokens, cot, gact, wao, wmo, wg, wu, wd, gain2)


def branch_body(
    core_ref, gb_m, gb_y, mixed_ref, z_ref, cq_ref, cum_ref, wao_ref, wmo_ref, gated_ref, exp_ref,
    gnear_ref, gfar_ref, gmixed_ref, gz_m, gz_y, adj_ref, adj, offset, *, rows, blocks,
):
    b = pl.program_id(1)

    @pl.when(b == 0)
    def _():
        adj[...] = jnp.zeros_like(adj)
        offset[...] = jnp.zeros_like(offset)

    core = core_ref[0]
    gb = halves_in(core, gb_m[0], gb_y[0])
    gattn = low(dot(gb, wao_ref[...], NT))

    @pl.when(b < blocks // 2)
    def _():
        gnear_ref[0] = gattn

    @pl.when(b >= blocks // 2)
    def _():
        gfar_ref[0] = gattn

    gn = low(dot(gb, wmo_ref[...], NT)).astype(F32)
    mixed = mixed_ref[0]
    z = z_ref[0].astype(F32)
    sg = sigmoid(z)
    silu = z * sg
    v = mixed * silu
    scale = lax.rsqrt(jnp.mean(v * v, -1, keepdims=True) + EPS)
    unit = v * scale
    g = gn * gated_ref[...]
    g = scale * (g - unit * jnp.mean(g * unit, -1, keepdims=True))
    gmixed = g * silu
    gmixed_ref[0] = low(gmixed)
    halves_out(core, (low(g * mixed * (sg * (1.0 + z * (1.0 - sg)))),), gz_m, gz_y)
    cum = cum_ref[0]
    logs = []
    for c in range(rows // CHUNK):
        here = cum[c * CHUNK : (c + 1) * CHUNK]
        logs.append(here + offset[...])
        offset[...] += here[CHUNK - 1 :]
    wide = widen(jnp.exp2(jnp.concatenate(logs, 0)), exp_ref[...])
    adj[...] += dot(cq_ref[0], low(gmixed * wide), TN)

    @pl.when(b == blocks - 1)
    def _():
        adj_ref[0, :STATE] = low(adj[...])
        adj_ref[0, STATE:] = total_rows(offset[...], exp_ref[...])


def branch_back(core, mine, yours, mixed, z, cq, cum, wao, wmo, gated, expand):
    seqs, span, packed = mine.shape
    half_width = wao.shape[1] // 2
    gb = pl.BlockSpec((1, min(256, span // 2), half_width), lambda s, b: (s, b, packed // half_width - 1))
    rows = min(256, span // 2)
    blocks = span // rows
    lower = pl.BlockSpec((1, rows, 512), lambda s, b: (s, jnp.minimum(b, blocks // 2 - 1), 0))
    upper = pl.BlockSpec((1, rows, 512), lambda s, b: (s, jnp.maximum(b - blocks // 2, 0), 0))

    def row(n):
        return pl.BlockSpec((1, rows, n), lambda s, b: (s, b, 0))

    def shape(n, kind):
        return jax.ShapeDtypeStruct((seqs, span, n), kind)

    half = jax.ShapeDtypeStruct((seqs, span // 2, 512), BF16)
    return pl.pallas_call(
        functools.partial(branch_body, rows=rows, blocks=blocks),
        grid=(seqs, blocks),
        in_specs=[SCALARS, gb, gb, row(WIDE), row(WIDE), row(STATE), row(128)]
        + [full_spec(v.shape) for v in (wao, wmo, gated, expand)],
        out_specs=[
            lower, upper, row(WIDE), row(WIDE // 2), row(WIDE // 2),
            pl.BlockSpec((1, STATE + 16, WIDE), lambda s, b: (s, 0, 0)),
        ],
        out_shape=[
            half, half, shape(WIDE, BF16), shape(WIDE // 2, BF16), shape(WIDE // 2, BF16),
            jax.ShapeDtypeStruct((seqs, STATE + 16, WIDE), BF16),
        ],
        scratch_shapes=[pltpu.VMEM((STATE, WIDE), F32), pltpu.VMEM((1, 128), F32)],
        compiler_params=params(),
        cost_estimate=cost(6),
        name="branch_back",
    )(core, mine, yours, mixed, z, cq, cum, wao, wmo, gated, expand)


def scan_back_body(
    x_ref, bk_ref, cq_ref, dt_ref, sg_ref, cum_ref, cumt_ref, dy_ref, mix_ref, st_ref, pre_ref, cl_ref,
    skip_ref, a_ref, cw_ref, exp_ref, core_ref, *rest, chunks, conv_width,
):
    *later, gc_m, gc_y, tail_ref, head_ref, gw_ref, gskip_ref, small_ref, adj, after, gact = rest
    s = pl.program_id(0)
    c = pl.program_id(1)

    @pl.when((s == 0) & (c == 0))
    def _():
        gw_ref[...] = jnp.zeros_like(gw_ref)
        gskip_ref[...] = jnp.zeros_like(gskip_ref)
        small_ref[...] = jnp.zeros_like(small_ref)

    @pl.when(c == 0)
    def _():
        adj[...] = joined_later(later)
        after[...] = jnp.zeros_like(after)

    x = x_ref[0].astype(F32)
    bk, cq = bk_ref[0], cq_ref[0]
    dt = dt_ref[0]
    cum = cum_ref[0]
    last = cum[CHUNK - 1 :]
    expand = exp_ref[...]
    dt_wide = widen(dt, expand)
    ends = widen(
        jnp.concatenate([jnp.exp2(cum), jnp.exp2(last - cum), jnp.broadcast_to(jnp.exp2(last), (16, 128))], 0),
        expand,
    )
    to_end = ends[CHUNK : 2 * CHUNK]
    all_wide = ends[2 * CHUNK : 2 * CHUNK + 1]
    xdt = x * dt_wide
    dy_low = dy_ref[0]
    dy = dy_low.astype(F32)
    dy_in = low(dy * ends[:CHUNK])
    state = st_ref[0, 0]
    gstate = adj[...]
    gstate_low = low(gstate)
    from_end = dot(bk, gstate_low) * to_end
    gb = dot(low(xdt * to_end), gstate_low, NT)
    gc = dot(dy_in, state, NT)
    gfinal = all_wide * jnp.sum(gstate * state.astype(F32), 0, keepdims=True) + jnp.sum(
        xdt * from_end, 0, keepdims=True
    )
    adj[...] = gstate * all_wide + dot(cq, dy_in, TN)
    xdt_low = low(xdt)
    u = lax.broadcasted_iota(jnp.int32, (CHUNK, CHUNK), 0)
    t = lax.broadcasted_iota(jnp.int32, (CHUNK, CHUNK), 1)
    inter = jnp.where(t >= u, dot(bk, cq, NT), 0.0)
    ginter = jnp.zeros((CHUNK, CHUNK), F32)
    for p in range(SSM_HEADS // 2):
        cols = slice(p * 128, p * 128 + 128)
        dy_rows = pair_rows(dy_low[:, cols])
        gmix = dot(xdt_low[:, cols], dy_rows, NT)
        parts = []
        for n, h in enumerate((2 * p, 2 * p + 1)):
            decay = jnp.exp2(jnp.minimum(cumt_ref[0, h : h + 1, :] - cum[:, h : h + 1], 0.0))
            parts.append(low(inter * decay))
            ginter = ginter + gmix[:, n * CHUNK : (n + 1) * CHUNK] * decay
        gact[:, cols] = dot(jnp.concatenate(parts, 1), dy_rows)
    ginter = low(jnp.where(t >= u, ginter, 0.0))
    gact[:, WIDE : WIDE + STATE] = gb + dot(ginter, cq)
    gact[:, WIDE + STATE :] = gc + dot(ginter, bk, TN)
    gxdt = gact[:, :WIDE] + from_end
    skip = skip_ref[...]
    gact[:, :WIDE] = dt_wide * gxdt + skip * dy
    gskip_ref[...] += jnp.sum(dy * x, 0, keepdims=True)
    sums = head_sums(
        jnp.concatenate([x * gxdt, dy * (mix_ref[0] - skip * x), jnp.broadcast_to(gfinal, (16, WIDE))], 0), expand
    )
    direct = sums[:CHUNK]
    gcum = sums[CHUNK : 2 * CHUNK] - dt * direct
    gld = dot_exact(jnp.where(t >= u, 1.0, 0.0), gcum) + sums[2 * CHUNK : 2 * CHUNK + 1]
    a = a_ref[...]
    gstep = (direct + a * gld) * sg_ref[0]
    small_ref[0:1] += jnp.sum(dt * gld, 0, keepdims=True) * a
    small_ref[1:2] += jnp.sum(gstep, 0, keepdims=True)
    pre = pre_ref[0].astype(F32)
    sg = sigmoid(pre)
    gpre = gact[...] * (sg * (1.0 + pre * (1.0 - sg)))
    ext = jnp.concatenate([gpre, after[...]], 0)
    after[...] = gpre[:8]
    conv = cl_ref[0].astype(F32)
    gconv = cw_ref[3:4] * gpre
    gw_ref[3:4] += jnp.sum(conv * gpre, 0, keepdims=True)
    gw_ref[4:5] += jnp.sum(gpre, 0, keepdims=True)
    for ahead in range(1, 4):
        moved = pltpu.roll(ext, CHUNK + 8 - ahead, 0)[:CHUNK]
        gconv = gconv + cw_ref[3 - ahead : 4 - ahead] * moved
        gw_ref[3 - ahead : 4 - ahead] += jnp.sum(conv * moved, 0, keepdims=True)
    everything = jnp.concatenate([low(gconv), low(gstep), jnp.zeros((CHUNK, 128), BF16)], 1)
    halves_out(core_ref[0], (everything,), gc_m, gc_y)

    @pl.when(c == 0)
    def _():
        tail_ref[0, :, :conv_width] = gconv[CHUNK - 8 :]
        tail_ref[0, :, conv_width : conv_width + 128] = gstep[CHUNK - 8 :]
        tail_ref[0, :, conv_width + 128 :] = jnp.zeros((8, 128), F32)

    @pl.when(c == chunks - 1)
    def _():
        head_ref[0] = gpre[:8]


def scan_backward(x, bk, cq, dt, sg, cum, cumt, dy, mixed, states, pre, conv, skip, a, cw, expand, core, adjoints):
    seqs, span, _ = x.shape
    chunks = span // CHUNK
    conv_width = pre.shape[2]

    def row(n):
        return pl.BlockSpec((1, CHUNK, n), lambda s, c: (s, chunks - 1 - c, 0))

    def once(m, n):
        return pl.BlockSpec((m, n), lambda s, c: (0, 0))

    edge = pl.BlockSpec((1, 8, conv_width), lambda s, c: (s, 0, 0))
    return pl.pallas_call(
        functools.partial(scan_back_body, chunks=chunks, conv_width=conv_width),
        grid=(seqs, chunks),
        in_specs=[
            row(WIDE), row(STATE), row(STATE), row(128), row(128), row(128),
            pl.BlockSpec((1, 32, CHUNK), lambda s, c: (s, 0, chunks - 1 - c)),
            row(WIDE), row(WIDE),
            pl.BlockSpec((1, 1, STATE, WIDE), lambda s, c: (s, chunks - 1 - c, 0, 0)),
            row(conv_width), row(conv_width),
            full_spec(skip.shape), full_spec(a.shape), full_spec(cw.shape), full_spec(expand.shape), SCALARS,
        ]
        + [
            pl.BlockSpec((1, STATE + 16, WIDE), lambda s, c: (s, 0, 0), pipeline_mode=pl.Buffered(1))
            for _ in adjoints
        ],
        out_specs=[
            row((conv_width + 256) // 2), row((conv_width + 256) // 2),
            pl.BlockSpec((1, 8, conv_width + 256), lambda s, c: (s, 0, 0)), edge, once(8, conv_width), once(1, WIDE), once(8, 128),
        ],
        out_shape=[
            jax.ShapeDtypeStruct((seqs, span, (conv_width + 256) // 2), BF16),
            jax.ShapeDtypeStruct((seqs, span, (conv_width + 256) // 2), BF16),
            jax.ShapeDtypeStruct((seqs, 8, conv_width + 256), F32),
            jax.ShapeDtypeStruct((seqs, 8, conv_width), F32),
            jax.ShapeDtypeStruct((8, conv_width), F32),
            jax.ShapeDtypeStruct((1, WIDE), F32),
            jax.ShapeDtypeStruct((8, 128), F32),
        ],
        scratch_shapes=[
            pltpu.VMEM((STATE, WIDE), F32), pltpu.VMEM((8, conv_width), F32), pltpu.VMEM((CHUNK, conv_width), F32),
        ],
        compiler_params=params(),
        cost_estimate=cost(4),
        name="scan_backward",
    )(x, bk, cq, dt, sg, cum, cumt, dy, mixed, states, pre, conv, skip, a, cw, expand, core, *adjoints)


def leave_mixer_body(core_ref, gz_m, gz_y, gc_m, gc_y, wz_ref, wc_ref, ws_ref, gh_ref, *, conv_width):
    core = core_ref[0]
    gz = halves_in(core, gz_m[0], gz_y[0])
    gc = halves_in(core, gc_m[0], gc_y[0])
    gh = dot(gz, wz_ref[...], NT) + dot(gc[:, :conv_width], wc_ref[...], NT)
    gh_ref[0] = low(gh + dot(gc[:, conv_width : conv_width + 128], ws_ref[...], NT))


def leave_mixer(core, gz, gc, wz, wc, ws):
    seqs, span, _ = gz[0].shape
    rows = min(256, span)

    def row(n):
        return pl.BlockSpec((1, rows, n), lambda s, b: (s, b, 0))

    width = wz.shape[0]
    return pl.pallas_call(
        functools.partial(leave_mixer_body, conv_width=wc.shape[1]),
        grid=(seqs, span // rows),
        in_specs=[SCALARS]
        + [row(v.shape[2]) for v in (*gz, *gc)]
        + [full_spec(v.shape) for v in (wz, wc, ws)],
        out_specs=row(width),
        out_shape=jax.ShapeDtypeStruct((seqs, span, width), BF16),
        compiler_params=params(),
        cost_estimate=cost(0),
        name="leave_mixer",
    )(core, *gz, *gc, wz, wc, ws)


def heads_body(core_ref, place_ref, cos_ref, sin_ref, cos0_ref, sin0_ref, *rest, blocks, count):
    near, far = rest[:2], rest[2:4]
    pieces = rest[4 : 4 + 2 * count]
    gq_m, gq_y, gkv_m, gkv_y = rest[4 + 2 * count :]
    core = core_ref[0]
    b = pl.program_id(1)
    halves_out(core, (jnp.concatenate([jnp.where(b < blocks // 2, near[j][0], far[j][0]) for j in range(2)], 1),), gq_m, gq_y)
    sums = []
    for j in range(2):
        t = pieces[j * count][0].astype(F32)
        for r in range(1, count):
            t = t + pieces[j * count + r][0].astype(F32)
        sums.append(t)
    lane = lax.broadcasted_iota(jnp.int32, sums[0].shape, 1)
    gk = jnp.where(lane < 64, sums[0], pltpu.roll(sums[1], 64, 1))
    gv = low(jnp.where(lane < 64, pltpu.roll(sums[0], 64, 1), sums[1]))
    place = place_ref[0]
    cosine, sine = turned(cos_ref[...], sin_ref[...], cos0_ref[place], sin0_ref[place])
    gk = low(gk * cosine - swap_halves(gk) * sine)
    halves_out(core, (jnp.concatenate([gk, gv], 1),), gkv_m, gkv_y)


def heads_back(core, place, tables, near, far, pieces):
    seqs, half, _ = near[0].shape
    span = 2 * half
    rows = min(256, half)
    blocks = span // rows
    table = pl.BlockSpec((rows, 128), lambda s, b: (b, 0))
    lower = pl.BlockSpec((1, rows, 256), lambda s, b: (s, jnp.minimum(b, blocks // 2 - 1), 0))
    upper = pl.BlockSpec((1, rows, 256), lambda s, b: (s, jnp.maximum(b - blocks // 2, 0), 0))

    def row(n):
        return pl.BlockSpec((1, rows, n), lambda s, b: (s, b, 0))

    return pl.pallas_call(
        functools.partial(heads_body, blocks=blocks, count=len(pieces) // 2),
        grid=(seqs, blocks),
        in_specs=[SCALARS, SCALARS, table, table]
        + [full_spec(v.shape) for v in tables[2:]]
        + [lower, lower, upper, upper] + [row(128)] * len(pieces),
        out_specs=[row(256), row(256), row(128), row(128)],
        out_shape=[jax.ShapeDtypeStruct((seqs, span, n), BF16) for n in (256, 256, 128, 128)],
        compiler_params=params(),
        cost_estimate=cost(0),
        name="heads_back",
    )(core, place, *tables, *near, *far, *pieces)


def leave_body(
    core_ref, tok_ref, gmid_ref, gh_ref, gq_m, gq_y, gkv_m, gkv_y, gain_ref, wq_ref, wk_ref, wv_ref, gt_ref
):
    core = core_ref[0]
    gh = gh_ref[0].astype(F32) + dot(halves_in(core, gq_m[0], gq_y[0]), wq_ref[...], NT)
    gkv = halves_in(core, gkv_m[0], gkv_y[0])
    gh = gh + dot(gkv[:, :128], wk_ref[...], NT) + dot(gkv[:, 128:], wv_ref[...], NT)
    v = tok_ref[0].astype(F32)
    scale = lax.rsqrt(jnp.mean(v * v, -1, keepdims=True) + EPS)
    unit = v * scale
    g = gh * gain_ref[...]
    gt_ref[0] = gmid_ref[0].astype(F32) + scale * (g - unit * jnp.mean(g * unit, -1, keepdims=True))


def leave(core, tokens, gmid, gh, heads, gain, wq, wk, wv):
    seqs, span, width = tokens.shape
    rows = min(256, span)

    def row(n):
        return pl.BlockSpec((1, rows, n), lambda s, b: (s, b, 0))

    return pl.pallas_call(
        leave_body,
        grid=(seqs, span // rows),
        in_specs=[SCALARS] + [row(width)] * 3 + [row(v.shape[2]) for v in heads] + [full_spec(v.shape) for v in (gain, wq, wk, wv)],
        out_specs=row(width),
        out_shape=jax.ShapeDtypeStruct((seqs, span, width), F32),
        compiler_params=params(),
        cost_estimate=cost(0),
        name="leave",
    )(core, tokens, gmid, gh, *heads, gain, wq, wk, wv)


def dup_halves(v):
    lane = lax.broadcasted_iota(jnp.int32, v.shape, 1)
    other = pltpu.roll(v, 64, 1)
    return low(jnp.where(lane < 64, v, other)), low(jnp.where(lane < 64, other, v))


def head_rows(v):
    lane = lax.broadcasted_iota(jnp.int32, (v.shape[0], 128), 1)
    heads = []
    for h in range(v.shape[1] // HEAD):
        t = v[:, (h // 2) * 128 : (h // 2) * 128 + 128]
        heads.append(jnp.where((lane < 64) if h % 2 == 0 else (lane >= 64), t, jnp.zeros_like(t)))
    return heads


def key_range(first, length, rows, keys):
    whole = jnp.minimum((first + 1) // keys, length // keys)
    some = jnp.minimum((first + rows + keys - 1) // keys, (length + keys - 1) // keys)
    return whole, some


def seen(i, first, length, rows, keys):
    key_at = i * keys + lax.broadcasted_iota(jnp.int32, (keys, rows), 0)
    query_at = first + lax.broadcasted_iota(jnp.int32, (keys, rows), 1)
    return (key_at <= query_at) & (key_at < length)


def attend_body(
    pos_ref, len_ref, from_ref, q_ref, other_ref, *rest, rows, keys, blocks, count, span,
):
    kv_refs = rest[:count]
    near_ref, far_ref, lse_ref, kd, vt, top, acc, score_a, score_b, top_a, top_b = rest[count:]
    s = pl.program_id(0)
    b = pl.program_id(1)
    prep = min(512, span)

    @pl.when(b == 0)
    def _():
        ones = jnp.ones((16, prep), F32)
        for r, kv_ref in enumerate(kv_refs):
            for i in range(span // prep):
                here = slice(i * prep, (i + 1) * prep)
                at = pl.ds(pl.multiple_of(from_ref[r] * span + i * prep, prep), prep)
                kd[0, at, :], kd[1, at, :] = dup_halves(kv_ref[0, here, :128].astype(F32))
                t = kv_ref[0, here, 128:].astype(F32).T
                vt[0, :, at] = low(jnp.concatenate([t[:64], ones], 0))
                vt[1, :, at] = low(jnp.concatenate([t[64:], ones], 0))

    first = pos_ref[b]
    length = len_ref[s]
    heads = head_rows(jnp.where(b < blocks // 2, q_ref[0], other_ref[0]))
    top[...] = jnp.full_like(top, LOWEST)
    acc[...] = jnp.zeros_like(acc)
    whole, some = key_range(first, length, rows, keys)

    def scores(i, buffer, tops, h, mask=None):
        at = pl.ds(pl.multiple_of(i * keys, keys), keys)
        t = dot(kd[h // 4, at, :], heads[h], NT)
        if mask is not None:
            t = jnp.where(mask, t, LOWEST)
        buffer[h] = t
        tops[h] = jnp.max(t, 0, keepdims=True)

    def add(i, buffer, tops, h):
        at = pl.ds(pl.multiple_of(i * keys, keys), keys)
        before = top[h]
        now = jnp.maximum(before, tops[h])
        p = low(jnp.exp2((buffer[h] - now) * SCORE2))
        acc[h] = acc[h] * jnp.exp2((before - now) * SCORE2) + dot(vt[h // 4, :, at], p)
        top[h] = now

    def edge(i, _):
        mask = seen(i, first, length, rows, keys)
        for h in range(HEADS):
            scores(i, score_a, top_a, h, mask)
        for h in range(HEADS):
            add(i, score_a, top_a, h)
        return 0

    lax.fori_loop(whole, some, edge, 0)
    last = jnp.maximum(whole - 1, 0)
    for h in range(HEADS):
        scores(0, score_a, top_a, h)

    def two(i, _):
        for h in range(HEADS):
            scores(2 * i + 1, score_b, top_b, h)
            add(2 * i, score_a, top_a, h)
        following = jnp.minimum(2 * i + 2, last)
        for h in range(HEADS):
            scores(following, score_a, top_a, h)
            add(2 * i + 1, score_b, top_b, h)
        return 0

    lax.fori_loop(0, whole // 2, two, 0)

    @pl.when(whole % 2 == 1)
    def _():
        for h in range(HEADS):
            add(last, score_a, top_a, h)

    outs = []
    for h in range(HEADS):
        t = acc[h]
        weight = t[64:65]
        outs.append(t[:64] / weight)
        lse_ref[0, h : h + 1, :] = top[h] * SCORE2 + jnp.log2(weight)
    result = low(jnp.concatenate(outs, 0).T)

    @pl.when(b < blocks // 2)
    def _():
        near_ref[0] = result

    @pl.when(b >= blocks // 2)
    def _():
        far_ref[0] = result


def halves_specs(rows, blocks, columns):
    lower = pl.BlockSpec((1, rows, columns), lambda s, b, *_: (s, jnp.minimum(b, blocks // 2 - 1), 0))
    upper = pl.BlockSpec((1, rows, columns), lambda s, b, *_: (s, jnp.maximum(b - blocks // 2, 0), 0))
    return lower, upper


def attend(pos, lens, sources, q, other, kvs):
    seqs, span, _ = q.shape
    count = len(kvs)
    total = count * span
    rows = min(256, span // 2)
    keys = 256
    blocks = span // rows
    lower, upper = halves_specs(rows, blocks, 512)
    half = jax.ShapeDtypeStruct((seqs, span // 2, 512), BF16)
    return pl.pallas_call(
        functools.partial(attend_body, rows=rows, keys=keys, blocks=blocks, count=count, span=span),
        grid_spec=pltpu.PrefetchScalarGridSpec(
            num_scalar_prefetch=3,
            grid=(seqs, blocks),
            in_specs=[lower, upper]
            + [pl.BlockSpec((1, span, 256), lambda s, b, *_: (s, 0, 0), pipeline_mode=pl.Buffered(1))] * count,
            out_specs=[lower, upper, pl.BlockSpec((1, 8, rows), lambda s, b, *_: (s, 0, b))],
            scratch_shapes=[
                pltpu.VMEM((2, total, 128), BF16), pltpu.VMEM((2, 80, total), BF16),
                pltpu.VMEM((8, 1, rows), F32), pltpu.VMEM((8, 80, rows), F32),
                pltpu.VMEM((8, keys, rows), F32), pltpu.VMEM((8, keys, rows), F32),
                pltpu.VMEM((8, 1, rows), F32), pltpu.VMEM((8, 1, rows), F32),
            ],
        ),
        out_shape=[half, half, jax.ShapeDtypeStruct((seqs, 8, span), F32)],
        compiler_params=params(),
        cost_estimate=cost(26),
        name="attend",
    )(pos, lens, sources, q, other, *kvs)


def attend_back_body(
    pos_ref, len_ref, from_ref, q_ref, other_ref, do_near_ref, do_far_ref, o_near_ref, o_far_ref, lse_ref,
    cos_ref, sin_ref, cos0_ref, sin0_ref, *rest, rows, keys, blocks, count, span, group,
):
    kv_refs = rest[:count]
    dq_near_ref, dq_far_ref = rest[count : count + 2]
    dkv_refs = rest[count + 2 : 2 * count + 2]
    kd, vd, kt, dk, dv, dq, score_a, grad_a, score_b, grad_b = rest[2 * count + 2 :]
    s = pl.program_id(0)
    b = pl.program_id(1)
    prep = min(512, span)

    @pl.when(b == 0)
    def _():
        for r, kv_ref in enumerate(kv_refs):
            for i in range(span // prep):
                here = slice(i * prep, (i + 1) * prep)
                at = pl.ds(pl.multiple_of(from_ref[r] * span + i * prep, prep), prep)
                k = kv_ref[0, here, :128].astype(F32)
                kd[at, :] = dup_halves(k)[group]
                vd[at, :] = dup_halves(kv_ref[0, here, 128:].astype(F32))[group]
                kt[:, at] = low(k.T[64 * group : 64 * group + 64])
        dk[...] = jnp.zeros_like(dk)
        dv[...] = jnp.zeros_like(dv)

    first = pos_ref[b]
    length = len_ref[s]
    is_near = b < blocks // 2
    heads = head_rows(jnp.where(is_near, q_ref[0], other_ref[0]))
    do = jnp.where(is_near, do_near_ref[0], do_far_ref[0])
    grads = head_rows(do)
    prod = do.astype(F32) * jnp.where(is_near, o_near_ref[0], o_far_ref[0]).astype(F32)
    col = lax.broadcasted_iota(jnp.int32, (8, 256), 1) // HEAD
    ones = low(jnp.where(col == lax.broadcasted_iota(jnp.int32, (8, 256), 0), 1.0, 0.0))
    high, remain = split_low(prod)
    delta = dot(ones, high, NT) + dot(ones, remain, NT)
    dq[...] = jnp.zeros_like(dq)
    whole, some = key_range(first, length, rows, keys)

    def scores(i, buffers, h):
        at = pl.ds(pl.multiple_of(i * keys, keys), keys)
        buffers[0][h] = dot(kd[at, :], heads[h], NT)
        buffers[1][h] = dot(vd[at, :], grads[h], NT)

    def add(i, buffers, h, sums, mask=None):
        at = pl.ds(pl.multiple_of(i * keys, keys), keys)
        x = buffers[0][h] * SCORE2 - lse_ref[0, 4 * group + h : 4 * group + h + 1, :]
        if mask is not None:
            x = jnp.where(mask, x, LOWEST)
        p = jnp.exp2(x)
        ds = low(p * (buffers[1][h] - delta[h : h + 1]))
        parts = dot(low(p), grads[h]), dot(ds, heads[h])
        dq[h] += dot(kt[:, at], ds)
        sums = parts if sums is None else (sums[0] + parts[0], sums[1] + parts[1])
        if h == 3:
            dv[at, :] += sums[0]
            dk[at, :] += sums[1]
        return sums

    early, late = (score_a, grad_a), (score_b, grad_b)

    def edge(i, _):
        mask = seen(i, first, length, rows, keys)
        for h in range(4):
            scores(i, early, h)
        sums = None
        for h in range(4):
            sums = add(i, early, h, sums, mask)
        return 0

    lax.fori_loop(whole, some, edge, 0)
    last = jnp.maximum(whole - 1, 0)
    for h in range(4):
        scores(0, early, h)

    def two(i, _):
        sums = None
        for h in range(4):
            scores(2 * i + 1, late, h)
            sums = add(2 * i, early, h, sums)
        following = jnp.minimum(2 * i + 2, last)
        sums = None
        for h in range(4):
            scores(following, early, h)
            sums = add(2 * i + 1, late, h, sums)
        return 0

    lax.fori_loop(0, whole // 2, two, 0)

    @pl.when(whole % 2 == 1)
    def _():
        sums = None
        for h in range(4):
            sums = add(last, early, h, sums)

    owner = jnp.where(is_near, from_ref[0], count - 1 - from_ref[0])
    cosine, sine = turned(cos_ref[...], sin_ref[...], cos0_ref[owner][:, :1], sin0_ref[owner][:, :1])
    parts = []
    for h in range(4):
        t = dq[h] * 0.125
        former, latter = t[:32], t[32:]
        parts += [former * cosine + latter * sine, latter * cosine - former * sine]
    result = low(jnp.concatenate(parts, 0).T)

    @pl.when(is_near)
    def _():
        dq_near_ref[0] = result

    @pl.when(jnp.logical_not(is_near))
    def _():
        dq_far_ref[0] = result

    @pl.when(b == blocks - 1)
    def _():
        lane = lax.broadcasted_iota(jnp.int32, (prep, 128), 1)
        for r, dkv_ref in enumerate(dkv_refs):
            for i in range(span // prep):
                at = pl.ds(pl.multiple_of(from_ref[r] * span + i * prep, prep), prep)
                k, v = dk[at, :], dv[at, :]
                k = (k + pltpu.roll(k, 64, 1)) * 0.125
                v = v + pltpu.roll(v, 64, 1)
                dkv_ref[0, i * prep : (i + 1) * prep] = low(jnp.where(lane < 64, k, v))


def attend_backward(group, pos, lens, sources, q, other, do_near, do_far, o_near, o_far, lse, tables, kvs):
    seqs, span, _ = q.shape
    count = len(kvs)
    total = count * span
    rows = min(256, span // 2)
    keys = 256
    blocks = span // rows
    lower = pl.BlockSpec((1, rows, 256), lambda s, b, *_: (s, jnp.minimum(b, blocks // 2 - 1), group))
    upper = pl.BlockSpec((1, rows, 256), lambda s, b, *_: (s, jnp.maximum(b - blocks // 2, 0), group))
    out_lower, out_upper = halves_specs(rows, blocks, 256)
    stat = pl.BlockSpec((1, 8, rows), lambda s, b, *_: (s, 0, b))
    table = pl.BlockSpec((32, rows), lambda s, b, *_: (0, b))
    half = jax.ShapeDtypeStruct((seqs, span // 2, 256), BF16)
    outs = pl.pallas_call(
        functools.partial(
            attend_back_body, rows=rows, keys=keys, blocks=blocks, count=count, span=span, group=group
        ),
        grid_spec=pltpu.PrefetchScalarGridSpec(
            num_scalar_prefetch=3,
            grid=(seqs, blocks),
            in_specs=[lower, upper, lower, upper, lower, upper, stat, table, table]
            + [full_spec(v.shape) for v in tables[2:]]
            + [pl.BlockSpec((1, span, 256), lambda s, b, *_: (s, 0, 0), pipeline_mode=pl.Buffered(1))] * count,
            out_specs=[out_lower, out_upper]
            + [pl.BlockSpec((1, span, 128), lambda s, b, *_: (s, 0, 0))] * count,
            scratch_shapes=[
                pltpu.VMEM((total, 128), BF16), pltpu.VMEM((total, 128), BF16), pltpu.VMEM((64, total), BF16),
                pltpu.VMEM((total, 128), F32), pltpu.VMEM((total, 128), F32), pltpu.VMEM((4, 64, rows), F32),
            ]
            + [pltpu.VMEM((4, keys, rows), F32)] * 4,
        ),
        out_shape=[half, half] + [jax.ShapeDtypeStruct((seqs, span, 128), BF16)] * count,
        compiler_params=params(),
        cost_estimate=cost(1 if group else 20),
        name="attend_backward",
    )(pos, lens, sources, q, other, do_near, do_far, o_near, o_far, lse, *tables, *kvs)
    return outs[0], outs[1], outs[2:]


def in_hbm(shape):
    return pltpu.HBM(shape, BF16)


def both(left, right):
    return dot(left[0][...], right[0][...], TN) + dot(left[1][...], right[1][...], TN)


def tall_body(place_ref, left_a, left_b, *rest, n, widths, square):
    rights = [rest[2 * k : 2 * k + 2] for k in range(len(widths))]
    outs = rest[2 * len(widths) :]
    rows = left_a.shape[1] // n
    i = pl.program_id(0)
    start = 0
    for part, (right, steps) in enumerate(zip(rights, widths)):

        @pl.when((i >= start) & (i < start + steps))
        def _(part=part, right=right):
            if square:
                if square == "hops":
                    own, to_x, keep_x, to_y, keep_y = outs
                    first, keep = ((to_x, keep_x), (to_y, keep_y))[part]
                for k in range(4):
                    block = jnp.bitwise_xor(place_ref[0], k)
                    columns = pl.ds(pl.multiple_of(block * rows, rows), rows)
                    value = low(both((left_a.at[:, columns], left_b.at[:, columns]), right))
                    if square == "direct":
                        outs[k][...] = value
                    elif k == 0:
                        own[...] = value
                    elif k == 3:
                        first[1] = value
                    elif k == part + 1:
                        first[0] = value
                    else:
                        keep[...] = value
            else:
                value = low(both((left_a, left_b), right))
                for j in range(n):
                    outs[0][j] = value[j * rows : (j + 1) * rows]

        start += steps


def tall_grad(place, left, rights, chunk, n, square="", micros=0.0, name="grad"):
    tokens, width = left[0].shape[0], left[3]
    widths = [v[3] // chunk for v in rights]
    steps = sum(widths)
    rows = width // n
    starts = [0, widths[0]]
    parts = range(len(rights))

    def within(k, i):
        return jnp.clip(i - starts[k], 0, widths[k] - 1)

    def right_spec(k):
        return pl.BlockSpec((tokens, chunk), lambda i, place: (0, rights[k][2] // chunk + within(k, i)))

    left_spec = pl.BlockSpec(
        (tokens, width), lambda i, place: (0, left[2] // width), pipeline_mode=pl.Buffered(1)
    )

    if square == "direct":
        out_specs = [pl.BlockSpec((rows, chunk), lambda i, place: (i, 0))] * 4
        out_shape = [in_hbm((steps * rows, chunk))] * 4
    elif square:
        out_specs = [pl.BlockSpec((rows, chunk), lambda i, place: (i, 0))]
        out_shape = [jax.ShapeDtypeStruct((steps * rows, chunk), BF16)]
        for k in parts:
            out_specs.append(pl.BlockSpec((2, rows, chunk), lambda i, place, k=k: (0, within(k, i), 0)))
            out_specs.append(pl.BlockSpec((rows, chunk), lambda i, place, k=k: (within(k, i), 0)))
            out_shape.append(in_hbm((2, widths[k] * rows, chunk)))
            out_shape.append(jax.ShapeDtypeStruct((widths[k] * rows, chunk), BF16))
    else:
        out_specs = pl.BlockSpec((n, rows, chunk), lambda i, place: (0, i, 0))
        out_shape = jax.ShapeDtypeStruct((n, steps * rows, chunk), BF16)
    return pl.pallas_call(
        functools.partial(tall_body, n=n, widths=widths, square=square),
        grid_spec=pltpu.PrefetchScalarGridSpec(
            num_scalar_prefetch=1,
            grid=(steps,),
            in_specs=[left_spec] * 2 + [right_spec(k) for k in parts for _ in range(2)],
            out_specs=out_specs,
        ),
        out_shape=out_shape,
        compiler_params=pltpu.CompilerParams(vmem_limit_bytes=VMEM_LIMIT),
        cost_estimate=cost(micros),
        name=name,
    )(place, *left[:2], *[v for right in rights for v in right[:2]])


PIECE = 256


def wide_body(place_ref, *rest, parts, group, square, split):
    lefts = [rest[2 * k : 2 * k + 2] for k in range(parts)]
    rights = [rest[2 * k : 2 * k + 2] for k in range(parts, 2 * parts)]
    outs = rest[4 * parts :]
    values = [low(both(left, right)) for left, right in zip(lefts, rights)]
    values = [v[:, c : c + PIECE] for v in values for c in range(0, v.shape[1], PIECE)]
    if square:
        own, to_x, keep_x, to_y, keep_y = outs
        value = jnp.concatenate(values, 0)
        for k in range(4):

            @pl.when(pl.program_id(0) == k)
            def _(k=k):
                if k == 0:
                    own[...] = value
                    return
                for part, (first, keep) in enumerate(((to_x, keep_x), (to_y, keep_y))):
                    here = value[split:] if part else value[:split]
                    if k == 3:
                        first[1] = here
                    elif k == part + 1:
                        first[0] = here
                    else:
                        keep[...] = here
    else:
        for j in range(group):
            start = 0
            for v in values:
                rows = v.shape[0] // group
                outs[0][j, start : start + rows] = v[j * rows : (j + 1) * rows]
                start += rows


def wide_grad(place, lefts, rights, n, square="", micros=0.0, name="grad"):
    tokens = lefts[0][0].shape[0]
    steps = min(n, 4)
    rows = [v[3] // n * (g[3] // PIECE) for v, g in zip(lefts, rights)]
    total = sum(rows)
    split = total // 32 * 16

    def turn(i, place):
        return jnp.bitwise_xor(place[0], i) if square else i

    def once(*dims):
        return pl.BlockSpec(dims, lambda i, place: (0,) * len(dims), pipeline_mode=pl.Buffered(1))

    def left_spec(v):
        size = v[3] // steps
        return pl.BlockSpec((tokens, size), lambda i, place: (0, v[2] // size + turn(i, place)))

    def right_spec(v):
        return pl.BlockSpec((tokens, v[3]), lambda i, place: (0, v[2] // v[3]), pipeline_mode=pl.Buffered(1))

    if square:
        dims = [(total, PIECE)]
        for size in (split, total - split):
            dims += [(2, size, PIECE), (size, PIECE)]
        out_specs = [once(*d) for d in dims]
        out_shape = [in_hbm(d) for d in dims]
    else:
        out_specs = pl.BlockSpec((n // steps, total, PIECE), lambda i, place: (i, 0, 0))
        out_shape = jax.ShapeDtypeStruct((n, total, PIECE), BF16)
    return pl.pallas_call(
        functools.partial(wide_body, parts=len(lefts), group=n // steps, square=square, split=split),
        grid_spec=pltpu.PrefetchScalarGridSpec(
            num_scalar_prefetch=1,
            grid=(steps,),
            in_specs=[left_spec(v) for v in lefts for _ in range(2)] + [right_spec(v) for v in rights for _ in range(2)],
            out_specs=out_specs,
        ),
        out_shape=out_shape,
        compiler_params=pltpu.CompilerParams(vmem_limit_bytes=VMEM_LIMIT),
        cost_estimate=cost(micros),
        name=name,
    )(place, *[v for left in lefts for v in left[:2]], *[v for right in rights for v in right[:2]])


def in_place(body, args, outs, name, columns=None):
    def spec(shape):
        if columns is None:
            return full_spec(shape)
        return pl.BlockSpec((*shape[:-1], columns), lambda i: (0,) * (len(shape) - 1) + (i,))

    return pl.pallas_call(
        body,
        grid=(1 if columns is None else outs[0].shape[-1] // columns,),
        in_specs=[SCALARS if v.ndim == 1 else spec(v.shape) for v in args],
        out_specs=[spec(v.shape) for v in outs],
        out_shape=outs,
        compiler_params=pltpu.CompilerParams(vmem_limit_bytes=VMEM_LIMIT),
        cost_estimate=cost(0),
        name=name,
    )(*args)


def like(v):
    return in_hbm(v.shape)


def first_body(keep_x, keep_y, from_x, from_y, to_y, to_x):
    to_y[...] = low(keep_x[...].astype(F32) + from_x[1].astype(F32))
    to_x[...] = low(keep_y[...].astype(F32) + from_y[1].astype(F32))


def second_body(own, from_x, from_y, late_y, late_x, out):
    split = late_y.shape[0]
    for at, first, last in ((slice(0, split), from_x, late_y), (slice(split, None), from_y, late_x)):
        out[at] = low(own[at].astype(F32) + first[0].astype(F32) + last[...].astype(F32))


def sum_body(*refs):
    total = refs[0][...].astype(F32)
    for ref in refs[1:-1]:
        total = total + ref[...].astype(F32)
    refs[-1][...] = low(total)


def square_body(own, one, two, three, out):
    near = own[...].astype(F32) + one[...].astype(F32)
    out[...] = low(near + (two[...].astype(F32) + three[...].astype(F32)))


def unpack_body(at_ref, own, other, *rest, plan, summed, grads):
    weights = dict(zip(summed, rest))
    outs = rest[len(summed) : len(summed) + grads]
    sums = dict(zip(summed, rest[len(summed) + grads :]))
    first = at_ref[0] == 0
    totals = {}
    for out, column, columns, half, start, rows in plan:
        at = slice(start, start + rows)
        a, b = (own, other) if half == 0 else (other, own)
        value = jnp.where(first, a[at], b[at])[:, :columns].astype(F32)
        here = slice(column, column + columns)
        outs[out][:, here] = value
        if out in weights:
            part = jnp.sum(value * weights[out][:, here].astype(F32), 1, keepdims=True)
            totals[out] = totals[out] + part if out in totals else part
    for out, ref in sums.items():
        ref[...] = jnp.broadcast_to(totals[out], ref.shape)


def unpack(at, own, other, matrices):
    piece = own.shape[1]
    plan, shapes, weights, start = [], [], {}, 0
    for rows, pieces, parts in matrices:
        ends = np.cumsum([0] + [w.shape[1] for w, _ in parts])
        for half in range(2):
            for i in range(pieces):
                column = (half * pieces + i) * piece
                for k, (w, _) in enumerate(parts):
                    if ends[k] <= column < ends[k + 1]:
                        offset = int(column - ends[k])
                        plan.append(
                            (len(shapes) + k, offset, min(piece, w.shape[1] - offset), half, start + i * rows, rows)
                        )
        for w, wanted in parts:
            if wanted:
                weights[len(shapes)] = w
            shapes.append(jax.ShapeDtypeStruct((rows, w.shape[1]), F32))
        start += pieces * rows
    grads = len(shapes)
    summed = list(weights)
    shapes += [jax.ShapeDtypeStruct((shapes[k].shape[0], 128), F32) for k in summed]

    def whole(shape):
        return pl.BlockSpec(shape, lambda i, at: (0, 0))

    outs = pl.pallas_call(
        functools.partial(unpack_body, plan=plan, summed=summed, grads=grads),
        grid_spec=pltpu.PrefetchScalarGridSpec(
            num_scalar_prefetch=1,
            grid=(1,),
            in_specs=[whole(own.shape), whole(other.shape)]
            + [pl.BlockSpec(shapes[k].shape, lambda i, at: (at[1], 0)) for k in summed],
            out_specs=[whole(v.shape) for v in shapes],
        ),
        out_shape=shapes,
        compiler_params=pltpu.CompilerParams(vmem_limit_bytes=VMEM_LIMIT),
        cost_estimate=cost(0),
        name="unpack",
    )(at, own, other, *weights.values())
    return outs[:grads], [v[:, 0] for v in outs[grads:]]


def ring(value, steps):
    n = lax.axis_size("seq")
    return lax.ppermute(value, "seq", [(i, (i + steps) % n) for i in range(n)])


def along(value, steps):
    n = lax.axis_size("seq")
    return lax.ppermute(value, "seq", [(i, i + steps) for i in range(n) if 0 <= i + steps < n])


def mirror(value):
    n = lax.axis_size("seq")
    return lax.ppermute(value, "seq", [(i, n - 1 - i) for i in range(n)])


def flip_dp(value, bit):
    n = lax.axis_size("dp")
    return lax.ppermute(value, "dp", [(i, i ^ bit) for i in range(n)])


def other_core(value):
    return flip_dp(value, 1)


def after(value, *done):
    return lax.optimization_barrier((value, done))[0]


def scatter_seq(value):
    return lax.psum_scatter(value, "seq", scatter_dimension=0, tiled=True)[0]


def flip_seq(value, bit):
    n = lax.axis_size("seq")
    return lax.ppermute(value, "seq", [(i, i ^ bit) for i in range(n)])


def add_low(*values):
    return in_place(sum_body, values, [like(values[0])], "add")[0]


def direct_sum(pieces):
    return add_low(pieces[0], *[flip_seq(v, k) for k, v in enumerate(pieces) if k])


def first_hop(pieces, *done):
    own, to_x, keep_x, to_y, keep_y = pieces
    from_x, from_y = flip_seq(to_x, 1), flip_seq(to_y, 2)
    held = in_place(
        first_body, (after(keep_x, *done), keep_y, from_x, from_y), [like(keep_x), like(keep_y)], "first_hop"
    )
    return (*held, own, from_x, from_y)


def second_hop(held, *done):
    to_y, to_x, own, from_x, from_y = held
    args = (after(own, *done), from_x, from_y, flip_seq(to_y, 2), flip_seq(to_x, 1))
    return in_place(second_body, args, [like(own)], "second_hop")[0]


def offloaded_sum_z(value, which):
    n = lax.axis_size("dp")
    groups = [list(range(c, n, 2))[:: -1 if which & 1 else 1] for c in range(2)]
    return lax.psum(value, "dp", axis_index_groups=groups[:: -1 if which & 2 else 1])


def sum_four(value, *done):
    got = [flip_dp(value, bit) for bit in (2, 4, 6)]
    return in_place(square_body, (after(value, *done), *got), [like(value)], "add")[0]


def sum_z(value, first=2, last=None):
    bit = first
    while bit < (last or lax.axis_size("dp")):
        value = add_low(value, flip_dp(value, bit))
        bit *= 2
    return value


def on_device(
    tokens, cotangent, lengths, norm_one, w_query, w_key, w_value, w_gatez, w_conv_in, w_step, conv_weight,
    conv_bias, step_bias, decay_log, skip_gain, gated_gain, w_attn_out, w_mix_out, norm_two, w_gate, w_up, w_down,
):
    seqs, span, width = tokens.shape
    half = span // 2
    taps, conv_width = conv_weight.shape
    count = lax.axis_size("seq")
    place = lax.axis_index("seq").astype(jnp.int32)
    core = (lax.axis_index("dp") % 2).astype(jnp.int32)
    first = place * span
    mirrored = (count - 1 - place) * span + half
    row_tables = rotation(span, count, "rows")
    column_tables = rotation(span, count, "columns")
    rate = -jnp.exp(decay_log)
    pad = (0, 128 - SSM_HEADS)
    rate_row = jnp.pad(rate, pad)[None]
    step_row = jnp.pad(step_bias, pad)[None]
    w_step_wide = jnp.pad(w_step, ((0, 0), pad))
    skip_row = jnp.repeat(skip_gain, SSM_HEAD)[None]
    ones = (np.arange(WIDE)[None, :] // SSM_HEAD == np.arange(128)[:, None]).astype(np.float32)
    expand = jnp.asarray(np.concatenate([ones, ones], 0), BF16)
    pos = jnp.stack([first, core])
    core_here = core[None]
    rows = min(256, half)
    blocks = jnp.concatenate([base + jnp.arange(0, half, rows, dtype=jnp.int32) for base in (first, mirrored)])
    sources = lax.rem(place - jnp.arange(count, dtype=jnp.int32) + count, count)
    here = place[None]

    def flat(v):
        return v.reshape(seqs * span, v.shape[2])

    def with_other(mine, yours=None):
        mine, yours = flat(mine), flat(mine if yours is None else yours)
        return mine, other_core(yours), 0, mine.shape[1]

    halo = along(tokens[:, span - 16 :], 1)
    hidden, q, kv = enter(here, after(tokens, halo), norm_one[None], w_query, w_key, w_value, row_tables)
    kvs = [kv] + [ring(kv, r) for r in range(1, count)]
    q_other = mirror(q[:, half:])
    z, conv, pre, x, bk, cq, dt, sg, cum, cumt, state = mixer(
        pos, lengths, hidden, halo, norm_one[None], w_gatez, w_conv_in, w_step_wide, conv_weight, conv_bias[None],
        step_row, rate_row * LOG2E, expand,
    )
    states = lax.all_gather(state, "seq")
    skip_row, blocks, sources = [after(v, state) for v in (skip_row, blocks, sources)]
    gated_row = after(gated_gain, state)[None]
    gact = grad_act(pos, lengths, after(cotangent, state), w_down)
    o_near, o_far, lse = attend(blocks, lengths, sources, after(q, gact), q_other, kvs)
    o_back = mirror(o_far)
    mixed, mix_low, held = scan_forward(
        here, after(x, o_near), bk, cq, dt, cum, cumt, skip_row, z, gated_row, expand, states
    )
    hid = with_other(hidden)
    mix_pair = with_other(mix_low)
    output, lefts, mine, yours, grad_mid = middle(
        pos, lengths, o_near, o_back, after(mix_low, hid[1]), tokens, cotangent, gact, w_attn_out, w_mix_out, w_gate, w_up, w_down,
        norm_two[None],
    )
    square = "hops" if count == 4 else ""
    ff = w_gate.shape[1]
    lefts, rights = with_other(lefts), with_other(mine, yours)
    ffn_left = (*lefts[:2], 0, width)
    ffn_rights = [(*rights[:2], k * ff // 2, ff // 2) for k in range(2)]
    grad_ffn, grad_branch = [(*rights[:2], ff + k * width // 2, width // 2) for k in range(2)]
    out_lefts = ((*lefts[:2], width, ff), (*lefts[:2], width + ff, w_attn_out.shape[0]), mix_pair, hid)
    do_near, do_far, grad_mixed, gz_m, gz_y, adjoint = branch_back(
        core_here, mine, yours, mixed, z, cq, cum, w_attn_out, w_mix_out, gated_row, expand
    )
    adjoints = [along(adjoint, -r) for r in range(1, count)]
    part_ffn = tall_grad(after(here, do_near), ffn_left, ffn_rights, 512, count, square, name="grad_ffn_in")
    part_out = wide_grad(
        after(here, part_ffn[0], *adjoints), out_lefts, (grad_ffn, grad_branch, grad_branch, with_other(gz_m, gz_y)), count,
        square, micros=16, name="grad_outs",
    )
    ffn_held = first_hop(part_ffn, part_out[0]) if square else scatter_seq(part_ffn)
    gc_m, gc_y, tail, head, g_conv_small, g_skip, g_small = scan_backward(
        after(x, part_out[0], ffn_held), bk, cq, dt, sg, cum, cumt, grad_mixed, mixed, held, pre, conv, skip_row, rate_row,
        conv_weight, expand, core_here, adjoints,
    )
    do_other = mirror(after(do_far, head))
    ffn_sum = second_hop(ffn_held) if square else ffn_held
    out_held = first_hop([after(v, ffn_held) for v in part_out]) if square else scatter_seq(part_out)
    head = after(head, ffn_sum, out_held)
    ffn_sum = offloaded_sum_z(ffn_sum, 0)
    returned = along(low(head), -1).astype(F32)[:, : taps - 1]
    g_conv_weight = g_conv_small[:taps]
    beside = ((0, 0), (0, 0), (0, tail.shape[2] - conv_width))
    for ahead in range(1, taps):
        tap = taps - 1 - ahead
        fill = jnp.pad(returned[:, :ahead], ((0, 0), (8 - ahead, 0), (0, 0)))
        tail = tail + jnp.pad(conv_weight[tap] * fill, beside)
        g_conv_weight = g_conv_weight.at[tap].add(jnp.sum(fill * conv[:, span - 8 :].astype(F32), (0, 1)))
    tail = low(tail)
    size = tail.shape[2] // 2
    tails = tail[:, :, :size], tail[:, :, size:]
    gc_m, gc_y = [
        lax.dynamic_update_slice(v, jnp.where(core == i, *tails), (0, span - 8, 0)) for i, v in enumerate((gc_m, gc_y))
    ]
    part_in = tall_grad(
        here, hid, (with_other(gc_m, gc_y),), 256, count, "direct" if square else "", name="grad_conv_in"
    )
    small = [
        g_conv_weight.reshape(-1), g_conv_small[taps], g_skip[0],
        g_small[0], g_small[1],
    ]
    sizes = [v.shape[0] for v in small]
    total = jnp.concatenate(small)
    total = jnp.pad(total, (0, -total.shape[0] % 1024)).reshape(-1, 128)
    hops = [("seq", 1 << k) for k in range(count.bit_length() - 1)]
    hops += [("dp", 2 << k) for k in range(lax.axis_size("dp").bit_length() - 2)] + [("dp", 1)]

    def flip(value, axis, bit):
        return flip_seq(value, bit) if axis == "seq" else flip_dp(value, bit)

    def small_step(total, *done):
        axis, bit = hops.pop(0)
        return after(total, *done) + flip(total, axis, bit)

    def back(group, order):
        near, far, parts = attend_backward(
            group, blocks, lengths, sources, after(q, *order), q_other, do_near, do_other, o_near, o_far, lse,
            column_tables, kvs,
        )
        return near, mirror(far), [parts[0]] + [ring(parts[r], -r) for r in range(1, count)]

    dq_near, dq_far, pieces = back(0, (part_in[0],))
    out_sum = second_hop(out_held, dq_near) if square else out_held
    in_sum = direct_sum([after(part_in[0], dq_near), *part_in[1:]]) if square else scatter_seq(part_in)
    results = back(1, (dq_near, in_sum, ffn_sum, out_sum))
    four = lax.axis_size("dp") == 8
    out_sum, in_sum = offloaded_sum_z((out_sum, in_sum), 1)
    total = small_step(after(total, dq_near))
    gh = leave_mixer(
        core_here, (after(gz_m, results[0], dq_far, total, *pieces), gz_y), (gc_m, gc_y), w_gatez, w_conv_in, w_step_wide
    )
    total = small_step(after(total, results[0]))
    heads = heads_back(
        core_here, after(here, gh, total), row_tables, (dq_near, results[0]), (dq_far, results[1]), pieces + results[2]
    )
    heads_pairs = with_other(*heads[:2]), with_other(*heads[2:])
    part_qkv = tall_grad(here, hid, heads_pairs, 128, count, square, name="grad_qkv")
    grad_tokens = leave(
        core_here, tokens, grad_mid, after(gh, part_qkv[0], out_sum, in_sum), heads, norm_one[None], w_query, w_key, w_value
    )
    total = small_step(after(total, part_qkv[0]), grad_tokens)
    at = jnp.stack([core, place])

    def matrix(pieces, *weights, wanted=True):
        return weights[0].shape[0] // count, pieces, [(w, wanted) for w in weights]

    done = (total, grad_tokens)
    qkv_held = first_hop(part_qkv, *done) if square else scatter_seq(part_qkv)
    ffn_sum = after(ffn_sum, heads[0])
    (s_gate, s_up), two_sums = unpack(
        at, after(ffn_sum, qkv_held), other_core(ffn_sum), [matrix(2, w_gate), matrix(2, w_up)]
    )
    total = small_step(after(total, qkv_held))
    qkv_sum = second_hop(qkv_held, total, s_gate) if square else qkv_held
    out_sum, in_sum = [after(v, qkv_held) for v in (out_sum, in_sum)]
    (s_down, s_attn_out, s_mix_out, s_gatez), (gated_sum, z_sum) = unpack(
        at, after(out_sum, qkv_sum), other_core(out_sum),
        [matrix(2, w_down, wanted=False), matrix(2, w_attn_out, wanted=False), matrix(2, w_mix_out), matrix(3, w_gatez)],
    )
    (s_conv, s_step), in_sums = unpack(
        at, after(in_sum, qkv_sum), other_core(in_sum), [matrix(4, w_conv_in, w_step)]
    )
    if four:
        total = small_step(after(total, qkv_sum))
        qkv_sum = sum_four(qkv_sum, s_conv, s_down, total)
    else:
        qkv_sum = sum_z(qkv_sum)
    got = other_core(qkv_sum)
    while hops:
        total = small_step(total)
    (s_query, s_key, s_value), qkv_sums = unpack(at, qkv_sum, got, [matrix(2, w_query), matrix(1, w_key, w_value)])
    total = total.reshape(-1)
    starts = np.cumsum([0] + sizes)
    small = [total[a:b] for a, b in zip(starts[:-1], starts[1:])]

    def own(v):
        n = v.shape[0] // count
        return lax.dynamic_slice(v, (place * n,), (n,))

    s_norm_one = (z_sum + in_sums[0] + in_sums[1] + qkv_sums[0] + qkv_sums[1] + qkv_sums[2]) / own(norm_one)
    s_norm_two = (two_sums[0] + two_sums[1]) / own(norm_two)
    s_gated = gated_sum / own(gated_gain)
    s_skip = jnp.sum(small[2].reshape(SSM_HEADS, SSM_HEAD), 1)
    return (
        output,
        grad_tokens,
        s_norm_one,
        s_query,
        s_key,
        s_value,
        s_gatez,
        s_conv,
        s_step,
        small[0].reshape(taps, -1),
        small[1],
        small[4][:SSM_HEADS],
        small[3][:SSM_HEADS],
        s_skip,
        s_gated,
        s_attn_out,
        s_mix_out,
        s_norm_two,
        s_gate,
        s_up,
        s_down,
    )


def solution(mesh):
    copied = (P(),) * 19
    return jax.shard_map(
        on_device,
        mesh=mesh,
        in_specs=(P("dp", "seq", None), P("dp", "seq", None), P("dp")) + copied,
        out_specs=(
            P("dp", "seq", None), P("dp", "seq", None), P("seq"),
            P("seq", None), P("seq", None), P("seq", None), P("seq", None), P("seq", None), P("seq", None),
            P(), P(), P(), P(), P(),
            P("seq"), P("seq", None), P("seq", None), P("seq"), P("seq", None), P("seq", None), P("seq", None),
        ),
        check_vma=False,
    )
```
